32 devices in a mesh: groups: 2 (over x), bl: 16 (over z, y, core).
Axes of the slice: x: 2, y: 2, z: 4, core: 2. Of those that a mesh axis runs over, the one named last changes fastest.
Arguments:
- visibilities: bfloat16 [4096, 8, 384], P(('groups', 'bl')), parts along dimension 0, may hold values from -6 to 6
- row_owner: int32 [4096, 1], P(('groups', 'bl')), parts along dimension 0, may hold values from 0 to 15; in each aligned block of 128 rows (0 to 127, 128 to 255, ...) at most 16 rows name the same one
- row_slot: int32 [4096], P(('groups', 'bl')), parts along dimension 0, may hold values from 0 to 63
- baseline_station_pairs: int32 [1024, 2], P('bl'), may hold values from 0 to 511
- gains_coarse: float32 [1024, 8, 6], P(('groups', 'bl')), parts along dimension 0, may hold values from -3 to 3
- band_weights: float32 [768, 3], P('groups'), parts along dimension 0, may hold values from 0.2 to 1
- band_offset: int32 [768], P('groups'), parts along dimension 0, may hold values from 0 to 3
Outputs:
- averaged: bfloat16 [2048, 8, 384], P(('groups', 'bl')), parts along dimension 0
The draws below stay inside these ranges and needn't reach their ends.
There are 2 independent parts, one for each index of `groups`. The reference program is written for one: setup_inputs(seed, part) draws one part's arguments, and reference() takes and returns one part's arrays. A program takes and returns all parts, laid end to end along the dimension named above; an argument that names none is the same for every part. Nothing has to cross between parts.
Inputs may be any that keep to these rules, and one draw needn't show every extreme that they name: `row_owner`: among the rows of one device no owner is named by more than 16 rows, a bound that some block reaches.
All inputs are finite; a program needn't handle non-finite values.
Results may differ from the reference program's by a relative error of at most 0.0062.
Values may be sent and summed in bfloat16 or wider, within the bound.
No kernel may reach another device: no remote copies, remote signals or barrier semaphores. Data moves between devices by JAX's collectives and lax.ppermute only.
A program may use at most 64 MiB of HBM per device.

```python
import math
import jax
import jax.numpy as jnp
import numpy as np
from jax import lax

STATION_COUNT = 512
CH = 384
COARSE = 6
ROWS_DEV = 128
BL_DEV = 64
ROWS = 2048
BASELINE_TOTAL = 1024
CAP = 16
N_BL = 16


def draw_gains_coarse(key, part):
    key = jax.random.fold_in(key, 11)
    noise = 0.3 * jax.random.normal(key, (STATION_COUNT, 8, COARSE), jnp.float32)
    diagonal_terms = jnp.zeros((8,), jnp.float32).at[0].set(1.0).at[3].set(1.0)
    return jnp.clip(noise + diagonal_terms[None, :, None], -3.0, 3.0)


def with_ends(values, stream_key, least, high):
    place = [jax.random.randint(jax.random.fold_in(stream_key, axis), (), 0, length) for axis, length in enumerate(values.shape)]
    longest = values.shape.index(max(values.shape))
    neighbour = place[:longest] + [(place[longest] + 1) % values.shape[longest]] + place[longest + 1:]
    return values.at[tuple(place)].set(least).at[tuple(neighbour)].set(high)


def level_of(stream_key, shape, shards, low, top_value):
    factor_of, own = 1.0, jax.random.fold_in(stream_key, 6)
    for axis_at, blocks in shards:
        heights = jnp.exp(jax.random.uniform(jax.random.fold_in(own, axis_at), (blocks,), jnp.float32, low / len(shards), top_value / len(shards)))
        factor_of = factor_of * jnp.repeat(heights, shape[axis_at] // blocks).reshape([-1 if axis == axis_at else 1 for axis in range(len(shape))])
    return factor_of


def routed_block(stream_key, own, number, rows, count, top, reach, lean):
    sequence = jax.random.permutation(stream_key, count)
    crowded, ordinary = shares(count, rows * top, reach, lean, True), shares(count, rows * top, reach, lean, False)
    places = jnp.arange(count)

    def named(lengths, offset_by):
        used = int((lengths > 0).sum())
        fixed = max(1, used // 4)
        moved = fixed + (places - fixed + offset_by * (used - fixed)) % max(1, count - fixed)
        return jnp.zeros((count,), jnp.int32).at[sequence[jnp.where(places < fixed, places, moved)]].set(jnp.asarray(lengths, jnp.int32))

    lengths = jnp.where(number % 4 == 0, named(crowded, number // 4), named(ordinary, number - number // 4 - 1))
    mixed = jax.random.permutation(jax.random.fold_in(own, 3), count)
    source_of, taker = mixed[0:count // 2 * 2:2], mixed[1:count // 2 * 2:2]
    margin = jnp.minimum(lengths[source_of] - 1, reach - lengths[taker]) // 2
    margin = jnp.where((source_of == sequence[0]) | (taker == sequence[0]) | (lengths[taker] == 0), 0, jnp.maximum(margin, 0))
    moved = jax.random.randint(jax.random.fold_in(own, 4), (count // 2,), 0, 1 << 20) % (margin + 1)
    lengths = lengths.at[source_of].add(-moved).at[taker].add(moved)
    members = jnp.searchsorted(jnp.cumsum(lengths), jnp.arange(rows * top), side="right").astype(jnp.int32)
    listing = members.reshape(top, rows).T
    listing = listing[jax.random.permutation(jax.random.fold_in(own, 1), rows)]
    offset_by = jax.random.randint(jax.random.fold_in(own, 2), (rows, 1), 0, top)
    return jnp.take_along_axis(listing, (jnp.arange(top)[None, :] + offset_by) % top, axis=1)


def shares(number_of, total, most, slope, full):
    portions = [(1 << 20) // math.isqrt(rank ** slope) + 1 for rank in range(1, number_of + 1)]
    largest = most if full else min(most, max(-(-total // number_of), total * portions[0] // sum(portions)))
    least = 1 if total - largest >= number_of - 1 else 0
    given, rest = [largest] + [least] * (number_of - 1), total - largest - least * (number_of - 1)
    while rest > 0:
        movable = [i for i in range(1, number_of) if given[i] < largest] or [i for i in range(1, number_of) if given[i] < most]
        mass, left = sum([portions[i] for i in movable]), rest
        for i in movable:
            extra = min(most - given[i], max(1, left * portions[i] // mass), rest)
            given[i] = given[i] + extra
            rest = rest - extra
    return np.array(given)


def scatter_about(stream_key, shape, spread, most, pieces=(), kind=jnp.bfloat16):
    entries = jax.random.normal(stream_key, shape, jnp.float32) * spread
    if len(pieces) > 0:
        entries = level_of(stream_key, shape, pieces, -0.22, 0.18) * entries
    return jnp.clip(entries, min=-most, max=most).astype(kind)


def setup_inputs(seed: int = 0, part: int = 0) -> dict:
    key_list = jax.random.split(jax.random.key(seed), 8)
    part_keys = jax.random.split(jax.random.fold_in(key_list[7], part), 8)
    visibilities = scatter_about(part_keys[0], (ROWS, 8, CH), 1.0, 6.0, ((0, 16),))
    row_owner_keys = jax.random.split(jax.random.fold_in(part_keys[1], 1), ROWS // ROWS_DEV)
    row_owner_turns = jax.random.permutation(jax.random.fold_in(part_keys[1], 3), ROWS // ROWS_DEV)
    row_owner = jax.vmap(lambda own, number: routed_block(jax.random.fold_in(part_keys[1], 2), own, number, ROWS_DEV, N_BL, 1, CAP, 2))(row_owner_keys, row_owner_turns).reshape((ROWS, 1))
    row_slot = with_ends(jax.random.randint(part_keys[2], (ROWS,), 0, BL_DEV), jax.random.fold_in(part_keys[2], 1), 0, BL_DEV - 1).astype(jnp.int32)
    baseline_station_pairs = with_ends(jax.random.randint(key_list[3], (BASELINE_TOTAL, 2), 0, STATION_COUNT), jax.random.fold_in(key_list[3], 1), 0, STATION_COUNT - 1).astype(jnp.int32)
    gains_coarse = draw_gains_coarse(jax.random.fold_in(jax.random.fold_in(key_list[7], part), 71), part)
    band_weights = jnp.clip(jax.random.uniform(part_keys[5], (CH, 3), jnp.float32, 0.2, 1.0), 0.2, 1.0)
    band_offset = with_ends(jax.random.randint(part_keys[6], (CH,), 0, COARSE - 2), jax.random.fold_in(part_keys[6], 1), 0, (COARSE - 2) - 1).astype(jnp.int32)
    return dict(visibilities=visibilities, row_owner=row_owner, row_slot=row_slot, baseline_station_pairs=baseline_station_pairs, gains_coarse=gains_coarse, band_weights=band_weights, band_offset=band_offset)


def spline_basis(band_weights, band_offset, coarse_count):
    knots = jnp.arange(coarse_count, dtype=jnp.int32)
    basis = jnp.zeros((coarse_count, band_weights.shape[0]), jnp.float32)
    for step in range(3):
        match = (knots[:, None] == (band_offset[None, :] + step)).astype(jnp.float32)
        basis = basis + match * band_weights[None, :, step]
    return basis


def interpolate(coarse, basis):
    return jnp.einsum("sjk,kc->sjc", coarse, basis, precision=lax.Precision.HIGHEST).astype(jnp.bfloat16)


def jones(block_vis, left_gain, right_gain):
    vis = block_vis.astype(jnp.float32)
    lhs = left_gain.astype(jnp.float32)
    rhs = right_gain.astype(jnp.float32)
    mid_re = []
    mid_im = []
    for row_a in range(2):
        for col_b in range(2):
            real_part = 0.0
            imag_part = 0.0
            for inner in range(2):
                lr = lhs[:, 2 * row_a + inner]
                li = lhs[:, 4 + 2 * row_a + inner]
                vr = vis[:, 2 * inner + col_b]
                vi = vis[:, 4 + 2 * inner + col_b]
                real_part = real_part + lr * vr - li * vi
                imag_part = imag_part + lr * vi + li * vr
            mid_re.append(real_part)
            mid_im.append(imag_part)
    out_re = []
    out_im = []
    for row_a in range(2):
        for col_b in range(2):
            real_part = 0.0
            imag_part = 0.0
            for inner in range(2):
                mr = mid_re[2 * row_a + inner]
                mi = mid_im[2 * row_a + inner]
                rr = rhs[:, 2 * col_b + inner]
                ri = rhs[:, 4 + 2 * col_b + inner]
                real_part = real_part + mr * rr + mi * ri
                imag_part = imag_part + mi * rr - mr * ri
            out_re.append(real_part)
            out_im.append(imag_part)
    return jnp.stack(out_re + out_im, axis=1).astype(jnp.bfloat16)


def reference(visibilities, row_owner, row_slot, baseline_station_pairs, gains_coarse, band_weights, band_offset):
    basis = spline_basis(band_weights, band_offset, gains_coarse.shape[2])
    table = interpolate(gains_coarse, basis)
    baseline_index = (row_owner[:, 0] * BL_DEV + row_slot).astype(jnp.int32)
    left_idx = baseline_station_pairs[baseline_index, 0]
    right_idx = baseline_station_pairs[baseline_index, 1]
    count = visibilities.shape[0]
    width = math.gcd(count, 1024)
    blocks = count // width

    def accumulate(totals, items):
        block_vis, block_base, left_block, right_block = items
        corrected = jones(block_vis, table[left_block], table[right_block])
        return totals.at[block_base].add(corrected.astype(jnp.float32)), None

    shaped = visibilities.reshape(blocks, width, visibilities.shape[1], visibilities.shape[2])
    start_offset = jnp.zeros((BASELINE_TOTAL, visibilities.shape[1], visibilities.shape[2]), jnp.float32)
    totals, unused = lax.scan(accumulate, start_offset, (shaped, baseline_index.reshape(blocks, width), left_idx.reshape(blocks, width), right_idx.reshape(blocks, width)))
    baseline_count = jax.ops.segment_sum(jnp.ones(baseline_index.shape, jnp.float32), baseline_index, num_segments=BASELINE_TOTAL)
    return (totals / jnp.maximum(baseline_count, 1.0)[:, None, None]).astype(jnp.bfloat16)
```

```python
import functools

import jax
import jax.numpy as jnp
from jax import lax
from jax.experimental import pallas as pl
from jax.experimental.pallas import tpu as pltpu
from jax.sharding import PartitionSpec as P

LANES = 128


def pack_kernel(capacity, owned, owner_s, vis_ref, owner_ref, slot_ref, coarse_ref, send_ref, aux_ref, count_s, turn_ref):
    rows = vis_ref.shape[0]
    devices = send_ref.shape[0] // capacity
    stations = coarse_ref.shape[1]
    half = stations // 2
    terms = coarse_ref.shape[0]
    for d in range(devices):
        count_s[d] = 0

    turn_ref[...] = jnp.zeros_like(turn_ref)
    turn_ref[0:terms, 0:half] = coarse_ref[:, 0:half]
    turn_ref[64 : 64 + terms, 0:half] = coarse_ref[:, half:stations]
    aux_ref[...] = jnp.full(aux_ref.shape, -1.0, jnp.float32)
    aux_ref[0:half, :] = turn_ref[...].T[0:half, :]
    codes = owner_ref[...] * owned + slot_ref[...]
    aux_ref[half : half + 1, 0:rows] = codes.astype(jnp.float32)

    def place(r, carry):
        d = owner_s[r]
        k = count_s[d]
        count_s[d] = k + 1
        send_ref[d * capacity + k] = vis_ref[r]
        return carry

    lax.fori_loop(0, rows, place, 0, unroll=8)


def prep_kernel(
    capacity,
    owned,
    stations,
    me_s,
    pairs_s,
    aux_ref,
    pairs_ref,
    weights_ref,
    offset_ref,
    left_ref,
    right_ref,
    recip_ref,
    slots_ref,
    pick_ref,
):
    devices, aux_rows, width = aux_ref.shape
    half = stations // 2
    channels = weights_ref.shape[1]
    me = me_s[0]
    first = (me * owned).astype(jnp.float32)

    codes = aux_ref[:, half, :] - first
    mine = jnp.logical_and(codes >= 0.0, codes < float(owned))
    mine_f = mine.astype(jnp.float32)
    before = (
        lax.broadcasted_iota(jnp.int32, (width, width), 0)
        < lax.broadcasted_iota(jnp.int32, (width, width), 1)
    ).astype(jnp.float32)
    rank = jnp.dot(mine_f, before, preferred_element_type=jnp.float32)
    lane = lax.broadcasted_iota(jnp.int32, (devices, LANES), 1)
    count = jnp.sum(mine_f, axis=1, keepdims=True)
    listing = jnp.where(lane < capacity, float(owned), 0.0)
    for k in range(capacity):
        here = jnp.logical_and(mine, rank == float(k))
        slot = jnp.sum(jnp.where(here, codes, 0.0), axis=1, keepdims=True)
        slot = jnp.where(count > float(k), slot, float(owned))
        listing = jnp.where(lane == k, slot, listing)
    listing = jnp.where(lane == capacity, count, listing)
    slots_ref[...] = listing.astype(jnp.int32)

    which = lax.broadcasted_iota(jnp.int32, (owned, width), 0).astype(jnp.float32)
    hits = jnp.zeros((owned, width), jnp.float32)
    for d in range(devices):
        hits = hits + (codes[d : d + 1, :] == which).astype(jnp.float32)
    tally = jnp.sum(hits, axis=1, keepdims=True)
    recip_ref[...] = jnp.broadcast_to(1.0 / jnp.maximum(tally, 1.0), recip_ref.shape)

    def pick(b, carry):
        for side in range(2):
            s = pairs_s[side, b]
            d = s // stations
            within = s - d * stations
            row = jnp.where(within >= half, within - half, within)
            pick_ref[pl.ds(side * owned + b, 1), :] = aux_ref[d, pl.ds(row, 1), :]
        return carry

    lax.fori_loop(0, owned, pick, 0, unroll=4)

    knot = lax.broadcasted_iota(jnp.int32, (LANES, channels), 0)
    knot = (knot & 63) >> 3
    basis = jnp.zeros((LANES, channels), jnp.float32)
    for step in range(3):
        basis = basis + jnp.where(
            knot == offset_ref[...] + step, weights_ref[step : step + 1, :], 0.0
        )
    part = lax.broadcasted_iota(jnp.int32, (LANES, channels), 0) & 7
    upper = lax.broadcasted_iota(jnp.int32, (owned, LANES), 1) >= 64
    for side, out in ((0, left_ref), (1, right_ref)):
        within = lax.rem(pairs_ref[:, side : side + 1], stations)
        picked = pick_ref[side * owned : (side + 1) * owned, :]
        picked = jnp.where(upper == (within >= half), picked, 0.0)
        for j in range(8):
            fine = jnp.dot(
                picked,
                jnp.where(part == j, basis, 0.0),
                precision=lax.Precision.HIGHEST,
                preferred_element_type=jnp.float32,
            )
            out[:, j * channels : (j + 1) * channels] = fine.astype(jnp.bfloat16).astype(jnp.float32)


def finish_kernel(capacity, slots_s, recv_ref, left_ref, right_ref, recip_ref, out_ref, acc_ref, res_ref):
    owned, parts, channels = out_ref.shape
    devices = recv_ref.shape[0] // capacity
    chunks = channels // LANES
    step = 4 if capacity % 4 == 0 else 1
    acc_ref[...] = jnp.zeros_like(acc_ref)

    def from_device(d, carry):
        count = slots_s[d, capacity]

        def some(i, inner):
            for u in range(step):
                k = i * step + u
                b = slots_s[d, k]
                row = recv_ref[d * capacity + k].astype(jnp.float32)
                for c in range(chunks):
                    acc_ref[c, b] += row[:, c * LANES : (c + 1) * LANES]
            return inner

        lax.fori_loop(0, (count + (step - 1)) // step, some, 0)
        return carry

    lax.fori_loop(0, devices, from_device, 0)

    flat = acc_ref.reshape(chunks * (owned + 1) * parts, LANES)
    done = res_ref.reshape(chunks * owned * parts, LANES)
    for b0 in range(0, owned, 8):
        for c in range(chunks):
            c0 = c * LANES
            from_row = (c * (owned + 1) + b0) * parts
            to_row = (c * owned + b0) * parts

            def plane(ref, j):
                return ref[b0 : b0 + 8, pl.ds(j * channels + c0, LANES)]

            vis = [flat[pl.ds(from_row + j, 8, stride=parts), :] for j in range(parts)]
            lhs = [plane(left_ref, j) for j in range(parts)]
            rhs = [plane(right_ref, j) for j in range(parts)]
            scale = recip_ref[b0 : b0 + 8, :]
            mid_re, mid_im = [], []
            for row_a in range(2):
                for col_b in range(2):
                    re = im = 0.0
                    for inner in range(2):
                        lr, li = lhs[2 * row_a + inner], lhs[4 + 2 * row_a + inner]
                        vr, vi = vis[2 * inner + col_b], vis[4 + 2 * inner + col_b]
                        re = re + lr * vr - li * vi
                        im = im + lr * vi + li * vr
                    mid_re.append(re * scale)
                    mid_im.append(im * scale)
            for row_a in range(2):
                for col_b in range(2):
                    re = im = 0.0
                    for inner in range(2):
                        mr, mi = mid_re[2 * row_a + inner], mid_im[2 * row_a + inner]
                        rr, ri = rhs[2 * col_b + inner], rhs[4 + 2 * col_b + inner]
                        re = re + mr * rr + mi * ri
                        im = im + mi * rr - mr * ri
                    j = 2 * row_a + col_b
                    done[pl.ds(to_row + j, 8, stride=parts), :] = re
                    done[pl.ds(to_row + 4 + j, 8, stride=parts), :] = im
    for c in range(chunks):
        out_ref[:, :, c * LANES : (c + 1) * LANES] = res_ref[c].astype(out_ref.dtype)


def on_device(
    visibilities,
    row_owner,
    row_slot,
    baseline_station_pairs,
    gains_coarse,
    band_weights,
    band_offset,
):
    devices = lax.axis_size("bl")
    rows, parts, channels = visibilities.shape
    capacity = 2 * rows // devices
    owned = baseline_station_pairs.shape[0]
    stations, _, knots = gains_coarse.shape
    half = stations // 2
    aux_rows = -(-(half + 1) // 8) * 8
    width = -(-rows // LANES) * LANES
    vmem = pl.BlockSpec(memory_space=pltpu.VMEM)
    smem = pl.BlockSpec(memory_space=pltpu.SMEM)
    params = pltpu.CompilerParams(vmem_limit_bytes=32 * 1024 * 1024)
    f32 = jnp.float32

    coarse = gains_coarse.transpose(2, 1, 0).reshape(knots * parts, stations)
    send, aux = pl.pallas_call(
        functools.partial(pack_kernel, capacity, owned),
        out_shape=(
            jax.ShapeDtypeStruct((devices * capacity, parts, channels), jnp.bfloat16),
            jax.ShapeDtypeStruct((aux_rows, width), f32),
        ),
        in_specs=[smem, vmem, vmem, vmem, vmem],
        out_specs=(vmem, vmem),
        scratch_shapes=[pltpu.SMEM((devices,), jnp.int32), pltpu.VMEM((LANES, LANES), f32)],
        compiler_params=params,
        name="pack_rows",
    )(
        row_owner.reshape(rows),
        visibilities,
        row_owner.reshape(1, rows),
        row_slot.reshape(1, rows),
        coarse,
    )
    every = lax.all_gather(aux, "bl", axis=0)
    received = lax.all_to_all(send, "bl", split_axis=0, concat_axis=0, tiled=True)

    me = lax.axis_index("bl").astype(jnp.int32).reshape(1)
    left, right, recip, slots = pl.pallas_call(
        functools.partial(prep_kernel, capacity, owned, stations),
        out_shape=(
            jax.ShapeDtypeStruct((owned, parts * channels), f32),
            jax.ShapeDtypeStruct((owned, parts * channels), f32),
            jax.ShapeDtypeStruct((owned, LANES), f32),
            jax.ShapeDtypeStruct((devices, LANES), jnp.int32),
        ),
        in_specs=[smem, smem, vmem, vmem, vmem, vmem],
        out_specs=(vmem, vmem, vmem, vmem),
        scratch_shapes=[pltpu.VMEM((2 * owned, LANES), f32)],
        compiler_params=params,
        name="gains_and_slots",
    )(
        me,
        baseline_station_pairs.T,
        every,
        baseline_station_pairs,
        band_weights.T,
        band_offset.reshape(1, channels),
    )
    return pl.pallas_call(
        functools.partial(finish_kernel, capacity),
        out_shape=jax.ShapeDtypeStruct((owned, parts, channels), jnp.bfloat16),
        in_specs=[smem, vmem, vmem, vmem, vmem],
        out_specs=vmem,
        scratch_shapes=[
            pltpu.VMEM((channels // LANES, owned + 1, parts, LANES), f32),
            pltpu.VMEM((channels // LANES, owned, parts, LANES), f32),
        ],
        compiler_params=params,
        name="sum_and_apply",
    )(slots, received, left, right, recip)


def solution(mesh):
    placed = (
        P(("groups", "bl"), None, None),
        P(("groups", "bl"), None),
        P(("groups", "bl")),
        P("bl", None),
        P(("groups", "bl"), None, None),
        P("groups", None),
        P("groups"),
    )
    return jax.shard_map(
        on_device,
        mesh=mesh,
        in_specs=placed,
        out_specs=P(("groups", "bl"), None, None),
        check_vma=False,
    )
```

```python
import functools

import jax
import jax.numpy as jnp
from jax import lax
from jax.experimental import pallas as pl
from jax.experimental.pallas import tpu as pltpu
from jax.sharding import PartitionSpec as P

LANES = 128
SUB = 8
SPARE = 48


def round_up(value, unit):
    return -(-value // unit) * unit


def pack_kernel(
    capacity,
    early,
    owned,
    owner_hbm,
    slot_hbm,
    vis_hbm,
    coarse_hbm,
    first_ref,
    second_ref,
    owner_s,
    slot_s,
    count_s,
    vis_ref,
    coarse_ref,
    turn_ref,
    slots_ref,
    sems,
):
    rows = vis_ref.shape[0]
    devices, meta, _ = slots_ref.shape
    chunks = vis_ref.shape[2] // LANES
    terms, stations = coarse_ref.shape
    half = stations // 2
    moves = [
        pltpu.make_async_copy(src, dst, sems.at[i])
        for i, (src, dst) in enumerate(
            (
                (vis_hbm, vis_ref),
                (coarse_hbm, coarse_ref),
                (owner_hbm, owner_s),
                (slot_hbm, slot_s),
            )
        )
    ]
    for move in moves:
        move.start()
    slots_ref[...] = jnp.full(slots_ref.shape, float(owned), jnp.float32)
    turn_ref[...] = jnp.zeros_like(turn_ref)
    for d in range(devices):
        count_s[d] = 0
    for move in moves[1:]:
        move.wait()

    turn_ref[0:terms, 0:half] = coarse_ref[:, 0:half]
    turn_ref[64 : 64 + terms, 0:half] = coarse_ref[:, half:stations]
    gains = turn_ref[...].T[0:meta, :]
    low = (gains - gains.astype(jnp.bfloat16).astype(jnp.float32)).astype(jnp.bfloat16)
    moves[0].wait()

    def place(r, carry):
        d = owner_s[r]
        k = count_s[d]
        count_s[d] = k + 1
        slots_ref[d, pl.ds(k, 1), :] = jnp.full((1, LANES), slot_s[r].astype(jnp.float32))

        @pl.when(k < early)
        def _():
            for c in range(chunks):
                first_ref[d, chunks * k + c] = vis_ref[r, :, c * LANES : (c + 1) * LANES]

        @pl.when(k >= early)
        def _():
            for c in range(chunks):
                second_ref[d, chunks * (k - early) + c] = vis_ref[r, :, c * LANES : (c + 1) * LANES]

        return carry

    lax.fori_loop(0, rows, place, 0, unroll=4)

    lane = lax.broadcasted_iota(jnp.int32, (meta, LANES), 1)
    spare = jnp.logical_and(lane >= SPARE, lane < 64)
    at = chunks * early
    for d in range(devices):
        high = jnp.where(spare, slots_ref[d], gains).astype(jnp.bfloat16)
        for i in range(meta // SUB):
            first_ref[d, at + i] = high[i * SUB : (i + 1) * SUB, :]
            first_ref[d, at + meta // SUB + i] = low[i * SUB : (i + 1) * SUB, :]


def add_rows(chunks, start, stop, base, d, slots_s, recv_ref, acc_ref):
    def add(k, carry):
        b = slots_s[d, k]
        for c in range(chunks):
            acc_ref[c, b] += recv_ref[d, chunks * (k - base) + c].astype(jnp.float32)
        return carry

    lax.fori_loop(start, stop, add, 0)


def early_kernel(
    capacity,
    early,
    owned,
    stations,
    pairs_s,
    recv_ref,
    pairs_ref,
    weights_ref,
    offset_ref,
    left_ref,
    right_ref,
    recip_ref,
    slots_ref,
    acc_ref,
    table_ref,
    pick_ref,
    slots_s,
    sem,
):
    devices = recv_ref.shape[0]
    half = stations // 2
    channels = weights_ref.shape[1]
    chunks = channels // LANES
    at = chunks * early
    tiles = (recv_ref.shape[1] - at) // 2
    meta = tiles * SUB

    sub = lax.broadcasted_iota(jnp.int32, (meta, LANES), 0)
    lane = lax.broadcasted_iota(jnp.int32, (meta, LANES), 1)
    lane_f = lane.astype(jnp.float32)
    hits = jnp.zeros((meta, LANES), jnp.float32)
    for d in range(devices):
        high = jnp.concatenate([recv_ref[d, at + i] for i in range(tiles)], axis=0).astype(jnp.float32)
        low = jnp.concatenate([recv_ref[d, at + tiles + i] for i in range(tiles)], axis=0).astype(jnp.float32)
        table_ref[d] = high + low
        slot = jnp.broadcast_to(high[:, SPARE : SPARE + 1], (meta, LANES))
        inside = jnp.logical_and(sub < capacity, slot < float(owned))
        hits = hits + jnp.where(jnp.logical_and(inside, slot == lane_f), 1.0, 0.0)
        line = jnp.sum(jnp.where(lane == sub, slot, 0.0), axis=0, keepdims=True)
        count = jnp.sum(inside.astype(jnp.float32), axis=0, keepdims=True)
        line = jnp.where(lane[0:1, :] == capacity, count, line)
        slots_ref[d : d + 1, :] = line.astype(jnp.int32)
    move = pltpu.make_async_copy(slots_ref, slots_s, sem)
    move.start()

    tally = jnp.broadcast_to(jnp.sum(hits, axis=0, keepdims=True), (owned, LANES))
    own = lax.broadcasted_iota(jnp.int32, (owned, LANES), 0) == lax.broadcasted_iota(
        jnp.int32, (owned, LANES), 1
    )
    tally = jnp.sum(jnp.where(own, tally, 0.0), axis=1, keepdims=True)
    recip_ref[...] = jnp.broadcast_to(1.0 / jnp.maximum(tally, 1.0), recip_ref.shape)

    acc_ref[...] = jnp.zeros_like(acc_ref)
    move.wait()

    def from_device(d, carry):
        stop = jnp.minimum(slots_s[d, capacity], early)
        add_rows(chunks, 0, stop, 0, d, slots_s, recv_ref, acc_ref)
        return carry

    lax.fori_loop(0, devices, from_device, 0)

    def pick(b, carry):
        for side in range(2):
            s = pairs_s[side, b]
            d = s // stations
            within = s - d * stations
            row = jnp.where(within >= half, within - half, within)
            pick_ref[pl.ds(side * owned + b, 1), :] = table_ref[d, pl.ds(row, 1), :]
        return carry

    lax.fori_loop(0, owned, pick, 0, unroll=4)

    knot = lax.broadcasted_iota(jnp.int32, (LANES, channels), 0)
    knot = (knot & 63) >> 3
    basis = jnp.zeros((LANES, channels), jnp.float32)
    for step in range(3):
        basis = basis + jnp.where(
            knot == offset_ref[...] + step, weights_ref[step : step + 1, :], 0.0
        )
    part = lax.broadcasted_iota(jnp.int32, (LANES, channels), 0) & 7
    column = lax.broadcasted_iota(jnp.int32, (owned, LANES), 1)
    used = (column & 63) < SPARE
    for side, out in ((0, left_ref), (1, right_ref)):
        within = lax.rem(pairs_ref[:, side : side + 1], stations)
        mine = jnp.logical_and(used, (column >= 64) == (within >= half))
        picked = jnp.where(mine, pick_ref[side * owned : (side + 1) * owned, :], 0.0)
        for j in range(8):
            fine = jnp.dot(
                picked,
                jnp.where(part == j, basis, 0.0),
                precision=lax.Precision.HIGHEST,
                preferred_element_type=jnp.float32,
            )
            out[:, j * channels : (j + 1) * channels] = fine.astype(jnp.bfloat16).astype(jnp.float32)


def finish_kernel(
    capacity, early, slots_s, recv_ref, sums_ref, left_ref, right_ref, recip_ref, out_ref, acc_ref, res_ref
):
    owned, parts, channels = out_ref.shape
    devices = recv_ref.shape[0]
    chunks = channels // LANES
    acc_ref[...] = sums_ref[...]

    def from_device(d, carry):
        add_rows(chunks, early, slots_s[d, capacity], early, d, slots_s, recv_ref, acc_ref)
        return carry

    lax.fori_loop(0, devices, from_device, 0)

    flat = acc_ref.reshape(chunks * owned * parts, LANES)
    done = res_ref.reshape(chunks * owned * parts, LANES)
    for b0 in range(0, owned, SUB):
        for c in range(chunks):
            row = (c * owned + b0) * parts

            def plane(ref, j):
                return ref[b0 : b0 + SUB, pl.ds(j * channels + c * LANES, LANES)]

            vis = [flat[pl.ds(row + j, SUB, stride=parts), :] for j in range(parts)]
            lhs = [plane(left_ref, j) for j in range(parts)]
            rhs = [plane(right_ref, j) for j in range(parts)]
            scale = recip_ref[b0 : b0 + SUB, :]
            mid_re, mid_im = [], []
            for row_a in range(2):
                for col_b in range(2):
                    re = im = 0.0
                    for inner in range(2):
                        lr, li = lhs[2 * row_a + inner], lhs[4 + 2 * row_a + inner]
                        vr, vi = vis[2 * inner + col_b], vis[4 + 2 * inner + col_b]
                        re = re + lr * vr - li * vi
                        im = im + lr * vi + li * vr
                    mid_re.append(re * scale)
                    mid_im.append(im * scale)
            for row_a in range(2):
                for col_b in range(2):
                    re = im = 0.0
                    for inner in range(2):
                        mr, mi = mid_re[2 * row_a + inner], mid_im[2 * row_a + inner]
                        rr, ri = rhs[2 * col_b + inner], rhs[4 + 2 * col_b + inner]
                        re = re + mr * rr + mi * ri
                        im = im + mi * rr - mr * ri
                    j = 2 * row_a + col_b
                    done[pl.ds(row + j, SUB, stride=parts), :] = re
                    done[pl.ds(row + 4 + j, SUB, stride=parts), :] = im
    for c in range(chunks):
        out_ref[:, :, c * LANES : (c + 1) * LANES] = res_ref[c].astype(out_ref.dtype)


def on_device(
    visibilities,
    row_owner,
    row_slot,
    baseline_station_pairs,
    gains_coarse,
    band_weights,
    band_offset,
):
    devices = lax.axis_size("bl")
    rows, parts, channels = visibilities.shape
    capacity = 2 * rows // devices
    early = capacity // 2
    owned = baseline_station_pairs.shape[0]
    stations, _, knots = gains_coarse.shape
    chunks = channels // LANES
    meta = round_up(max(stations // 2, capacity), SUB)
    vmem = pl.BlockSpec(memory_space=pltpu.VMEM)
    smem = pl.BlockSpec(memory_space=pltpu.SMEM)
    hbm = pl.BlockSpec(memory_space=pltpu.HBM)
    params = pltpu.CompilerParams(vmem_limit_bytes=32 * 1024 * 1024)
    f32, bf16, i32 = jnp.float32, jnp.bfloat16, jnp.int32

    coarse = gains_coarse.transpose(2, 1, 0).reshape(knots * parts, stations)
    first, second = pl.pallas_call(
        functools.partial(pack_kernel, capacity, early, owned),
        out_shape=(
            jax.ShapeDtypeStruct((devices, chunks * early + 2 * meta // SUB, parts, LANES), bf16),
            jax.ShapeDtypeStruct((devices, chunks * (capacity - early), parts, LANES), bf16),
        ),
        in_specs=[hbm] * 4,
        out_specs=(vmem, vmem),
        scratch_shapes=[
            pltpu.SMEM((rows,), i32),
            pltpu.SMEM((rows,), i32),
            pltpu.SMEM((devices,), i32),
            pltpu.VMEM((rows, parts, channels), bf16),
            pltpu.VMEM((knots * parts, stations), f32),
            pltpu.VMEM((LANES, LANES), f32),
            pltpu.VMEM((devices, meta, LANES), f32),
            pltpu.SemaphoreType.DMA((4,)),
        ],
        compiler_params=params,
        name="pack_rows",
    )(row_owner.reshape(rows), row_slot, visibilities, coarse)
    first = lax.all_to_all(first, "bl", split_axis=0, concat_axis=0, tiled=True)
    second = lax.all_to_all(second, "bl", split_axis=0, concat_axis=0, tiled=True)

    left, right, recip, slots, sums = pl.pallas_call(
        functools.partial(early_kernel, capacity, early, owned, stations),
        out_shape=(
            jax.ShapeDtypeStruct((owned, parts * channels), f32),
            jax.ShapeDtypeStruct((owned, parts * channels), f32),
            jax.ShapeDtypeStruct((owned, LANES), f32),
            jax.ShapeDtypeStruct((devices, LANES), i32),
            jax.ShapeDtypeStruct((chunks, owned, parts, LANES), f32),
        ),
        in_specs=[smem, vmem, vmem, vmem, vmem],
        out_specs=(vmem,) * 5,
        scratch_shapes=[
            pltpu.VMEM((devices, meta, LANES), f32),
            pltpu.VMEM((2 * owned, LANES), f32),
            pltpu.SMEM((devices, LANES), i32),
            pltpu.SemaphoreType.DMA,
        ],
        compiler_params=params,
        name="gains_and_early_sums",
    )(
        baseline_station_pairs.T,
        first,
        baseline_station_pairs,
        band_weights.T,
        band_offset.reshape(1, channels),
    )
    return pl.pallas_call(
        functools.partial(finish_kernel, capacity, early),
        out_shape=jax.ShapeDtypeStruct((owned, parts, channels), bf16),
        in_specs=[smem, vmem, vmem, vmem, vmem, vmem],
        out_specs=vmem,
        scratch_shapes=[
            pltpu.VMEM((chunks, owned, parts, LANES), f32),
            pltpu.VMEM((chunks, owned, parts, LANES), f32),
        ],
        compiler_params=params,
        name="late_sums_and_gains",
    )(slots, second, sums, left, right, recip)


def solution(mesh):
    placed = (
        P(("groups", "bl"), None, None),
        P(("groups", "bl"), None),
        P(("groups", "bl")),
        P("bl", None),
        P(("groups", "bl"), None, None),
        P("groups", None),
        P("groups"),
    )
    return jax.shard_map(
        on_device,
        mesh=mesh,
        in_specs=placed,
        out_specs=P(("groups", "bl"), None, None),
        check_vma=False,
    )
```

```python
import functools

import jax
import jax.numpy as jnp
from jax import lax
from jax.experimental import pallas as pl
from jax.experimental.pallas import tpu as pltpu
from jax.sharding import PartitionSpec as P

LANES = 128
SUB = 8
SPARE = 48
NO_ROW = 128
VMEM_BYTES = 60 * 1024 * 1024


def round_up(value, unit):
    return -(-value // unit) * unit


def pack_kernel(
    capacity,
    owned,
    me_s,
    owner_hbm,
    slot_hbm,
    vis_hbm,
    coarse_hbm,
    *rest,
):
    outs, (owner_s, slot_s, count_s, vis_ref, coarse_ref, turn_ref, slots_ref, block_ref, sems) = rest[:-9], rest[-9:]
    rows = vis_ref.shape[0]
    devices, meta, _ = slots_ref.shape
    chunks = vis_ref.shape[2] // LANES
    terms, stations = coarse_ref.shape
    half = stations // 2
    moves = [
        pltpu.make_async_copy(src, dst, sems.at[i])
        for i, (src, dst) in enumerate(
            (
                (vis_hbm, vis_ref),
                (coarse_hbm, coarse_ref),
                (owner_hbm, owner_s),
                (slot_hbm, slot_s),
            )
        )
    ]
    for move in moves:
        move.start()
    slots_ref[...] = jnp.full(slots_ref.shape, float(NO_ROW), jnp.float32)
    turn_ref[...] = jnp.zeros_like(turn_ref)
    for d in range(devices):
        count_s[d] = 0
    for move in moves[1:]:
        move.wait()

    turn_ref[0:terms, 0:half] = coarse_ref[:, 0:half]
    turn_ref[64 : 64 + terms, 0:half] = coarse_ref[:, half:stations]
    gains = turn_ref[...].T[0:meta, :]
    low = (gains - gains.astype(jnp.bfloat16).astype(jnp.float32)).astype(jnp.bfloat16)
    me = me_s[0]
    moves[0].wait()

    def place(r, carry):
        m = owner_s[r] ^ me
        k = count_s[m]
        count_s[m] = k + 1
        slots_ref[m, pl.ds(k, 1), :] = jnp.full((1, LANES), slot_s[r].astype(jnp.float32))
        for c in range(chunks):
            block_ref[m, chunks * k + c] = vis_ref[r, :, c * LANES : (c + 1) * LANES]
        return carry

    lax.fori_loop(0, rows, place, 0, unroll=8)

    lane = lax.broadcasted_iota(jnp.int32, (meta, LANES), 1)
    spare = jnp.logical_and(lane >= SPARE, lane < 64)
    at = chunks * capacity
    sends = []
    for m in range(devices):
        high = jnp.where(spare, slots_ref[m], gains).astype(jnp.bfloat16)
        for i in range(meta // SUB):
            block_ref[m, at + i] = high[i * SUB : (i + 1) * SUB, :]
            block_ref[m, at + meta // SUB + i] = low[i * SUB : (i + 1) * SUB, :]
        if len(outs) > 1:
            sends.append(pltpu.make_async_copy(block_ref.at[m], outs[m], sems.at[4 + m]))
            sends[-1].start()
    if len(outs) == 1:
        sends.append(pltpu.make_async_copy(block_ref, outs[0], sems.at[4]))
        sends[-1].start()
    for send in sends:
        send.wait()


def finish_kernel(capacity, stations, me_s, pairs_s, pairs_ref, weights_ref, offset_ref, *rest):
    (out_ref, recv_ref, table_ref, pick_ref, gains_ref, slots_ref, slots_s, acc_ref, res_ref, sems) = rest[-10:]
    blocks = rest[:-10]
    owned, parts, channels = out_ref.shape
    devices = recv_ref.shape[0]
    half = stations // 2
    chunks = channels // LANES
    at = chunks * capacity
    tiles = (recv_ref.shape[1] - at) // 2
    meta = tiles * SUB
    me = me_s[0]
    if len(blocks) == 1:
        moves = [pltpu.make_async_copy(blocks[0], recv_ref, sems.at[0])]
    else:
        moves = [pltpu.make_async_copy(b, recv_ref.at[i], sems.at[i]) for i, b in enumerate(blocks)]
    for move in moves:
        move.start()
    acc_ref[...] = jnp.zeros_like(acc_ref)
    for move in moves:
        move.wait()

    sub = lax.broadcasted_iota(jnp.int32, (meta, LANES), 0)
    lane = lax.broadcasted_iota(jnp.int32, (meta, LANES), 1)
    lane_f = lane.astype(jnp.float32)
    hits = jnp.zeros((meta, LANES), jnp.float32)
    for d in range(devices):
        high = jnp.concatenate([recv_ref[d, at + i] for i in range(tiles)], axis=0).astype(jnp.float32)
        low = jnp.concatenate([recv_ref[d, at + tiles + i] for i in range(tiles)], axis=0).astype(jnp.float32)
        table_ref[d] = high + low
        slot = jnp.broadcast_to(high[:, SPARE : SPARE + 1], (meta, LANES))
        inside = jnp.logical_and(sub < capacity, slot < float(NO_ROW))
        hits = hits + jnp.where(jnp.logical_and(inside, slot == lane_f), 1.0, 0.0)
        line = jnp.sum(jnp.where(lane == sub, slot, 0.0), axis=0, keepdims=True)
        count = jnp.sum(inside.astype(jnp.float32), axis=0, keepdims=True)
        line = jnp.where(lane[0:1, :] == capacity, count, line)
        slots_ref[d : d + 1, :] = line.astype(jnp.int32)
    move = pltpu.make_async_copy(slots_ref, slots_s, sems.at[0])
    move.start()

    tally = jnp.broadcast_to(jnp.sum(hits, axis=0, keepdims=True), (owned, LANES))
    own = lax.broadcasted_iota(jnp.int32, (owned, LANES), 0) == lax.broadcasted_iota(
        jnp.int32, (owned, LANES), 1
    )
    tally = jnp.sum(jnp.where(own, tally, 0.0), axis=1, keepdims=True)
    recip = jnp.broadcast_to(1.0 / jnp.maximum(tally, 1.0), (owned, LANES))

    def pick(b, carry):
        for side in range(2):
            s = pairs_s[side, b]
            d = s // stations
            within = s - d * stations
            row = jnp.where(within >= half, within - half, within)
            pick_ref[pl.ds(side * owned + b, 1), :] = table_ref[d ^ me, pl.ds(row, 1), :]
        return carry

    lax.fori_loop(0, owned, pick, 0, unroll=4)

    knot = lax.broadcasted_iota(jnp.int32, (LANES, channels), 0)
    knot = (knot & 63) >> 3
    basis = jnp.zeros((LANES, channels), jnp.float32)
    for step in range(3):
        basis = basis + jnp.where(
            knot == offset_ref[...] + step, weights_ref[step : step + 1, :], 0.0
        )
    part = lax.broadcasted_iota(jnp.int32, (LANES, channels), 0) & 7
    column = lax.broadcasted_iota(jnp.int32, (owned, LANES), 1)
    used = (column & 63) < SPARE
    picked = []
    for side in range(2):
        within = lax.rem(pairs_ref[:, side : side + 1], stations)
        mine = jnp.logical_and(used, (column >= 64) == (within >= half))
        picked.append(jnp.where(mine, pick_ref[side * owned : (side + 1) * owned, :], 0.0))
    both = jnp.concatenate(picked, axis=0)
    both_high = both.astype(jnp.bfloat16)
    both_low = (both - both_high.astype(jnp.float32)).astype(jnp.bfloat16)
    both_two = jnp.concatenate([both_high, both_low], axis=1)
    for j in range(8):
        there = jnp.where(part == j, basis, 0.0)
        high = there.astype(jnp.bfloat16)
        low = (there - high.astype(jnp.float32)).astype(jnp.bfloat16)
        fine = jnp.dot(
            both_two, jnp.concatenate([high, high], axis=0), preferred_element_type=jnp.float32
        ) + jnp.dot(both_high, low, preferred_element_type=jnp.float32)
        gains_ref[j] = fine.astype(jnp.bfloat16).astype(jnp.float32)

    move.wait()

    def from_device(d, carry):
        def add(k, inner):
            b = slots_s[d, k]
            for c in range(chunks):
                acc_ref[c, b] += recv_ref[d, chunks * k + c].astype(jnp.float32)
            return inner

        lax.fori_loop(0, slots_s[d, capacity], add, 0)
        return carry

    lax.fori_loop(0, devices, from_device, 0)

    flat = acc_ref.reshape(chunks * owned * parts, LANES)
    done = res_ref.reshape(chunks * owned * parts, LANES)
    for b0 in range(0, owned, SUB):
        scale = recip[b0 : b0 + SUB, :]
        for c in range(chunks):
            row = (c * owned + b0) * parts
            cols = slice(c * LANES, (c + 1) * LANES)
            vis = [flat[pl.ds(row + j, SUB, stride=parts), :] for j in range(parts)]
            lhs = [gains_ref[j, b0 : b0 + SUB, cols] for j in range(parts)]
            rhs = [gains_ref[j, owned + b0 : owned + b0 + SUB, cols] for j in range(parts)]
            mid_re, mid_im = [], []
            for row_a in range(2):
                for col_b in range(2):
                    re = im = 0.0
                    for inner in range(2):
                        lr, li = lhs[2 * row_a + inner], lhs[4 + 2 * row_a + inner]
                        vr, vi = vis[2 * inner + col_b], vis[4 + 2 * inner + col_b]
                        re = re + lr * vr - li * vi
                        im = im + lr * vi + li * vr
                    mid_re.append(re * scale)
                    mid_im.append(im * scale)
            for row_a in range(2):
                for col_b in range(2):
                    re = im = 0.0
                    for inner in range(2):
                        mr, mi = mid_re[2 * row_a + inner], mid_im[2 * row_a + inner]
                        rr, ri = rhs[2 * col_b + inner], rhs[4 + 2 * col_b + inner]
                        re = re + mr * rr + mi * ri
                        im = im + mi * rr - mr * ri
                    j = 2 * row_a + col_b
                    done[pl.ds(row + j, SUB, stride=parts), :] = re
                    done[pl.ds(row + 4 + j, SUB, stride=parts), :] = im
    for c in range(chunks):
        out_ref[:, :, c * LANES : (c + 1) * LANES] = res_ref[c].astype(out_ref.dtype)


def on_device(
    visibilities,
    row_owner,
    row_slot,
    baseline_station_pairs,
    gains_coarse,
    band_weights,
    band_offset,
):
    devices = lax.axis_size("bl")
    rows, parts, channels = visibilities.shape
    capacity = 2 * rows // devices
    owned = baseline_station_pairs.shape[0]
    stations, _, knots = gains_coarse.shape
    chunks = channels // LANES
    meta = round_up(max(stations // 2, capacity), SUB)
    depth = chunks * capacity + 2 * meta // SUB
    pairwise = devices <= 16
    count = devices if pairwise else 1
    vmem = pl.BlockSpec(memory_space=pltpu.VMEM)
    smem = pl.BlockSpec(memory_space=pltpu.SMEM)
    hbm = pl.BlockSpec(memory_space=pltpu.HBM)
    anywhere = pl.BlockSpec(memory_space=pl.ANY)
    params = pltpu.CompilerParams(vmem_limit_bytes=VMEM_BYTES)
    f32, bf16, i32 = jnp.float32, jnp.bfloat16, jnp.int32

    me = lax.axis_index("bl").astype(i32)
    turn = (me if pairwise else jnp.zeros_like(me)).reshape(1)
    coarse = gains_coarse.transpose(2, 1, 0).reshape(knots * parts, stations)
    block = (depth, parts, LANES)
    blocks = pl.pallas_call(
        functools.partial(pack_kernel, capacity, owned),
        out_shape=[jax.ShapeDtypeStruct(block if pairwise else (devices,) + block, bf16)] * count,
        in_specs=[smem] + [hbm] * 4,
        out_specs=[hbm] * count,
        scratch_shapes=[
            pltpu.SMEM((rows,), i32),
            pltpu.SMEM((rows,), i32),
            pltpu.SMEM((devices,), i32),
            pltpu.VMEM((rows, parts, channels), bf16),
            pltpu.VMEM((knots * parts, stations), f32),
            pltpu.VMEM((LANES, LANES), f32),
            pltpu.VMEM((devices, meta, LANES), f32),
            pltpu.VMEM((devices,) + block, bf16),
            pltpu.SemaphoreType.DMA((4 + count,)),
        ],
        compiler_params=params,
        name="pack_rows",
    )(turn, row_owner.reshape(rows), row_slot, visibilities, coarse)
    if pairwise:
        arrived = list(blocks)
        for m in list(range(devices // 2, devices)) + list(range(1, devices // 2)):
            arrived[m] = lax.ppermute(blocks[m], "bl", [(d, d ^ m) for d in range(devices)])
    else:
        arrived = [lax.all_to_all(blocks[0], "bl", split_axis=0, concat_axis=0, tiled=True)]

    return pl.pallas_call(
        functools.partial(finish_kernel, capacity, stations),
        out_shape=jax.ShapeDtypeStruct((owned, parts, channels), bf16),
        in_specs=[smem, smem, vmem, vmem, vmem] + [anywhere] * count,
        out_specs=vmem,
        scratch_shapes=[
            pltpu.VMEM((devices,) + block, bf16),
            pltpu.VMEM((devices, meta, LANES), f32),
            pltpu.VMEM((2 * owned, LANES), f32),
            pltpu.VMEM((parts, 2 * owned, channels), f32),
            pltpu.VMEM((devices, LANES), i32),
            pltpu.SMEM((devices, LANES), i32),
            pltpu.VMEM((chunks, owned, parts, LANES), f32),
            pltpu.VMEM((chunks, owned, parts, LANES), f32),
            pltpu.SemaphoreType.DMA((count,)),
        ],
        compiler_params=pltpu.CompilerParams(vmem_limit_bytes=VMEM_BYTES // 2),
        name="sum_and_apply",
    )(
        turn,
        baseline_station_pairs.T,
        baseline_station_pairs,
        band_weights.T,
        band_offset.reshape(1, channels),
        *arrived,
    )


def solution(mesh):
    placed = (
        P(("groups", "bl"), None, None),
        P(("groups", "bl"), None),
        P(("groups", "bl")),
        P("bl", None),
        P(("groups", "bl"), None, None),
        P("groups", None),
        P("groups"),
    )
    return jax.shard_map(
        on_device,
        mesh=mesh,
        in_specs=placed,
        out_specs=P(("groups", "bl"), None, None),
        check_vma=False,
    )
```

```python
import functools

import jax
import jax.numpy as jnp
from jax import lax
from jax.experimental import pallas as pl
from jax.experimental.pallas import tpu as pltpu
from jax.sharding import PartitionSpec as P

LANES = 128
SUB = 8
USED = 48
ALL_VMEM = 60 * 1024 * 1024
SOME_VMEM = 24 * 1024 * 1024


def round_up(value, unit):
    return -(-value // unit) * unit


def start_all(pairs, sems):
    moves = [pltpu.make_async_copy(src, dst, sems.at[i]) for i, (src, dst) in enumerate(pairs)]
    for move in moves:
        move.start()
    return moves


def pack_kernel(
    capacity,
    tiles,
    owner_hbm,
    owner_row_hbm,
    slot_row_hbm,
    vis_hbm,
    coarse_hbm,
    direct_ref,
    meta_ref,
    owner_s,
    count_s,
    owner_ref,
    slot_ref,
    vis_ref,
    coarse_ref,
    turn_ref,
    sems,
):
    rows = vis_ref.shape[0]
    devices = direct_ref.shape[0]
    terms, stations = coarse_ref.shape
    half = stations // 2
    gain_tiles = (meta_ref.shape[0] - 1) // 2
    moves = start_all(
        (
            (vis_hbm.at[:, :, pl.ds(0, tiles * LANES)], vis_ref),
            (coarse_hbm, coarse_ref),
            (owner_hbm, owner_s),
            (owner_row_hbm, owner_ref),
            (slot_row_hbm, slot_ref),
        ),
        sems,
    )
    turn_ref[...] = jnp.zeros_like(turn_ref)
    for d in range(devices):
        count_s[d] = 0
    for move in moves[1:]:
        move.wait()

    turn_ref[0:terms, 0:half] = coarse_ref[:, 0:half]
    turn_ref[64 : 64 + terms, 0:half] = coarse_ref[:, half:stations]
    gains = turn_ref[...].T
    high = gains.astype(jnp.bfloat16)
    low = (gains - high.astype(jnp.float32)).astype(jnp.bfloat16)
    for i in range(gain_tiles):
        meta_ref[i] = high[i * SUB : (i + 1) * SUB, :]
        meta_ref[gain_tiles + i] = low[i * SUB : (i + 1) * SUB, :]
    sub = lax.broadcasted_iota(jnp.int32, (SUB, LANES), 0)
    codes = jnp.where(sub == 0, owner_ref[...], slot_ref[...])
    meta_ref[2 * gain_tiles] = codes.astype(jnp.float32).astype(jnp.bfloat16)
    moves[0].wait()

    def place(r, carry):
        d = owner_s[r]
        k = count_s[d]
        count_s[d] = k + 1
        for c in range(tiles):
            direct_ref[d, tiles * k + c] = vis_ref[r, :, c * LANES : (c + 1) * LANES]
        return carry

    lax.fori_loop(0, rows, place, 0, unroll=8)


def pack_shared_kernel(capacity, tiles, me_s, owner_hbm, vis_hbm, meta_hbm, partner_hbm, *rest):
    outs = rest[:-7]
    owner_s, count_s, vis_ref, meta_ref, partner_ref, block_ref, sems = rest[-7:]
    rows = vis_ref.shape[0]
    shared = vis_ref.shape[2] // LANES
    near = block_ref.shape[0]
    depth = meta_ref.shape[0]
    at = 2 * capacity * shared
    moves = start_all(
        (
            (vis_hbm.at[:, :, pl.ds(tiles * LANES, shared * LANES)], vis_ref),
            (owner_hbm, owner_s),
            (meta_hbm, meta_ref),
            (partner_hbm, partner_ref),
        ),
        sems,
    )
    for x in range(2 * near):
        count_s[x] = 0
    me = me_s[0]
    for move in moves[1:]:
        move.wait()
    for m in range(near):
        for i in range(depth):
            block_ref[m, at + i] = meta_ref[i]
            block_ref[m, at + depth + i] = partner_ref[i]
    moves[0].wait()

    def place(r, carry):
        x = owner_s[r] ^ me
        k = count_s[x]
        count_s[x] = k + 1
        far = jnp.where(x >= near, 1, 0)
        for c in range(shared):
            block_ref[x - far * near, (far * capacity + k) * shared + c] = vis_ref[
                r, :, c * LANES : (c + 1) * LANES
            ]
        return carry

    lax.fori_loop(0, rows, place, 0, unroll=8)
    sends = start_all([(block_ref.at[m], outs[m]) for m in range(near)], sems)
    for send in sends:
        send.wait()


def list_rows(owner, slot, target, capacity):
    senders = owner.shape[0]
    mine = owner == target
    counted = mine.astype(jnp.float32)
    before = lax.broadcasted_iota(jnp.int32, (LANES, LANES), 0) < lax.broadcasted_iota(
        jnp.int32, (LANES, LANES), 1
    )
    rank = jnp.dot(
        counted.astype(jnp.bfloat16),
        before.astype(jnp.float32).astype(jnp.bfloat16),
        preferred_element_type=jnp.float32,
    )
    lane = lax.broadcasted_iota(jnp.int32, (senders, LANES), 1)
    count = jnp.sum(counted, axis=1, keepdims=True)
    listing = jnp.where(lane == capacity, count, 0.0)
    for k in range(capacity):
        here = jnp.logical_and(mine, rank == float(k))
        kth = jnp.sum(jnp.where(here, slot, 0.0), axis=1, keepdims=True)
        listing = jnp.where(lane == k, kth, listing)
    return listing.astype(jnp.int32), mine


def add_rows(acc_ref, first_tile, slots_s, line, capacity, rows_ref, block, tiles):
    def add(k, carry):
        b = slots_s[line, k]
        for c in range(tiles):
            acc_ref[first_tile + c, b] += rows_ref[block, tiles * k + c].astype(jnp.float32)
        return carry

    lax.fori_loop(0, slots_s[line, capacity], add, 0)


def helper_kernel(capacity, shared, me_s, *rest):
    blocks = rest[:-7]
    out_ref, rows_ref, codes_ref, acc_ref, slots_ref, slots_s, sems = rest[-7:]
    near = rows_ref.shape[0]
    depth = (blocks[0].shape[0] - 2 * capacity * shared) // 2
    code_at = 2 * capacity * shared + depth - 1
    part = capacity * shared
    moves = start_all(
        [(blocks[m].at[code_at], codes_ref.at[m]) for m in range(near)]
        + [(blocks[m].at[pl.ds(part, part)], rows_ref.at[m]) for m in range(near)],
        sems,
    )
    for c in range(shared):
        acc_ref[c] = jnp.zeros_like(acc_ref[c])
    for move in moves[:near]:
        move.wait()
    codes = [codes_ref[m].astype(jnp.float32) for m in range(near)]
    owner = jnp.concatenate([c[0:1, :] for c in codes], axis=0)
    slot = jnp.concatenate([c[1:2, :] for c in codes], axis=0)
    target = (me_s[0] ^ near).astype(jnp.float32)
    slots_ref[...], _ = list_rows(owner, slot, target, capacity)
    move = pltpu.make_async_copy(slots_ref, slots_s, sems.at[0])
    move.start()
    for other in moves[near:]:
        other.wait()
    move.wait()
    for m in range(near):
        add_rows(acc_ref, 0, slots_s, m, capacity, rows_ref, m, shared)
    for c in range(shared):
        out_ref[c] = acc_ref[c].astype(out_ref.dtype)


def prepare_kernel(
    capacity, shared, stations, turn_s, me_s, pairs_s, pairs_ref, weights_ref, offset_ref, *rest
):
    inputs = rest[:-12]
    (gains_ref, recip_ref, slots_ref, sums_ref) = rest[-12:-8]
    (metas_ref, table_ref, pick_ref, rows_ref, codes_ref, slots_s, slots_v, sems) = rest[-8:]
    devices, depth, _, _ = metas_ref.shape
    owned = recip_ref.shape[0]
    channels = weights_ref.shape[1]
    half = stations // 2
    gain_tiles = (depth - 1) // 2
    near = len(inputs)
    if near == 1:
        moves = start_all([(inputs[0], metas_ref)], sems)
    else:
        at = 2 * capacity * shared
        moves = start_all(
            [(inputs[m].at[pl.ds(at, depth)], metas_ref.at[m]) for m in range(near)]
            + [(inputs[m].at[pl.ds(at + depth, depth)], metas_ref.at[near + m]) for m in range(near)]
            + [(inputs[m].at[pl.ds(0, capacity * shared)], rows_ref.at[m]) for m in range(near)],
            sems,
        )
    for move in moves:
        move.wait()

    for x in range(devices):
        for i in range(gain_tiles):
            table_ref[x, i * SUB : (i + 1) * SUB, :] = metas_ref[x, i].astype(
                jnp.float32
            ) + metas_ref[x, gain_tiles + i].astype(jnp.float32)
        code = metas_ref[x, 2 * gain_tiles].astype(jnp.float32)
        codes_ref[0, x : x + 1, :] = code[0:1, :]
        codes_ref[1, x : x + 1, :] = code[1:2, :]
    owner, slot = codes_ref[0], codes_ref[1]
    listing, mine = list_rows(owner, slot, me_s[0].astype(jnp.float32), capacity)
    slots_ref[...] = listing
    slots_v[...] = listing
    move = pltpu.make_async_copy(slots_v, slots_s, sems.at[0])
    move.start()

    which = lax.broadcasted_iota(jnp.int32, (owned, LANES), 0).astype(jnp.float32)
    codes_ref[0] = jnp.where(mine, slot, -1.0)
    hits = jnp.zeros((owned, LANES), jnp.float32)
    for x in range(devices):
        hits = hits + (codes_ref[0, x : x + 1, :] == which).astype(jnp.float32)
    tally = jnp.sum(hits, axis=1, keepdims=True)
    recip_ref[...] = jnp.broadcast_to(1.0 / jnp.maximum(tally, 1.0), recip_ref.shape)

    turn = turn_s[0]

    def pick(b, carry):
        for side in range(2):
            s = pairs_s[side, b]
            d = s // stations
            within = s - d * stations
            row = jnp.where(within >= half, within - half, within)
            pick_ref[pl.ds(side * owned + b, 1), :] = table_ref[d ^ turn, pl.ds(row, 1), :]
        return carry

    lax.fori_loop(0, owned, pick, 0, unroll=4)

    knot = (lax.broadcasted_iota(jnp.int32, (LANES, channels), 0) & 63) >> 3
    basis = jnp.zeros((LANES, channels), jnp.float32)
    for step in range(3):
        basis = basis + jnp.where(
            knot == offset_ref[...] + step, weights_ref[step : step + 1, :], 0.0
        )
    part = lax.broadcasted_iota(jnp.int32, (LANES, channels), 0) & 7
    column = lax.broadcasted_iota(jnp.int32, (owned, LANES), 1)
    used = (column & 63) < USED
    picked = []
    for side in range(2):
        within = lax.rem(pairs_ref[:, side : side + 1], stations)
        keep = jnp.logical_and(used, (column >= 64) == (within >= half))
        picked.append(jnp.where(keep, pick_ref[side * owned : (side + 1) * owned, :], 0.0))
    both = jnp.concatenate(picked, axis=0)
    for j in range(8):
        fine = jnp.dot(
            both,
            jnp.where(part == j, basis, 0.0),
            precision=lax.Precision.HIGHEST,
            preferred_element_type=jnp.float32,
        )
        gains_ref[j] = fine.astype(jnp.bfloat16).astype(jnp.float32)

    for c in range(sums_ref.shape[0]):
        sums_ref[c] = jnp.zeros_like(sums_ref[c])
    move.wait()
    if near > 1:
        for m in range(near):
            add_rows(sums_ref, 0, slots_s, m, capacity, rows_ref, m, shared)


def finish_kernel(
    capacity, shared, turn_s, slots_s, direct_ref, sums_ref, gains_ref, recip_ref, *rest
):
    far = rest[:-3]
    out_ref, acc_ref, res_ref = rest[-3:]
    owned, parts, channels = out_ref.shape
    devices = direct_ref.shape[0]
    chunks = channels // LANES
    tiles = chunks - shared
    turn = turn_s[0]
    for c in range(tiles):
        acc_ref[c] = jnp.zeros_like(acc_ref[c])
    for c in range(shared):
        acc_ref[tiles + c] = sums_ref[c] + far[0][c].astype(jnp.float32)

    def from_device(d, carry):
        add_rows(acc_ref, 0, slots_s, d ^ turn, capacity, direct_ref, d, tiles)
        return carry

    lax.fori_loop(0, devices, from_device, 0)

    flat = acc_ref.reshape(chunks * owned * parts, LANES)
    done = res_ref.reshape(chunks * owned * parts, LANES)
    for b0 in range(0, owned, SUB):
        scale = recip_ref[b0 : b0 + SUB, :]
        for c in range(chunks):
            row = (c * owned + b0) * parts
            cols = slice(c * LANES, (c + 1) * LANES)
            vis = [flat[pl.ds(row + j, SUB, stride=parts), :] for j in range(parts)]
            lhs = [gains_ref[j, b0 : b0 + SUB, cols] for j in range(parts)]
            rhs = [gains_ref[j, owned + b0 : owned + b0 + SUB, cols] for j in range(parts)]
            mid_re, mid_im = [], []
            for row_a in range(2):
                for col_b in range(2):
                    re = im = 0.0
                    for inner in range(2):
                        lr, li = lhs[2 * row_a + inner], lhs[4 + 2 * row_a + inner]
                        vr, vi = vis[2 * inner + col_b], vis[4 + 2 * inner + col_b]
                        re = re + lr * vr - li * vi
                        im = im + lr * vi + li * vr
                    mid_re.append(re * scale)
                    mid_im.append(im * scale)
            for row_a in range(2):
                for col_b in range(2):
                    re = im = 0.0
                    for inner in range(2):
                        mr, mi = mid_re[2 * row_a + inner], mid_im[2 * row_a + inner]
                        rr, ri = rhs[2 * col_b + inner], rhs[4 + 2 * col_b + inner]
                        re = re + mr * rr + mi * ri
                        im = im + mi * rr - mr * ri
                    j = 2 * row_a + col_b
                    done[pl.ds(row + j, SUB, stride=parts), :] = re
                    done[pl.ds(row + 4 + j, SUB, stride=parts), :] = im
    for c in range(chunks):
        out_ref[:, :, c * LANES : (c + 1) * LANES] = res_ref[c].astype(out_ref.dtype)


def on_device(
    visibilities,
    row_owner,
    row_slot,
    baseline_station_pairs,
    gains_coarse,
    band_weights,
    band_offset,
):
    devices = lax.axis_size("bl")
    rows, parts, channels = visibilities.shape
    capacity = 2 * rows // devices
    owned = baseline_station_pairs.shape[0]
    stations, _, knots = gains_coarse.shape
    chunks = channels // LANES
    gain_tiles = round_up(stations // 2, SUB) // SUB
    depth = 2 * gain_tiles + 1
    near = devices // 2 if devices <= 16 else 1
    shared = 1 if near > 1 else 0
    tiles = chunks - shared
    f32, bf16, i32 = jnp.float32, jnp.bfloat16, jnp.int32
    vmem = pl.BlockSpec(memory_space=pltpu.VMEM)
    smem = pl.BlockSpec(memory_space=pltpu.SMEM)
    hbm = pl.BlockSpec(memory_space=pltpu.HBM)
    anywhere = pl.BlockSpec(memory_space=pl.ANY)
    most = pltpu.CompilerParams(vmem_limit_bytes=ALL_VMEM)
    some = pltpu.CompilerParams(vmem_limit_bytes=SOME_VMEM)
    shape = jax.ShapeDtypeStruct
    dma = pltpu.SemaphoreType.DMA

    me = lax.axis_index("bl").astype(i32).reshape(1)
    turn = me if shared else jnp.zeros_like(me)
    owner = row_owner.reshape(rows)
    coarse = gains_coarse.transpose(2, 1, 0).reshape(knots * parts, stations)
    direct, meta = pl.pallas_call(
        functools.partial(pack_kernel, capacity, tiles),
        out_shape=(
            shape((devices, tiles * capacity, parts, LANES), bf16),
            shape((depth, SUB, LANES), bf16),
        ),
        in_specs=[hbm] * 5,
        out_specs=(vmem, vmem),
        scratch_shapes=[
            pltpu.SMEM((rows,), i32),
            pltpu.SMEM((devices,), i32),
            pltpu.VMEM((1, rows), i32),
            pltpu.VMEM((1, rows), i32),
            pltpu.VMEM((rows, parts, tiles * LANES), bf16),
            pltpu.VMEM((knots * parts, stations), f32),
            pltpu.VMEM((LANES, LANES), f32),
            dma((5,)),
        ],
        compiler_params=most,
        name="pack_direct",
    )(owner, row_owner.reshape(1, rows), row_slot.reshape(1, rows), visibilities, coarse)

    if shared:
        partner = lax.ppermute(meta, "bl", [(d, d ^ near) for d in range(devices)])
    received = lax.all_to_all(direct, "bl", split_axis=0, concat_axis=0, tiled=True)
    if shared:
        block = (2 * capacity * shared + 2 * depth, parts, LANES)
        blocks = pl.pallas_call(
            functools.partial(pack_shared_kernel, capacity, tiles),
            out_shape=[shape(block, bf16)] * near,
            in_specs=[smem] + [hbm] * 4,
            out_specs=[hbm] * near,
            scratch_shapes=[
                pltpu.SMEM((rows,), i32),
                pltpu.SMEM((devices,), i32),
                pltpu.VMEM((rows, parts, shared * LANES), bf16),
                pltpu.VMEM((depth, SUB, LANES), bf16),
                pltpu.VMEM((depth, SUB, LANES), bf16),
                pltpu.VMEM((near,) + block, bf16),
                dma((near,)),
            ],
            compiler_params=most,
            name="pack_shared",
        )(me, owner, visibilities, meta, partner)
        inputs = [blocks[0]] + [
            lax.ppermute(blocks[m], "bl", [(d, d ^ m) for d in range(devices)])
            for m in range(1, near)
        ]
        helped = pl.pallas_call(
            functools.partial(helper_kernel, capacity, shared),
            out_shape=shape((shared, owned, parts, LANES), bf16),
            in_specs=[smem] + [anywhere] * near,
            out_specs=vmem,
            scratch_shapes=[
                pltpu.VMEM((near, capacity * shared, parts, LANES), bf16),
                pltpu.VMEM((near, SUB, LANES), bf16),
                pltpu.VMEM((shared, owned, parts, LANES), f32),
                pltpu.VMEM((near, LANES), i32),
                pltpu.SMEM((near, LANES), i32),
                dma((2 * near,)),
            ],
            compiler_params=some,
            name="help_partner",
        )(me, *inputs)
        far = [lax.ppermute(helped, "bl", [(d, d ^ near) for d in range(devices)])]
    else:
        inputs = [lax.all_gather(meta, "bl", axis=0)]
        far = []

    gains, recip, slots, sums = pl.pallas_call(
        functools.partial(prepare_kernel, capacity, shared, stations),
        out_shape=(
            shape((parts, 2 * owned, channels), f32),
            shape((owned, LANES), f32),
            shape((devices, LANES), i32),
            shape((max(shared, 1), owned, parts, LANES), f32),
        ),
        in_specs=[smem, smem, smem, vmem, vmem, vmem] + [anywhere] * near,
        out_specs=(vmem,) * 4,
        scratch_shapes=[
            pltpu.VMEM((devices, depth, SUB, LANES), bf16),
            pltpu.VMEM((devices, gain_tiles * SUB, LANES), f32),
            pltpu.VMEM((2 * owned, LANES), f32),
            pltpu.VMEM((near, capacity * max(shared, 1), parts, LANES), bf16),
            pltpu.VMEM((2, devices, LANES), f32),
            pltpu.SMEM((devices, LANES), i32),
            pltpu.VMEM((devices, LANES), i32),
            dma((3 * near,)),
        ],
        compiler_params=some,
        name="gains_and_lists",
    )(
        turn,
        me,
        baseline_station_pairs.T,
        baseline_station_pairs,
        band_weights.T,
        band_offset.reshape(1, channels),
        *inputs,
    )
    return pl.pallas_call(
        functools.partial(finish_kernel, capacity, shared),
        out_shape=shape((owned, parts, channels), bf16),
        in_specs=[smem, smem] + [vmem] * (4 + len(far)),
        out_specs=vmem,
        scratch_shapes=[
            pltpu.VMEM((chunks, owned, parts, LANES), f32),
            pltpu.VMEM((chunks, owned, parts, LANES), f32),
        ],
        compiler_params=some,
        name="sum_and_apply",
    )(turn, slots, received, sums, gains, recip, *far)


def solution(mesh):
    placed = (
        P(("groups", "bl"), None, None),
        P(("groups", "bl"), None),
        P(("groups", "bl")),
        P("bl", None),
        P(("groups", "bl"), None, None),
        P("groups", None),
        P("groups"),
    )
    return jax.shard_map(
        on_device,
        mesh=mesh,
        in_specs=placed,
        out_specs=P(("groups", "bl"), None, None),
        check_vma=False,
    )
```

```python
import functools

import jax
import jax.numpy as jnp
from jax import lax
from jax.experimental import pallas as pl
from jax.experimental.pallas import tpu as pltpu
from jax.sharding import PartitionSpec as P

LANES = 128
SUB = 8
USED = 48
ALL_VMEM = 60 * 1024 * 1024
SOME_VMEM = 24 * 1024 * 1024


def round_up(value, unit):
    return -(-value // unit) * unit


def start_all(pairs, sems):
    moves = [pltpu.make_async_copy(src, dst, sems.at[i]) for i, (src, dst) in enumerate(pairs)]
    for move in moves:
        move.start()
    return moves


def pack_kernel(
    capacity,
    near,
    me_s,
    owner_hbm,
    owner_row_hbm,
    slot_row_hbm,
    vis_hbm,
    coarse_hbm,
    meta_hbm,
    *rest,
):
    outs = rest[:-10]
    (
        owner_s,
        count_s,
        owner_ref,
        slot_ref,
        vis_ref,
        coarse_ref,
        turn_ref,
        meta_ref,
        block_ref,
        sems,
    ) = rest[-10:]
    rows = vis_ref.shape[0]
    chunks = vis_ref.shape[2] // LANES
    devices = block_ref.shape[0]
    terms, stations = coarse_ref.shape
    half = stations // 2
    gain_tiles = (meta_ref.shape[0] - 1) // 2
    moves = start_all(
        (
            (vis_hbm, vis_ref),
            (coarse_hbm, coarse_ref),
            (owner_hbm, owner_s),
            (owner_row_hbm, owner_ref),
            (slot_row_hbm, slot_ref),
        ),
        sems,
    )
    turn_ref[...] = jnp.zeros_like(turn_ref)
    for d in range(devices):
        count_s[d] = 0
    me = me_s[0]
    for move in moves[1:]:
        move.wait()

    turn_ref[0:terms, 0:half] = coarse_ref[:, 0:half]
    turn_ref[64 : 64 + terms, 0:half] = coarse_ref[:, half:stations]
    gains = turn_ref[...].T
    high = gains.astype(jnp.bfloat16)
    low = (gains - high.astype(jnp.float32)).astype(jnp.bfloat16)
    for i in range(gain_tiles):
        meta_ref[i] = high[i * SUB : (i + 1) * SUB, :]
        meta_ref[gain_tiles + i] = low[i * SUB : (i + 1) * SUB, :]
    sub = lax.broadcasted_iota(jnp.int32, (SUB, LANES), 0)
    codes = jnp.where(sub == 0, owner_ref[...], slot_ref[...])
    meta_ref[2 * gain_tiles] = codes.astype(jnp.float32).astype(jnp.bfloat16)
    sends = start_all([(meta_ref, meta_hbm)], sems.at[pl.ds(1, 1)])
    moves[0].wait()

    def place(r, carry):
        x = owner_s[r] ^ me
        k = count_s[x]
        count_s[x] = k + 1
        for c in range(chunks):
            block_ref[x, chunks * k + c] = vis_ref[r, :, c * LANES : (c + 1) * LANES]
        return carry

    lax.fori_loop(0, rows, place, 0, unroll=8)
    if near > 1:
        pairs = [(block_ref.at[near + i], outs[i]) for i in range(near)]
    else:
        pairs = [(block_ref, outs[0])]
    sends += start_all(pairs, sems.at[pl.ds(2, len(pairs))])
    for send in sends:
        send.wait()


def pack_near_kernel(
    capacity,
    me_s,
    owner_hbm,
    vis_hbm,
    meta_hbm,
    partner_hbm,
    out_ref,
    owner_s,
    count_s,
    vis_ref,
    meta_ref,
    partner_ref,
    sems,
):
    rows = vis_ref.shape[0]
    chunks = vis_ref.shape[2] // LANES
    near = out_ref.shape[0]
    depth = meta_ref.shape[0]
    at = capacity * chunks
    moves = start_all(
        (
            (vis_hbm, vis_ref),
            (owner_hbm, owner_s),
            (meta_hbm, meta_ref),
            (partner_hbm, partner_ref),
        ),
        sems,
    )
    for d in range(near):
        count_s[d] = 0
    half = me_s[0] & near
    for move in moves[1:]:
        move.wait()
    for d in range(near):
        for i in range(depth):
            out_ref[d, at + i] = meta_ref[i]
            out_ref[d, at + depth + i] = partner_ref[i]
    moves[0].wait()

    def place(r, carry):
        x = owner_s[r] ^ half

        @pl.when(x < near)
        def _():
            k = count_s[x]
            count_s[x] = k + 1
            for c in range(chunks):
                out_ref[x, chunks * k + c] = vis_ref[r, :, c * LANES : (c + 1) * LANES]

        return carry

    lax.fori_loop(0, rows, place, 0, unroll=4)


def list_rows(owner, slot, target, capacity):
    senders = owner.shape[0]
    mine = owner == target
    counted = mine.astype(jnp.float32)
    before = lax.broadcasted_iota(jnp.int32, (LANES, LANES), 0) < lax.broadcasted_iota(
        jnp.int32, (LANES, LANES), 1
    )
    rank = jnp.dot(
        counted.astype(jnp.bfloat16),
        before.astype(jnp.float32).astype(jnp.bfloat16),
        preferred_element_type=jnp.float32,
    )
    lane = lax.broadcasted_iota(jnp.int32, (senders, LANES), 1)
    count = jnp.sum(counted, axis=1, keepdims=True)
    listing = jnp.where(lane == capacity, count, 0.0)
    for k in range(capacity):
        here = jnp.logical_and(mine, rank == float(k))
        kth = jnp.sum(jnp.where(here, slot, 0.0), axis=1, keepdims=True)
        listing = jnp.where(lane == k, kth, listing)
    return listing.astype(jnp.int32), mine


def add_rows(acc_ref, slots_s, line, capacity, rows_ref):
    chunks = acc_ref.shape[0]

    def add(k, carry):
        b = slots_s[line, k]
        for c in range(chunks):
            acc_ref[c, b] += rows_ref[chunks * k + c].astype(jnp.float32)
        return carry

    lax.fori_loop(0, slots_s[line, capacity], add, 0)


def prepare_kernel(
    capacity,
    near,
    stations,
    turn_s,
    me_s,
    pairs_s,
    arrived_hbm,
    pairs_ref,
    weights_ref,
    offset_ref,
    gains_ref,
    recip_ref,
    slots_ref,
    sums_ref,
    metas_ref,
    table_ref,
    pick_ref,
    rows_ref,
    codes_ref,
    slots_s,
    slots_v,
    sems,
):
    devices, depth, _, _ = metas_ref.shape
    owned = recip_ref.shape[0]
    channels = weights_ref.shape[1]
    half = stations // 2
    gain_tiles = (depth - 1) // 2
    chunks = channels // LANES
    if near == 1:
        moves = start_all([(arrived_hbm, metas_ref)], sems)
    else:
        at = capacity * chunks
        moves = start_all(
            (
                (arrived_hbm.at[:, pl.ds(at, depth)], metas_ref.at[pl.ds(0, near)]),
                (arrived_hbm.at[:, pl.ds(at + depth, depth)], metas_ref.at[pl.ds(near, near)]),
                (arrived_hbm.at[:, pl.ds(0, at)], rows_ref),
            ),
            sems,
        )
    for move in moves:
        move.wait()

    for x in range(devices):
        for i in range(gain_tiles):
            table_ref[x, i * SUB : (i + 1) * SUB, :] = metas_ref[x, i].astype(
                jnp.float32
            ) + metas_ref[x, gain_tiles + i].astype(jnp.float32)
        code = metas_ref[x, 2 * gain_tiles].astype(jnp.float32)
        codes_ref[0, x : x + 1, :] = code[0:1, :]
        codes_ref[1, x : x + 1, :] = code[1:2, :]
    owner, slot = codes_ref[0], codes_ref[1]
    listing, mine = list_rows(owner, slot, me_s[0].astype(jnp.float32), capacity)
    slots_ref[...] = listing
    slots_v[...] = listing
    move = pltpu.make_async_copy(slots_v, slots_s, sems.at[0])
    move.start()

    which = lax.broadcasted_iota(jnp.int32, (owned, LANES), 0).astype(jnp.float32)
    codes_ref[0] = jnp.where(mine, slot, -1.0)
    hits = jnp.zeros((owned, LANES), jnp.float32)
    for x in range(devices):
        hits = hits + (codes_ref[0, x : x + 1, :] == which).astype(jnp.float32)
    tally = jnp.sum(hits, axis=1, keepdims=True)
    recip_ref[...] = jnp.broadcast_to(1.0 / jnp.maximum(tally, 1.0), recip_ref.shape)

    turn = turn_s[0]

    def pick(b, carry):
        for side in range(2):
            s = pairs_s[side, b]
            d = s // stations
            within = s - d * stations
            row = jnp.where(within >= half, within - half, within)
            pick_ref[pl.ds(side * owned + b, 1), :] = table_ref[d ^ turn, pl.ds(row, 1), :]
        return carry

    lax.fori_loop(0, owned, pick, 0, unroll=4)

    knot = (lax.broadcasted_iota(jnp.int32, (LANES, channels), 0) & 63) >> 3
    basis = jnp.zeros((LANES, channels), jnp.float32)
    for step in range(3):
        basis = basis + jnp.where(
            knot == offset_ref[...] + step, weights_ref[step : step + 1, :], 0.0
        )
    part = lax.broadcasted_iota(jnp.int32, (LANES, channels), 0) & 7
    column = lax.broadcasted_iota(jnp.int32, (owned, LANES), 1)
    used = (column & 63) < USED
    picked = []
    for side in range(2):
        within = lax.rem(pairs_ref[:, side : side + 1], stations)
        keep = jnp.logical_and(used, (column >= 64) == (within >= half))
        picked.append(jnp.where(keep, pick_ref[side * owned : (side + 1) * owned, :], 0.0))
    both = jnp.concatenate(picked, axis=0)
    for j in range(8):
        fine = jnp.dot(
            both,
            jnp.where(part == j, basis, 0.0),
            precision=lax.Precision.HIGHEST,
            preferred_element_type=jnp.float32,
        )
        gains_ref[j] = fine.astype(jnp.bfloat16).astype(jnp.float32)

    for c in range(sums_ref.shape[0]):
        sums_ref[c] = jnp.zeros_like(sums_ref[c])
    move.wait()
    if near > 1:
        for m in range(near):
            add_rows(sums_ref, slots_s, m, capacity, rows_ref.at[m])


def finish_kernel(capacity, turn_s, me_s, slots_s, sums_ref, gains_ref, recip_ref, *rest):
    far = rest[:-3]
    out_ref, acc_ref, res_ref = rest[-3:]
    owned, parts, channels = out_ref.shape
    chunks = channels // LANES
    acc_ref[...] = sums_ref[...]
    if len(far) > 1:
        for i in range(len(far)):
            line = me_s[0] ^ turn_s[0] ^ (len(far) + i)
            add_rows(acc_ref, slots_s, line, capacity, far[i])
    else:

        def from_device(d, carry):
            add_rows(acc_ref, slots_s, d, capacity, far[0].at[d])
            return carry

        lax.fori_loop(0, far[0].shape[0], from_device, 0)

    flat = acc_ref.reshape(chunks * owned * parts, LANES)
    done = res_ref.reshape(chunks * owned * parts, LANES)
    for b0 in range(0, owned, SUB):
        scale = recip_ref[b0 : b0 + SUB, :]
        for c in range(chunks):
            row = (c * owned + b0) * parts
            cols = slice(c * LANES, (c + 1) * LANES)
            vis = [flat[pl.ds(row + j, SUB, stride=parts), :] for j in range(parts)]
            lhs = [gains_ref[j, b0 : b0 + SUB, cols] for j in range(parts)]
            rhs = [gains_ref[j, owned + b0 : owned + b0 + SUB, cols] for j in range(parts)]
            mid_re, mid_im = [], []
            for row_a in range(2):
                for col_b in range(2):
                    re = im = 0.0
                    for inner in range(2):
                        lr, li = lhs[2 * row_a + inner], lhs[4 + 2 * row_a + inner]
                        vr, vi = vis[2 * inner + col_b], vis[4 + 2 * inner + col_b]
                        re = re + lr * vr - li * vi
                        im = im + lr * vi + li * vr
                    mid_re.append(re * scale)
                    mid_im.append(im * scale)
            for row_a in range(2):
                for col_b in range(2):
                    re = im = 0.0
                    for inner in range(2):
                        mr, mi = mid_re[2 * row_a + inner], mid_im[2 * row_a + inner]
                        rr, ri = rhs[2 * col_b + inner], rhs[4 + 2 * col_b + inner]
                        re = re + mr * rr + mi * ri
                        im = im + mi * rr - mr * ri
                    j = 2 * row_a + col_b
                    done[pl.ds(row + j, SUB, stride=parts), :] = re
                    done[pl.ds(row + 4 + j, SUB, stride=parts), :] = im
    for c in range(chunks):
        out_ref[:, :, c * LANES : (c + 1) * LANES] = res_ref[c].astype(out_ref.dtype)


def on_device(
    visibilities,
    row_owner,
    row_slot,
    baseline_station_pairs,
    gains_coarse,
    band_weights,
    band_offset,
):
    devices = lax.axis_size("bl")
    rows, parts, channels = visibilities.shape
    capacity = 2 * rows // devices
    owned = baseline_station_pairs.shape[0]
    stations, _, knots = gains_coarse.shape
    chunks = channels // LANES
    gain_tiles = round_up(stations // 2, SUB) // SUB
    depth = 2 * gain_tiles + 1
    near = devices // 2 if devices <= 16 else 1
    halves = near > 1
    f32, bf16, i32 = jnp.float32, jnp.bfloat16, jnp.int32
    vmem = pl.BlockSpec(memory_space=pltpu.VMEM)
    smem = pl.BlockSpec(memory_space=pltpu.SMEM)
    hbm = pl.BlockSpec(memory_space=pltpu.HBM)
    anywhere = pl.BlockSpec(memory_space=pl.ANY)
    most = pltpu.CompilerParams(vmem_limit_bytes=ALL_VMEM)
    some = pltpu.CompilerParams(vmem_limit_bytes=SOME_VMEM)
    shape = jax.ShapeDtypeStruct
    dma = pltpu.SemaphoreType.DMA

    me = lax.axis_index("bl").astype(i32).reshape(1)
    turn = me & near if halves else jnp.zeros_like(me)
    owner = row_owner.reshape(rows)
    coarse = gains_coarse.transpose(2, 1, 0).reshape(knots * parts, stations)
    block = (chunks * capacity, parts, LANES)
    meta, *sent = pl.pallas_call(
        functools.partial(pack_kernel, capacity, near),
        out_shape=[shape((depth, SUB, LANES), bf16)]
        + [shape(block if halves else (devices,) + block, bf16)] * near,
        in_specs=[smem] + [hbm] * 5,
        out_specs=[hbm] * (1 + near),
        scratch_shapes=[
            pltpu.SMEM((rows,), i32),
            pltpu.SMEM((devices,), i32),
            pltpu.VMEM((1, rows), i32),
            pltpu.VMEM((1, rows), i32),
            pltpu.VMEM((rows, parts, channels), bf16),
            pltpu.VMEM((knots * parts, stations), f32),
            pltpu.VMEM((LANES, LANES), f32),
            pltpu.VMEM((depth, SUB, LANES), bf16),
            pltpu.VMEM((devices,) + block, bf16),
            dma((5 + near,)),
        ],
        compiler_params=most,
        name="pack_rows",
    )(
        me if halves else turn,
        owner,
        row_owner.reshape(1, rows),
        row_slot.reshape(1, rows),
        visibilities,
        coarse,
    )

    if halves:
        partner = lax.ppermute(meta, "bl", [(d, d ^ near) for d in range(devices)])
        far = [
            lax.ppermute(sent[i], "bl", [(d, d ^ (near + i)) for d in range(devices)])
            for i in range(near)
        ]
        packed = pl.pallas_call(
            functools.partial(pack_near_kernel, capacity),
            out_shape=shape((near, chunks * capacity + 2 * depth, parts, LANES), bf16),
            in_specs=[smem] + [hbm] * 4,
            out_specs=vmem,
            scratch_shapes=[
                pltpu.SMEM((rows,), i32),
                pltpu.SMEM((near,), i32),
                pltpu.VMEM((rows, parts, channels), bf16),
                pltpu.VMEM((depth, SUB, LANES), bf16),
                pltpu.VMEM((depth, SUB, LANES), bf16),
                dma((4,)),
            ],
            compiler_params=most,
            name="pack_near",
        )(me, owner, visibilities, meta, partner)
        groups = [list(range(0, near)), list(range(near, devices))]
        arrived = lax.all_to_all(
            packed, "bl", split_axis=0, concat_axis=0, axis_index_groups=groups, tiled=True
        )
    else:
        far = [lax.all_to_all(sent[0], "bl", split_axis=0, concat_axis=0, tiled=True)]
        arrived = lax.all_gather(meta, "bl", axis=0)

    gains, recip, slots, sums = pl.pallas_call(
        functools.partial(prepare_kernel, capacity, near, stations),
        out_shape=(
            shape((parts, 2 * owned, channels), f32),
            shape((owned, LANES), f32),
            shape((devices, LANES), i32),
            shape((chunks, owned, parts, LANES), f32),
        ),
        in_specs=[smem, smem, smem, anywhere, vmem, vmem, vmem],
        out_specs=(vmem,) * 4,
        scratch_shapes=[
            pltpu.VMEM((devices, depth, SUB, LANES), bf16),
            pltpu.VMEM((devices, gain_tiles * SUB, LANES), f32),
            pltpu.VMEM((2 * owned, LANES), f32),
            pltpu.VMEM((near,) + block, bf16),
            pltpu.VMEM((2, devices, LANES), f32),
            pltpu.SMEM((devices, LANES), i32),
            pltpu.VMEM((devices, LANES), i32),
            dma((3,)),
        ],
        compiler_params=some,
        name="gains_and_near",
    )(
        turn,
        me,
        baseline_station_pairs.T,
        arrived,
        baseline_station_pairs,
        band_weights.T,
        band_offset.reshape(1, channels),
    )
    return pl.pallas_call(
        functools.partial(finish_kernel, capacity),
        out_shape=shape((owned, parts, channels), bf16),
        in_specs=[smem, smem, smem] + [vmem] * (3 + len(far)),
        out_specs=vmem,
        scratch_shapes=[
            pltpu.VMEM((chunks, owned, parts, LANES), f32),
            pltpu.VMEM((chunks, owned, parts, LANES), f32),
        ],
        compiler_params=some,
        name="sum_and_apply",
    )(turn, me, slots, sums, gains, recip, *far)


def solution(mesh):
    placed = (
        P(("groups", "bl"), None, None),
        P(("groups", "bl"), None),
        P(("groups", "bl")),
        P("bl", None),
        P(("groups", "bl"), None, None),
        P("groups", None),
        P("groups"),
    )
    return jax.shard_map(
        on_device,
        mesh=mesh,
        in_specs=placed,
        out_specs=P(("groups", "bl"), None, None),
        check_vma=False,
    )
```

```python
import functools

import jax
import jax.numpy as jnp
from jax import lax
from jax.experimental import pallas as pl
from jax.experimental.pallas import tpu as pltpu
from jax.sharding import PartitionSpec as P

LANES = 128
SUB = 8
USED = 48
ALL_VMEM = 60 * 1024 * 1024
SOME_VMEM = 24 * 1024 * 1024


def round_up(value, unit):
    return -(-value // unit) * unit


def start_all(pairs, sems):
    moves = [pltpu.make_async_copy(src, dst, sems.at[i]) for i, (src, dst) in enumerate(pairs)]
    for move in moves:
        move.start()
    return moves


def pack_kernel(
    capacity,
    near,
    me_s,
    owner_hbm,
    owner_row_hbm,
    slot_row_hbm,
    vis_hbm,
    coarse_hbm,
    *rest,
):
    outs = rest[:-10]
    (
        owner_s,
        count_s,
        owner_ref,
        slot_ref,
        vis_ref,
        coarse_ref,
        turn_ref,
        meta_ref,
        block_ref,
        sems,
    ) = rest[-10:]
    rows = vis_ref.shape[0]
    chunks = vis_ref.shape[2] // LANES
    devices = block_ref.shape[0]
    terms, stations = coarse_ref.shape
    half = stations // 2
    depth = meta_ref.shape[0]
    gain_tiles = (depth - 1) // 2
    moves = start_all(
        (
            (vis_hbm, vis_ref),
            (coarse_hbm, coarse_ref),
            (owner_hbm, owner_s),
            (owner_row_hbm, owner_ref),
            (slot_row_hbm, slot_ref),
        ),
        sems,
    )
    turn_ref[...] = jnp.zeros_like(turn_ref)
    for d in range(devices):
        count_s[d] = 0
    me = me_s[0]
    for move in moves[1:]:
        move.wait()

    turn_ref[0:terms, 0:half] = coarse_ref[:, 0:half]
    turn_ref[64 : 64 + terms, 0:half] = coarse_ref[:, half:stations]
    gains = turn_ref[...].T
    high = gains.astype(jnp.bfloat16)
    low = (gains - high.astype(jnp.float32)).astype(jnp.bfloat16)
    for i in range(gain_tiles):
        meta_ref[i] = high[i * SUB : (i + 1) * SUB, :]
        meta_ref[gain_tiles + i] = low[i * SUB : (i + 1) * SUB, :]
    sub = lax.broadcasted_iota(jnp.int32, (SUB, LANES), 0)
    codes = jnp.where(sub == 0, owner_ref[...], slot_ref[...])
    meta_ref[2 * gain_tiles] = codes.astype(jnp.float32).astype(jnp.bfloat16)
    at = chunks * capacity
    if near > 1:
        pairs = [(meta_ref, outs[0].at[pl.ds(at, depth)])]
        pairs += [(meta_ref, outs[near].at[d, pl.ds(at, depth)]) for d in range(near)]
    else:
        pairs = [(meta_ref, outs[1])]
    sends = start_all(pairs, sems.at[pl.ds(1, len(pairs))])
    moves[0].wait()

    def place(r, carry):
        d = owner_s[r]
        x = d ^ me
        if near > 1:
            x = jnp.where(x < near, d & (near - 1), x)
        k = count_s[x]
        count_s[x] = k + 1
        for c in range(chunks):
            block_ref[x, chunks * k + c] = vis_ref[r, :, c * LANES : (c + 1) * LANES]
        return carry

    lax.fori_loop(0, rows, place, 0, unroll=8)
    start = 1 + len(pairs)
    if near > 1:
        pairs = [(block_ref.at[near + i], outs[i].at[pl.ds(0, at)]) for i in range(near)]
        pairs += [(block_ref.at[pl.ds(0, near)], outs[near].at[:, pl.ds(0, at)])]
    else:
        pairs = [(block_ref, outs[0])]
    sends += start_all(pairs, sems.at[pl.ds(start, len(pairs))])
    for send in sends:
        send.wait()


def add_partner_kernel(at, depth, first_hbm, _, out_hbm, sems):
    near = out_hbm.shape[0]
    moves = start_all(
        [
            (first_hbm.at[pl.ds(at, depth)], out_hbm.at[d, pl.ds(at + depth, depth)])
            for d in range(near)
        ],
        sems,
    )
    for move in moves:
        move.wait()


def list_rows(owner, slot, target, capacity):
    senders = owner.shape[0]
    mine = owner == target
    counted = mine.astype(jnp.float32)
    before = lax.broadcasted_iota(jnp.int32, (LANES, LANES), 0) < lax.broadcasted_iota(
        jnp.int32, (LANES, LANES), 1
    )
    rank = jnp.dot(
        counted.astype(jnp.bfloat16),
        before.astype(jnp.float32).astype(jnp.bfloat16),
        preferred_element_type=jnp.float32,
    )
    lane = lax.broadcasted_iota(jnp.int32, (senders, LANES), 1)
    count = jnp.sum(counted, axis=1, keepdims=True)
    listing = jnp.where(lane == capacity, count, 0.0)
    for k in range(capacity):
        here = jnp.logical_and(mine, rank == float(k))
        kth = jnp.sum(jnp.where(here, slot, 0.0), axis=1, keepdims=True)
        listing = jnp.where(lane == k, kth, listing)
    return listing.astype(jnp.int32), mine


def add_rows(acc_ref, slots_s, line, capacity, rows_ref):
    chunks = acc_ref.shape[0]

    def add(k, carry):
        b = slots_s[line, k]
        for c in range(chunks):
            acc_ref[c, b] += rows_ref[chunks * k + c].astype(jnp.float32)
        return carry

    lax.fori_loop(0, slots_s[line, capacity], add, 0)


def prepare_kernel(
    capacity,
    near,
    stations,
    turn_s,
    me_s,
    pairs_s,
    arrived_hbm,
    pairs_ref,
    weights_ref,
    offset_ref,
    gains_ref,
    recip_ref,
    slots_ref,
    sums_ref,
    metas_ref,
    table_ref,
    pick_ref,
    rows_ref,
    codes_ref,
    slots_s,
    slots_v,
    sems,
):
    devices, depth, _, _ = metas_ref.shape
    owned = recip_ref.shape[0]
    channels = weights_ref.shape[1]
    half = stations // 2
    gain_tiles = (depth - 1) // 2
    chunks = channels // LANES
    if near == 1:
        moves = start_all([(arrived_hbm, metas_ref)], sems)
    else:
        at = capacity * chunks
        moves = start_all(
            (
                (arrived_hbm.at[:, pl.ds(at, depth)], metas_ref.at[pl.ds(0, near)]),
                (arrived_hbm.at[:, pl.ds(at + depth, depth)], metas_ref.at[pl.ds(near, near)]),
                (arrived_hbm.at[:, pl.ds(0, at)], rows_ref),
            ),
            sems,
        )
    for move in moves:
        move.wait()

    for x in range(devices):
        for i in range(gain_tiles):
            table_ref[x, i * SUB : (i + 1) * SUB, :] = metas_ref[x, i].astype(
                jnp.float32
            ) + metas_ref[x, gain_tiles + i].astype(jnp.float32)
        code = metas_ref[x, 2 * gain_tiles].astype(jnp.float32)
        codes_ref[0, x : x + 1, :] = code[0:1, :]
        codes_ref[1, x : x + 1, :] = code[1:2, :]
    owner, slot = codes_ref[0], codes_ref[1]
    listing, mine = list_rows(owner, slot, me_s[0].astype(jnp.float32), capacity)
    slots_ref[...] = listing
    slots_v[...] = listing
    move = pltpu.make_async_copy(slots_v, slots_s, sems.at[0])
    move.start()

    which = lax.broadcasted_iota(jnp.int32, (owned, LANES), 0).astype(jnp.float32)
    codes_ref[0] = jnp.where(mine, slot, -1.0)
    hits = jnp.zeros((owned, LANES), jnp.float32)
    for x in range(devices):
        hits = hits + (codes_ref[0, x : x + 1, :] == which).astype(jnp.float32)
    tally = jnp.sum(hits, axis=1, keepdims=True)
    recip_ref[...] = jnp.broadcast_to(1.0 / jnp.maximum(tally, 1.0), recip_ref.shape)

    turn = turn_s[0]

    def pick(b, carry):
        for side in range(2):
            s = pairs_s[side, b]
            d = s // stations
            within = s - d * stations
            row = jnp.where(within >= half, within - half, within)
            pick_ref[pl.ds(side * owned + b, 1), :] = table_ref[d ^ turn, pl.ds(row, 1), :]
        return carry

    lax.fori_loop(0, owned, pick, 0, unroll=4)

    knot = (lax.broadcasted_iota(jnp.int32, (LANES, channels), 0) & 63) >> 3
    basis = jnp.zeros((LANES, channels), jnp.float32)
    for step in range(3):
        basis = basis + jnp.where(
            knot == offset_ref[...] + step, weights_ref[step : step + 1, :], 0.0
        )
    part = lax.broadcasted_iota(jnp.int32, (LANES, channels), 0) & 7
    column = lax.broadcasted_iota(jnp.int32, (owned, LANES), 1)
    used = (column & 63) < USED
    picked = []
    for side in range(2):
        within = lax.rem(pairs_ref[:, side : side + 1], stations)
        keep = jnp.logical_and(used, (column >= 64) == (within >= half))
        picked.append(jnp.where(keep, pick_ref[side * owned : (side + 1) * owned, :], 0.0))
    both = jnp.concatenate(picked, axis=0)
    for j in range(8):
        fine = jnp.dot(
            both,
            jnp.where(part == j, basis, 0.0),
            precision=lax.Precision.HIGHEST,
            preferred_element_type=jnp.float32,
        )
        gains_ref[j] = fine.astype(jnp.bfloat16).astype(jnp.float32)

    for c in range(sums_ref.shape[0]):
        sums_ref[c] = jnp.zeros_like(sums_ref[c])
    move.wait()
    if near > 1:
        for m in range(near):
            add_rows(sums_ref, slots_s, m, capacity, rows_ref.at[m])


def finish_kernel(capacity, turn_s, me_s, slots_s, sums_ref, gains_ref, recip_ref, *rest):
    far = rest[:-3]
    out_ref, acc_ref, res_ref = rest[-3:]
    owned, parts, channels = out_ref.shape
    chunks = channels // LANES
    acc_ref[...] = sums_ref[...]
    if len(far) > 1:
        for i in range(len(far)):
            line = me_s[0] ^ turn_s[0] ^ (len(far) + i)
            add_rows(acc_ref, slots_s, line, capacity, far[i])
    else:

        def from_device(d, carry):
            add_rows(acc_ref, slots_s, d, capacity, far[0].at[d])
            return carry

        lax.fori_loop(0, far[0].shape[0], from_device, 0)

    flat = acc_ref.reshape(chunks * owned * parts, LANES)
    done = res_ref.reshape(chunks * owned * parts, LANES)
    for b0 in range(0, owned, SUB):
        scale = recip_ref[b0 : b0 + SUB, :]
        for c in range(chunks):
            row = (c * owned + b0) * parts
            cols = slice(c * LANES, (c + 1) * LANES)
            vis = [flat[pl.ds(row + j, SUB, stride=parts), :] for j in range(parts)]
            lhs = [gains_ref[j, b0 : b0 + SUB, cols] for j in range(parts)]
            rhs = [gains_ref[j, owned + b0 : owned + b0 + SUB, cols] for j in range(parts)]
            mid_re, mid_im = [], []
            for row_a in range(2):
                for col_b in range(2):
                    re = im = 0.0
                    for inner in range(2):
                        lr, li = lhs[2 * row_a + inner], lhs[4 + 2 * row_a + inner]
                        vr, vi = vis[2 * inner + col_b], vis[4 + 2 * inner + col_b]
                        re = re + lr * vr - li * vi
                        im = im + lr * vi + li * vr
                    mid_re.append(re * scale)
                    mid_im.append(im * scale)
            for row_a in range(2):
                for col_b in range(2):
                    re = im = 0.0
                    for inner in range(2):
                        mr, mi = mid_re[2 * row_a + inner], mid_im[2 * row_a + inner]
                        rr, ri = rhs[2 * col_b + inner], rhs[4 + 2 * col_b + inner]
                        re = re + mr * rr + mi * ri
                        im = im + mi * rr - mr * ri
                    j = 2 * row_a + col_b
                    done[pl.ds(row + j, SUB, stride=parts), :] = re
                    done[pl.ds(row + 4 + j, SUB, stride=parts), :] = im
    for c in range(chunks):
        out_ref[:, :, c * LANES : (c + 1) * LANES] = res_ref[c].astype(out_ref.dtype)


def on_device(
    visibilities,
    row_owner,
    row_slot,
    baseline_station_pairs,
    gains_coarse,
    band_weights,
    band_offset,
):
    devices = lax.axis_size("bl")
    rows, parts, channels = visibilities.shape
    capacity = 2 * rows // devices
    owned = baseline_station_pairs.shape[0]
    stations, _, knots = gains_coarse.shape
    chunks = channels // LANES
    gain_tiles = round_up(stations // 2, SUB) // SUB
    depth = 2 * gain_tiles + 1
    near = devices // 2 if devices <= 16 else 1
    halves = near > 1
    f32, bf16, i32 = jnp.float32, jnp.bfloat16, jnp.int32
    vmem = pl.BlockSpec(memory_space=pltpu.VMEM)
    smem = pl.BlockSpec(memory_space=pltpu.SMEM)
    hbm = pl.BlockSpec(memory_space=pltpu.HBM)
    anywhere = pl.BlockSpec(memory_space=pl.ANY)
    most = pltpu.CompilerParams(vmem_limit_bytes=ALL_VMEM)
    some = pltpu.CompilerParams(vmem_limit_bytes=SOME_VMEM)
    shape = jax.ShapeDtypeStruct
    dma = pltpu.SemaphoreType.DMA

    me = lax.axis_index("bl").astype(i32).reshape(1)
    turn = me & near if halves else jnp.zeros_like(me)
    owner = row_owner.reshape(rows)
    coarse = gains_coarse.transpose(2, 1, 0).reshape(knots * parts, stations)
    block = (chunks * capacity, parts, LANES)
    rows_at = chunks * capacity
    if halves:
        outs = [shape((rows_at + depth, parts, LANES), bf16)]
        outs += [shape(block, bf16)] * (near - 1)
        outs += [shape((near, rows_at + 2 * depth, parts, LANES), bf16)]
    else:
        outs = [shape((devices,) + block, bf16), shape((depth, SUB, LANES), bf16)]
    *sent, last = pl.pallas_call(
        functools.partial(pack_kernel, capacity, near),
        out_shape=outs,
        in_specs=[smem] + [hbm] * 5,
        out_specs=[hbm] * len(outs),
        scratch_shapes=[
            pltpu.SMEM((rows,), i32),
            pltpu.SMEM((devices,), i32),
            pltpu.VMEM((1, rows), i32),
            pltpu.VMEM((1, rows), i32),
            pltpu.VMEM((rows, parts, channels), bf16),
            pltpu.VMEM((knots * parts, stations), f32),
            pltpu.VMEM((LANES, LANES), f32),
            pltpu.VMEM((depth, SUB, LANES), bf16),
            pltpu.VMEM((devices,) + block, bf16),
            dma((5 + 2 * near + 2,)),
        ],
        compiler_params=most,
        name="pack_rows",
    )(
        me if halves else turn,
        owner,
        row_owner.reshape(1, rows),
        row_slot.reshape(1, rows),
        visibilities,
        coarse,
    )

    if halves:
        far = [
            lax.ppermute(sent[i], "bl", [(d, d ^ (near + i)) for d in range(devices)])
            for i in range(near)
        ]
        packed = pl.pallas_call(
            functools.partial(add_partner_kernel, rows_at, depth),
            out_shape=shape(last.shape, last.dtype),
            in_specs=[anywhere, hbm],
            out_specs=hbm,
            scratch_shapes=[dma((near,))],
            input_output_aliases={1: 0},
            compiler_params=some,
            name="add_partner",
        )(far[0], last)
        groups = [list(range(0, near)), list(range(near, devices))]
        arrived = lax.all_to_all(
            packed, "bl", split_axis=0, concat_axis=0, axis_index_groups=groups, tiled=True
        )
    else:
        far = [lax.all_to_all(sent[0], "bl", split_axis=0, concat_axis=0, tiled=True)]
        arrived = lax.all_gather(last, "bl", axis=0)

    gains, recip, slots, sums = pl.pallas_call(
        functools.partial(prepare_kernel, capacity, near, stations),
        out_shape=(
            shape((parts, 2 * owned, channels), f32),
            shape((owned, LANES), f32),
            shape((devices, LANES), i32),
            shape((chunks, owned, parts, LANES), f32),
        ),
        in_specs=[smem, smem, smem, anywhere, vmem, vmem, vmem],
        out_specs=(vmem,) * 4,
        scratch_shapes=[
            pltpu.VMEM((devices, depth, SUB, LANES), bf16),
            pltpu.VMEM((devices, gain_tiles * SUB, LANES), f32),
            pltpu.VMEM((2 * owned, LANES), f32),
            pltpu.VMEM((near,) + block, bf16),
            pltpu.VMEM((2, devices, LANES), f32),
            pltpu.SMEM((devices, LANES), i32),
            pltpu.VMEM((devices, LANES), i32),
            dma((3,)),
        ],
        compiler_params=some,
        name="gains_and_near",
    )(
        turn,
        me,
        baseline_station_pairs.T,
        arrived,
        baseline_station_pairs,
        band_weights.T,
        band_offset.reshape(1, channels),
    )
    return pl.pallas_call(
        functools.partial(finish_kernel, capacity),
        out_shape=shape((owned, parts, channels), bf16),
        in_specs=[smem, smem, smem] + [vmem] * (3 + len(far)),
        out_specs=vmem,
        scratch_shapes=[
            pltpu.VMEM((chunks, owned, parts, LANES), f32),
            pltpu.VMEM((chunks, owned, parts, LANES), f32),
        ],
        compiler_params=some,
        name="sum_and_apply",
    )(turn, me, slots, sums, gains, recip, *far)


def solution(mesh):
    placed = (
        P(("groups", "bl"), None, None),
        P(("groups", "bl"), None),
        P(("groups", "bl")),
        P("bl", None),
        P(("groups", "bl"), None, None),
        P("groups", None),
        P("groups"),
    )
    return jax.shard_map(
        on_device,
        mesh=mesh,
        in_specs=placed,
        out_specs=P(("groups", "bl"), None, None),
        check_vma=False,
    )
```

```python
import functools

import jax
import jax.numpy as jnp
from jax import lax
from jax.experimental import pallas as pl
from jax.experimental.pallas import tpu as pltpu
from jax.sharding import PartitionSpec as P

LANES = 128
SUB = 8
USED = 48
ALL_VMEM = 60 * 1024 * 1024
SOME_VMEM = 24 * 1024 * 1024


def round_up(value, unit):
    return -(-value // unit) * unit


def start_all(pairs, sems):
    moves = [pltpu.make_async_copy(src, dst, sems.at[i]) for i, (src, dst) in enumerate(pairs)]
    for move in moves:
        move.start()
    return moves


def pack_kernel(
    capacity,
    near,
    me_s,
    owner_hbm,
    owner_row_hbm,
    slot_row_hbm,
    vis_hbm,
    coarse_hbm,
    *rest,
):
    outs = rest[:-10]
    (
        owner_s,
        count_s,
        owner_ref,
        slot_ref,
        vis_ref,
        coarse_ref,
        turn_ref,
        meta_ref,
        block_ref,
        sems,
    ) = rest[-10:]
    rows = vis_ref.shape[0]
    chunks = vis_ref.shape[2] // LANES
    devices = block_ref.shape[0]
    terms, stations = coarse_ref.shape
    half = stations // 2
    depth = meta_ref.shape[0]
    gain_tiles = (depth - 1) // 2
    moves = start_all(
        (
            (vis_hbm, vis_ref),
            (coarse_hbm, coarse_ref),
            (owner_hbm, owner_s),
            (owner_row_hbm, owner_ref),
            (slot_row_hbm, slot_ref),
        ),
        sems,
    )
    turn_ref[...] = jnp.zeros_like(turn_ref)
    for d in range(devices):
        count_s[d] = 0
    me = me_s[0]
    for move in moves[1:]:
        move.wait()

    turn_ref[0:terms, 0:half] = coarse_ref[:, 0:half]
    turn_ref[64 : 64 + terms, 0:half] = coarse_ref[:, half:stations]
    gains = turn_ref[...].T
    high = gains.astype(jnp.bfloat16)
    low = (gains - high.astype(jnp.float32)).astype(jnp.bfloat16)
    for i in range(gain_tiles):
        meta_ref[i] = high[i * SUB : (i + 1) * SUB, :]
        meta_ref[gain_tiles + i] = low[i * SUB : (i + 1) * SUB, :]
    sub = lax.broadcasted_iota(jnp.int32, (SUB, LANES), 0)
    codes = jnp.where(sub == 0, owner_ref[...], slot_ref[...])
    meta_ref[2 * gain_tiles] = codes.astype(jnp.float32).astype(jnp.bfloat16)
    at = chunks * capacity
    if near > 1:
        pairs = [(meta_ref, outs[x].at[pl.ds(at, depth)]) for x in range(near + 1)]
    else:
        pairs = [(meta_ref, outs[1])]
    sends = start_all(pairs, sems.at[pl.ds(1, len(pairs))])
    moves[0].wait()

    def place(r, carry):
        x = owner_s[r] ^ me
        k = count_s[x]
        count_s[x] = k + 1
        for c in range(chunks):
            block_ref[x, chunks * k + c] = vis_ref[r, :, c * LANES : (c + 1) * LANES]
        return carry

    lax.fori_loop(0, rows, place, 0, unroll=8)
    start = 1 + len(pairs)
    if near > 1:
        pairs = [(block_ref.at[x], outs[x].at[pl.ds(0, at)]) for x in range(devices)]
    else:
        pairs = [(block_ref, outs[0])]
    sends += start_all(pairs, sems.at[pl.ds(start, len(pairs))])
    for send in sends:
        send.wait()


def add_partner_kernel(at, depth, first_hbm, *rest):
    sems = rest[-1]
    outs = rest[len(rest) // 2 : -1]
    moves = start_all(
        [(first_hbm.at[pl.ds(at, depth)], out.at[pl.ds(at + depth, depth)]) for out in outs], sems
    )
    for move in moves:
        move.wait()


def list_rows(owner, slot, target, capacity):
    senders = owner.shape[0]
    mine = owner == target
    counted = mine.astype(jnp.float32)
    before = lax.broadcasted_iota(jnp.int32, (LANES, LANES), 0) < lax.broadcasted_iota(
        jnp.int32, (LANES, LANES), 1
    )
    rank = jnp.dot(
        counted.astype(jnp.bfloat16),
        before.astype(jnp.float32).astype(jnp.bfloat16),
        preferred_element_type=jnp.float32,
    )
    lane = lax.broadcasted_iota(jnp.int32, (senders, LANES), 1)
    count = jnp.sum(counted, axis=1, keepdims=True)
    listing = jnp.where(lane == capacity, count, 0.0)
    for k in range(capacity):
        here = jnp.logical_and(mine, rank == float(k))
        kth = jnp.sum(jnp.where(here, slot, 0.0), axis=1, keepdims=True)
        listing = jnp.where(lane == k, kth, listing)
    return listing.astype(jnp.int32), mine


def add_rows(acc_ref, slots_s, line, capacity, rows_ref):
    chunks = acc_ref.shape[0]

    def add(k, carry):
        b = slots_s[line, k]
        for c in range(chunks):
            acc_ref[c, b] += rows_ref[chunks * k + c].astype(jnp.float32)
        return carry

    lax.fori_loop(0, slots_s[line, capacity], add, 0)


def prepare_kernel(
    capacity,
    near,
    stations,
    order,
    turn_s,
    me_s,
    pairs_s,
    pairs_ref,
    weights_ref,
    offset_ref,
    *rest,
):
    arrived = dict(zip(order, rest[:-12]))
    gains_ref, recip_ref, slots_ref, sums_ref = rest[-12:-8]
    metas_ref, table_ref, pick_ref, rows_ref, codes_ref, slots_s, slots_v, sems = rest[-8:]
    devices, depth, _, _ = metas_ref.shape
    owned = recip_ref.shape[0]
    channels = weights_ref.shape[1]
    half = stations // 2
    gain_tiles = (depth - 1) // 2
    chunks = channels // LANES
    at = capacity * chunks
    if near == 1:
        pairs = [(arrived[0], metas_ref)]
    else:
        pairs = [(arrived[x].at[pl.ds(at, depth)], metas_ref.at[x]) for x in range(near)]
        pairs += [
            (arrived[x].at[pl.ds(at + depth, depth)], metas_ref.at[near + x]) for x in range(near)
        ]
        pairs += [(arrived[x].at[pl.ds(0, at)], rows_ref.at[i]) for i, x in enumerate(order)]
    moves = start_all(pairs, sems)
    early = min(len(moves), 2 * near)
    for move in moves[:early]:
        move.wait()

    for x in range(devices):
        for i in range(gain_tiles):
            table_ref[x, i * SUB : (i + 1) * SUB, :] = metas_ref[x, i].astype(
                jnp.float32
            ) + metas_ref[x, gain_tiles + i].astype(jnp.float32)
        code = metas_ref[x, 2 * gain_tiles].astype(jnp.float32)
        codes_ref[0, x : x + 1, :] = code[0:1, :]
        codes_ref[1, x : x + 1, :] = code[1:2, :]
    owner, slot = codes_ref[0], codes_ref[1]
    listing, mine = list_rows(owner, slot, me_s[0].astype(jnp.float32), capacity)
    slots_ref[...] = listing
    slots_v[...] = listing
    move = pltpu.make_async_copy(slots_v, slots_s, sems.at[0])
    move.start()

    which = lax.broadcasted_iota(jnp.int32, (owned, LANES), 0).astype(jnp.float32)
    codes_ref[0] = jnp.where(mine, slot, -1.0)
    hits = jnp.zeros((owned, LANES), jnp.float32)
    for x in range(devices):
        hits = hits + (codes_ref[0, x : x + 1, :] == which).astype(jnp.float32)
    tally = jnp.sum(hits, axis=1, keepdims=True)
    recip_ref[...] = jnp.broadcast_to(1.0 / jnp.maximum(tally, 1.0), recip_ref.shape)

    turn = turn_s[0]

    def pick(b, carry):
        for side in range(2):
            s = pairs_s[side, b]
            d = s // stations
            within = s - d * stations
            row = jnp.where(within >= half, within - half, within)
            pick_ref[pl.ds(side * owned + b, 1), :] = table_ref[d ^ turn, pl.ds(row, 1), :]
        return carry

    lax.fori_loop(0, owned, pick, 0, unroll=4)

    knot = (lax.broadcasted_iota(jnp.int32, (LANES, channels), 0) & 63) >> 3
    basis = jnp.zeros((LANES, channels), jnp.float32)
    for step in range(3):
        basis = basis + jnp.where(
            knot == offset_ref[...] + step, weights_ref[step : step + 1, :], 0.0
        )
    part = lax.broadcasted_iota(jnp.int32, (LANES, channels), 0) & 7
    column = lax.broadcasted_iota(jnp.int32, (owned, LANES), 1)
    used = (column & 63) < USED
    picked = []
    for side in range(2):
        within = lax.rem(pairs_ref[:, side : side + 1], stations)
        keep = jnp.logical_and(used, (column >= 64) == (within >= half))
        picked.append(jnp.where(keep, pick_ref[side * owned : (side + 1) * owned, :], 0.0))
    both = jnp.concatenate(picked, axis=0)
    for j in range(8):
        fine = jnp.dot(
            both,
            jnp.where(part == j, basis, 0.0),
            precision=lax.Precision.HIGHEST,
            preferred_element_type=jnp.float32,
        )
        gains_ref[j] = fine.astype(jnp.bfloat16).astype(jnp.float32)

    for c in range(sums_ref.shape[0]):
        sums_ref[c] = jnp.zeros_like(sums_ref[c])
    for other in moves[early:]:
        other.wait()
    move.wait()
    if near > 1:
        for i, x in enumerate(order):
            add_rows(sums_ref, slots_s, x, capacity, rows_ref.at[i])


def finish_kernel(capacity, order, slots_s, sums_ref, gains_ref, recip_ref, *rest):
    far = rest[:-3]
    out_ref, acc_ref, res_ref = rest[-3:]
    owned, parts, channels = out_ref.shape
    chunks = channels // LANES
    acc_ref[...] = sums_ref[...]
    if len(far) > 1:
        for x, rows_ref in zip(order, far):
            add_rows(acc_ref, slots_s, x, capacity, rows_ref)
    else:

        def from_device(d, carry):
            add_rows(acc_ref, slots_s, d, capacity, far[0].at[d])
            return carry

        lax.fori_loop(0, far[0].shape[0], from_device, 0)

    flat = acc_ref.reshape(chunks * owned * parts, LANES)
    done = res_ref.reshape(chunks * owned * parts, LANES)
    for b0 in range(0, owned, SUB):
        scale = recip_ref[b0 : b0 + SUB, :]
        for c in range(chunks):
            row = (c * owned + b0) * parts
            cols = slice(c * LANES, (c + 1) * LANES)
            vis = [flat[pl.ds(row + j, SUB, stride=parts), :] for j in range(parts)]
            lhs = [gains_ref[j, b0 : b0 + SUB, cols] for j in range(parts)]
            rhs = [gains_ref[j, owned + b0 : owned + b0 + SUB, cols] for j in range(parts)]
            mid_re, mid_im = [], []
            for row_a in range(2):
                for col_b in range(2):
                    re = im = 0.0
                    for inner in range(2):
                        lr, li = lhs[2 * row_a + inner], lhs[4 + 2 * row_a + inner]
                        vr, vi = vis[2 * inner + col_b], vis[4 + 2 * inner + col_b]
                        re = re + lr * vr - li * vi
                        im = im + lr * vi + li * vr
                    mid_re.append(re * scale)
                    mid_im.append(im * scale)
            for row_a in range(2):
                for col_b in range(2):
                    re = im = 0.0
                    for inner in range(2):
                        mr, mi = mid_re[2 * row_a + inner], mid_im[2 * row_a + inner]
                        rr, ri = rhs[2 * col_b + inner], rhs[4 + 2 * col_b + inner]
                        re = re + mr * rr + mi * ri
                        im = im + mi * rr - mr * ri
                    j = 2 * row_a + col_b
                    done[pl.ds(row + j, SUB, stride=parts), :] = re
                    done[pl.ds(row + 4 + j, SUB, stride=parts), :] = im
    for c in range(chunks):
        out_ref[:, :, c * LANES : (c + 1) * LANES] = res_ref[c].astype(out_ref.dtype)


def on_device(
    visibilities,
    row_owner,
    row_slot,
    baseline_station_pairs,
    gains_coarse,
    band_weights,
    band_offset,
):
    devices = lax.axis_size("bl")
    rows, parts, channels = visibilities.shape
    capacity = 2 * rows // devices
    owned = baseline_station_pairs.shape[0]
    stations, _, knots = gains_coarse.shape
    chunks = channels // LANES
    gain_tiles = round_up(stations // 2, SUB) // SUB
    depth = 2 * gain_tiles + 1
    near = devices // 2 if devices <= 16 else 1
    halves = near > 1
    f32, bf16, i32 = jnp.float32, jnp.bfloat16, jnp.int32
    vmem = pl.BlockSpec(memory_space=pltpu.VMEM)
    smem = pl.BlockSpec(memory_space=pltpu.SMEM)
    hbm = pl.BlockSpec(memory_space=pltpu.HBM)
    anywhere = pl.BlockSpec(memory_space=pl.ANY)
    most = pltpu.CompilerParams(vmem_limit_bytes=ALL_VMEM)
    some = pltpu.CompilerParams(vmem_limit_bytes=SOME_VMEM)
    shape = jax.ShapeDtypeStruct
    dma = pltpu.SemaphoreType.DMA

    me = lax.axis_index("bl").astype(i32).reshape(1)
    turn = me if halves else jnp.zeros_like(me)
    owner = row_owner.reshape(rows)
    coarse = gains_coarse.transpose(2, 1, 0).reshape(knots * parts, stations)
    block = (chunks * capacity, parts, LANES)
    rows_at = chunks * capacity
    if halves:
        outs = [shape((rows_at + 2 * depth, parts, LANES), bf16)] * near
        outs += [shape((rows_at + depth, parts, LANES), bf16)]
        outs += [shape(block, bf16)] * (near - 1)
    else:
        outs = [shape((devices,) + block, bf16), shape((depth, SUB, LANES), bf16)]
    sent = pl.pallas_call(
        functools.partial(pack_kernel, capacity, near),
        out_shape=outs,
        in_specs=[smem] + [hbm] * 5,
        out_specs=[hbm] * len(outs),
        scratch_shapes=[
            pltpu.SMEM((rows,), i32),
            pltpu.SMEM((devices,), i32),
            pltpu.VMEM((1, rows), i32),
            pltpu.VMEM((1, rows), i32),
            pltpu.VMEM((rows, parts, channels), bf16),
            pltpu.VMEM((knots * parts, stations), f32),
            pltpu.VMEM((LANES, LANES), f32),
            pltpu.VMEM((depth, SUB, LANES), bf16),
            pltpu.VMEM((devices,) + block, bf16),
            dma((5 + near + devices,)),
        ],
        compiler_params=most,
        name="pack_rows",
    )(
        turn,
        owner,
        row_owner.reshape(1, rows),
        row_slot.reshape(1, rows),
        visibilities,
        coarse,
    )

    def swap(array, x):
        return lax.ppermute(array, "bl", [(d, d ^ x) for d in range(devices)])

    if halves:
        arrived = {near: swap(sent[near], near)}
        packed = pl.pallas_call(
            functools.partial(add_partner_kernel, rows_at, depth),
            out_shape=[shape(a.shape, a.dtype) for a in sent[:near]],
            in_specs=[hbm] * (1 + near),
            out_specs=[hbm] * near,
            scratch_shapes=[dma((near,))],
            input_output_aliases={1 + x: x for x in range(near)},
            compiler_params=most,
            name="add_partner",
        )(arrived[near], *sent[:near])
        arrived[0] = packed[0]
        for x in range(1, near):
            arrived[x] = swap(packed[x], x)
            arrived[near + x] = swap(sent[near + x], near + x)
        spread = list(range(near + 4, devices - 2)) + [None] * near
        order = list(range(near, near + 4))
        for x in range(1, near):
            order += [x] + ([spread.pop(0)] if x % 2 else [])
        order = [0] + [x for x in order if x is not None]
        late = [x for x in range(devices) if x not in order]
    else:
        arrived = {
            0: lax.all_gather(sent[1], "bl", axis=0),
            1: lax.all_to_all(sent[0], "bl", split_axis=0, concat_axis=0, tiled=True),
        }
        order, late = [0], [1]

    gains, recip, slots, sums = pl.pallas_call(
        functools.partial(prepare_kernel, capacity, near, stations, order),
        out_shape=(
            shape((parts, 2 * owned, channels), f32),
            shape((owned, LANES), f32),
            shape((devices, LANES), i32),
            shape((chunks, owned, parts, LANES), f32),
        ),
        in_specs=[smem, smem, smem, vmem, vmem, vmem] + [anywhere] * len(order),
        out_specs=(vmem,) * 4,
        scratch_shapes=[
            pltpu.VMEM((devices, depth, SUB, LANES), bf16),
            pltpu.VMEM((devices, gain_tiles * SUB, LANES), f32),
            pltpu.VMEM((2 * owned, LANES), f32),
            pltpu.VMEM((len(order),) + block, bf16),
            pltpu.VMEM((2, devices, LANES), f32),
            pltpu.SMEM((devices, LANES), i32),
            pltpu.VMEM((devices, LANES), i32),
            dma((2 * near + len(order),)),
        ],
        compiler_params=some,
        name="gains_and_sums",
    )(
        turn,
        me,
        baseline_station_pairs.T,
        baseline_station_pairs,
        band_weights.T,
        band_offset.reshape(1, channels),
        *[arrived[x] for x in order],
    )
    return pl.pallas_call(
        functools.partial(finish_kernel, capacity, late),
        out_shape=shape((owned, parts, channels), bf16),
        in_specs=[smem] + [vmem] * (3 + len(late)),
        out_specs=vmem,
        scratch_shapes=[
            pltpu.VMEM((chunks, owned, parts, LANES), f32),
            pltpu.VMEM((chunks, owned, parts, LANES), f32),
        ],
        compiler_params=some,
        name="sum_and_apply",
    )(slots, sums, gains, recip, *[arrived[x] for x in late])


def solution(mesh):
    placed = (
        P(("groups", "bl"), None, None),
        P(("groups", "bl"), None),
        P(("groups", "bl")),
        P("bl", None),
        P(("groups", "bl"), None, None),
        P("groups", None),
        P("groups"),
    )
    return jax.shard_map(
        on_device,
        mesh=mesh,
        in_specs=placed,
        out_specs=P(("groups", "bl"), None, None),
        check_vma=False,
    )
```

```python
import functools

import jax
import jax.numpy as jnp
from jax import lax
from jax.experimental import pallas as pl
from jax.experimental.pallas import tpu as pltpu
from jax.sharding import PartitionSpec as P

LANES = 128
SUB = 8
USED = 48
ALL_VMEM = 60 * 1024 * 1024
SOME_VMEM = 24 * 1024 * 1024


def round_up(value, unit):
    return -(-value // unit) * unit


def with_gains(near):
    return list(range(near)) + list(range(near, 2 * near, 2))


def start_all(pairs, sems):
    moves = [pltpu.make_async_copy(src, dst, sems.at[i]) for i, (src, dst) in enumerate(pairs)]
    for move in moves:
        move.start()
    return moves


def pack_kernel(
    capacity,
    near,
    me_s,
    owner_hbm,
    owner_row_hbm,
    slot_row_hbm,
    vis_hbm,
    coarse_hbm,
    *rest,
):
    outs = rest[:-10]
    (
        owner_s,
        count_s,
        owner_ref,
        slot_ref,
        vis_ref,
        coarse_ref,
        turn_ref,
        meta_ref,
        block_ref,
        sems,
    ) = rest[-10:]
    rows = vis_ref.shape[0]
    chunks = vis_ref.shape[2] // LANES
    devices = block_ref.shape[0]
    terms, stations = coarse_ref.shape
    half = stations // 2
    depth = meta_ref.shape[0]
    gain_tiles = (depth - 1) // 2
    moves = start_all(
        (
            (vis_hbm, vis_ref),
            (coarse_hbm, coarse_ref),
            (owner_hbm, owner_s),
            (owner_row_hbm, owner_ref),
            (slot_row_hbm, slot_ref),
        ),
        sems,
    )
    turn_ref[...] = jnp.zeros_like(turn_ref)
    for d in range(devices):
        count_s[d] = 0
    me = me_s[0]
    for move in moves[1:]:
        move.wait()

    turn_ref[0:terms, 0:half] = coarse_ref[:, 0:half]
    turn_ref[64 : 64 + terms, 0:half] = coarse_ref[:, half:stations]
    gains = turn_ref[...].T
    high = gains.astype(jnp.bfloat16)
    low = (gains - high.astype(jnp.float32)).astype(jnp.bfloat16)
    for i in range(gain_tiles):
        meta_ref[i] = high[i * SUB : (i + 1) * SUB, :]
        meta_ref[gain_tiles + i] = low[i * SUB : (i + 1) * SUB, :]
    sub = lax.broadcasted_iota(jnp.int32, (SUB, LANES), 0)
    codes = jnp.where(sub == 0, owner_ref[...], slot_ref[...])
    meta_ref[2 * gain_tiles] = codes.astype(jnp.float32).astype(jnp.bfloat16)
    at = chunks * capacity
    if near > 1:
        pairs = [(meta_ref, outs[x].at[pl.ds(at, depth)]) for x in with_gains(near)]
    else:
        pairs = [(meta_ref, outs[1])]
    sends = start_all(pairs, sems.at[pl.ds(1, len(pairs))])
    moves[0].wait()

    def place(r, carry):
        x = owner_s[r] ^ me
        k = count_s[x]
        count_s[x] = k + 1
        for c in range(chunks):
            block_ref[x, chunks * k + c] = vis_ref[r, :, c * LANES : (c + 1) * LANES]
        return carry

    lax.fori_loop(0, rows, place, 0, unroll=8)
    start = 1 + len(pairs)
    if near > 1:
        pairs = [(block_ref.at[x], outs[x].at[pl.ds(0, at)]) for x in range(devices)]
    else:
        pairs = [(block_ref, outs[0])]
    sends += start_all(pairs, sems.at[pl.ds(start, len(pairs))])
    for send in sends:
        send.wait()


def collect_kernel(at, depth, *rest):
    blocks, (out_ref, sems) = rest[:-2], rest[-2:]
    moves = start_all(
        [
            (block.at[pl.ds(at, depth)], out_ref.at[pl.ds(i * depth, depth)])
            for i, block in enumerate(blocks)
        ],
        sems,
    )
    for move in moves:
        move.wait()


def list_rows(owner, slot, target, capacity):
    senders = owner.shape[0]
    mine = owner == target
    counted = mine.astype(jnp.float32)
    before = lax.broadcasted_iota(jnp.int32, (LANES, LANES), 0) < lax.broadcasted_iota(
        jnp.int32, (LANES, LANES), 1
    )
    rank = jnp.dot(
        counted.astype(jnp.bfloat16),
        before.astype(jnp.float32).astype(jnp.bfloat16),
        preferred_element_type=jnp.float32,
    )
    lane = lax.broadcasted_iota(jnp.int32, (senders, LANES), 1)
    count = jnp.sum(counted, axis=1, keepdims=True)
    listing = jnp.where(lane == capacity, count, 0.0)
    for k in range(capacity):
        here = jnp.logical_and(mine, rank == float(k))
        kth = jnp.sum(jnp.where(here, slot, 0.0), axis=1, keepdims=True)
        listing = jnp.where(lane == k, kth, listing)
    return listing.astype(jnp.int32), mine


def add_rows(acc_ref, slots_s, line, capacity, rows_ref):
    chunks = acc_ref.shape[0]

    def add(k, carry):
        b = slots_s[line, k]
        for c in range(chunks):
            acc_ref[c, b] += rows_ref[chunks * k + c].astype(jnp.float32)
        return carry

    lax.fori_loop(0, slots_s[line, capacity], add, 0)


def prepare_kernel(
    capacity,
    near,
    stations,
    order,
    turn_s,
    me_s,
    pairs_s,
    pairs_ref,
    weights_ref,
    offset_ref,
    *rest,
):
    arrived, passed = dict(zip(order, rest)), rest[len(order)]
    gains_ref, recip_ref, slots_ref, sums_ref = rest[-12:-8]
    metas_ref, table_ref, pick_ref, rows_ref, codes_ref, slots_s, slots_v, sems = rest[-8:]
    devices, depth, _, _ = metas_ref.shape
    owned = recip_ref.shape[0]
    channels = weights_ref.shape[1]
    half = stations // 2
    gain_tiles = (depth - 1) // 2
    chunks = channels // LANES
    at = capacity * chunks
    if near == 1:
        pairs = [(arrived[0], metas_ref)]
    else:
        pairs = [(arrived[x].at[pl.ds(at, depth)], metas_ref.at[x]) for x in with_gains(near)]
        pairs += [
            (passed.at[pl.ds(i * depth, depth)], metas_ref.at[near + 1 + 2 * i])
            for i in range(near // 2)
        ]
        pairs += [(arrived[x].at[pl.ds(0, at)], rows_ref.at[i]) for i, x in enumerate(order)]
    moves = start_all(pairs, sems)
    early = min(len(moves), 2 * near)
    for move in moves[:early]:
        move.wait()

    for x in range(devices):
        for i in range(gain_tiles):
            table_ref[x, i * SUB : (i + 1) * SUB, :] = metas_ref[x, i].astype(
                jnp.float32
            ) + metas_ref[x, gain_tiles + i].astype(jnp.float32)
        code = metas_ref[x, 2 * gain_tiles].astype(jnp.float32)
        codes_ref[0, x : x + 1, :] = code[0:1, :]
        codes_ref[1, x : x + 1, :] = code[1:2, :]
    owner, slot = codes_ref[0], codes_ref[1]
    listing, mine = list_rows(owner, slot, me_s[0].astype(jnp.float32), capacity)
    slots_ref[...] = listing
    slots_v[...] = listing
    move = pltpu.make_async_copy(slots_v, slots_s, sems.at[0])
    move.start()

    which = lax.broadcasted_iota(jnp.int32, (owned, LANES), 0).astype(jnp.float32)
    codes_ref[0] = jnp.where(mine, slot, -1.0)
    hits = jnp.zeros((owned, LANES), jnp.float32)
    for x in range(devices):
        hits = hits + (codes_ref[0, x : x + 1, :] == which).astype(jnp.float32)
    tally = jnp.sum(hits, axis=1, keepdims=True)
    recip_ref[...] = jnp.broadcast_to(1.0 / jnp.maximum(tally, 1.0), recip_ref.shape)

    turn = turn_s[0]

    def pick(b, carry):
        for side in range(2):
            s = pairs_s[side, b]
            d = s // stations
            within = s - d * stations
            row = jnp.where(within >= half, within - half, within)
            pick_ref[pl.ds(side * owned + b, 1), :] = table_ref[d ^ turn, pl.ds(row, 1), :]
        return carry

    lax.fori_loop(0, owned, pick, 0, unroll=4)

    knot = (lax.broadcasted_iota(jnp.int32, (LANES, channels), 0) & 63) >> 3
    basis = jnp.zeros((LANES, channels), jnp.float32)
    for step in range(3):
        basis = basis + jnp.where(
            knot == offset_ref[...] + step, weights_ref[step : step + 1, :], 0.0
        )
    part = lax.broadcasted_iota(jnp.int32, (LANES, channels), 0) & 7
    column = lax.broadcasted_iota(jnp.int32, (owned, LANES), 1)
    used = (column & 63) < USED
    picked = []
    for side in range(2):
        within = lax.rem(pairs_ref[:, side : side + 1], stations)
        keep = jnp.logical_and(used, (column >= 64) == (within >= half))
        picked.append(jnp.where(keep, pick_ref[side * owned : (side + 1) * owned, :], 0.0))
    both = jnp.concatenate(picked, axis=0)
    for j in range(8):
        fine = jnp.dot(
            both,
            jnp.where(part == j, basis, 0.0),
            precision=lax.Precision.HIGHEST,
            preferred_element_type=jnp.float32,
        )
        gains_ref[j] = fine.astype(jnp.bfloat16).astype(jnp.float32)

    for c in range(sums_ref.shape[0]):
        sums_ref[c] = jnp.zeros_like(sums_ref[c])
    for other in moves[early:]:
        other.wait()
    move.wait()
    if near > 1:
        for i, x in enumerate(order):
            add_rows(sums_ref, slots_s, x, capacity, rows_ref.at[i])


def finish_kernel(capacity, order, slots_s, sums_ref, gains_ref, recip_ref, *rest):
    far = rest[:-3]
    out_ref, acc_ref, res_ref = rest[-3:]
    owned, parts, channels = out_ref.shape
    chunks = channels // LANES
    acc_ref[...] = sums_ref[...]
    if len(far) > 1:
        for x, rows_ref in zip(order, far):
            add_rows(acc_ref, slots_s, x, capacity, rows_ref)
    else:

        def from_device(d, carry):
            add_rows(acc_ref, slots_s, d, capacity, far[0].at[d])
            return carry

        lax.fori_loop(0, far[0].shape[0], from_device, 0)

    flat = acc_ref.reshape(chunks * owned * parts, LANES)
    done = res_ref.reshape(chunks * owned * parts, LANES)
    for b0 in range(0, owned, SUB):
        scale = recip_ref[b0 : b0 + SUB, :]
        for c in range(chunks):
            row = (c * owned + b0) * parts
            cols = slice(c * LANES, (c + 1) * LANES)
            vis = [flat[pl.ds(row + j, SUB, stride=parts), :] for j in range(parts)]
            lhs = [gains_ref[j, b0 : b0 + SUB, cols] for j in range(parts)]
            rhs = [gains_ref[j, owned + b0 : owned + b0 + SUB, cols] for j in range(parts)]
            mid_re, mid_im = [], []
            for row_a in range(2):
                for col_b in range(2):
                    re = im = 0.0
                    for inner in range(2):
                        lr, li = lhs[2 * row_a + inner], lhs[4 + 2 * row_a + inner]
                        vr, vi = vis[2 * inner + col_b], vis[4 + 2 * inner + col_b]
                        re = re + lr * vr - li * vi
                        im = im + lr * vi + li * vr
                    mid_re.append(re * scale)
                    mid_im.append(im * scale)
            for row_a in range(2):
                for col_b in range(2):
                    re = im = 0.0
                    for inner in range(2):
                        mr, mi = mid_re[2 * row_a + inner], mid_im[2 * row_a + inner]
                        rr, ri = rhs[2 * col_b + inner], rhs[4 + 2 * col_b + inner]
                        re = re + mr * rr + mi * ri
                        im = im + mi * rr - mr * ri
                    j = 2 * row_a + col_b
                    done[pl.ds(row + j, SUB, stride=parts), :] = re
                    done[pl.ds(row + 4 + j, SUB, stride=parts), :] = im
    for c in range(chunks):
        out_ref[:, :, c * LANES : (c + 1) * LANES] = res_ref[c].astype(out_ref.dtype)


def on_device(
    visibilities,
    row_owner,
    row_slot,
    baseline_station_pairs,
    gains_coarse,
    band_weights,
    band_offset,
):
    devices = lax.axis_size("bl")
    rows, parts, channels = visibilities.shape
    capacity = 2 * rows // devices
    owned = baseline_station_pairs.shape[0]
    stations, _, knots = gains_coarse.shape
    chunks = channels // LANES
    gain_tiles = round_up(stations // 2, SUB) // SUB
    depth = 2 * gain_tiles + 1
    near = devices // 2 if devices <= 16 else 1
    halves = near > 1
    f32, bf16, i32 = jnp.float32, jnp.bfloat16, jnp.int32
    vmem = pl.BlockSpec(memory_space=pltpu.VMEM)
    smem = pl.BlockSpec(memory_space=pltpu.SMEM)
    hbm = pl.BlockSpec(memory_space=pltpu.HBM)
    anywhere = pl.BlockSpec(memory_space=pl.ANY)
    most = pltpu.CompilerParams(vmem_limit_bytes=ALL_VMEM)
    some = pltpu.CompilerParams(vmem_limit_bytes=SOME_VMEM)
    shape = jax.ShapeDtypeStruct
    dma = pltpu.SemaphoreType.DMA

    me = lax.axis_index("bl").astype(i32).reshape(1)
    turn = me if halves else jnp.zeros_like(me)
    owner = row_owner.reshape(rows)
    coarse = gains_coarse.transpose(2, 1, 0).reshape(knots * parts, stations)
    block = (chunks * capacity, parts, LANES)
    rows_at = chunks * capacity
    if halves:
        outs = [
            shape((rows_at + (depth if x in with_gains(near) else 0), parts, LANES), bf16)
            for x in range(devices)
        ]
    else:
        outs = [shape((devices,) + block, bf16), shape((depth, SUB, LANES), bf16)]
    sent = pl.pallas_call(
        functools.partial(pack_kernel, capacity, near),
        out_shape=outs,
        in_specs=[smem] + [hbm] * 5,
        out_specs=[hbm] * len(outs),
        scratch_shapes=[
            pltpu.SMEM((rows,), i32),
            pltpu.SMEM((devices,), i32),
            pltpu.VMEM((1, rows), i32),
            pltpu.VMEM((1, rows), i32),
            pltpu.VMEM((rows, parts, channels), bf16),
            pltpu.VMEM((knots * parts, stations), f32),
            pltpu.VMEM((LANES, LANES), f32),
            pltpu.VMEM((depth, SUB, LANES), bf16),
            pltpu.VMEM((devices,) + block, bf16),
            dma((5 + 2 * devices,)),
        ],
        compiler_params=most,
        name="pack_rows",
    )(
        turn,
        owner,
        row_owner.reshape(1, rows),
        row_slot.reshape(1, rows),
        visibilities,
        coarse,
    )

    def swap(array, x):
        return lax.ppermute(array, "bl", [(d, d ^ x) for d in range(devices)])

    if halves:
        arrived = {0: sent[0]}
        for x in range(1, devices):
            arrived[x] = swap(sent[x], x)
        even = list(range(near, devices, 2))
        collected = pl.pallas_call(
            functools.partial(collect_kernel, rows_at, depth),
            out_shape=shape((len(even) * depth, parts, LANES), bf16),
            in_specs=[anywhere] * len(even),
            out_specs=vmem,
            scratch_shapes=[dma((len(even),))],
            compiler_params=some,
            name="collect_gains",
        )(*[arrived[x] for x in even])
        passed = swap(collected, 1)
        order = [0]
        cross = even + [x + 1 for x in even]
        for i, x in enumerate(cross[: near // 2 + 1]):
            order += [x] + ([i] if 0 < i < near // 2 else [])
        order += [x for x in range(1, near) if x not in order]
        late = [x for x in cross if x not in order]
    else:
        arrived = {
            0: lax.all_gather(sent[1], "bl", axis=0),
            1: lax.all_to_all(sent[0], "bl", split_axis=0, concat_axis=0, tiled=True),
        }
        order, late, passed = [0], [1], arrived[0]

    gains, recip, slots, sums = pl.pallas_call(
        functools.partial(prepare_kernel, capacity, near, stations, order),
        out_shape=(
            shape((parts, 2 * owned, channels), f32),
            shape((owned, LANES), f32),
            shape((devices, LANES), i32),
            shape((chunks, owned, parts, LANES), f32),
        ),
        in_specs=[smem, smem, smem, vmem, vmem, vmem, hbm] + [anywhere] * len(order),
        out_specs=(vmem,) * 4,
        scratch_shapes=[
            pltpu.VMEM((devices, depth, SUB, LANES), bf16),
            pltpu.VMEM((devices, gain_tiles * SUB, LANES), f32),
            pltpu.VMEM((2 * owned, LANES), f32),
            pltpu.VMEM((len(order),) + block, bf16),
            pltpu.VMEM((2, devices, LANES), f32),
            pltpu.SMEM((devices, LANES), i32),
            pltpu.VMEM((devices, LANES), i32),
            dma((2 * near + len(order),)),
        ],
        compiler_params=some,
        name="gains_and_sums",
    )(
        turn,
        me,
        baseline_station_pairs.T,
        baseline_station_pairs,
        band_weights.T,
        band_offset.reshape(1, channels),
        *[arrived[x] for x in order],
        passed,
    )
    return pl.pallas_call(
        functools.partial(finish_kernel, capacity, late),
        out_shape=shape((owned, parts, channels), bf16),
        in_specs=[smem] + [vmem] * (3 + len(late)),
        out_specs=vmem,
        scratch_shapes=[
            pltpu.VMEM((chunks, owned, parts, LANES), f32),
            pltpu.VMEM((chunks, owned, parts, LANES), f32),
        ],
        compiler_params=some,
        name="sum_and_apply",
    )(slots, sums, gains, recip, *[arrived[x] for x in late])


def solution(mesh):
    placed = (
        P(("groups", "bl"), None, None),
        P(("groups", "bl"), None),
        P(("groups", "bl")),
        P("bl", None),
        P(("groups", "bl"), None, None),
        P("groups", None),
        P("groups"),
    )
    return jax.shard_map(
        on_device,
        mesh=mesh,
        in_specs=placed,
        out_specs=P(("groups", "bl"), None, None),
        check_vma=False,
    )
```

```python
import functools

import jax
import jax.numpy as jnp
from jax import lax
from jax.experimental import pallas as pl
from jax.experimental.pallas import tpu as pltpu
from jax.sharding import PartitionSpec as P

LANES = 128
SUB = 8
USED = 48
ALL_VMEM = 60 * 1024 * 1024
SOME_VMEM = 24 * 1024 * 1024


def round_up(value, unit):
    return -(-value // unit) * unit


def with_gains(near):
    return list(range(near)) + list(range(near, 2 * near, 2))


def start_all(pairs, sems):
    moves = [pltpu.make_async_copy(src, dst, sems.at[i]) for i, (src, dst) in enumerate(pairs)]
    for move in moves:
        move.start()
    return moves


def pack_kernel(
    capacity,
    near,
    me_s,
    owner_hbm,
    owner_row_hbm,
    slot_row_hbm,
    vis_hbm,
    coarse_hbm,
    *rest,
):
    outs = rest[:-10]
    (
        owner_s,
        count_s,
        owner_ref,
        slot_ref,
        vis_ref,
        coarse_ref,
        turn_ref,
        meta_ref,
        block_ref,
        sems,
    ) = rest[-10:]
    rows = vis_ref.shape[0]
    chunks = vis_ref.shape[2] // LANES
    devices = block_ref.shape[0]
    terms, stations = coarse_ref.shape
    half = stations // 2
    depth = meta_ref.shape[0]
    gain_tiles = (depth - 1) // 2
    moves = start_all(
        (
            (vis_hbm, vis_ref),
            (coarse_hbm, coarse_ref),
            (owner_hbm, owner_s),
            (owner_row_hbm, owner_ref),
            (slot_row_hbm, slot_ref),
        ),
        sems,
    )
    turn_ref[...] = jnp.zeros_like(turn_ref)
    for d in range(devices):
        count_s[d] = 0
    me = me_s[0]
    for move in moves[1:]:
        move.wait()

    turn_ref[0:terms, 0:half] = coarse_ref[:, 0:half]
    turn_ref[64 : 64 + terms, 0:half] = coarse_ref[:, half:stations]
    gains = turn_ref[...].T
    high = gains.astype(jnp.bfloat16)
    low = (gains - high.astype(jnp.float32)).astype(jnp.bfloat16)
    for i in range(gain_tiles):
        meta_ref[i] = high[i * SUB : (i + 1) * SUB, :]
        meta_ref[gain_tiles + i] = low[i * SUB : (i + 1) * SUB, :]
    sub = lax.broadcasted_iota(jnp.int32, (SUB, LANES), 0)
    codes = jnp.where(sub == 0, owner_ref[...], slot_ref[...])
    meta_ref[2 * gain_tiles] = codes.astype(jnp.float32).astype(jnp.bfloat16)
    at = chunks * capacity
    if near > 1:
        pairs = [(meta_ref, outs[x].at[pl.ds(at, depth)]) for x in with_gains(near)]
    else:
        pairs = [(meta_ref, outs[1])]
    sends = start_all(pairs, sems.at[pl.ds(1, len(pairs))])
    moves[0].wait()

    def place(r, carry):
        x = owner_s[r] ^ me
        k = count_s[x]
        count_s[x] = k + 1
        for c in range(chunks):
            block_ref[x, chunks * k + c] = vis_ref[r, :, c * LANES : (c + 1) * LANES]
        return carry

    lax.fori_loop(0, rows, place, 0, unroll=8)
    start = 1 + len(pairs)
    if near > 1:
        pairs = [(block_ref.at[x], outs[x].at[pl.ds(0, at)]) for x in range(devices)]
    else:
        pairs = [(block_ref, outs[0])]
    sends += start_all(pairs, sems.at[pl.ds(start, len(pairs))])
    for send in sends:
        send.wait()


def interpolation(weights, offset, high_ref, low_ref):
    channels = weights.shape[1]
    index = lax.broadcasted_iota(jnp.int32, (LANES, channels), 0)
    knot = (index & 63) >> 3
    basis = jnp.zeros((LANES, channels), jnp.float32)
    for step in range(3):
        basis = basis + jnp.where(knot == offset + step, weights[step : step + 1, :], 0.0)
    high = basis.astype(jnp.bfloat16).astype(jnp.float32)
    low = basis - high
    part = index & 7
    for j in range(8):
        high_ref[j] = jnp.where(part == j, high, 0.0).astype(jnp.bfloat16)
        low_ref[j] = jnp.where(part == j, low, 0.0).astype(jnp.bfloat16)


def collect_kernel(
    at, depth, pairs_ref, weights_ref, offset_ref, own_ref, *rest
):
    blocks = rest[:-6]
    out_ref, own_out_ref, pairs_out_ref, high_ref, low_ref, sems = rest[-6:]
    moves = start_all(
        [
            (block.at[pl.ds(at, depth)], out_ref.at[pl.ds(i * depth, depth)])
            for i, block in enumerate(blocks)
        ]
        + [(own_ref, own_out_ref)],
        sems,
    )
    pairs_out_ref[...] = pairs_ref[...]
    interpolation(weights_ref[...], offset_ref[...], high_ref, low_ref)
    for move in moves:
        move.wait()


def list_rows(owner, slot, target, capacity):
    senders = owner.shape[0]
    mine = owner == target
    counted = mine.astype(jnp.float32)
    before = lax.broadcasted_iota(jnp.int32, (LANES, LANES), 0) < lax.broadcasted_iota(
        jnp.int32, (LANES, LANES), 1
    )
    rank = jnp.dot(
        counted.astype(jnp.bfloat16),
        before.astype(jnp.float32).astype(jnp.bfloat16),
        preferred_element_type=jnp.float32,
    )
    lane = lax.broadcasted_iota(jnp.int32, (senders, LANES), 1)
    count = jnp.sum(counted, axis=1, keepdims=True)
    listing = jnp.where(lane == capacity, count, 0.0)
    for k in range(capacity):
        here = jnp.logical_and(mine, rank == float(k))
        kth = jnp.sum(jnp.where(here, slot, 0.0), axis=1, keepdims=True)
        listing = jnp.where(lane == k, kth, listing)
    return listing.astype(jnp.int32), mine


def add_rows(acc_ref, slots_s, line, capacity, rows_ref):
    chunks = acc_ref.shape[0]

    def add(k, carry):
        b = slots_s[line, k]
        for c in range(chunks):
            acc_ref[c, b] += rows_ref[chunks * k + c].astype(jnp.float32)
        return carry

    lax.fori_loop(0, slots_s[line, capacity], add, 0)


def prepare_kernel(
    capacity,
    near,
    stations,
    order,
    turn_s,
    me_s,
    pairs_s,
    high_ref,
    low_ref,
    *rest,
):
    arrived, passed = dict(zip(order, rest)), rest[len(order)]
    gains_ref, recip_ref, slots_ref, sums_ref = rest[-12:-8]
    metas_ref, table_ref, pick_ref, rows_ref, codes_ref, slots_s, slots_v, sems = rest[-8:]
    devices, depth, _, _ = metas_ref.shape
    owned = recip_ref.shape[0]
    channels = high_ref.shape[2]
    half = stations // 2
    gain_tiles = (depth - 1) // 2
    chunks = channels // LANES
    at = capacity * chunks
    if near == 1:
        pairs = [(arrived[0], metas_ref)]
    else:
        pairs = [(arrived[x].at[pl.ds(at, depth)], metas_ref.at[x]) for x in with_gains(near)]
        pairs += [
            (passed.at[pl.ds(i * depth, depth)], metas_ref.at[near + 1 + 2 * i])
            for i in range(near // 2)
        ]
        pairs += [(arrived[x].at[pl.ds(0, at)], rows_ref.at[i]) for i, x in enumerate(order)]
    moves = start_all(pairs, sems)
    early = min(len(moves), 2 * near)
    for move in moves[:early]:
        move.wait()

    for x in range(devices):
        for i in range(gain_tiles):
            table_ref[x, i * SUB : (i + 1) * SUB, :] = metas_ref[x, i].astype(
                jnp.float32
            ) + metas_ref[x, gain_tiles + i].astype(jnp.float32)
        code = metas_ref[x, 2 * gain_tiles].astype(jnp.float32)
        codes_ref[0, x : x + 1, :] = code[0:1, :]
        codes_ref[1, x : x + 1, :] = code[1:2, :]
    owner, slot = codes_ref[0], codes_ref[1]
    listing, mine = list_rows(owner, slot, me_s[0].astype(jnp.float32), capacity)
    slots_ref[...] = listing
    slots_v[...] = listing
    move = pltpu.make_async_copy(slots_v, slots_s, sems.at[0])
    move.start()

    which = lax.broadcasted_iota(jnp.int32, (owned, LANES), 0).astype(jnp.float32)
    codes_ref[0] = jnp.where(mine, slot, -1.0)
    hits = jnp.zeros((owned, LANES), jnp.float32)
    for x in range(devices):
        hits = hits + (codes_ref[0, x : x + 1, :] == which).astype(jnp.float32)
    tally = jnp.sum(hits, axis=1, keepdims=True)
    recip_ref[...] = jnp.broadcast_to(1.0 / jnp.maximum(tally, 1.0), recip_ref.shape)

    turn = turn_s[0]
    column = lax.broadcasted_iota(jnp.int32, (1, LANES), 1)
    used = (column & 63) < USED
    upper = (column >> 6).astype(jnp.int32)

    def pick(b, carry):
        for side in range(2):
            s = pairs_s[side, b]
            d = s // stations
            within = s - d * stations
            second = jnp.where(within >= half, 1, 0)
            row = table_ref[d ^ turn, pl.ds(within - second * half, 1), :]
            keep = jnp.logical_and(used, upper == second)
            pick_ref[pl.ds(side * owned + b, 1), :] = jnp.where(keep, row, 0.0)
        return carry

    lax.fori_loop(0, owned, pick, 0, unroll=4)
    both = pick_ref[...]
    both_high = both.astype(jnp.bfloat16)
    both_low = (both - both_high.astype(jnp.float32)).astype(jnp.bfloat16)
    both_two = jnp.concatenate([both_high, both_low], axis=1)
    for j in range(8):
        high = high_ref[j]
        fine = jnp.dot(
            both_two, jnp.concatenate([high, high], axis=0), preferred_element_type=jnp.float32
        ) + jnp.dot(both_high, low_ref[j], preferred_element_type=jnp.float32)
        gains_ref[j] = fine.astype(jnp.bfloat16).astype(jnp.float32)

    for c in range(sums_ref.shape[0]):
        sums_ref[c] = jnp.zeros_like(sums_ref[c])
    for other in moves[early:]:
        other.wait()
    move.wait()
    if near > 1:
        for i, x in enumerate(order):
            add_rows(sums_ref, slots_s, x, capacity, rows_ref.at[i])


def finish_kernel(capacity, order, slots_s, sums_ref, gains_ref, recip_ref, *rest):
    far = rest[:-3]
    out_ref, acc_ref, res_ref = rest[-3:]
    owned, parts, channels = out_ref.shape
    chunks = channels // LANES
    acc_ref[...] = sums_ref[...]
    if len(far) > 1:
        for x, rows_ref in zip(order, far):
            add_rows(acc_ref, slots_s, x, capacity, rows_ref)
    else:

        def from_device(d, carry):
            add_rows(acc_ref, slots_s, d, capacity, far[0].at[d])
            return carry

        lax.fori_loop(0, far[0].shape[0], from_device, 0)

    flat = acc_ref.reshape(chunks * owned * parts, LANES)
    done = res_ref.reshape(chunks * owned * parts, LANES)
    for b0 in range(0, owned, SUB):
        scale = recip_ref[b0 : b0 + SUB, :]
        for c in range(chunks):
            row = (c * owned + b0) * parts
            cols = slice(c * LANES, (c + 1) * LANES)
            vis = [flat[pl.ds(row + j, SUB, stride=parts), :] for j in range(parts)]
            lhs = [gains_ref[j, b0 : b0 + SUB, cols] for j in range(parts)]
            rhs = [gains_ref[j, owned + b0 : owned + b0 + SUB, cols] for j in range(parts)]
            mid_re, mid_im = [], []
            for row_a in range(2):
                for col_b in range(2):
                    re = im = 0.0
                    for inner in range(2):
                        lr, li = lhs[2 * row_a + inner], lhs[4 + 2 * row_a + inner]
                        vr, vi = vis[2 * inner + col_b], vis[4 + 2 * inner + col_b]
                        re = re + lr * vr - li * vi
                        im = im + lr * vi + li * vr
                    mid_re.append(re * scale)
                    mid_im.append(im * scale)
            for row_a in range(2):
                for col_b in range(2):
                    re = im = 0.0
                    for inner in range(2):
                        mr, mi = mid_re[2 * row_a + inner], mid_im[2 * row_a + inner]
                        rr, ri = rhs[2 * col_b + inner], rhs[4 + 2 * col_b + inner]
                        re = re + mr * rr + mi * ri
                        im = im + mi * rr - mr * ri
                    j = 2 * row_a + col_b
                    done[pl.ds(row + j, SUB, stride=parts), :] = re
                    done[pl.ds(row + 4 + j, SUB, stride=parts), :] = im
    for c in range(chunks):
        out_ref[:, :, c * LANES : (c + 1) * LANES] = res_ref[c].astype(out_ref.dtype)


def on_device(
    visibilities,
    row_owner,
    row_slot,
    baseline_station_pairs,
    gains_coarse,
    band_weights,
    band_offset,
):
    devices = lax.axis_size("bl")
    rows, parts, channels = visibilities.shape
    capacity = 2 * rows // devices
    owned = baseline_station_pairs.shape[0]
    stations, _, knots = gains_coarse.shape
    chunks = channels // LANES
    gain_tiles = round_up(stations // 2, SUB) // SUB
    depth = 2 * gain_tiles + 1
    near = devices // 2 if devices <= 16 else 1
    halves = near > 1
    f32, bf16, i32 = jnp.float32, jnp.bfloat16, jnp.int32
    vmem = pl.BlockSpec(memory_space=pltpu.VMEM)
    smem = pl.BlockSpec(memory_space=pltpu.SMEM)
    hbm = pl.BlockSpec(memory_space=pltpu.HBM)
    anywhere = pl.BlockSpec(memory_space=pl.ANY)
    most = pltpu.CompilerParams(vmem_limit_bytes=ALL_VMEM)
    some = pltpu.CompilerParams(vmem_limit_bytes=SOME_VMEM)
    shape = jax.ShapeDtypeStruct
    dma = pltpu.SemaphoreType.DMA

    me = lax.axis_index("bl").astype(i32).reshape(1)
    turn = me if halves else jnp.zeros_like(me)
    owner = row_owner.reshape(rows)
    coarse = gains_coarse.transpose(2, 1, 0).reshape(knots * parts, stations)
    block = (chunks * capacity, parts, LANES)
    rows_at = chunks * capacity
    if halves:
        wide = with_gains(near) + [near + 1, near + 3]
        outs = [
            shape((rows_at + (depth if x in wide else 0), parts, LANES), bf16)
            for x in range(devices)
        ]
    else:
        outs = [shape((devices,) + block, bf16), shape((depth, SUB, LANES), bf16)]
    sent = pl.pallas_call(
        functools.partial(pack_kernel, capacity, near),
        out_shape=outs,
        in_specs=[smem] + [hbm] * 5,
        out_specs=[hbm] * len(outs),
        scratch_shapes=[
            pltpu.SMEM((rows,), i32),
            pltpu.SMEM((devices,), i32),
            pltpu.VMEM((1, rows), i32),
            pltpu.VMEM((1, rows), i32),
            pltpu.VMEM((rows, parts, channels), bf16),
            pltpu.VMEM((knots * parts, stations), f32),
            pltpu.VMEM((LANES, LANES), f32),
            pltpu.VMEM((depth, SUB, LANES), bf16),
            pltpu.VMEM((devices,) + block, bf16),
            dma((5 + 2 * devices,)),
        ],
        compiler_params=most,
        name="pack_rows",
    )(
        turn,
        owner,
        row_owner.reshape(1, rows),
        row_slot.reshape(1, rows),
        visibilities,
        coarse,
    )

    pairs = baseline_station_pairs.T
    weights = band_weights.T
    offset = band_offset.reshape(1, channels)

    def swap(array, x):
        return lax.ppermute(array, "bl", [(d, d ^ x) for d in range(devices)])

    if halves:
        arrived = {0: sent[0]}
        for x in range(1, devices):
            arrived[x] = swap(sent[x], x)
        even = list(range(near, devices, 2))
        collected, own, pairs, high, low = pl.pallas_call(
            functools.partial(collect_kernel, rows_at, depth),
            out_shape=[
                shape((len(even) * depth, parts, LANES), bf16),
                shape(sent[0].shape, bf16),
                shape((2, owned), i32),
            ]
            + [shape((parts, LANES, channels), bf16)] * 2,
            in_specs=[vmem] * 3 + [anywhere] * (1 + len(even)),
            out_specs=[vmem] * 5,
            scratch_shapes=[dma((1 + len(even),))],
            compiler_params=some,
            name="collect_gains",
        )(pairs, weights, offset, sent[0], *[arrived[x] for x in even])
        arrived[0] = own
        passed = swap(collected, 1)
        cross = even + [x + 1 for x in even]
        late = cross[near // 2 + 2 :]
        close = list(range(1, near))
        order = [0, cross[0]]
        for x in cross[1 : near // 2 + 2]:
            order += [x, close.pop(0)]
        order += close
    else:
        arrived = {
            0: lax.all_gather(sent[1], "bl", axis=0),
            1: lax.all_to_all(sent[0], "bl", split_axis=0, concat_axis=0, tiled=True),
        }
        order, late, passed = [0], [1], arrived[0]
        high, low = pl.pallas_call(
            lambda w, o, h, l: interpolation(w[...], o[...], h, l),
            out_shape=[shape((parts, LANES, channels), bf16)] * 2,
            in_specs=[vmem] * 2,
            out_specs=[vmem] * 2,
            compiler_params=some,
            name="interpolation",
        )(weights, offset)

    gains, recip, slots, sums = pl.pallas_call(
        functools.partial(prepare_kernel, capacity, near, stations, order),
        out_shape=(
            shape((parts, 2 * owned, channels), f32),
            shape((owned, LANES), f32),
            shape((devices, LANES), i32),
            shape((chunks, owned, parts, LANES), f32),
        ),
        in_specs=[smem, smem, smem, vmem, vmem] + [anywhere] * (1 + len(order)),
        out_specs=(vmem,) * 4,
        scratch_shapes=[
            pltpu.VMEM((devices, depth, SUB, LANES), bf16),
            pltpu.VMEM((devices, gain_tiles * SUB, LANES), f32),
            pltpu.VMEM((2 * owned, LANES), f32),
            pltpu.VMEM((len(order),) + block, bf16),
            pltpu.VMEM((2, devices, LANES), f32),
            pltpu.SMEM((devices, LANES), i32),
            pltpu.VMEM((devices, LANES), i32),
            dma((2 * near + len(order),)),
        ],
        compiler_params=some,
        name="gains_and_sums",
    )(
        turn,
        me,
        pairs,
        high,
        low,
        *[arrived[x] for x in order],
        passed,
    )
    return pl.pallas_call(
        functools.partial(finish_kernel, capacity, late),
        out_shape=shape((owned, parts, channels), bf16),
        in_specs=[smem] + [vmem] * (3 + len(late)),
        out_specs=vmem,
        scratch_shapes=[
            pltpu.VMEM((chunks, owned, parts, LANES), f32),
            pltpu.VMEM((chunks, owned, parts, LANES), f32),
        ],
        compiler_params=some,
        name="sum_and_apply",
    )(slots, sums, gains, recip, *[arrived[x] for x in late])


def solution(mesh):
    placed = (
        P(("groups", "bl"), None, None),
        P(("groups", "bl"), None),
        P(("groups", "bl")),
        P("bl", None),
        P(("groups", "bl"), None, None),
        P("groups", None),
        P("groups"),
    )
    return jax.shard_map(
        on_device,
        mesh=mesh,
        in_specs=placed,
        out_specs=P(("groups", "bl"), None, None),
        check_vma=False,
    )
```

```python
import functools

import jax
import jax.numpy as jnp
from jax import lax
from jax.experimental import pallas as pl
from jax.experimental.pallas import tpu as pltpu
from jax.sharding import PartitionSpec as P

LANES = 128
SUB = 8
USED = 48
ALL_VMEM = 60 * 1024 * 1024
SOME_VMEM = 24 * 1024 * 1024


def round_up(value, unit):
    return -(-value // unit) * unit


def with_gains(near):
    return list(range(near)) + list(range(near, 2 * near, 2))


def start_all(pairs, sems):
    moves = [pltpu.make_async_copy(src, dst, sems.at[i]) for i, (src, dst) in enumerate(pairs)]
    for move in moves:
        move.start()
    return moves


def pack_kernel(
    capacity,
    near,
    me_s,
    owner_hbm,
    owner_row_hbm,
    slot_row_hbm,
    vis_hbm,
    coarse_hbm,
    *rest,
):
    outs = rest[:-10]
    (
        owner_s,
        count_s,
        owner_ref,
        slot_ref,
        vis_ref,
        coarse_ref,
        turn_ref,
        meta_ref,
        block_ref,
        sems,
    ) = rest[-10:]
    rows = vis_ref.shape[0]
    chunks = vis_ref.shape[2] // LANES
    devices = block_ref.shape[0]
    terms, stations = coarse_ref.shape
    half = stations // 2
    depth = meta_ref.shape[0]
    gain_tiles = (depth - 1) // 2
    moves = start_all(
        (
            (vis_hbm, vis_ref),
            (coarse_hbm, coarse_ref),
            (owner_hbm, owner_s),
            (owner_row_hbm, owner_ref),
            (slot_row_hbm, slot_ref),
        ),
        sems,
    )
    turn_ref[...] = jnp.zeros_like(turn_ref)
    for d in range(devices):
        count_s[d] = 0
    me = me_s[0]
    for move in moves[1:]:
        move.wait()

    turn_ref[0:terms, 0:half] = coarse_ref[:, 0:half]
    turn_ref[64 : 64 + terms, 0:half] = coarse_ref[:, half:stations]
    gains = turn_ref[...].T
    high = gains.astype(jnp.bfloat16)
    low = (gains - high.astype(jnp.float32)).astype(jnp.bfloat16)
    for i in range(gain_tiles):
        meta_ref[i] = high[i * SUB : (i + 1) * SUB, :]
        meta_ref[gain_tiles + i] = low[i * SUB : (i + 1) * SUB, :]
    sub = lax.broadcasted_iota(jnp.int32, (SUB, LANES), 0)
    codes = jnp.where(sub == 0, owner_ref[...], slot_ref[...])
    meta_ref[2 * gain_tiles] = codes.astype(jnp.float32).astype(jnp.bfloat16)
    at = chunks * capacity
    if near > 1:
        pairs = [(meta_ref, outs[x].at[pl.ds(at, depth)]) for x in with_gains(near)]
    else:
        pairs = [(meta_ref, outs[1])]
    sends = start_all(pairs, sems.at[pl.ds(1, len(pairs))])
    moves[0].wait()

    def place(r, carry):
        x = owner_s[r] ^ me
        k = count_s[x]
        count_s[x] = k + 1
        for c in range(chunks):
            block_ref[x, chunks * k + c] = vis_ref[r, :, c * LANES : (c + 1) * LANES]
        return carry

    lax.fori_loop(0, rows, place, 0, unroll=8)
    start = 1 + len(pairs)
    if near > 1:
        pairs = [(block_ref.at[x], outs[x].at[pl.ds(0, at)]) for x in range(devices)]
    else:
        pairs = [(block_ref, outs[0])]
    sends += start_all(pairs, sems.at[pl.ds(start, len(pairs))])
    for send in sends:
        send.wait()


def interpolation(weights, offset, high_ref, low_ref):
    channels = weights.shape[1]
    offset = jnp.concatenate([offset[c : c + 1, :] for c in range(offset.shape[0])], axis=1)
    index = lax.broadcasted_iota(jnp.int32, (LANES, channels), 0)
    knot = (index & 63) >> 3
    basis = jnp.zeros((LANES, channels), jnp.float32)
    for step in range(3):
        basis = basis + jnp.where(knot == offset + step, weights[step : step + 1, :], 0.0)
    high = basis.astype(jnp.bfloat16).astype(jnp.float32)
    low = basis - high
    part = index & 7
    for j in range(8):
        high_ref[j] = jnp.where(part == j, high, 0.0).astype(jnp.bfloat16)
        low_ref[j] = jnp.where(part == j, low, 0.0).astype(jnp.bfloat16)


def collect_kernel(
    at, depth, pairs_ref, weights_ref, offset_ref, own_ref, *rest
):
    blocks, hold_ref = rest[:-8], rest[-8]
    out_ref, own_out_ref, hold_out_ref, pairs_out_ref, high_ref, low_ref, sems = rest[-7:]
    moves = start_all(
        [
            (block.at[pl.ds(at, depth)], out_ref.at[pl.ds(i * depth, depth)])
            for i, block in enumerate(blocks)
        ]
        + [(own_ref, own_out_ref), (hold_ref, hold_out_ref)],
        sems,
    )
    pairs_out_ref[...] = pairs_ref[...]
    interpolation(weights_ref[...], offset_ref[...], high_ref, low_ref)
    for move in moves:
        move.wait()


def list_rows(owner, slot, target, capacity):
    senders = owner.shape[0]
    mine = owner == target
    counted = mine.astype(jnp.float32)
    before = lax.broadcasted_iota(jnp.int32, (LANES, LANES), 0) < lax.broadcasted_iota(
        jnp.int32, (LANES, LANES), 1
    )
    rank = jnp.dot(
        counted.astype(jnp.bfloat16),
        before.astype(jnp.float32).astype(jnp.bfloat16),
        preferred_element_type=jnp.float32,
    )
    lane = lax.broadcasted_iota(jnp.int32, (senders, LANES), 1)
    count = jnp.sum(counted, axis=1, keepdims=True)
    listing = jnp.where(lane == capacity, count, 0.0)
    for k in range(capacity):
        here = jnp.logical_and(mine, rank == float(k))
        kth = jnp.sum(jnp.where(here, slot, 0.0), axis=1, keepdims=True)
        listing = jnp.where(lane == k, kth, listing)
    return listing.astype(jnp.int32), mine


def add_rows(acc_ref, slots_s, line, capacity, rows_ref):
    chunks = acc_ref.shape[0]

    def add(k, carry):
        b = slots_s[line, k]
        for c in range(chunks):
            acc_ref[c, b] += rows_ref[chunks * k + c].astype(jnp.float32)
        return carry

    lax.fori_loop(0, slots_s[line, capacity], add, 0)


def prepare_kernel(
    capacity,
    near,
    stations,
    order,
    turn_s,
    me_s,
    pairs_s,
    high_ref,
    low_ref,
    *rest,
):
    arrived, passed = dict(zip(order, rest)), rest[order.index(None)]
    gains_ref, recip_ref, slots_ref, sums_ref = rest[-10:-6]
    table_ref, pick_ref, codes_ref, slots_s, slots_v, sem = rest[-6:]
    devices = codes_ref.shape[1]
    depth = 2 * (table_ref.shape[1] // SUB) + 1
    owned = recip_ref.shape[0]
    channels = high_ref.shape[2]
    half = stations // 2
    gain_tiles = (depth - 1) // 2
    chunks = channels // LANES
    at = capacity * chunks

    def meta(x, i):
        if near == 1:
            return arrived[0][x, i]
        if x in with_gains(near):
            return arrived[x][at + i]
        return passed[(x - near) // 2 * depth + i]

    for x in range(devices):
        for i in range(gain_tiles):
            table_ref[x, i * SUB : (i + 1) * SUB, :] = meta(x, i).astype(jnp.float32) + meta(
                x, gain_tiles + i
            ).astype(jnp.float32)
        code = meta(x, 2 * gain_tiles).astype(jnp.float32)
        codes_ref[0, x : x + 1, :] = code[0:1, :]
        codes_ref[1, x : x + 1, :] = code[1:2, :]
    owner, slot = codes_ref[0], codes_ref[1]
    listing, mine = list_rows(owner, slot, me_s[0].astype(jnp.float32), capacity)
    slots_ref[...] = listing
    slots_v[...] = listing
    move = pltpu.make_async_copy(slots_v, slots_s, sem)
    move.start()

    which = lax.broadcasted_iota(jnp.int32, (owned, LANES), 0).astype(jnp.float32)
    codes_ref[0] = jnp.where(mine, slot, -1.0)
    hits = jnp.zeros((owned, LANES), jnp.float32)
    for x in range(devices):
        hits = hits + (codes_ref[0, x : x + 1, :] == which).astype(jnp.float32)
    tally = jnp.sum(hits, axis=1, keepdims=True)
    recip_ref[...] = jnp.broadcast_to(1.0 / jnp.maximum(tally, 1.0), recip_ref.shape)

    turn = turn_s[0]
    column = lax.broadcasted_iota(jnp.int32, (1, LANES), 1)
    used = (column & 63) < USED
    upper = (column >> 6).astype(jnp.int32)

    def pick(b, carry):
        for side in range(2):
            s = pairs_s[side, b]
            d = s // stations
            within = s - d * stations
            second = jnp.where(within >= half, 1, 0)
            row = table_ref[d ^ turn, pl.ds(within - second * half, 1), :]
            keep = jnp.logical_and(used, upper == second)
            pick_ref[pl.ds(side * owned + b, 1), :] = jnp.where(keep, row, 0.0)
        return carry

    lax.fori_loop(0, owned, pick, 0, unroll=4)
    both = pick_ref[...]
    both_high = both.astype(jnp.bfloat16)
    both_low = (both - both_high.astype(jnp.float32)).astype(jnp.bfloat16)
    both_two = jnp.concatenate([both_high, both_low], axis=1)
    for j in range(8):
        high = high_ref[j]
        fine = jnp.dot(
            both_two, jnp.concatenate([high, high], axis=0), preferred_element_type=jnp.float32
        ) + jnp.dot(both_high, low_ref[j], preferred_element_type=jnp.float32)
        gains_ref[j] = fine.astype(jnp.bfloat16).astype(jnp.float32)

    for c in range(sums_ref.shape[0]):
        sums_ref[c] = jnp.zeros_like(sums_ref[c])
    move.wait()
    if near > 1:
        for x in order:
            if x is not None:
                add_rows(sums_ref, slots_s, x, capacity, arrived[x])


def finish_kernel(capacity, order, slots_s, sums_ref, gains_ref, recip_ref, *rest):
    far = rest[:-3]
    out_ref, acc_ref, res_ref = rest[-3:]
    owned, parts, channels = out_ref.shape
    chunks = channels // LANES
    acc_ref[...] = sums_ref[...]
    if len(far) > 1:
        for x, rows_ref in zip(order, far):
            add_rows(acc_ref, slots_s, x, capacity, rows_ref)
    else:

        def from_device(d, carry):
            add_rows(acc_ref, slots_s, d, capacity, far[0].at[d])
            return carry

        lax.fori_loop(0, far[0].shape[0], from_device, 0)

    flat = acc_ref.reshape(chunks * owned * parts, LANES)
    done = res_ref.reshape(chunks * owned * parts, LANES)
    for b0 in range(0, owned, SUB):
        scale = recip_ref[b0 : b0 + SUB, :]
        for c in range(chunks):
            row = (c * owned + b0) * parts
            cols = slice(c * LANES, (c + 1) * LANES)
            vis = [flat[pl.ds(row + j, SUB, stride=parts), :] for j in range(parts)]
            lhs = [gains_ref[j, b0 : b0 + SUB, cols] for j in range(parts)]
            rhs = [gains_ref[j, owned + b0 : owned + b0 + SUB, cols] for j in range(parts)]
            mid_re, mid_im = [], []
            for row_a in range(2):
                for col_b in range(2):
                    re = im = 0.0
                    for inner in range(2):
                        lr, li = lhs[2 * row_a + inner], lhs[4 + 2 * row_a + inner]
                        vr, vi = vis[2 * inner + col_b], vis[4 + 2 * inner + col_b]
                        re = re + lr * vr - li * vi
                        im = im + lr * vi + li * vr
                    mid_re.append(re * scale)
                    mid_im.append(im * scale)
            for row_a in range(2):
                for col_b in range(2):
                    re = im = 0.0
                    for inner in range(2):
                        mr, mi = mid_re[2 * row_a + inner], mid_im[2 * row_a + inner]
                        rr, ri = rhs[2 * col_b + inner], rhs[4 + 2 * col_b + inner]
                        re = re + mr * rr + mi * ri
                        im = im + mi * rr - mr * ri
                    j = 2 * row_a + col_b
                    done[pl.ds(row + j, SUB, stride=parts), :] = re
                    done[pl.ds(row + 4 + j, SUB, stride=parts), :] = im
    for c in range(chunks):
        out_ref[:, :, c * LANES : (c + 1) * LANES] = res_ref[c].astype(out_ref.dtype)


def on_device(
    visibilities,
    row_owner,
    row_slot,
    baseline_station_pairs,
    gains_coarse,
    band_weights,
    band_offset,
):
    devices = lax.axis_size("bl")
    rows, parts, channels = visibilities.shape
    capacity = 2 * rows // devices
    owned = baseline_station_pairs.shape[0]
    stations, _, knots = gains_coarse.shape
    chunks = channels // LANES
    gain_tiles = round_up(stations // 2, SUB) // SUB
    depth = 2 * gain_tiles + 1
    near = devices // 2 if devices <= 16 else 1
    halves = near > 1
    f32, bf16, i32 = jnp.float32, jnp.bfloat16, jnp.int32
    vmem = pl.BlockSpec(memory_space=pltpu.VMEM)
    smem = pl.BlockSpec(memory_space=pltpu.SMEM)
    hbm = pl.BlockSpec(memory_space=pltpu.HBM)
    anywhere = pl.BlockSpec(memory_space=pl.ANY)
    most = pltpu.CompilerParams(vmem_limit_bytes=ALL_VMEM)
    some = pltpu.CompilerParams(vmem_limit_bytes=SOME_VMEM)
    shape = jax.ShapeDtypeStruct
    dma = pltpu.SemaphoreType.DMA

    me = lax.axis_index("bl").astype(i32).reshape(1)
    turn = me if halves else jnp.zeros_like(me)
    owner = row_owner.reshape(rows)
    coarse = gains_coarse.transpose(2, 1, 0).reshape(knots * parts, stations)
    block = (chunks * capacity, parts, LANES)
    rows_at = chunks * capacity
    if halves:
        wide = with_gains(near) + [near + 1, near + 3]
        outs = [
            shape((rows_at + (depth if x in wide else 0), parts, LANES), bf16)
            for x in range(devices)
        ]
    else:
        outs = [shape((devices,) + block, bf16), shape((depth, SUB, LANES), bf16)]
    sent = pl.pallas_call(
        functools.partial(pack_kernel, capacity, near),
        out_shape=outs,
        in_specs=[smem] + [hbm] * 5,
        out_specs=[hbm] * len(outs),
        scratch_shapes=[
            pltpu.SMEM((rows,), i32),
            pltpu.SMEM((devices,), i32),
            pltpu.VMEM((1, rows), i32),
            pltpu.VMEM((1, rows), i32),
            pltpu.VMEM((rows, parts, channels), bf16),
            pltpu.VMEM((knots * parts, stations), f32),
            pltpu.VMEM((LANES, LANES), f32),
            pltpu.VMEM((depth, SUB, LANES), bf16),
            pltpu.VMEM((devices,) + block, bf16),
            dma((5 + 2 * devices,)),
        ],
        compiler_params=most,
        name="pack_rows",
    )(
        turn,
        owner,
        row_owner.reshape(1, rows),
        row_slot.reshape(1, rows),
        visibilities,
        coarse,
    )

    pairs = baseline_station_pairs.T
    weights = band_weights.T
    offset = band_offset.reshape(chunks, LANES)

    def swap(array, x):
        return lax.ppermute(array, "bl", [(d, d ^ x) for d in range(devices)])

    if halves:
        even = list(range(near, devices, 2))
        hold = near // 2 + 1
        arrived = {x: swap(sent[x], x) for x in range(1, devices) if x != hold}
        collected, own, held, pairs, high, low = pl.pallas_call(
            functools.partial(collect_kernel, rows_at, depth),
            out_shape=[
                shape((len(even) * depth, parts, LANES), bf16),
                shape(sent[0].shape, bf16),
                shape(sent[hold].shape, bf16),
                shape((2, owned), i32),
            ]
            + [shape((parts, LANES, channels), bf16)] * 2,
            in_specs=[vmem] * 3 + [anywhere] * (2 + len(even)),
            out_specs=[vmem] * 6,
            scratch_shapes=[dma((2 + len(even),))],
            compiler_params=some,
            name="collect_gains",
        )(pairs, weights, offset, sent[0], *[arrived[x] for x in even], sent[hold])
        arrived[hold] = swap(held, hold)
        arrived[0] = own
        passed = swap(collected, 1)
        cross = even + [x + 1 for x in even]
        close = list(range(1, near))
        then = near // 2 + 2
        order = [0] + cross[:2] + close[:1] + cross[2:then] + close[1:] + [None]
        late = cross[then:]
    else:
        arrived = {
            0: lax.all_gather(sent[1], "bl", axis=0),
            1: lax.all_to_all(sent[0], "bl", split_axis=0, concat_axis=0, tiled=True),
        }
        order, late, passed = [0, None], [1], arrived[0]
        high, low = pl.pallas_call(
            lambda w, o, h, l: interpolation(w[...], o[...], h, l),
            out_shape=[shape((parts, LANES, channels), bf16)] * 2,
            in_specs=[vmem] * 2,
            out_specs=[vmem] * 2,
            compiler_params=some,
            name="interpolation",
        )(weights, offset)

    gains, recip, slots, sums = pl.pallas_call(
        functools.partial(prepare_kernel, capacity, near, stations, order),
        out_shape=(
            shape((parts, 2 * owned, channels), f32),
            shape((owned, LANES), f32),
            shape((devices, LANES), i32),
            shape((chunks, owned, parts, LANES), f32),
        ),
        in_specs=[smem, smem, smem] + [vmem] * (2 + len(order)),
        out_specs=(vmem,) * 4,
        scratch_shapes=[
            pltpu.VMEM((devices, gain_tiles * SUB, LANES), f32),
            pltpu.VMEM((2 * owned, LANES), f32),
            pltpu.VMEM((2, devices, LANES), f32),
            pltpu.SMEM((devices, LANES), i32),
            pltpu.VMEM((devices, LANES), i32),
            dma,
        ],
        compiler_params=some,
        name="gains_and_sums",
    )(
        turn,
        me,
        pairs,
        high,
        low,
        *[passed if x is None else arrived[x] for x in order],
    )
    return pl.pallas_call(
        functools.partial(finish_kernel, capacity, late),
        out_shape=shape((owned, parts, channels), bf16),
        in_specs=[smem] + [vmem] * (3 + len(late)),
        out_specs=vmem,
        scratch_shapes=[
            pltpu.VMEM((chunks, owned, parts, LANES), f32),
            pltpu.VMEM((chunks, owned, parts, LANES), f32),
        ],
        compiler_params=some,
        name="sum_and_apply",
    )(slots, sums, gains, recip, *[arrived[x] for x in late])


def solution(mesh):
    placed = (
        P(("groups", "bl"), None, None),
        P(("groups", "bl"), None),
        P(("groups", "bl")),
        P("bl", None),
        P(("groups", "bl"), None, None),
        P("groups", None),
        P("groups"),
    )
    return jax.shard_map(
        on_device,
        mesh=mesh,
        in_specs=placed,
        out_specs=P(("groups", "bl"), None, None),
        check_vma=False,
    )
```

```python
import functools

import jax
import jax.numpy as jnp
from jax import lax
from jax.experimental import pallas as pl
from jax.experimental.pallas import tpu as pltpu
from jax.sharding import PartitionSpec as P

LANES = 128
SUB = 8
USED = 48
ALL_VMEM = 60 * 1024 * 1024
SOME_VMEM = 24 * 1024 * 1024


def round_up(value, unit):
    return -(-value // unit) * unit


def schedule(near):
    cross = list(range(near, 2 * near, 2)) + list(range(near + 1, 2 * near, 2))
    close = list(range(1, near))
    order = [0] + cross[:2] + close[:3] + cross[2:4] + close[3:4]
    for x in cross[4:-2]:
        order += [x] + close[4:5]
        close = close[:4] + close[5:]
    return order + close[4:], cross[-2:]


def start_all(pairs, sems):
    moves = [pltpu.make_async_copy(src, dst, sems.at[i]) for i, (src, dst) in enumerate(pairs)]
    for move in moves:
        move.start()
    return moves


def pack_kernel(
    capacity,
    near,
    me_s,
    owner_hbm,
    owner_row_hbm,
    slot_row_hbm,
    vis_hbm,
    coarse_hbm,
    *rest,
):
    outs = rest[:-10]
    (
        owner_s,
        count_s,
        owner_ref,
        slot_ref,
        vis_ref,
        coarse_ref,
        turn_ref,
        meta_ref,
        block_ref,
        sems,
    ) = rest[-10:]
    rows = vis_ref.shape[0]
    chunks = vis_ref.shape[2] // LANES
    devices = block_ref.shape[0]
    terms, stations = coarse_ref.shape
    half = stations // 2
    depth = meta_ref.shape[0]
    gain_tiles = (depth - 1) // 2
    moves = start_all(
        (
            (vis_hbm, vis_ref),
            (coarse_hbm, coarse_ref),
            (owner_hbm, owner_s),
            (owner_row_hbm, owner_ref),
            (slot_row_hbm, slot_ref),
        ),
        sems,
    )
    turn_ref[...] = jnp.zeros_like(turn_ref)
    for d in range(devices):
        count_s[d] = 0
    me = me_s[0]
    for move in moves[1:]:
        move.wait()

    turn_ref[0:terms, 0:half] = coarse_ref[:, 0:half]
    turn_ref[64 : 64 + terms, 0:half] = coarse_ref[:, half:stations]
    gains = turn_ref[...].T
    high = gains.astype(jnp.bfloat16)
    low = (gains - high.astype(jnp.float32)).astype(jnp.bfloat16)
    for i in range(gain_tiles):
        meta_ref[i] = high[i * SUB : (i + 1) * SUB, :]
        meta_ref[gain_tiles + i] = low[i * SUB : (i + 1) * SUB, :]
    sub = lax.broadcasted_iota(jnp.int32, (SUB, LANES), 0)
    codes = jnp.where(sub == 0, owner_ref[...], slot_ref[...])
    meta_ref[2 * gain_tiles] = codes.astype(jnp.float32).astype(jnp.bfloat16)
    at = chunks * capacity
    if near > 1:
        pairs = [(meta_ref, outs[x].at[pl.ds(at, depth)]) for x in schedule(near)[0]]
    else:
        pairs = [(meta_ref, outs[1])]
    sends = start_all(pairs, sems.at[pl.ds(1, len(pairs))])
    moves[0].wait()

    def place(r, carry):
        x = owner_s[r] ^ me
        k = count_s[x]
        count_s[x] = k + 1
        for c in range(chunks):
            block_ref[x, chunks * k + c] = vis_ref[r, :, c * LANES : (c + 1) * LANES]
        return carry

    lax.fori_loop(0, rows, place, 0, unroll=8)
    start = 1 + len(pairs)
    if near > 1:
        pairs = [(block_ref.at[x], outs[x].at[pl.ds(0, at)]) for x in range(devices)]
    else:
        pairs = [(block_ref, outs[0])]
    sends += start_all(pairs, sems.at[pl.ds(start, len(pairs))])
    for send in sends:
        send.wait()


def interpolation(weights, offset, high_ref, low_ref):
    channels = weights.shape[1]
    offset = jnp.concatenate([offset[c : c + 1, :] for c in range(offset.shape[0])], axis=1)
    index = lax.broadcasted_iota(jnp.int32, (LANES, channels), 0)
    knot = (index & 63) >> 3
    basis = jnp.zeros((LANES, channels), jnp.float32)
    for step in range(3):
        basis = basis + jnp.where(knot == offset + step, weights[step : step + 1, :], 0.0)
    high = basis.astype(jnp.bfloat16).astype(jnp.float32)
    low = basis - high
    part = index & 7
    for j in range(8):
        high_ref[j] = jnp.where(part == j, high, 0.0).astype(jnp.bfloat16)
        low_ref[j] = jnp.where(part == j, low, 0.0).astype(jnp.bfloat16)


def ready_kernel(at, pairs_ref, weights_ref, offset_ref, own_ref, _, *rest):
    meta_ref, own_out_ref, pairs_out_ref, high_ref, low_ref, sems = rest
    moves = start_all(
        [(own_ref.at[pl.ds(at, meta_ref.shape[0])], meta_ref), (own_ref, own_out_ref)], sems
    )
    pairs_out_ref[...] = pairs_ref[...]
    interpolation(weights_ref[...], offset_ref[...], high_ref, low_ref)
    for move in moves:
        move.wait()


def list_rows(owner, slot, target, capacity):
    senders = owner.shape[0]
    mine = owner == target
    counted = mine.astype(jnp.float32)
    before = lax.broadcasted_iota(jnp.int32, (LANES, LANES), 0) < lax.broadcasted_iota(
        jnp.int32, (LANES, LANES), 1
    )
    rank = jnp.dot(
        counted.astype(jnp.bfloat16),
        before.astype(jnp.float32).astype(jnp.bfloat16),
        preferred_element_type=jnp.float32,
    )
    lane = lax.broadcasted_iota(jnp.int32, (senders, LANES), 1)
    count = jnp.sum(counted, axis=1, keepdims=True)
    listing = jnp.where(lane == capacity, count, 0.0)
    for k in range(capacity):
        here = jnp.logical_and(mine, rank == float(k))
        kth = jnp.sum(jnp.where(here, slot, 0.0), axis=1, keepdims=True)
        listing = jnp.where(lane == k, kth, listing)
    return listing.astype(jnp.int32), mine


def add_rows(acc_ref, slots_s, line, capacity, rows_ref):
    chunks = acc_ref.shape[0]

    def add(k, carry):
        b = slots_s[line, k]
        for c in range(chunks):
            acc_ref[c, b] += rows_ref[chunks * k + c].astype(jnp.float32)
        return carry

    lax.fori_loop(0, slots_s[line, capacity], add, 0)


def prepare_kernel(
    capacity,
    near,
    stations,
    order,
    late,
    turn_s,
    me_s,
    pairs_s,
    high_ref,
    low_ref,
    *rest,
):
    arrived, passed = dict(zip(order, rest)), dict(zip(late, rest[len(order) :]))
    gains_ref, recip_ref, slots_ref, sums_ref = rest[-10:-6]
    table_ref, pick_ref, codes_ref, slots_s, slots_v, sem = rest[-6:]
    devices = codes_ref.shape[1]
    depth = 2 * (table_ref.shape[1] // SUB) + 1
    owned = recip_ref.shape[0]
    channels = high_ref.shape[2]
    half = stations // 2
    gain_tiles = (depth - 1) // 2
    chunks = channels // LANES
    at = capacity * chunks

    def meta(x, i):
        if near == 1:
            return arrived[0][x, i]
        return passed[x][i] if x in late else arrived[x][at + i]

    for x in range(devices):
        for i in range(gain_tiles):
            table_ref[x, i * SUB : (i + 1) * SUB, :] = meta(x, i).astype(jnp.float32) + meta(
                x, gain_tiles + i
            ).astype(jnp.float32)
        code = meta(x, 2 * gain_tiles).astype(jnp.float32)
        codes_ref[0, x : x + 1, :] = code[0:1, :]
        codes_ref[1, x : x + 1, :] = code[1:2, :]
    owner, slot = codes_ref[0], codes_ref[1]
    listing, mine = list_rows(owner, slot, me_s[0].astype(jnp.float32), capacity)
    slots_ref[...] = listing
    slots_v[...] = listing
    move = pltpu.make_async_copy(slots_v, slots_s, sem)
    move.start()

    which = lax.broadcasted_iota(jnp.int32, (owned, LANES), 0).astype(jnp.float32)
    codes_ref[0] = jnp.where(mine, slot, -1.0)
    hits = jnp.zeros((owned, LANES), jnp.float32)
    for x in range(devices):
        hits = hits + (codes_ref[0, x : x + 1, :] == which).astype(jnp.float32)
    tally = jnp.sum(hits, axis=1, keepdims=True)
    recip_ref[...] = jnp.broadcast_to(1.0 / jnp.maximum(tally, 1.0), recip_ref.shape)

    turn = turn_s[0]
    column = lax.broadcasted_iota(jnp.int32, (1, LANES), 1)
    used = (column & 63) < USED
    upper = (column >> 6).astype(jnp.int32)

    def pick(b, carry):
        for side in range(2):
            s = pairs_s[side, b]
            d = s // stations
            within = s - d * stations
            second = jnp.where(within >= half, 1, 0)
            row = table_ref[d ^ turn, pl.ds(within - second * half, 1), :]
            keep = jnp.logical_and(used, upper == second)
            pick_ref[pl.ds(side * owned + b, 1), :] = jnp.where(keep, row, 0.0)
        return carry

    lax.fori_loop(0, owned, pick, 0, unroll=4)
    both = pick_ref[...]
    both_high = both.astype(jnp.bfloat16)
    both_low = (both - both_high.astype(jnp.float32)).astype(jnp.bfloat16)
    both_two = jnp.concatenate([both_high, both_low], axis=1)
    for j in range(8):
        high = high_ref[j]
        fine = jnp.dot(
            both_two, jnp.concatenate([high, high], axis=0), preferred_element_type=jnp.float32
        ) + jnp.dot(both_high, low_ref[j], preferred_element_type=jnp.float32)
        gains_ref[j] = fine.astype(jnp.bfloat16).astype(jnp.float32)

    for c in range(sums_ref.shape[0]):
        sums_ref[c] = jnp.zeros_like(sums_ref[c])
    move.wait()
    if near > 1:
        for x in order:
            add_rows(sums_ref, slots_s, x, capacity, arrived[x])


def finish_kernel(capacity, order, slots_s, sums_ref, gains_ref, recip_ref, *rest):
    far = rest[:-3]
    out_ref, acc_ref, res_ref = rest[-3:]
    owned, parts, channels = out_ref.shape
    chunks = channels // LANES
    acc_ref[...] = sums_ref[...]
    if len(far) > 1:
        for x, rows_ref in zip(order, far):
            add_rows(acc_ref, slots_s, x, capacity, rows_ref)
    else:

        def from_device(d, carry):
            add_rows(acc_ref, slots_s, d, capacity, far[0].at[d])
            return carry

        lax.fori_loop(0, far[0].shape[0], from_device, 0)

    flat = acc_ref.reshape(chunks * owned * parts, LANES)
    done = res_ref.reshape(chunks * owned * parts, LANES)
    for b0 in range(0, owned, SUB):
        scale = recip_ref[b0 : b0 + SUB, :]
        for c in range(chunks):
            row = (c * owned + b0) * parts
            cols = slice(c * LANES, (c + 1) * LANES)
            vis = [flat[pl.ds(row + j, SUB, stride=parts), :] for j in range(parts)]
            lhs = [gains_ref[j, b0 : b0 + SUB, cols] for j in range(parts)]
            rhs = [gains_ref[j, owned + b0 : owned + b0 + SUB, cols] for j in range(parts)]
            mid_re, mid_im = [], []
            for row_a in range(2):
                for col_b in range(2):
                    re = im = 0.0
                    for inner in range(2):
                        lr, li = lhs[2 * row_a + inner], lhs[4 + 2 * row_a + inner]
                        vr, vi = vis[2 * inner + col_b], vis[4 + 2 * inner + col_b]
                        re = re + lr * vr - li * vi
                        im = im + lr * vi + li * vr
                    mid_re.append(re * scale)
                    mid_im.append(im * scale)
            for row_a in range(2):
                for col_b in range(2):
                    re = im = 0.0
                    for inner in range(2):
                        mr, mi = mid_re[2 * row_a + inner], mid_im[2 * row_a + inner]
                        rr, ri = rhs[2 * col_b + inner], rhs[4 + 2 * col_b + inner]
                        re = re + mr * rr + mi * ri
                        im = im + mi * rr - mr * ri
                    j = 2 * row_a + col_b
                    done[pl.ds(row + j, SUB, stride=parts), :] = re
                    done[pl.ds(row + 4 + j, SUB, stride=parts), :] = im
    for c in range(chunks):
        out_ref[:, :, c * LANES : (c + 1) * LANES] = res_ref[c].astype(out_ref.dtype)


def on_device(
    visibilities,
    row_owner,
    row_slot,
    baseline_station_pairs,
    gains_coarse,
    band_weights,
    band_offset,
):
    devices = lax.axis_size("bl")
    rows, parts, channels = visibilities.shape
    capacity = 2 * rows // devices
    owned = baseline_station_pairs.shape[0]
    stations, _, knots = gains_coarse.shape
    chunks = channels // LANES
    gain_tiles = round_up(stations // 2, SUB) // SUB
    depth = 2 * gain_tiles + 1
    near = devices // 2 if devices <= 16 else 1
    halves = near > 1
    f32, bf16, i32 = jnp.float32, jnp.bfloat16, jnp.int32
    vmem = pl.BlockSpec(memory_space=pltpu.VMEM)
    smem = pl.BlockSpec(memory_space=pltpu.SMEM)
    hbm = pl.BlockSpec(memory_space=pltpu.HBM)
    anywhere = pl.BlockSpec(memory_space=pl.ANY)
    most = pltpu.CompilerParams(vmem_limit_bytes=ALL_VMEM)
    some = pltpu.CompilerParams(vmem_limit_bytes=SOME_VMEM)
    shape = jax.ShapeDtypeStruct
    dma = pltpu.SemaphoreType.DMA

    me = lax.axis_index("bl").astype(i32).reshape(1)
    turn = me if halves else jnp.zeros_like(me)
    owner = row_owner.reshape(rows)
    coarse = gains_coarse.transpose(2, 1, 0).reshape(knots * parts, stations)
    block = (chunks * capacity, parts, LANES)
    rows_at = chunks * capacity
    if halves:
        order, late = schedule(near)
        outs = [
            shape((rows_at + (0 if x in late else depth), parts, LANES), bf16)
            for x in range(devices)
        ]
    else:
        outs = [shape((devices,) + block, bf16), shape((depth, SUB, LANES), bf16)]
    sent = pl.pallas_call(
        functools.partial(pack_kernel, capacity, near),
        out_shape=outs,
        in_specs=[smem] + [hbm] * 5,
        out_specs=[hbm] * len(outs),
        scratch_shapes=[
            pltpu.SMEM((rows,), i32),
            pltpu.SMEM((devices,), i32),
            pltpu.VMEM((1, rows), i32),
            pltpu.VMEM((1, rows), i32),
            pltpu.VMEM((rows, parts, channels), bf16),
            pltpu.VMEM((knots * parts, stations), f32),
            pltpu.VMEM((LANES, LANES), f32),
            pltpu.VMEM((depth, SUB, LANES), bf16),
            pltpu.VMEM((devices,) + block, bf16),
            dma((5 + 2 * devices,)),
        ],
        compiler_params=most,
        name="pack_rows",
    )(
        turn,
        owner,
        row_owner.reshape(1, rows),
        row_slot.reshape(1, rows),
        visibilities,
        coarse,
    )

    pairs = baseline_station_pairs.T
    weights = band_weights.T
    offset = band_offset.reshape(chunks, LANES)

    def swap(array, x):
        return lax.ppermute(array, "bl", [(d, d ^ x) for d in range(devices)])

    if halves:
        arrived = {x: swap(sent[x], x) for x in range(1, devices)}
        meta, arrived[0], pairs, high, low = pl.pallas_call(
            functools.partial(ready_kernel, rows_at),
            out_shape=[
                shape((depth, parts, LANES), bf16),
                shape(sent[0].shape, bf16),
                shape((2, owned), i32),
            ]
            + [shape((parts, LANES, channels), bf16)] * 2,
            in_specs=[vmem] * 3 + [anywhere] * 2,
            out_specs=[vmem] * 5,
            scratch_shapes=[dma((2,))],
            compiler_params=some,
            name="interpolation",
        )(pairs, weights, offset, sent[0], arrived[near])
        passed = [swap(meta, x) for x in late]
    else:
        arrived = {
            0: lax.all_gather(sent[1], "bl", axis=0),
            1: lax.all_to_all(sent[0], "bl", split_axis=0, concat_axis=0, tiled=True),
        }
        order, late, passed = [0], [1], []
        high, low = pl.pallas_call(
            lambda w, o, h, l: interpolation(w[...], o[...], h, l),
            out_shape=[shape((parts, LANES, channels), bf16)] * 2,
            in_specs=[vmem] * 2,
            out_specs=[vmem] * 2,
            compiler_params=some,
            name="interpolation",
        )(weights, offset)

    gains, recip, slots, sums = pl.pallas_call(
        functools.partial(prepare_kernel, capacity, near, stations, order, late),
        out_shape=(
            shape((parts, 2 * owned, channels), f32),
            shape((owned, LANES), f32),
            shape((devices, LANES), i32),
            shape((chunks, owned, parts, LANES), f32),
        ),
        in_specs=[smem, smem, smem] + [vmem] * (2 + len(order) + len(passed)),
        out_specs=(vmem,) * 4,
        scratch_shapes=[
            pltpu.VMEM((devices, gain_tiles * SUB, LANES), f32),
            pltpu.VMEM((2 * owned, LANES), f32),
            pltpu.VMEM((2, devices, LANES), f32),
            pltpu.SMEM((devices, LANES), i32),
            pltpu.VMEM((devices, LANES), i32),
            dma,
        ],
        compiler_params=some,
        name="gains_and_sums",
    )(
        turn,
        me,
        pairs,
        high,
        low,
        *[arrived[x] for x in order],
        *passed,
    )
    return pl.pallas_call(
        functools.partial(finish_kernel, capacity, late),
        out_shape=shape((owned, parts, channels), bf16),
        in_specs=[smem] + [vmem] * (3 + len(late)),
        out_specs=vmem,
        scratch_shapes=[
            pltpu.VMEM((chunks, owned, parts, LANES), f32),
            pltpu.VMEM((chunks, owned, parts, LANES), f32),
        ],
        compiler_params=some,
        name="sum_and_apply",
    )(slots, sums, gains, recip, *[arrived[x] for x in late])


def solution(mesh):
    placed = (
        P(("groups", "bl"), None, None),
        P(("groups", "bl"), None),
        P(("groups", "bl")),
        P("bl", None),
        P(("groups", "bl"), None, None),
        P("groups", None),
        P("groups"),
    )
    return jax.shard_map(
        on_device,
        mesh=mesh,
        in_specs=placed,
        out_specs=P(("groups", "bl"), None, None),
        check_vma=False,
    )
```

```python
import functools

import jax
import jax.numpy as jnp
from jax import lax
from jax.experimental import pallas as pl
from jax.experimental.pallas import tpu as pltpu
from jax.sharding import PartitionSpec as P

LANES = 128
SUB = 8
USED = 48
ALL_VMEM = 60 * 1024 * 1024
SOME_VMEM = 24 * 1024 * 1024


def round_up(value, unit):
    return -(-value // unit) * unit


def schedule(near):
    cross = list(range(near, 2 * near, 2)) + list(range(near + 1, 2 * near, 2))
    close = list(range(1, near))
    order = [0] + cross[:2] + close[:3] + cross[2:4] + close[3:4]
    for x in cross[4:-2]:
        order += [x] + close[4:5]
        close = close[:4] + close[5:]
    return order + close[4:], cross[-2:]


def start_all(pairs, sems):
    moves = [pltpu.make_async_copy(src, dst, sems.at[i]) for i, (src, dst) in enumerate(pairs)]
    for move in moves:
        move.start()
    return moves


def pack_kernel(
    capacity,
    near,
    me_s,
    owner_hbm,
    owner_row_hbm,
    slot_row_hbm,
    vis_hbm,
    coarse_hbm,
    *rest,
):
    outs = rest[:-10]
    (
        owner_s,
        count_s,
        owner_ref,
        slot_ref,
        vis_ref,
        coarse_ref,
        turn_ref,
        meta_ref,
        block_ref,
        sems,
    ) = rest[-10:]
    rows = vis_ref.shape[0]
    chunks = vis_ref.shape[2] // LANES
    devices = block_ref.shape[0]
    terms, stations = coarse_ref.shape
    half = stations // 2
    depth = meta_ref.shape[0]
    gain_tiles = (depth - 1) // 2
    moves = start_all(
        (
            (vis_hbm, vis_ref),
            (coarse_hbm, coarse_ref),
            (owner_hbm, owner_s),
            (owner_row_hbm, owner_ref),
            (slot_row_hbm, slot_ref),
        ),
        sems,
    )
    turn_ref[...] = jnp.zeros_like(turn_ref)
    for d in range(devices):
        count_s[d] = 0
    me = me_s[0]
    for move in moves[1:]:
        move.wait()

    turn_ref[0:terms, 0:half] = coarse_ref[:, 0:half]
    turn_ref[64 : 64 + terms, 0:half] = coarse_ref[:, half:stations]
    gains = turn_ref[...].T
    high = gains.astype(jnp.bfloat16)
    low = (gains - high.astype(jnp.float32)).astype(jnp.bfloat16)
    for i in range(gain_tiles):
        meta_ref[i] = high[i * SUB : (i + 1) * SUB, :]
        meta_ref[gain_tiles + i] = low[i * SUB : (i + 1) * SUB, :]
    sub = lax.broadcasted_iota(jnp.int32, (SUB, LANES), 0)
    codes = jnp.where(sub == 0, owner_ref[...], slot_ref[...])
    meta_ref[2 * gain_tiles] = codes.astype(jnp.float32).astype(jnp.bfloat16)
    at = chunks * capacity
    if near > 1:
        pairs = [(meta_ref, outs[x].at[pl.ds(at, depth)]) for x in schedule(near)[0]]
        pairs += [(meta_ref, outs[devices])]
    else:
        pairs = [(meta_ref, outs[1])]
    sends = start_all(pairs, sems.at[pl.ds(1, len(pairs))])
    moves[0].wait()

    def place(r, carry):
        x = owner_s[r] ^ me
        k = count_s[x]
        count_s[x] = k + 1
        for c in range(chunks):
            block_ref[x, chunks * k + c] = vis_ref[r, :, c * LANES : (c + 1) * LANES]
        return carry

    lax.fori_loop(0, rows, place, 0, unroll=8)
    start = 1 + len(pairs)
    if near > 1:
        pairs = [(block_ref.at[x], outs[x].at[pl.ds(0, at)]) for x in range(devices)]
    else:
        pairs = [(block_ref, outs[0])]
    sends += start_all(pairs, sems.at[pl.ds(start, len(pairs))])
    for send in sends:
        send.wait()


def interpolation(weights, offset, high_ref, low_ref):
    channels = weights.shape[1]
    offset = jnp.concatenate([offset[c : c + 1, :] for c in range(offset.shape[0])], axis=1)
    index = lax.broadcasted_iota(jnp.int32, (LANES, channels), 0)
    knot = (index & 63) >> 3
    basis = jnp.zeros((LANES, channels), jnp.float32)
    for step in range(3):
        basis = basis + jnp.where(knot == offset + step, weights[step : step + 1, :], 0.0)
    high = basis.astype(jnp.bfloat16).astype(jnp.float32)
    low = basis - high
    part = index & 7
    for j in range(8):
        high_ref[j] = jnp.where(part == j, high, 0.0).astype(jnp.bfloat16)
        low_ref[j] = jnp.where(part == j, low, 0.0).astype(jnp.bfloat16)


def list_rows(owner, slot, target, capacity):
    senders = owner.shape[0]
    mine = owner == target
    counted = mine.astype(jnp.float32)
    before = lax.broadcasted_iota(jnp.int32, (LANES, LANES), 0) < lax.broadcasted_iota(
        jnp.int32, (LANES, LANES), 1
    )
    rank = jnp.dot(
        counted.astype(jnp.bfloat16),
        before.astype(jnp.float32).astype(jnp.bfloat16),
        preferred_element_type=jnp.float32,
    )
    lane = lax.broadcasted_iota(jnp.int32, (senders, LANES), 1)
    count = jnp.sum(counted, axis=1, keepdims=True)
    listing = jnp.where(lane == capacity, count, 0.0)
    for k in range(capacity):
        here = jnp.logical_and(mine, rank == float(k))
        kth = jnp.sum(jnp.where(here, slot, 0.0), axis=1, keepdims=True)
        listing = jnp.where(lane == k, kth, listing)
    return listing.astype(jnp.int32), mine


def add_rows(acc_ref, slots_s, line, capacity, rows_ref):
    chunks = acc_ref.shape[0]

    def add(k, carry):
        b = slots_s[line, k]
        for c in range(chunks):
            acc_ref[c, b] += rows_ref[chunks * k + c].astype(jnp.float32)
        return carry

    lax.fori_loop(0, slots_s[line, capacity], add, 0)


def prepare_kernel(
    capacity,
    near,
    stations,
    order,
    late,
    turn_s,
    me_s,
    pairs_s,
    high_ref,
    low_ref,
    *rest,
):
    arrived, passed = dict(zip(order, rest)), dict(zip(late, rest[len(order) :]))
    gains_ref, recip_ref, slots_ref, sums_ref = rest[-10:-6]
    table_ref, pick_ref, codes_ref, slots_s, slots_v, sem = rest[-6:]
    devices = codes_ref.shape[1]
    depth = 2 * (table_ref.shape[1] // SUB) + 1
    owned = recip_ref.shape[0]
    channels = high_ref.shape[2]
    half = stations // 2
    gain_tiles = (depth - 1) // 2
    chunks = channels // LANES
    at = capacity * chunks

    def meta(x, i):
        if near == 1:
            return arrived[0][x, i]
        return passed[x][i] if x in late else arrived[x][at + i]

    for x in range(devices):
        for i in range(gain_tiles):
            table_ref[x, i * SUB : (i + 1) * SUB, :] = meta(x, i).astype(jnp.float32) + meta(
                x, gain_tiles + i
            ).astype(jnp.float32)
        code = meta(x, 2 * gain_tiles).astype(jnp.float32)
        codes_ref[0, x : x + 1, :] = code[0:1, :]
        codes_ref[1, x : x + 1, :] = code[1:2, :]
    owner, slot = codes_ref[0], codes_ref[1]
    listing, mine = list_rows(owner, slot, me_s[0].astype(jnp.float32), capacity)
    slots_ref[...] = listing
    slots_v[...] = listing
    move = pltpu.make_async_copy(slots_v, slots_s, sem)
    move.start()

    which = lax.broadcasted_iota(jnp.int32, (owned, LANES), 0).astype(jnp.float32)
    codes_ref[0] = jnp.where(mine, slot, -1.0)
    hits = jnp.zeros((owned, LANES), jnp.float32)
    for x in range(devices):
        hits = hits + (codes_ref[0, x : x + 1, :] == which).astype(jnp.float32)
    tally = jnp.sum(hits, axis=1, keepdims=True)
    recip_ref[...] = jnp.broadcast_to(1.0 / jnp.maximum(tally, 1.0), recip_ref.shape)

    turn = turn_s[0]
    column = lax.broadcasted_iota(jnp.int32, (1, LANES), 1)
    used = (column & 63) < USED
    upper = (column >> 6).astype(jnp.int32)

    def pick(b, carry):
        for side in range(2):
            s = pairs_s[side, b]
            d = s // stations
            within = s - d * stations
            second = jnp.where(within >= half, 1, 0)
            row = table_ref[d ^ turn, pl.ds(within - second * half, 1), :]
            keep = jnp.logical_and(used, upper == second)
            pick_ref[pl.ds(side * owned + b, 1), :] = jnp.where(keep, row, 0.0)
        return carry

    lax.fori_loop(0, owned, pick, 0, unroll=4)
    both = pick_ref[...]
    both_high = both.astype(jnp.bfloat16)
    both_low = (both - both_high.astype(jnp.float32)).astype(jnp.bfloat16)
    both_two = jnp.concatenate([both_high, both_low], axis=1)
    for j in range(8):
        high = high_ref[j]
        fine = jnp.dot(
            both_two, jnp.concatenate([high, high], axis=0), preferred_element_type=jnp.float32
        ) + jnp.dot(both_high, low_ref[j], preferred_element_type=jnp.float32)
        gains_ref[j] = fine.astype(jnp.bfloat16).astype(jnp.float32)

    for c in range(sums_ref.shape[0]):
        sums_ref[c] = jnp.zeros_like(sums_ref[c])
    move.wait()
    if near > 1:
        for x in order:
            add_rows(sums_ref, slots_s, x, capacity, arrived[x])


def finish_kernel(capacity, order, slots_s, sums_ref, gains_ref, recip_ref, *rest):
    far = rest[:-3]
    out_ref, acc_ref, res_ref = rest[-3:]
    owned, parts, channels = out_ref.shape
    chunks = channels // LANES
    acc_ref[...] = sums_ref[...]
    if len(far) > 1:
        for x, rows_ref in zip(order, far):
            add_rows(acc_ref, slots_s, x, capacity, rows_ref)
    else:

        def from_device(d, carry):
            add_rows(acc_ref, slots_s, d, capacity, far[0].at[d])
            return carry

        lax.fori_loop(0, far[0].shape[0], from_device, 0)

    flat = acc_ref.reshape(chunks * owned * parts, LANES)
    done = res_ref.reshape(chunks * owned * parts, LANES)
    for b0 in range(0, owned, SUB):
        scale = recip_ref[b0 : b0 + SUB, :]
        for c in range(chunks):
            row = (c * owned + b0) * parts
            cols = slice(c * LANES, (c + 1) * LANES)
            vis = [flat[pl.ds(row + j, SUB, stride=parts), :] for j in range(parts)]
            lhs = [gains_ref[j, b0 : b0 + SUB, cols] for j in range(parts)]
            rhs = [gains_ref[j, owned + b0 : owned + b0 + SUB, cols] for j in range(parts)]
            mid_re, mid_im = [], []
            for row_a in range(2):
                for col_b in range(2):
                    re = im = 0.0
                    for inner in range(2):
                        lr, li = lhs[2 * row_a + inner], lhs[4 + 2 * row_a + inner]
                        vr, vi = vis[2 * inner + col_b], vis[4 + 2 * inner + col_b]
                        re = re + lr * vr - li * vi
                        im = im + lr * vi + li * vr
                    mid_re.append(re * scale)
                    mid_im.append(im * scale)
            for row_a in range(2):
                for col_b in range(2):
                    re = im = 0.0
                    for inner in range(2):
                        mr, mi = mid_re[2 * row_a + inner], mid_im[2 * row_a + inner]
                        rr, ri = rhs[2 * col_b + inner], rhs[4 + 2 * col_b + inner]
                        re = re + mr * rr + mi * ri
                        im = im + mi * rr - mr * ri
                    j = 2 * row_a + col_b
                    done[pl.ds(row + j, SUB, stride=parts), :] = re
                    done[pl.ds(row + 4 + j, SUB, stride=parts), :] = im
    for c in range(chunks):
        out_ref[:, :, c * LANES : (c + 1) * LANES] = res_ref[c].astype(out_ref.dtype)


def on_device(
    visibilities,
    row_owner,
    row_slot,
    baseline_station_pairs,
    gains_coarse,
    band_weights,
    band_offset,
):
    devices = lax.axis_size("bl")
    rows, parts, channels = visibilities.shape
    capacity = 2 * rows // devices
    owned = baseline_station_pairs.shape[0]
    stations, _, knots = gains_coarse.shape
    chunks = channels // LANES
    gain_tiles = round_up(stations // 2, SUB) // SUB
    depth = 2 * gain_tiles + 1
    near = devices // 2 if devices <= 16 else 1
    halves = near > 1
    f32, bf16, i32 = jnp.float32, jnp.bfloat16, jnp.int32
    vmem = pl.BlockSpec(memory_space=pltpu.VMEM)
    smem = pl.BlockSpec(memory_space=pltpu.SMEM)
    hbm = pl.BlockSpec(memory_space=pltpu.HBM)
    anywhere = pl.BlockSpec(memory_space=pl.ANY)
    most = pltpu.CompilerParams(vmem_limit_bytes=ALL_VMEM)
    some = pltpu.CompilerParams(vmem_limit_bytes=SOME_VMEM)
    shape = jax.ShapeDtypeStruct
    dma = pltpu.SemaphoreType.DMA

    me = lax.axis_index("bl").astype(i32).reshape(1)
    turn = me if halves else jnp.zeros_like(me)
    owner = row_owner.reshape(rows)
    coarse = gains_coarse.transpose(2, 1, 0).reshape(knots * parts, stations)
    block = (chunks * capacity, parts, LANES)
    rows_at = chunks * capacity
    if halves:
        order, late = schedule(near)
        outs = [
            shape((rows_at + (0 if x in late else depth), parts, LANES), bf16)
            for x in range(devices)
        ]
        outs += [shape((depth, SUB, LANES), bf16)]
    else:
        outs = [shape((devices,) + block, bf16), shape((depth, SUB, LANES), bf16)]
    sent = pl.pallas_call(
        functools.partial(pack_kernel, capacity, near),
        out_shape=outs,
        in_specs=[smem] + [hbm] * 5,
        out_specs=[hbm] * len(outs),
        scratch_shapes=[
            pltpu.SMEM((rows,), i32),
            pltpu.SMEM((devices,), i32),
            pltpu.VMEM((1, rows), i32),
            pltpu.VMEM((1, rows), i32),
            pltpu.VMEM((rows, parts, channels), bf16),
            pltpu.VMEM((knots * parts, stations), f32),
            pltpu.VMEM((LANES, LANES), f32),
            pltpu.VMEM((depth, SUB, LANES), bf16),
            pltpu.VMEM((devices,) + block, bf16),
            dma((6 + 2 * devices,)),
        ],
        compiler_params=most,
        name="pack_rows",
    )(
        turn,
        owner,
        row_owner.reshape(1, rows),
        row_slot.reshape(1, rows),
        visibilities,
        coarse,
    )

    pairs = baseline_station_pairs.T
    weights = band_weights.T
    offset = band_offset.reshape(chunks, LANES)

    def swap(array, x):
        return lax.ppermute(array, "bl", [(d, d ^ x) for d in range(devices)])

    if halves:
        passed = [swap(sent[devices], x) for x in late]
        arrived = {x: swap(sent[x], x) if x else sent[x] for x in range(devices)}
    else:
        arrived = {
            0: lax.all_gather(sent[1], "bl", axis=0),
            1: lax.all_to_all(sent[0], "bl", split_axis=0, concat_axis=0, tiled=True),
        }
        order, late, passed = [0], [1], []
    high, low = pl.pallas_call(
        lambda w, o, h, l: interpolation(w[...], o[...], h, l),
        out_shape=[shape((parts, LANES, channels), bf16)] * 2,
        in_specs=[vmem] * 2,
        out_specs=[vmem] * 2,
        compiler_params=some,
        name="interpolation",
    )(weights, offset)
    gains, recip, slots, sums = pl.pallas_call(
        functools.partial(prepare_kernel, capacity, near, stations, order, late),
        out_shape=(
            shape((parts, 2 * owned, channels), f32),
            shape((owned, LANES), f32),
            shape((devices, LANES), i32),
            shape((chunks, owned, parts, LANES), f32),
        ),
        in_specs=[smem, smem, smem] + [vmem] * (2 + len(order) + len(passed)),
        out_specs=(vmem,) * 4,
        scratch_shapes=[
            pltpu.VMEM((devices, gain_tiles * SUB, LANES), f32),
            pltpu.VMEM((2 * owned, LANES), f32),
            pltpu.VMEM((2, devices, LANES), f32),
            pltpu.SMEM((devices, LANES), i32),
            pltpu.VMEM((devices, LANES), i32),
            dma,
        ],
        compiler_params=some,
        name="gains_and_sums",
    )(
        turn,
        me,
        pairs,
        high,
        low,
        *[arrived[x] for x in order],
        *passed,
    )
    return pl.pallas_call(
        functools.partial(finish_kernel, capacity, late),
        out_shape=shape((owned, parts, channels), bf16),
        in_specs=[smem] + [vmem] * (3 + len(late)),
        out_specs=vmem,
        scratch_shapes=[
            pltpu.VMEM((chunks, owned, parts, LANES), f32),
            pltpu.VMEM((chunks, owned, parts, LANES), f32),
        ],
        compiler_params=some,
        name="sum_and_apply",
    )(slots, sums, gains, recip, *[arrived[x] for x in late])


def solution(mesh):
    placed = (
        P(("groups", "bl"), None, None),
        P(("groups", "bl"), None),
        P(("groups", "bl")),
        P("bl", None),
        P(("groups", "bl"), None, None),
        P("groups", None),
        P("groups"),
    )
    return jax.shard_map(
        on_device,
        mesh=mesh,
        in_specs=placed,
        out_specs=P(("groups", "bl"), None, None),
        check_vma=False,
    )
```

```python
import functools

import jax
import jax.numpy as jnp
from jax import lax
from jax.experimental import pallas as pl
from jax.experimental.pallas import tpu as pltpu
from jax.sharding import PartitionSpec as P

LANES = 128
SUB = 8
USED = 48
ALL_VMEM = 60 * 1024 * 1024
SOME_VMEM = 24 * 1024 * 1024


def round_up(value, unit):
    return -(-value // unit) * unit


def schedule(near):
    cross = list(range(near, 2 * near, 2)) + list(range(near + 1, 2 * near, 2))
    close = list(range(near // 2, near)) + list(range(1, near // 2))
    order = [0] + cross[:2] + close[:3]
    cross, close, late = cross[2:-2], close[3:], cross[-2:]
    while cross or close:
        order += close[:1] + cross[:1]
        cross, close = cross[1:], close[1:]
    return order, late


def start_all(pairs, sems):
    moves = [pltpu.make_async_copy(src, dst, sems.at[i]) for i, (src, dst) in enumerate(pairs)]
    for move in moves:
        move.start()
    return moves


def pack_kernel(
    capacity,
    near,
    me_s,
    owner_hbm,
    owner_row_hbm,
    slot_row_hbm,
    vis_hbm,
    coarse_hbm,
    *rest,
):
    outs = rest[:-10]
    (
        owner_s,
        count_s,
        owner_ref,
        slot_ref,
        vis_ref,
        coarse_ref,
        turn_ref,
        meta_ref,
        block_ref,
        sems,
    ) = rest[-10:]
    rows = vis_ref.shape[0]
    chunks = vis_ref.shape[2] // LANES
    devices = block_ref.shape[0]
    terms, stations = coarse_ref.shape
    half = stations // 2
    depth = meta_ref.shape[0]
    gain_tiles = (depth - 1) // 2
    moves = start_all(
        (
            (vis_hbm, vis_ref),
            (coarse_hbm, coarse_ref),
            (owner_hbm, owner_s),
            (owner_row_hbm, owner_ref),
            (slot_row_hbm, slot_ref),
        ),
        sems,
    )
    turn_ref[...] = jnp.zeros_like(turn_ref)
    for d in range(devices):
        count_s[d] = 0
    me = me_s[0]
    for move in moves[1:]:
        move.wait()

    turn_ref[0:terms, 0:half] = coarse_ref[:, 0:half]
    turn_ref[64 : 64 + terms, 0:half] = coarse_ref[:, half:stations]
    gains = turn_ref[...].T
    high = gains.astype(jnp.bfloat16)
    low = (gains - high.astype(jnp.float32)).astype(jnp.bfloat16)
    for i in range(gain_tiles):
        meta_ref[i] = high[i * SUB : (i + 1) * SUB, :]
        meta_ref[gain_tiles + i] = low[i * SUB : (i + 1) * SUB, :]
    sub = lax.broadcasted_iota(jnp.int32, (SUB, LANES), 0)
    codes = jnp.where(sub == 0, owner_ref[...], slot_ref[...])
    meta_ref[2 * gain_tiles] = codes.astype(jnp.float32).astype(jnp.bfloat16)
    at = chunks * capacity
    if near > 1:
        pairs = [(meta_ref, outs[x].at[pl.ds(at, depth)]) for x in range(devices)]
    else:
        pairs = [(meta_ref, outs[1])]
    sends = start_all(pairs, sems.at[pl.ds(1, len(pairs))])
    moves[0].wait()

    def place(r, carry):
        x = owner_s[r] ^ me
        k = count_s[x]
        count_s[x] = k + 1
        for c in range(chunks):
            block_ref[x, chunks * k + c] = vis_ref[r, :, c * LANES : (c + 1) * LANES]
        return carry

    lax.fori_loop(0, rows, place, 0, unroll=8)
    start = 1 + len(pairs)
    if near > 1:
        pairs = [(block_ref.at[x], outs[x].at[pl.ds(0, at)]) for x in range(devices)]
    else:
        pairs = [(block_ref, outs[0])]
    sends += start_all(pairs, sems.at[pl.ds(start, len(pairs))])
    for send in sends:
        send.wait()


def interpolation(weights, offset, high_ref, low_ref):
    channels = weights.shape[1]
    offset = jnp.concatenate([offset[c : c + 1, :] for c in range(offset.shape[0])], axis=1)
    index = lax.broadcasted_iota(jnp.int32, (LANES, channels), 0)
    knot = (index & 63) >> 3
    basis = jnp.zeros((LANES, channels), jnp.float32)
    for step in range(3):
        basis = basis + jnp.where(knot == offset + step, weights[step : step + 1, :], 0.0)
    high = basis.astype(jnp.bfloat16).astype(jnp.float32)
    low = basis - high
    part = index & 7
    for j in range(8):
        high_ref[j] = jnp.where(part == j, high, 0.0).astype(jnp.bfloat16)
        low_ref[j] = jnp.where(part == j, low, 0.0).astype(jnp.bfloat16)


def list_rows(owner, slot, target, capacity):
    senders = owner.shape[0]
    mine = owner == target
    counted = mine.astype(jnp.float32)
    before = lax.broadcasted_iota(jnp.int32, (LANES, LANES), 0) < lax.broadcasted_iota(
        jnp.int32, (LANES, LANES), 1
    )
    rank = jnp.dot(
        counted.astype(jnp.bfloat16),
        before.astype(jnp.float32).astype(jnp.bfloat16),
        preferred_element_type=jnp.float32,
    )
    lane = lax.broadcasted_iota(jnp.int32, (senders, LANES), 1)
    count = jnp.sum(counted, axis=1, keepdims=True)
    listing = jnp.where(lane == capacity, count, 0.0)
    for k in range(capacity):
        here = jnp.logical_and(mine, rank == float(k))
        kth = jnp.sum(jnp.where(here, slot, 0.0), axis=1, keepdims=True)
        listing = jnp.where(lane == k, kth, listing)
    return listing.astype(jnp.int32), mine


def add_rows(acc_ref, slots_s, line, capacity, rows_ref):
    chunks = acc_ref.shape[0]

    def add(k, carry):
        b = slots_s[line, k]
        for c in range(chunks):
            acc_ref[c, b] += rows_ref[chunks * k + c].astype(jnp.float32)
        return carry

    lax.fori_loop(0, slots_s[line, capacity], add, 0)


def add_table(table_ref, x, block, at, depth):
    gain_tiles = (depth - 1) // 2
    for i in range(gain_tiles):
        table_ref[x, i * SUB : (i + 1) * SUB, :] = block[at + i].astype(jnp.float32) + block[
            at + gain_tiles + i
        ].astype(jnp.float32)
    return block[at + 2 * gain_tiles].astype(jnp.float32)


def count_rows(hits, mine, slot):
    which = lax.broadcasted_iota(jnp.int32, hits.shape, 0).astype(jnp.float32)
    slot = jnp.where(mine, slot, -1.0)
    for x in range(slot.shape[0]):
        hits = hits + (slot[x : x + 1, :] == which).astype(jnp.float32)
    return hits


def middle_kernel(capacity, order, me_s, pairs_ref, weights_ref, offset_ref, *rest):
    arrived = dict(zip(order, rest[:-12]))
    table_ref, pairs_out_ref, high_ref, low_ref, hits_ref, slots_ref, sums_ref = rest[-12:-5]
    owner_ref, slot_ref, slots_v, slots_s, sem = rest[-5:]
    devices = table_ref.shape[0]
    chunks = sums_ref.shape[0]
    depth = 2 * (table_ref.shape[1] // SUB) + 1
    pairs_out_ref[...] = pairs_ref[...]
    owner_ref[...] = jnp.full(owner_ref.shape, -1.0, jnp.float32)
    slot_ref[...] = jnp.zeros_like(slot_ref)
    table_ref[...] = jnp.zeros_like(table_ref)
    whole = len(order) == 1
    for x in range(devices) if whole else order:
        if whole:
            code = add_table(table_ref, x, arrived[0].at[x], 0, depth)
        else:
            code = add_table(table_ref, x, arrived[x], chunks * capacity, depth)
        owner_ref[x : x + 1, :] = code[0:1, :]
        slot_ref[x : x + 1, :] = code[1:2, :]
    slot = slot_ref[...]
    listing, mine = list_rows(owner_ref[...], slot, me_s[0].astype(jnp.float32), capacity)
    slots_ref[...] = listing
    slots_v[...] = listing
    move = pltpu.make_async_copy(slots_v, slots_s, sem)
    move.start()
    hits_ref[...] = count_rows(jnp.zeros(hits_ref.shape, jnp.float32), mine, slot)
    interpolation(weights_ref[...], offset_ref[...], high_ref, low_ref)
    sums_ref[...] = jnp.zeros_like(sums_ref)
    move.wait()
    if not whole:
        for x in order:
            add_rows(sums_ref, slots_s, x, capacity, arrived[x])


def finish_kernel(
    capacity,
    stations,
    late,
    turn_s,
    me_s,
    pairs_s,
    slots_in_s,
    high_ref,
    low_ref,
    early_ref,
    hits_ref,
    sums_ref,
    *rest,
):
    far = rest[: len(late)]
    (
        out_hbm,
        table_ref,
        pick_ref,
        gains_ref,
        owner_ref,
        slot_ref,
        slots_v,
        slots_s,
        acc_ref,
        res_ref,
        out_ref,
        sems,
    ) = rest[len(late) :]
    owned, parts, channels = out_hbm.shape
    chunks = channels // LANES
    half = stations // 2
    depth = 2 * (table_ref.shape[1] // SUB) + 1
    table_ref[...] = early_ref[...]
    hits = hits_ref[...]
    if len(late) > 1:
        owner_ref[...] = jnp.full(owner_ref.shape, -1.0, jnp.float32)
        slot_ref[...] = jnp.zeros_like(slot_ref)
        for i, x in enumerate(late):
            code = add_table(table_ref, x, far[i], chunks * capacity, depth)
            owner_ref[i : i + 1, :] = code[0:1, :]
            slot_ref[i : i + 1, :] = code[1:2, :]
        slot = slot_ref[...]
        listing, mine = list_rows(owner_ref[...], slot, me_s[0].astype(jnp.float32), capacity)
        slots_v[...] = listing
        move = pltpu.make_async_copy(slots_v, slots_s, sems.at[0])
        move.start()
        hits = count_rows(hits, mine[0 : len(late)], slot[0 : len(late)])

    turn = turn_s[0]
    column = lax.broadcasted_iota(jnp.int32, (1, LANES), 1)
    used = (column & 63) < USED
    upper = column >> 6

    def pick(b, carry):
        for side in range(2):
            s = pairs_s[side, b]
            d = s // stations
            within = s - d * stations
            second = jnp.where(within >= half, 1, 0)
            row = table_ref[d ^ turn, pl.ds(within - second * half, 1), :]
            keep = jnp.logical_and(used, upper == second)
            pick_ref[pl.ds(side * owned + b, 1), :] = jnp.where(keep, row, 0.0)
        return carry

    lax.fori_loop(0, owned, pick, 0, unroll=8)
    both = pick_ref[...]
    both_high = both.astype(jnp.bfloat16)
    both_low = (both - both_high.astype(jnp.float32)).astype(jnp.bfloat16)
    both_two = jnp.concatenate([both_high, both_low], axis=1)
    for j in range(parts):
        high = high_ref[j]
        fine = jnp.dot(
            both_two, jnp.concatenate([high, high], axis=0), preferred_element_type=jnp.float32
        ) + jnp.dot(both_high, low_ref[j], preferred_element_type=jnp.float32)
        gains_ref[j] = fine.astype(jnp.bfloat16).astype(jnp.float32)

    acc_ref[...] = sums_ref[...]
    tally = jnp.sum(hits, axis=1, keepdims=True)
    recip = jnp.broadcast_to(1.0 / jnp.maximum(tally, 1.0), (owned, LANES))
    if len(late) > 1:
        move.wait()
        for i in range(len(late)):
            add_rows(acc_ref, slots_s, i, capacity, far[i])
    else:

        def from_device(d, carry):
            add_rows(acc_ref, slots_in_s, d, capacity, far[0].at[d])
            return carry

        lax.fori_loop(0, far[0].shape[0], from_device, 0)

    flat = acc_ref.reshape(chunks * owned * parts, LANES)
    done = res_ref.reshape(chunks * owned * parts, LANES)
    sends = []
    for c in range(chunks):
        cols = slice(c * LANES, (c + 1) * LANES)
        for b0 in range(0, owned, SUB):
            scale = recip[b0 : b0 + SUB, :]
            row = (c * owned + b0) * parts
            vis = [flat[pl.ds(row + j, SUB, stride=parts), :] for j in range(parts)]
            lhs = [gains_ref[j, b0 : b0 + SUB, cols] for j in range(parts)]
            rhs = [gains_ref[j, owned + b0 : owned + b0 + SUB, cols] for j in range(parts)]
            mid_re, mid_im = [], []
            for row_a in range(2):
                for col_b in range(2):
                    re = im = 0.0
                    for inner in range(2):
                        lr, li = lhs[2 * row_a + inner], lhs[4 + 2 * row_a + inner]
                        vr, vi = vis[2 * inner + col_b], vis[4 + 2 * inner + col_b]
                        re = re + lr * vr - li * vi
                        im = im + lr * vi + li * vr
                    mid_re.append(re * scale)
                    mid_im.append(im * scale)
            for row_a in range(2):
                for col_b in range(2):
                    re = im = 0.0
                    for inner in range(2):
                        mr, mi = mid_re[2 * row_a + inner], mid_im[2 * row_a + inner]
                        rr, ri = rhs[2 * col_b + inner], rhs[4 + 2 * col_b + inner]
                        re = re + mr * rr + mi * ri
                        im = im + mi * rr - mr * ri
                    j = 2 * row_a + col_b
                    done[pl.ds(row + j, SUB, stride=parts), :] = re
                    done[pl.ds(row + 4 + j, SUB, stride=parts), :] = im
        out_ref[c] = res_ref[c].astype(out_ref.dtype)
        sends.append(
            pltpu.make_async_copy(
                out_ref.at[c], out_hbm.at[:, :, pl.ds(c * LANES, LANES)], sems.at[1 + c]
            )
        )
        sends[-1].start()
    for send in sends:
        send.wait()


def on_device(
    visibilities,
    row_owner,
    row_slot,
    baseline_station_pairs,
    gains_coarse,
    band_weights,
    band_offset,
):
    devices = lax.axis_size("bl")
    rows, parts, channels = visibilities.shape
    capacity = 2 * rows // devices
    owned = baseline_station_pairs.shape[0]
    stations, _, knots = gains_coarse.shape
    chunks = channels // LANES
    gain_tiles = round_up(stations // 2, SUB) // SUB
    depth = 2 * gain_tiles + 1
    near = devices // 2 if devices <= 16 else 1
    halves = near > 1
    f32, bf16, i32 = jnp.float32, jnp.bfloat16, jnp.int32
    vmem = pl.BlockSpec(memory_space=pltpu.VMEM)
    smem = pl.BlockSpec(memory_space=pltpu.SMEM)
    hbm = pl.BlockSpec(memory_space=pltpu.HBM)
    anywhere = pl.BlockSpec(memory_space=pl.ANY)
    most = pltpu.CompilerParams(vmem_limit_bytes=ALL_VMEM)
    some = pltpu.CompilerParams(vmem_limit_bytes=SOME_VMEM)
    shape = jax.ShapeDtypeStruct
    dma = pltpu.SemaphoreType.DMA

    me = lax.axis_index("bl").astype(i32).reshape(1)
    turn = me if halves else jnp.zeros_like(me)
    owner = row_owner.reshape(rows)
    coarse = gains_coarse.transpose(2, 1, 0).reshape(knots * parts, stations)
    block = (chunks * capacity, parts, LANES)
    rows_at = chunks * capacity
    if halves:
        outs = [shape((rows_at + depth, parts, LANES), bf16)] * devices
    else:
        outs = [shape((devices,) + block, bf16), shape((depth, SUB, LANES), bf16)]
    sent = pl.pallas_call(
        functools.partial(pack_kernel, capacity, near),
        out_shape=outs,
        in_specs=[smem] + [hbm] * 5,
        out_specs=[hbm] * len(outs),
        scratch_shapes=[
            pltpu.SMEM((rows,), i32),
            pltpu.SMEM((devices,), i32),
            pltpu.VMEM((1, rows), i32),
            pltpu.VMEM((1, rows), i32),
            pltpu.VMEM((rows, parts, channels), bf16),
            pltpu.VMEM((knots * parts, stations), f32),
            pltpu.VMEM((LANES, LANES), f32),
            pltpu.VMEM((depth, SUB, LANES), bf16),
            pltpu.VMEM((devices,) + block, bf16),
            dma((5 + 2 * devices,)),
        ],
        compiler_params=most,
        name="pack_rows",
    )(
        turn,
        owner,
        row_owner.reshape(1, rows),
        row_slot.reshape(1, rows),
        visibilities,
        coarse,
    )

    pairs = baseline_station_pairs.T
    weights = band_weights.T
    offset = band_offset.reshape(chunks, LANES)

    def swap(array, x):
        return lax.ppermute(array, "bl", [(d, d ^ x) for d in range(devices)])

    if halves:
        arrived = {x: swap(sent[x], x) if x else sent[x] for x in range(devices)}
        order, late = schedule(near)
    else:
        arrived = {
            0: lax.all_gather(sent[1], "bl", axis=0),
            1: lax.all_to_all(sent[0], "bl", split_axis=0, concat_axis=0, tiled=True),
        }
        order, late = [0], [1]

    table, pairs, high, low, hits, slots, sums = pl.pallas_call(
        functools.partial(middle_kernel, capacity, order),
        out_shape=(
            shape((devices, gain_tiles * SUB, LANES), f32),
            shape((2, owned), i32),
            shape((parts, LANES, channels), bf16),
            shape((parts, LANES, channels), bf16),
            shape((owned, LANES), f32),
            shape((devices, LANES), i32),
            shape((chunks, owned, parts, LANES), f32),
        ),
        in_specs=[smem] + [vmem] * (3 + len(order)),
        out_specs=(vmem,) * 7,
        scratch_shapes=[
            pltpu.VMEM((devices, LANES), f32),
            pltpu.VMEM((devices, LANES), f32),
            pltpu.VMEM((devices, LANES), i32),
            pltpu.SMEM((devices, LANES), i32),
            dma,
        ],
        compiler_params=some,
        name="sum_early",
    )(me, pairs, weights, offset, *[arrived[x] for x in order])
    return pl.pallas_call(
        functools.partial(finish_kernel, capacity, stations, late),
        out_shape=shape((owned, parts, channels), bf16),
        in_specs=[smem] * 4 + [vmem] * (5 + len(late)),
        out_specs=hbm,
        scratch_shapes=[
            pltpu.VMEM((devices, gain_tiles * SUB, LANES), f32),
            pltpu.VMEM((2 * owned, LANES), f32),
            pltpu.VMEM((parts, 2 * owned, channels), f32),
            pltpu.VMEM((SUB, LANES), f32),
            pltpu.VMEM((SUB, LANES), f32),
            pltpu.VMEM((SUB, LANES), i32),
            pltpu.SMEM((SUB, LANES), i32),
            pltpu.VMEM((chunks, owned, parts, LANES), f32),
            pltpu.VMEM((chunks, owned, parts, LANES), f32),
            pltpu.VMEM((chunks, owned, parts, LANES), bf16),
            dma((1 + chunks,)),
        ],
        compiler_params=some,
        name="sum_and_apply",
    )(turn, me, pairs, slots, high, low, table, hits, sums, *[arrived[x] for x in late])


def solution(mesh):
    placed = (
        P(("groups", "bl"), None, None),
        P(("groups", "bl"), None),
        P(("groups", "bl")),
        P("bl", None),
        P(("groups", "bl"), None, None),
        P("groups", None),
        P("groups"),
    )
    return jax.shard_map(
        on_device,
        mesh=mesh,
        in_specs=placed,
        out_specs=P(("groups", "bl"), None, None),
        check_vma=False,
    )
```

```python
import functools

import jax
import jax.numpy as jnp
from jax import lax
from jax.experimental import pallas as pl
from jax.experimental.pallas import tpu as pltpu
from jax.sharding import PartitionSpec as P

LANES = 128
SUB = 8
USED = 48
ALL_VMEM = 60 * 1024 * 1024
SOME_VMEM = 24 * 1024 * 1024


def round_up(value, unit):
    return -(-value // unit) * unit


def schedule(near):
    even, odd = list(range(near, 2 * near, 2)), list(range(near + 1, 2 * near, 2))
    close = list(range(near // 2, near)) + list(range(1, near // 2))
    cross, late = even[2:] + odd[1:-2], odd[-2:]
    order = [0] + even[:2] + close[:3]
    close = close[3:]
    while cross:
        order += cross[:1] + close[:1]
        cross, close = cross[1:], close[1:]
    return order + close + odd[:1], late


def with_gains(near):
    return list(range(near)) + list(range(near, 2 * near, 2))


def start_all(pairs, sems):
    moves = [pltpu.make_async_copy(src, dst, sems.at[i]) for i, (src, dst) in enumerate(pairs)]
    for move in moves:
        move.start()
    return moves


def pack_kernel(
    capacity,
    near,
    me_s,
    owner_hbm,
    owner_row_hbm,
    slot_row_hbm,
    vis_hbm,
    coarse_hbm,
    weights_hbm,
    offset_hbm,
    pairs_hbm,
    *rest,
):
    outs = rest[:-14]
    (
        weights_ref,
        offset_ref,
        pairs_ref,
        small_ref,
        owner_s,
        count_s,
        owner_ref,
        slot_ref,
        vis_ref,
        coarse_ref,
        turn_ref,
        meta_ref,
        block_ref,
        sems,
    ) = rest[-14:]
    rows = vis_ref.shape[0]
    chunks = vis_ref.shape[2] // LANES
    devices = block_ref.shape[0]
    terms, stations = coarse_ref.shape
    half = stations // 2
    depth = meta_ref.shape[0]
    gain_tiles = (depth - 1) // 2
    moves = start_all(
        (
            (vis_hbm, vis_ref),
            (coarse_hbm, coarse_ref),
            (owner_hbm, owner_s),
            (owner_row_hbm, owner_ref),
            (slot_row_hbm, slot_ref),
            (weights_hbm, weights_ref),
            (offset_hbm, offset_ref),
            (pairs_hbm, pairs_ref),
        ),
        sems,
    )
    turn_ref[...] = jnp.zeros_like(turn_ref)
    for d in range(devices):
        count_s[d] = 0
    me = me_s[0]
    for move in moves[1:]:
        move.wait()

    turn_ref[0:terms, 0:half] = coarse_ref[:, 0:half]
    turn_ref[64 : 64 + terms, 0:half] = coarse_ref[:, half:stations]
    gains = turn_ref[...].T
    high = gains.astype(jnp.bfloat16)
    low = (gains - high.astype(jnp.float32)).astype(jnp.bfloat16)
    for i in range(gain_tiles):
        meta_ref[i] = high[i * SUB : (i + 1) * SUB, :]
        meta_ref[gain_tiles + i] = low[i * SUB : (i + 1) * SUB, :]
    sub = lax.broadcasted_iota(jnp.int32, (SUB, LANES), 0)
    codes = jnp.where(sub == 0, owner_ref[...], slot_ref[...])
    meta_ref[2 * gain_tiles] = codes.astype(jnp.float32).astype(jnp.bfloat16)
    steps = weights_ref.shape[0]
    small_ref[...] = jnp.zeros_like(small_ref)
    small_ref[0:steps, :] = weights_ref[...]
    for c in range(chunks):
        lanes = slice(c * LANES, (c + 1) * LANES)
        small_ref[steps : steps + 1, lanes] = offset_ref[c : c + 1, :].astype(jnp.float32)
    small_ref[4:6, 0 : pairs_ref.shape[1]] = pairs_ref[...].astype(jnp.float32)

    at = chunks * capacity
    if near > 1:
        pairs = [(meta_ref, outs[x].at[pl.ds(at, depth)]) for x in with_gains(near)]
    else:
        pairs = [(meta_ref, outs[1])]
    pairs += [(small_ref, outs[-1])]
    sends = start_all(pairs, sems.at[pl.ds(8, len(pairs))])
    moves[0].wait()

    def place(r, carry):
        x = owner_s[r] ^ me
        k = count_s[x]
        count_s[x] = k + 1
        for c in range(chunks):
            block_ref[x, chunks * k + c] = vis_ref[r, :, c * LANES : (c + 1) * LANES]
        return carry

    lax.fori_loop(0, rows, place, 0, unroll=8)
    start = 8 + len(pairs)
    if near > 1:
        pairs = [(block_ref.at[x], outs[x].at[pl.ds(0, at)]) for x in range(devices)]
    else:
        pairs = [(block_ref, outs[0])]
    sends += start_all(pairs, sems.at[pl.ds(start, len(pairs))])
    for send in sends:
        send.wait()


def interpolation(small):
    channels = small.shape[1]
    index = lax.broadcasted_iota(jnp.int32, (LANES, channels), 0)
    knot = ((index & 63) >> 3).astype(jnp.float32)
    basis = jnp.zeros((LANES, channels), jnp.float32)
    for step in range(3):
        basis = basis + jnp.where(knot == small[3:4, :] + float(step), small[step : step + 1, :], 0.0)
    high = basis.astype(jnp.bfloat16).astype(jnp.float32)
    part = index & 7
    return [
        (
            jnp.where(part == j, high, 0.0).astype(jnp.bfloat16),
            jnp.where(part == j, basis - high, 0.0).astype(jnp.bfloat16),
        )
        for j in range(8)
    ]


def collect_kernel(at, depth, *rest):
    blocks, (out_ref, sems) = rest[:-2], rest[-2:]
    moves = start_all(
        [
            (block.at[pl.ds(at, depth)], out_ref.at[pl.ds(i * depth, depth)])
            for i, block in enumerate(blocks)
        ],
        sems,
    )
    for move in moves:
        move.wait()


def list_rows(owner, slot, target, capacity):
    senders = owner.shape[0]
    mine = owner == target
    counted = mine.astype(jnp.float32)
    before = lax.broadcasted_iota(jnp.int32, (LANES, LANES), 0) < lax.broadcasted_iota(
        jnp.int32, (LANES, LANES), 1
    )
    rank = jnp.dot(
        counted.astype(jnp.bfloat16),
        before.astype(jnp.float32).astype(jnp.bfloat16),
        preferred_element_type=jnp.float32,
    )
    lane = lax.broadcasted_iota(jnp.int32, (senders, LANES), 1)
    count = jnp.sum(counted, axis=1, keepdims=True)
    listing = jnp.where(lane == capacity, count, 0.0)
    for k in range(capacity):
        here = jnp.logical_and(mine, rank == float(k))
        kth = jnp.sum(jnp.where(here, slot, 0.0), axis=1, keepdims=True)
        listing = jnp.where(lane == k, kth, listing)
    return listing.astype(jnp.int32), mine


def add_rows(acc_ref, slots_s, line, capacity, rows_ref):
    chunks = acc_ref.shape[0]

    def add(k, carry):
        b = slots_s[line, k]
        for c in range(chunks):
            acc_ref[c, b] += rows_ref[chunks * k + c].astype(jnp.float32)
        return carry

    lax.fori_loop(0, slots_s[line, capacity], add, 0)


def add_table(table_ref, x, block, at, depth):
    gain_tiles = (depth - 1) // 2
    for i in range(gain_tiles):
        table_ref[x, i * SUB : (i + 1) * SUB, :] = block[at + i].astype(jnp.float32) + block[
            at + gain_tiles + i
        ].astype(jnp.float32)
    return block[at + 2 * gain_tiles].astype(jnp.float32)


def count_rows(hits, mine, slot):
    which = lax.broadcasted_iota(jnp.int32, hits.shape, 0).astype(jnp.float32)
    slot = jnp.where(mine, slot, -1.0)
    for x in range(slot.shape[0]):
        hits = hits + (slot[x : x + 1, :] == which).astype(jnp.float32)
    return hits


def middle_kernel(capacity, near, stations, order, turn_s, me_s, small_ref, *rest):
    arrived, passed = dict(zip(order, rest)), rest[len(order) : -13]
    gains_ref, recip_ref, slots_ref, sums_ref = rest[-13:-9]
    table_ref, pick_ref, owner_ref, slot_ref, slots_v, slots_s, pairs_v, pairs_s, sems = rest[-9:]
    devices = table_ref.shape[0]
    owned = recip_ref.shape[0]
    chunks = sums_ref.shape[0]
    half = stations // 2
    depth = 2 * (table_ref.shape[1] // SUB) + 1
    small = small_ref[...]
    pairs_v[...] = small[0:SUB, 0:LANES].astype(jnp.int32)
    scalars = [pltpu.make_async_copy(pairs_v, pairs_s, sems.at[0])]
    scalars[0].start()
    for x in range(devices):
        if near == 1:
            code = add_table(table_ref, x, arrived[0].at[x], 0, depth)
        elif x in with_gains(near):
            code = add_table(table_ref, x, arrived[x], chunks * capacity, depth)
        else:
            code = add_table(table_ref, x, passed[0], (x - near) // 2 * depth, depth)
        owner_ref[x : x + 1, :] = code[0:1, :]
        slot_ref[x : x + 1, :] = code[1:2, :]
    slot = slot_ref[...]
    listing, mine = list_rows(owner_ref[...], slot, me_s[0].astype(jnp.float32), capacity)
    slots_ref[...] = listing
    slots_v[...] = listing
    scalars.append(pltpu.make_async_copy(slots_v, slots_s, sems.at[1]))
    scalars[1].start()
    hits = count_rows(jnp.zeros((owned, LANES), jnp.float32), mine, slot)
    tally = jnp.sum(hits, axis=1, keepdims=True)
    recip_ref[...] = jnp.broadcast_to(1.0 / jnp.maximum(tally, 1.0), recip_ref.shape)

    scalars[0].wait()
    turn = turn_s[0]
    column = lax.broadcasted_iota(jnp.int32, (1, LANES), 1)
    used = (column & 63) < USED
    upper = column >> 6

    def pick(b, carry):
        for side in range(2):
            s = pairs_s[4 + side, b]
            d = s // stations
            within = s - d * stations
            second = jnp.where(within >= half, 1, 0)
            row = table_ref[d ^ turn, pl.ds(within - second * half, 1), :]
            keep = jnp.logical_and(used, upper == second)
            pick_ref[pl.ds(side * owned + b, 1), :] = jnp.where(keep, row, 0.0)
        return carry

    lax.fori_loop(0, owned, pick, 0, unroll=8)
    both = pick_ref[...]
    both_high = both.astype(jnp.bfloat16)
    both_low = (both - both_high.astype(jnp.float32)).astype(jnp.bfloat16)
    both_two = jnp.concatenate([both_high, both_low], axis=1)
    for j, (high, low) in enumerate(interpolation(small)):
        fine = jnp.dot(
            both_two, jnp.concatenate([high, high], axis=0), preferred_element_type=jnp.float32
        ) + jnp.dot(both_high, low, preferred_element_type=jnp.float32)
        gains_ref[j] = fine.astype(jnp.bfloat16).astype(jnp.float32)

    sums_ref[...] = jnp.zeros_like(sums_ref)
    scalars[1].wait()
    if near > 1:
        for x in order:
            add_rows(sums_ref, slots_s, x, capacity, arrived[x])


def finish_kernel(capacity, late, slots_s, gains_ref, recip_ref, sums_ref, *rest):
    far = rest[: len(late)]
    out_hbm, acc_ref, res_ref, out_ref, sems = rest[len(late) :]
    owned, parts, channels = out_hbm.shape
    chunks = channels // LANES
    acc_ref[...] = sums_ref[...]
    if len(late) > 1:
        for x, rows_ref in zip(late, far):
            add_rows(acc_ref, slots_s, x, capacity, rows_ref)
    else:

        def from_device(d, carry):
            add_rows(acc_ref, slots_s, d, capacity, far[0].at[d])
            return carry

        lax.fori_loop(0, far[0].shape[0], from_device, 0)

    flat = acc_ref.reshape(chunks * owned * parts, LANES)
    done = res_ref.reshape(chunks * owned * parts, LANES)
    sends = []
    for c in range(chunks):
        cols = slice(c * LANES, (c + 1) * LANES)
        for b0 in range(0, owned, SUB):
            scale = recip_ref[b0 : b0 + SUB, :]
            row = (c * owned + b0) * parts
            vis = [flat[pl.ds(row + j, SUB, stride=parts), :] for j in range(parts)]
            lhs = [gains_ref[j, b0 : b0 + SUB, cols] for j in range(parts)]
            rhs = [gains_ref[j, owned + b0 : owned + b0 + SUB, cols] for j in range(parts)]
            mid_re, mid_im = [], []
            for row_a in range(2):
                for col_b in range(2):
                    re = im = 0.0
                    for inner in range(2):
                        lr, li = lhs[2 * row_a + inner], lhs[4 + 2 * row_a + inner]
                        vr, vi = vis[2 * inner + col_b], vis[4 + 2 * inner + col_b]
                        re = re + lr * vr - li * vi
                        im = im + lr * vi + li * vr
                    mid_re.append(re * scale)
                    mid_im.append(im * scale)
            for row_a in range(2):
                for col_b in range(2):
                    re = im = 0.0
                    for inner in range(2):
                        mr, mi = mid_re[2 * row_a + inner], mid_im[2 * row_a + inner]
                        rr, ri = rhs[2 * col_b + inner], rhs[4 + 2 * col_b + inner]
                        re = re + mr * rr + mi * ri
                        im = im + mi * rr - mr * ri
                    j = 2 * row_a + col_b
                    done[pl.ds(row + j, SUB, stride=parts), :] = re
                    done[pl.ds(row + 4 + j, SUB, stride=parts), :] = im
        out_ref[c] = res_ref[c].astype(out_ref.dtype)
        sends.append(
            pltpu.make_async_copy(
                out_ref.at[c], out_hbm.at[:, :, pl.ds(c * LANES, LANES)], sems.at[c]
            )
        )
        sends[-1].start()
    for send in sends:
        send.wait()


def on_device(
    visibilities,
    row_owner,
    row_slot,
    baseline_station_pairs,
    gains_coarse,
    band_weights,
    band_offset,
):
    devices = lax.axis_size("bl")
    rows, parts, channels = visibilities.shape
    capacity = 2 * rows // devices
    owned = baseline_station_pairs.shape[0]
    stations, _, knots = gains_coarse.shape
    chunks = channels // LANES
    gain_tiles = round_up(stations // 2, SUB) // SUB
    depth = 2 * gain_tiles + 1
    near = devices // 2 if devices <= 16 else 1
    halves = near > 1
    f32, bf16, i32 = jnp.float32, jnp.bfloat16, jnp.int32
    vmem = pl.BlockSpec(memory_space=pltpu.VMEM)
    smem = pl.BlockSpec(memory_space=pltpu.SMEM)
    hbm = pl.BlockSpec(memory_space=pltpu.HBM)
    anywhere = pl.BlockSpec(memory_space=pl.ANY)
    most = pltpu.CompilerParams(vmem_limit_bytes=ALL_VMEM)
    some = pltpu.CompilerParams(vmem_limit_bytes=SOME_VMEM)
    shape = jax.ShapeDtypeStruct
    dma = pltpu.SemaphoreType.DMA

    me = lax.axis_index("bl").astype(i32).reshape(1)
    turn = me if halves else jnp.zeros_like(me)
    owner = row_owner.reshape(rows)
    coarse = gains_coarse.transpose(2, 1, 0).reshape(knots * parts, stations)
    block = (chunks * capacity, parts, LANES)
    rows_at = chunks * capacity
    if halves:
        long = with_gains(near) + [near + 3]
        outs = [
            shape((rows_at + (depth if x in long else 0), parts, LANES), bf16)
            for x in range(devices)
        ]
    else:
        outs = [shape((devices,) + block, bf16), shape((depth, SUB, LANES), bf16)]
    outs += [shape((SUB, channels), f32)]
    pairs = baseline_station_pairs.T
    weights = band_weights.T
    offset = band_offset.reshape(chunks, LANES)
    sent = pl.pallas_call(
        functools.partial(pack_kernel, capacity, near),
        out_shape=outs,
        in_specs=[smem] + [hbm] * 8,
        out_specs=[hbm] * len(outs),
        scratch_shapes=[
            pltpu.VMEM(weights.shape, f32),
            pltpu.VMEM(offset.shape, i32),
            pltpu.VMEM(pairs.shape, i32),
            pltpu.VMEM((SUB, channels), f32),
            pltpu.SMEM((rows,), i32),
            pltpu.SMEM((devices,), i32),
            pltpu.VMEM((1, rows), i32),
            pltpu.VMEM((1, rows), i32),
            pltpu.VMEM((rows, parts, channels), bf16),
            pltpu.VMEM((knots * parts, stations), f32),
            pltpu.VMEM((LANES, LANES), f32),
            pltpu.VMEM((depth, SUB, LANES), bf16),
            pltpu.VMEM((devices,) + block, bf16),
            dma((9 + 2 * devices,)),
        ],
        compiler_params=most,
        name="pack_rows",
    )(
        turn,
        owner,
        row_owner.reshape(1, rows),
        row_slot.reshape(1, rows),
        visibilities,
        coarse,
        weights,
        offset,
        pairs,
    )


    def swap(array, x):
        return lax.ppermute(array, "bl", [(d, d ^ x) for d in range(devices)])

    if halves:
        arrived = {x: swap(sent[x], x) if x else sent[x] for x in range(devices)}
        order, late = schedule(near)
        even = list(range(near, devices, 2))
        collected = pl.pallas_call(
            functools.partial(collect_kernel, rows_at, depth),
            out_shape=shape((len(even) * depth, parts, LANES), bf16),
            in_specs=[anywhere] * len(even),
            out_specs=vmem,
            scratch_shapes=[dma((len(even),))],
            compiler_params=some,
            name="collect_gains",
        )(*[arrived[x] for x in even])
        passed = [swap(collected, 1)]
    else:
        arrived = {
            0: lax.all_gather(sent[1], "bl", axis=0),
            1: lax.all_to_all(sent[0], "bl", split_axis=0, concat_axis=0, tiled=True),
        }
        order, late, passed = [0], [1], []

    gains, recip, slots, sums = pl.pallas_call(
        functools.partial(middle_kernel, capacity, near, stations, order),
        out_shape=(
            shape((parts, 2 * owned, channels), f32),
            shape((owned, LANES), f32),
            shape((devices, LANES), i32),
            shape((chunks, owned, parts, LANES), f32),
        ),
        in_specs=[smem] * 2 + [vmem] * (1 + len(order) + len(passed)),
        out_specs=(vmem,) * 4,
        scratch_shapes=[
            pltpu.VMEM((devices, gain_tiles * SUB, LANES), f32),
            pltpu.VMEM((2 * owned, LANES), f32),
            pltpu.VMEM((devices, LANES), f32),
            pltpu.VMEM((devices, LANES), f32),
            pltpu.VMEM((devices, LANES), i32),
            pltpu.SMEM((devices, LANES), i32),
            pltpu.VMEM((SUB, LANES), i32),
            pltpu.SMEM((SUB, LANES), i32),
            dma((2,)),
        ],
        compiler_params=some,
        name="gains_and_sums",
    )(turn, me, sent[-1], *[arrived[x] for x in order], *passed)
    return pl.pallas_call(
        functools.partial(finish_kernel, capacity, late),
        out_shape=shape((owned, parts, channels), bf16),
        in_specs=[smem] + [vmem] * (3 + len(late)),
        out_specs=hbm,
        scratch_shapes=[
            pltpu.VMEM((chunks, owned, parts, LANES), f32),
            pltpu.VMEM((chunks, owned, parts, LANES), f32),
            pltpu.VMEM((chunks, owned, parts, LANES), bf16),
            dma((chunks,)),
        ],
        compiler_params=some,
        name="sum_and_apply",
    )(slots, gains, recip, sums, *[arrived[x] for x in late])


def solution(mesh):
    placed = (
        P(("groups", "bl"), None, None),
        P(("groups", "bl"), None),
        P(("groups", "bl")),
        P("bl", None),
        P(("groups", "bl"), None, None),
        P("groups", None),
        P("groups"),
    )
    return jax.shard_map(
        on_device,
        mesh=mesh,
        in_specs=placed,
        out_specs=P(("groups", "bl"), None, None),
        check_vma=False,
    )
```

```python
import functools

import jax
import jax.numpy as jnp
from jax import lax
from jax.experimental import pallas as pl
from jax.experimental.pallas import tpu as pltpu
from jax.sharding import PartitionSpec as P

LANES = 128
SUB = 8
USED = 48
PARTS = 4
ALL_VMEM = 60 * 1024 * 1024
SOME_VMEM = 24 * 1024 * 1024


def round_up(value, unit):
    return -(-value // unit) * unit


def schedule(near):
    even, odd = list(range(near, 2 * near, 2)), list(range(near + 1, 2 * near, 2))
    close = list(range(near // 2, near)) + list(range(1, near // 2))
    cross, late = even[2:] + odd[1:-2], odd[-2:]
    order = [0] + even[:2] + close[:2]
    close = close[2:]
    while cross:
        order += cross[:1] + close[:1]
        cross, close = cross[1:], close[1:]
    return order + close + odd[:1], late


def with_gains(near):
    return list(range(near)) + list(range(near, 2 * near, 2))


def start_all(pairs, sems):
    moves = [pltpu.make_async_copy(src, dst, sems.at[i]) for i, (src, dst) in enumerate(pairs)]
    for move in moves:
        move.start()
    return moves


def pack_kernel(
    capacity,
    near,
    me_s,
    owner_hbm,
    owner_row_hbm,
    slot_row_hbm,
    vis_hbm,
    coarse_hbm,
    weights_hbm,
    offset_hbm,
    pairs_hbm,
    *rest,
):
    outs = rest[:-15]
    (
        weights_ref,
        offset_ref,
        pairs_ref,
        small_ref,
        owner_s,
        place_s,
        count_s,
        owner_ref,
        slot_ref,
        vis_ref,
        coarse_ref,
        turn_ref,
        meta_ref,
        block_ref,
        sems,
    ) = rest[-15:]
    rows = vis_ref.shape[0]
    chunks = vis_ref.shape[2] // LANES
    devices = block_ref.shape[0]
    terms, stations = coarse_ref.shape
    half = stations // 2
    depth = meta_ref.shape[0]
    gain_tiles = (depth - 1) // 2
    span = rows // PARTS
    moves = start_all(
        (
            (owner_hbm, owner_s),
            (coarse_hbm, coarse_ref),
            (owner_row_hbm, owner_ref),
            (slot_row_hbm, slot_ref),
            (weights_hbm, weights_ref),
            (offset_hbm, offset_ref),
            (pairs_hbm, pairs_ref),
        ),
        sems,
    )
    fetches = start_all(
        [
            (vis_hbm.at[pl.ds(i * span, span)], vis_ref.at[pl.ds(i * span, span)])
            for i in range(PARTS)
        ],
        sems.at[pl.ds(len(moves), PARTS)],
    )
    turn_ref[...] = jnp.zeros_like(turn_ref)
    for d in range(devices):
        count_s[d] = 0
    me = me_s[0]
    moves[0].wait()

    def rank(r, carry):
        x = owner_s[r] ^ me
        k = count_s[x]
        count_s[x] = k + 1
        place_s[r] = x * capacity + k
        return carry

    lax.fori_loop(0, rows, rank, 0, unroll=8)
    for move in moves[1:]:
        move.wait()

    turn_ref[0:terms, 0:half] = coarse_ref[:, 0:half]
    turn_ref[64 : 64 + terms, 0:half] = coarse_ref[:, half:stations]
    gains = turn_ref[...].T
    high = gains.astype(jnp.bfloat16)
    low = (gains - high.astype(jnp.float32)).astype(jnp.bfloat16)
    for i in range(gain_tiles):
        meta_ref[i] = high[i * SUB : (i + 1) * SUB, :]
        meta_ref[gain_tiles + i] = low[i * SUB : (i + 1) * SUB, :]
    sub = lax.broadcasted_iota(jnp.int32, (SUB, LANES), 0)
    codes = jnp.where(sub == 0, owner_ref[...], slot_ref[...])
    meta_ref[2 * gain_tiles] = codes.astype(jnp.float32).astype(jnp.bfloat16)
    steps = weights_ref.shape[0]
    small_ref[...] = jnp.zeros_like(small_ref)
    small_ref[0:steps, :] = weights_ref[...]
    for c in range(chunks):
        lanes = slice(c * LANES, (c + 1) * LANES)
        small_ref[steps : steps + 1, lanes] = offset_ref[c : c + 1, :].astype(jnp.float32)
    small_ref[4:6, 0 : pairs_ref.shape[1]] = pairs_ref[...].astype(jnp.float32)

    at = chunks * capacity
    if near > 1:
        pairs = [(meta_ref, outs[x].at[pl.ds(at, depth)]) for x in with_gains(near)]
    else:
        pairs = [(meta_ref, outs[1])]
    pairs += [(small_ref, outs[-1])]
    start = len(moves) + PARTS
    sends = start_all(pairs, sems.at[pl.ds(start, len(pairs))])
    start += len(pairs)

    def place(r, carry):
        p = place_s[r]
        for c in range(chunks):
            flat_ref[p * chunks + c] = vis_ref[r, :, c * LANES : (c + 1) * LANES]
        return carry

    flat_ref = block_ref.reshape(devices * at, SUB, LANES)
    for i in range(PARTS):
        fetches[i].wait()
        lax.fori_loop(i * span, (i + 1) * span, place, 0, unroll=8)
    if near > 1:
        pairs = [(block_ref.at[x], outs[x].at[pl.ds(0, at)]) for x in range(devices)]
    else:
        pairs = [(block_ref, outs[0])]
    sends += start_all(pairs, sems.at[pl.ds(start, len(pairs))])
    for send in sends:
        send.wait()


def interpolation(small):
    channels = small.shape[1]
    index = lax.broadcasted_iota(jnp.int32, (LANES, channels), 0)
    knot = ((index & 63) >> 3).astype(jnp.float32)
    basis = jnp.zeros((LANES, channels), jnp.float32)
    for step in range(3):
        basis = basis + jnp.where(knot == small[3:4, :] + float(step), small[step : step + 1, :], 0.0)
    high = basis.astype(jnp.bfloat16).astype(jnp.float32)
    part = index & 7
    return [
        (
            jnp.where(part == j, high, 0.0).astype(jnp.bfloat16),
            jnp.where(part == j, basis - high, 0.0).astype(jnp.bfloat16),
        )
        for j in range(8)
    ]


def collect_kernel(at, depth, *rest):
    blocks, (out_ref, sems) = rest[:-2], rest[-2:]
    moves = start_all(
        [
            (block.at[pl.ds(at, depth)], out_ref.at[pl.ds(i * depth, depth)])
            for i, block in enumerate(blocks)
        ],
        sems,
    )
    for move in moves:
        move.wait()


def list_rows(owner, slot, target, capacity):
    senders = owner.shape[0]
    mine = owner == target
    counted = mine.astype(jnp.float32)
    before = lax.broadcasted_iota(jnp.int32, (LANES, LANES), 0) < lax.broadcasted_iota(
        jnp.int32, (LANES, LANES), 1
    )
    rank = jnp.dot(
        counted.astype(jnp.bfloat16),
        before.astype(jnp.float32).astype(jnp.bfloat16),
        preferred_element_type=jnp.float32,
    )
    lane = lax.broadcasted_iota(jnp.int32, (senders, LANES), 1)
    count = jnp.sum(counted, axis=1, keepdims=True)
    listing = jnp.where(lane == capacity, count, 0.0)
    for k in range(capacity):
        here = jnp.logical_and(mine, rank == float(k))
        kth = jnp.sum(jnp.where(here, slot, 0.0), axis=1, keepdims=True)
        listing = jnp.where(lane == k, kth, listing)
    return listing.astype(jnp.int32), mine


def add_rows(acc_ref, slots_s, line, capacity, rows_ref):
    chunks = acc_ref.shape[0]

    def add(k, carry):
        b = slots_s[line, k]
        for c in range(chunks):
            acc_ref[c, b] += rows_ref[chunks * k + c].astype(jnp.float32)
        return carry

    lax.fori_loop(0, slots_s[line, capacity], add, 0)


def add_table(table_ref, x, block, at, depth):
    gain_tiles = (depth - 1) // 2
    for i in range(gain_tiles):
        table_ref[x, i * SUB : (i + 1) * SUB, :] = block[at + i].astype(jnp.float32) + block[
            at + gain_tiles + i
        ].astype(jnp.float32)
    return block[at + 2 * gain_tiles].astype(jnp.float32)


def count_rows(hits, mine, slot):
    which = lax.broadcasted_iota(jnp.int32, hits.shape, 0).astype(jnp.float32)
    slot = jnp.where(mine, slot, -1.0)
    for x in range(slot.shape[0]):
        hits = hits + (slot[x : x + 1, :] == which).astype(jnp.float32)
    return hits


def middle_kernel(capacity, near, stations, order, turn_s, me_s, small_ref, *rest):
    arrived, passed = dict(zip(order, rest)), rest[len(order) : -13]
    gains_ref, recip_ref, slots_ref, sums_ref = rest[-13:-9]
    table_ref, pick_ref, owner_ref, slot_ref, slots_v, slots_s, pairs_v, pairs_s, sems = rest[-9:]
    devices = table_ref.shape[0]
    owned = recip_ref.shape[0]
    chunks = sums_ref.shape[0]
    half = stations // 2
    depth = 2 * (table_ref.shape[1] // SUB) + 1
    small = small_ref[...]
    pairs_v[...] = small[0:SUB, 0:LANES].astype(jnp.int32)
    scalars = [pltpu.make_async_copy(pairs_v, pairs_s, sems.at[0])]
    scalars[0].start()
    for x in range(devices):
        if near == 1:
            code = add_table(table_ref, x, arrived[0].at[x], 0, depth)
        elif x in with_gains(near):
            code = add_table(table_ref, x, arrived[x], chunks * capacity, depth)
        else:
            code = add_table(table_ref, x, passed[0], (x - near) // 2 * depth, depth)
        owner_ref[x : x + 1, :] = code[0:1, :]
        slot_ref[x : x + 1, :] = code[1:2, :]
    slot = slot_ref[...]
    listing, mine = list_rows(owner_ref[...], slot, me_s[0].astype(jnp.float32), capacity)
    slots_ref[...] = listing
    slots_v[...] = listing
    scalars.append(pltpu.make_async_copy(slots_v, slots_s, sems.at[1]))
    scalars[1].start()
    hits = count_rows(jnp.zeros((owned, LANES), jnp.float32), mine, slot)
    tally = jnp.sum(hits, axis=1, keepdims=True)
    recip_ref[...] = jnp.broadcast_to(1.0 / jnp.maximum(tally, 1.0), recip_ref.shape)

    scalars[0].wait()
    turn = turn_s[0]
    column = lax.broadcasted_iota(jnp.int32, (1, LANES), 1)
    used = (column & 63) < USED
    upper = column >> 6

    def pick(b, carry):
        for side in range(2):
            s = pairs_s[4 + side, b]
            d = s // stations
            within = s - d * stations
            second = jnp.where(within >= half, 1, 0)
            row = table_ref[d ^ turn, pl.ds(within - second * half, 1), :]
            keep = jnp.logical_and(used, upper == second)
            pick_ref[pl.ds(side * owned + b, 1), :] = jnp.where(keep, row, 0.0)
        return carry

    lax.fori_loop(0, owned, pick, 0, unroll=8)
    both = pick_ref[...]
    both_high = both.astype(jnp.bfloat16)
    both_low = (both - both_high.astype(jnp.float32)).astype(jnp.bfloat16)
    both_two = jnp.concatenate([both_high, both_low], axis=1)
    for j, (high, low) in enumerate(interpolation(small)):
        fine = jnp.dot(
            both_two, jnp.concatenate([high, high], axis=0), preferred_element_type=jnp.float32
        ) + jnp.dot(both_high, low, preferred_element_type=jnp.float32)
        gains_ref[j] = fine.astype(jnp.bfloat16).astype(jnp.float32)

    sums_ref[...] = jnp.zeros_like(sums_ref)
    scalars[1].wait()
    if near > 1:
        for x in order:
            add_rows(sums_ref, slots_s, x, capacity, arrived[x])


def finish_kernel(capacity, late, slots_s, gains_ref, recip_ref, sums_ref, *rest):
    far = rest[: len(late)]
    out_hbm, acc_ref, res_ref, out_ref, sems = rest[len(late) :]
    owned, parts, channels = out_hbm.shape
    chunks = channels // LANES
    acc_ref[...] = sums_ref[...]
    if len(late) > 1:
        for x, rows_ref in zip(late, far):
            add_rows(acc_ref, slots_s, x, capacity, rows_ref)
    else:

        def from_device(d, carry):
            add_rows(acc_ref, slots_s, d, capacity, far[0].at[d])
            return carry

        lax.fori_loop(0, far[0].shape[0], from_device, 0)

    flat = acc_ref.reshape(chunks * owned * parts, LANES)
    done = res_ref.reshape(chunks * owned * parts, LANES)
    sends = []
    for c in range(chunks):
        cols = slice(c * LANES, (c + 1) * LANES)
        for b0 in range(0, owned, SUB):
            scale = recip_ref[b0 : b0 + SUB, :]
            row = (c * owned + b0) * parts
            vis = [flat[pl.ds(row + j, SUB, stride=parts), :] for j in range(parts)]
            lhs = [gains_ref[j, b0 : b0 + SUB, cols] for j in range(parts)]
            rhs = [gains_ref[j, owned + b0 : owned + b0 + SUB, cols] for j in range(parts)]
            mid_re, mid_im = [], []
            for row_a in range(2):
                for col_b in range(2):
                    re = im = 0.0
                    for inner in range(2):
                        lr, li = lhs[2 * row_a + inner], lhs[4 + 2 * row_a + inner]
                        vr, vi = vis[2 * inner + col_b], vis[4 + 2 * inner + col_b]
                        re = re + lr * vr - li * vi
                        im = im + lr * vi + li * vr
                    mid_re.append(re * scale)
                    mid_im.append(im * scale)
            for row_a in range(2):
                for col_b in range(2):
                    re = im = 0.0
                    for inner in range(2):
                        mr, mi = mid_re[2 * row_a + inner], mid_im[2 * row_a + inner]
                        rr, ri = rhs[2 * col_b + inner], rhs[4 + 2 * col_b + inner]
                        re = re + mr * rr + mi * ri
                        im = im + mi * rr - mr * ri
                    j = 2 * row_a + col_b
                    done[pl.ds(row + j, SUB, stride=parts), :] = re
                    done[pl.ds(row + 4 + j, SUB, stride=parts), :] = im
        out_ref[c] = res_ref[c].astype(out_ref.dtype)
        sends.append(
            pltpu.make_async_copy(
                out_ref.at[c], out_hbm.at[:, :, pl.ds(c * LANES, LANES)], sems.at[c]
            )
        )
        sends[-1].start()
    for send in sends:
        send.wait()


def on_device(
    visibilities,
    row_owner,
    row_slot,
    baseline_station_pairs,
    gains_coarse,
    band_weights,
    band_offset,
):
    devices = lax.axis_size("bl")
    rows, parts, channels = visibilities.shape
    capacity = 2 * rows // devices
    owned = baseline_station_pairs.shape[0]
    stations, _, knots = gains_coarse.shape
    chunks = channels // LANES
    gain_tiles = round_up(stations // 2, SUB) // SUB
    depth = 2 * gain_tiles + 1
    near = devices // 2 if devices <= 16 else 1
    halves = near > 1
    f32, bf16, i32 = jnp.float32, jnp.bfloat16, jnp.int32
    vmem = pl.BlockSpec(memory_space=pltpu.VMEM)
    smem = pl.BlockSpec(memory_space=pltpu.SMEM)
    hbm = pl.BlockSpec(memory_space=pltpu.HBM)
    anywhere = pl.BlockSpec(memory_space=pl.ANY)
    most = pltpu.CompilerParams(vmem_limit_bytes=ALL_VMEM)
    some = pltpu.CompilerParams(vmem_limit_bytes=SOME_VMEM)
    shape = jax.ShapeDtypeStruct
    dma = pltpu.SemaphoreType.DMA

    me = lax.axis_index("bl").astype(i32).reshape(1)
    turn = me if halves else jnp.zeros_like(me)
    owner = row_owner.reshape(rows)
    coarse = gains_coarse.transpose(2, 1, 0).reshape(knots * parts, stations)
    block = (chunks * capacity, parts, LANES)
    rows_at = chunks * capacity
    if halves:
        long = with_gains(near) + [near + 3]
        outs = [
            shape((rows_at + (depth if x in long else 0), parts, LANES), bf16)
            for x in range(devices)
        ]
    else:
        outs = [shape((devices,) + block, bf16), shape((depth, SUB, LANES), bf16)]
    outs += [shape((SUB, channels), f32)]
    pairs = baseline_station_pairs.T
    weights = band_weights.T
    offset = band_offset.reshape(chunks, LANES)
    sent = pl.pallas_call(
        functools.partial(pack_kernel, capacity, near),
        out_shape=outs,
        in_specs=[smem] + [hbm] * 8,
        out_specs=[hbm] * len(outs),
        scratch_shapes=[
            pltpu.VMEM(weights.shape, f32),
            pltpu.VMEM(offset.shape, i32),
            pltpu.VMEM(pairs.shape, i32),
            pltpu.VMEM((SUB, channels), f32),
            pltpu.SMEM((rows,), i32),
            pltpu.SMEM((rows,), i32),
            pltpu.SMEM((devices,), i32),
            pltpu.VMEM((1, rows), i32),
            pltpu.VMEM((1, rows), i32),
            pltpu.VMEM((rows, parts, channels), bf16),
            pltpu.VMEM((knots * parts, stations), f32),
            pltpu.VMEM((LANES, LANES), f32),
            pltpu.VMEM((depth, SUB, LANES), bf16),
            pltpu.VMEM((devices,) + block, bf16),
            dma((9 + PARTS + 2 * devices,)),
        ],
        compiler_params=most,
        name="pack_rows",
    )(
        turn,
        owner,
        row_owner.reshape(1, rows),
        row_slot.reshape(1, rows),
        visibilities,
        coarse,
        weights,
        offset,
        pairs,
    )


    def swap(array, x):
        return lax.ppermute(array, "bl", [(d, d ^ x) for d in range(devices)])

    if halves:
        arrived = {x: swap(sent[x], x) if x else sent[x] for x in range(devices)}
        order, late = schedule(near)
        even = list(range(near, devices, 2))
        collected = pl.pallas_call(
            functools.partial(collect_kernel, rows_at, depth),
            out_shape=shape((len(even) * depth, parts, LANES), bf16),
            in_specs=[anywhere] * len(even),
            out_specs=vmem,
            scratch_shapes=[dma((len(even),))],
            compiler_params=some,
            name="collect_gains",
        )(*[arrived[x] for x in even])
        passed = [swap(collected, 1)]
    else:
        arrived = {
            0: lax.all_gather(sent[1], "bl", axis=0),
            1: lax.all_to_all(sent[0], "bl", split_axis=0, concat_axis=0, tiled=True),
        }
        order, late, passed = [0], [1], []

    gains, recip, slots, sums = pl.pallas_call(
        functools.partial(middle_kernel, capacity, near, stations, order),
        out_shape=(
            shape((parts, 2 * owned, channels), f32),
            shape((owned, LANES), f32),
            shape((devices, LANES), i32),
            shape((chunks, owned, parts, LANES), f32),
        ),
        in_specs=[smem] * 2 + [vmem] * (1 + len(order) + len(passed)),
        out_specs=(vmem,) * 4,
        scratch_shapes=[
            pltpu.VMEM((devices, gain_tiles * SUB, LANES), f32),
            pltpu.VMEM((2 * owned, LANES), f32),
            pltpu.VMEM((devices, LANES), f32),
            pltpu.VMEM((devices, LANES), f32),
            pltpu.VMEM((devices, LANES), i32),
            pltpu.SMEM((devices, LANES), i32),
            pltpu.VMEM((SUB, LANES), i32),
            pltpu.SMEM((SUB, LANES), i32),
            dma((2,)),
        ],
        compiler_params=some,
        name="gains_and_sums",
    )(turn, me, sent[-1], *[arrived[x] for x in order], *passed)
    return pl.pallas_call(
        functools.partial(finish_kernel, capacity, late),
        out_shape=shape((owned, parts, channels), bf16),
        in_specs=[smem] + [vmem] * (3 + len(late)),
        out_specs=hbm,
        scratch_shapes=[
            pltpu.VMEM((chunks, owned, parts, LANES), f32),
            pltpu.VMEM((chunks, owned, parts, LANES), f32),
            pltpu.VMEM((chunks, owned, parts, LANES), bf16),
            dma((chunks,)),
        ],
        compiler_params=some,
        name="sum_and_apply",
    )(slots, gains, recip, sums, *[arrived[x] for x in late])


def solution(mesh):
    placed = (
        P(("groups", "bl"), None, None),
        P(("groups", "bl"), None),
        P(("groups", "bl")),
        P("bl", None),
        P(("groups", "bl"), None, None),
        P("groups", None),
        P("groups"),
    )
    return jax.shard_map(
        on_device,
        mesh=mesh,
        in_specs=placed,
        out_specs=P(("groups", "bl"), None, None),
        check_vma=False,
    )
```

```python
import functools

import jax
import jax.numpy as jnp
from jax import lax
from jax.experimental import pallas as pl
from jax.experimental.pallas import tpu as pltpu
from jax.sharding import PartitionSpec as P

LANES = 128
SUB = 8
USED = 48
PARTS = 4
ALL_VMEM = 60 * 1024 * 1024
SOME_VMEM = 24 * 1024 * 1024


def round_up(value, unit):
    return -(-value // unit) * unit


def schedule(near):
    even, odd = list(range(near, 2 * near, 2)), list(range(near + 1, 2 * near, 2))
    close = list(range(near // 2, near)) + list(range(1, near // 2))
    order = [0] + even[:2] + close[:2]
    cross, close = even[2:], close[2:]
    while cross:
        order += cross[:1] + close[:1]
        cross, close = cross[1:], close[1:]
    return order + close + odd[:1], odd[1:]


def with_gains(near):
    return list(range(near)) + list(range(near, 2 * near, 2))


def start_all(pairs, sems):
    moves = [pltpu.make_async_copy(src, dst, sems.at[i]) for i, (src, dst) in enumerate(pairs)]
    for move in moves:
        move.start()
    return moves


def pack_kernel(
    capacity,
    near,
    targets,
    me_s,
    owner_hbm,
    owner_row_hbm,
    slot_row_hbm,
    vis_hbm,
    coarse_hbm,
    weights_hbm,
    offset_hbm,
    pairs_hbm,
    *rest,
):
    outs = rest[:-15]
    (
        weights_ref,
        offset_ref,
        pairs_ref,
        small_ref,
        owner_s,
        place_s,
        count_s,
        owner_ref,
        slot_ref,
        vis_ref,
        coarse_ref,
        turn_ref,
        meta_ref,
        block_ref,
        sems,
    ) = rest[-15:]
    rows = vis_ref.shape[0]
    chunks = vis_ref.shape[2] // LANES
    devices = block_ref.shape[0]
    terms, stations = coarse_ref.shape
    half = stations // 2
    depth = meta_ref.shape[0]
    gain_tiles = (depth - 1) // 2
    span = rows // PARTS
    moves = start_all(
        (
            (owner_hbm, owner_s),
            (coarse_hbm, coarse_ref),
            (owner_row_hbm, owner_ref),
            (slot_row_hbm, slot_ref),
            (weights_hbm, weights_ref),
            (offset_hbm, offset_ref),
            (pairs_hbm, pairs_ref),
        ),
        sems,
    )
    fetches = start_all(
        [
            (vis_hbm.at[pl.ds(i * span, span)], vis_ref.at[pl.ds(i * span, span)])
            for i in range(PARTS)
        ],
        sems.at[pl.ds(len(moves), PARTS)],
    )
    turn_ref[...] = jnp.zeros_like(turn_ref)
    for d in range(devices):
        count_s[d] = 0
    me = me_s[0]
    moves[0].wait()

    def rank(r, carry):
        x = owner_s[r] ^ me
        k = count_s[x]
        count_s[x] = k + 1
        place_s[r] = x * capacity + k
        return carry

    lax.fori_loop(0, rows, rank, 0, unroll=8)
    for move in moves[1:]:
        move.wait()

    turn_ref[0:terms, 0:half] = coarse_ref[:, 0:half]
    turn_ref[64 : 64 + terms, 0:half] = coarse_ref[:, half:stations]
    gains = turn_ref[...].T
    high = gains.astype(jnp.bfloat16)
    low = (gains - high.astype(jnp.float32)).astype(jnp.bfloat16)
    for i in range(gain_tiles):
        meta_ref[i] = high[i * SUB : (i + 1) * SUB, :]
        meta_ref[gain_tiles + i] = low[i * SUB : (i + 1) * SUB, :]
    sub = lax.broadcasted_iota(jnp.int32, (SUB, LANES), 0)
    codes = jnp.where(sub == 0, owner_ref[...], slot_ref[...])
    meta_ref[2 * gain_tiles] = codes.astype(jnp.float32).astype(jnp.bfloat16)
    steps = weights_ref.shape[0]
    small_ref[...] = jnp.zeros_like(small_ref)
    small_ref[0:steps, :] = weights_ref[...]
    for c in range(chunks):
        lanes = slice(c * LANES, (c + 1) * LANES)
        small_ref[steps : steps + 1, lanes] = offset_ref[c : c + 1, :].astype(jnp.float32)
    small_ref[4:6, 0 : pairs_ref.shape[1]] = pairs_ref[...].astype(jnp.float32)

    at = chunks * capacity
    if near > 1:
        pairs = [
            (meta_ref, out.at[pl.ds(at, depth)])
            for x, out in zip(targets, outs)
            if x in with_gains(near)
        ]
    else:
        pairs = [(meta_ref, outs[1])]
    if len(outs) > len(targets):
        pairs += [(small_ref, outs[-1])]
    start = len(moves) + PARTS
    sends = start_all(pairs, sems.at[pl.ds(start, len(pairs))])
    start += len(pairs)

    def place(r, carry):
        p = place_s[r]
        for c in range(chunks):
            flat_ref[p * chunks + c] = vis_ref[r, :, c * LANES : (c + 1) * LANES]
        return carry

    flat_ref = block_ref.reshape(devices * at, SUB, LANES)
    for i in range(PARTS):
        fetches[i].wait()
        lax.fori_loop(i * span, (i + 1) * span, place, 0, unroll=8)
    if near > 1:
        pairs = [(block_ref.at[x], out.at[pl.ds(0, at)]) for x, out in zip(targets, outs)]
    else:
        pairs = [(block_ref, outs[0])]
    sends += start_all(pairs, sems.at[pl.ds(start, len(pairs))])
    for send in sends:
        send.wait()


def interpolation(small):
    channels = small.shape[1]
    index = lax.broadcasted_iota(jnp.int32, (LANES, channels), 0)
    knot = ((index & 63) >> 3).astype(jnp.float32)
    basis = jnp.zeros((LANES, channels), jnp.float32)
    for step in range(3):
        basis = basis + jnp.where(knot == small[3:4, :] + float(step), small[step : step + 1, :], 0.0)
    high = basis.astype(jnp.bfloat16).astype(jnp.float32)
    part = index & 7
    return [
        (
            jnp.where(part == j, high, 0.0).astype(jnp.bfloat16),
            jnp.where(part == j, basis - high, 0.0).astype(jnp.bfloat16),
        )
        for j in range(8)
    ]


def collect_kernel(at, depth, *rest):
    blocks, (out_ref, sems) = rest[:-2], rest[-2:]
    moves = start_all(
        [
            (block.at[pl.ds(at, depth)], out_ref.at[pl.ds(i * depth, depth)])
            for i, block in enumerate(blocks)
        ],
        sems,
    )
    for move in moves:
        move.wait()


def list_rows(owner, slot, target, capacity):
    senders = owner.shape[0]
    mine = owner == target
    counted = mine.astype(jnp.float32)
    before = lax.broadcasted_iota(jnp.int32, (LANES, LANES), 0) < lax.broadcasted_iota(
        jnp.int32, (LANES, LANES), 1
    )
    rank = jnp.dot(
        counted.astype(jnp.bfloat16),
        before.astype(jnp.float32).astype(jnp.bfloat16),
        preferred_element_type=jnp.float32,
    )
    lane = lax.broadcasted_iota(jnp.int32, (senders, LANES), 1)
    count = jnp.sum(counted, axis=1, keepdims=True)
    listing = jnp.where(lane == capacity, count, 0.0)
    for k in range(capacity):
        here = jnp.logical_and(mine, rank == float(k))
        kth = jnp.sum(jnp.where(here, slot, 0.0), axis=1, keepdims=True)
        listing = jnp.where(lane == k, kth, listing)
    return listing.astype(jnp.int32), mine


def add_rows(acc_ref, slots_s, line, capacity, rows_ref):
    chunks = acc_ref.shape[0]

    def add(k, carry):
        b = slots_s[line, k]
        for c in range(chunks):
            acc_ref[c, b] += rows_ref[chunks * k + c].astype(jnp.float32)
        return carry

    lax.fori_loop(0, slots_s[line, capacity], add, 0)


def add_table(table_ref, x, block, at, depth):
    gain_tiles = (depth - 1) // 2
    for i in range(gain_tiles):
        table_ref[x, i * SUB : (i + 1) * SUB, :] = block[at + i].astype(jnp.float32) + block[
            at + gain_tiles + i
        ].astype(jnp.float32)
    return block[at + 2 * gain_tiles].astype(jnp.float32)


def count_rows(hits, mine, slot):
    which = lax.broadcasted_iota(jnp.int32, hits.shape, 0).astype(jnp.float32)
    slot = jnp.where(mine, slot, -1.0)
    for x in range(slot.shape[0]):
        hits = hits + (slot[x : x + 1, :] == which).astype(jnp.float32)
    return hits


def middle_kernel(capacity, near, stations, order, turn_s, me_s, small_ref, *rest):
    arrived, passed = dict(zip(order, rest)), rest[len(order) : -13]
    gains_ref, recip_ref, slots_ref, sums_ref = rest[-13:-9]
    table_ref, pick_ref, owner_ref, slot_ref, slots_v, slots_s, pairs_v, pairs_s, sems = rest[-9:]
    devices = table_ref.shape[0]
    owned = recip_ref.shape[0]
    chunks = sums_ref.shape[0]
    half = stations // 2
    depth = 2 * (table_ref.shape[1] // SUB) + 1
    small = small_ref[...]
    pairs_v[...] = small[0:SUB, 0:LANES].astype(jnp.int32)
    scalars = [pltpu.make_async_copy(pairs_v, pairs_s, sems.at[0])]
    scalars[0].start()
    for x in range(devices):
        if near == 1:
            code = add_table(table_ref, x, arrived[0].at[x], 0, depth)
        elif x in with_gains(near):
            code = add_table(table_ref, x, arrived[x], chunks * capacity, depth)
        else:
            code = add_table(table_ref, x, passed[0], (x - near) // 2 * depth, depth)
        owner_ref[x : x + 1, :] = code[0:1, :]
        slot_ref[x : x + 1, :] = code[1:2, :]
    slot = slot_ref[...]
    listing, mine = list_rows(owner_ref[...], slot, me_s[0].astype(jnp.float32), capacity)
    slots_ref[...] = listing
    slots_v[...] = listing
    scalars.append(pltpu.make_async_copy(slots_v, slots_s, sems.at[1]))
    scalars[1].start()
    hits = count_rows(jnp.zeros((owned, LANES), jnp.float32), mine, slot)
    tally = jnp.sum(hits, axis=1, keepdims=True)
    recip_ref[...] = jnp.broadcast_to(1.0 / jnp.maximum(tally, 1.0), recip_ref.shape)

    scalars[0].wait()
    turn = turn_s[0]
    column = lax.broadcasted_iota(jnp.int32, (1, LANES), 1)
    used = (column & 63) < USED
    upper = column >> 6

    def pick(b, carry):
        for side in range(2):
            s = pairs_s[4 + side, b]
            d = s // stations
            within = s - d * stations
            second = jnp.where(within >= half, 1, 0)
            row = table_ref[d ^ turn, pl.ds(within - second * half, 1), :]
            keep = jnp.logical_and(used, upper == second)
            pick_ref[pl.ds(side * owned + b, 1), :] = jnp.where(keep, row, 0.0)
        return carry

    lax.fori_loop(0, owned, pick, 0, unroll=8)
    both = pick_ref[...]
    both_high = both.astype(jnp.bfloat16)
    both_low = (both - both_high.astype(jnp.float32)).astype(jnp.bfloat16)
    both_two = jnp.concatenate([both_high, both_low], axis=1)
    for j, (high, low) in enumerate(interpolation(small)):
        fine = jnp.dot(
            both_two, jnp.concatenate([high, high], axis=0), preferred_element_type=jnp.float32
        ) + jnp.dot(both_high, low, preferred_element_type=jnp.float32)
        gains_ref[j] = fine.astype(jnp.bfloat16).astype(jnp.float32)

    sums_ref[...] = jnp.zeros_like(sums_ref)
    scalars[1].wait()
    if near > 1:
        for x in order:
            add_rows(sums_ref, slots_s, x, capacity, arrived[x])


def finish_kernel(capacity, late, slots_s, gains_ref, recip_ref, sums_ref, *rest):
    far = rest[: len(late)]
    out_hbm, acc_ref, res_ref, out_ref, sems = rest[len(late) :]
    owned, parts, channels = out_hbm.shape
    chunks = channels // LANES
    acc_ref[...] = sums_ref[...]
    if len(late) > 1:
        for x, rows_ref in zip(late, far):
            add_rows(acc_ref, slots_s, x, capacity, rows_ref)
    else:

        def from_device(d, carry):
            add_rows(acc_ref, slots_s, d, capacity, far[0].at[d])
            return carry

        lax.fori_loop(0, far[0].shape[0], from_device, 0)

    flat = acc_ref.reshape(chunks * owned * parts, LANES)
    done = res_ref.reshape(chunks * owned * parts, LANES)
    sends = []
    for c in range(chunks):
        cols = slice(c * LANES, (c + 1) * LANES)
        for b0 in range(0, owned, SUB):
            scale = recip_ref[b0 : b0 + SUB, :]
            row = (c * owned + b0) * parts
            vis = [flat[pl.ds(row + j, SUB, stride=parts), :] for j in range(parts)]
            lhs = [gains_ref[j, b0 : b0 + SUB, cols] for j in range(parts)]
            rhs = [gains_ref[j, owned + b0 : owned + b0 + SUB, cols] for j in range(parts)]
            mid_re, mid_im = [], []
            for row_a in range(2):
                for col_b in range(2):
                    re = im = 0.0
                    for inner in range(2):
                        lr, li = lhs[2 * row_a + inner], lhs[4 + 2 * row_a + inner]
                        vr, vi = vis[2 * inner + col_b], vis[4 + 2 * inner + col_b]
                        re = re + lr * vr - li * vi
                        im = im + lr * vi + li * vr
                    mid_re.append(re * scale)
                    mid_im.append(im * scale)
            for row_a in range(2):
                for col_b in range(2):
                    re = im = 0.0
                    for inner in range(2):
                        mr, mi = mid_re[2 * row_a + inner], mid_im[2 * row_a + inner]
                        rr, ri = rhs[2 * col_b + inner], rhs[4 + 2 * col_b + inner]
                        re = re + mr * rr + mi * ri
                        im = im + mi * rr - mr * ri
                    j = 2 * row_a + col_b
                    done[pl.ds(row + j, SUB, stride=parts), :] = re
                    done[pl.ds(row + 4 + j, SUB, stride=parts), :] = im
        out_ref[c] = res_ref[c].astype(out_ref.dtype)
        sends.append(
            pltpu.make_async_copy(
                out_ref.at[c], out_hbm.at[:, :, pl.ds(c * LANES, LANES)], sems.at[c]
            )
        )
        sends[-1].start()
    for send in sends:
        send.wait()


def on_device(
    visibilities,
    row_owner,
    row_slot,
    baseline_station_pairs,
    gains_coarse,
    band_weights,
    band_offset,
):
    devices = lax.axis_size("bl")
    rows, parts, channels = visibilities.shape
    capacity = 2 * rows // devices
    owned = baseline_station_pairs.shape[0]
    stations, _, knots = gains_coarse.shape
    chunks = channels // LANES
    gain_tiles = round_up(stations // 2, SUB) // SUB
    depth = 2 * gain_tiles + 1
    near = devices // 2 if devices <= 16 else 1
    halves = near > 1
    f32, bf16, i32 = jnp.float32, jnp.bfloat16, jnp.int32
    vmem = pl.BlockSpec(memory_space=pltpu.VMEM)
    smem = pl.BlockSpec(memory_space=pltpu.SMEM)
    hbm = pl.BlockSpec(memory_space=pltpu.HBM)
    anywhere = pl.BlockSpec(memory_space=pl.ANY)
    most = pltpu.CompilerParams(vmem_limit_bytes=ALL_VMEM)
    some = pltpu.CompilerParams(vmem_limit_bytes=SOME_VMEM)
    shape = jax.ShapeDtypeStruct
    dma = pltpu.SemaphoreType.DMA

    me = lax.axis_index("bl").astype(i32).reshape(1)
    turn = me if halves else jnp.zeros_like(me)
    owner = row_owner.reshape(rows)
    coarse = gains_coarse.transpose(2, 1, 0).reshape(knots * parts, stations)
    block = (chunks * capacity, parts, LANES)
    rows_at = chunks * capacity
    def pack(targets, outs):
        return pl.pallas_call(
            functools.partial(pack_kernel, capacity, near, targets),
            out_shape=outs,
            in_specs=[smem] + [hbm] * 8,
            out_specs=[hbm] * len(outs),
            scratch_shapes=[
                pltpu.VMEM(weights.shape, f32),
                pltpu.VMEM(offset.shape, i32),
                pltpu.VMEM(pairs.shape, i32),
                pltpu.VMEM((SUB, channels), f32),
                pltpu.SMEM((rows,), i32),
                pltpu.SMEM((rows,), i32),
                pltpu.SMEM((devices,), i32),
                pltpu.VMEM((1, rows), i32),
                pltpu.VMEM((1, rows), i32),
                pltpu.VMEM((rows, parts, channels), bf16),
                pltpu.VMEM((knots * parts, stations), f32),
                pltpu.VMEM((LANES, LANES), f32),
                pltpu.VMEM((depth, SUB, LANES), bf16),
                pltpu.VMEM((devices,) + block, bf16),
                dma((9 + PARTS + 2 * devices,)),
            ],
            compiler_params=most,
            name="pack_rows",
        )(
            turn,
            owner,
            row_owner.reshape(1, rows),
            row_slot.reshape(1, rows),
            visibilities,
            coarse,
            weights,
            offset,
            pairs,
        )

    pairs = baseline_station_pairs.T
    weights = band_weights.T
    offset = band_offset.reshape(chunks, LANES)
    small = shape((SUB, channels), f32)
    if halves:
        length = {x: rows_at + (depth if x in with_gains(near) else 0) for x in range(devices)}
        ahead = [near, near + 1, near + 2]
        behind = [x for x in range(devices) if x not in ahead]
        sent = dict(zip(ahead, pack(ahead, [shape((length[x], parts, LANES), bf16) for x in ahead])))
        *others, small = pack(
            behind, [shape((length[x], parts, LANES), bf16) for x in behind] + [small]
        )
        sent.update(zip(behind, others))
    else:
        outs = [shape((devices,) + block, bf16), shape((depth, SUB, LANES), bf16)]
        *sent, small = pack([0, 1], outs + [small])

    def swap(array, x):
        return lax.ppermute(array, "bl", [(d, d ^ x) for d in range(devices)])

    if halves:
        arrived = {x: swap(sent[x], x) if x else sent[x] for x in range(devices)}
        order, late = schedule(near)
        even = list(range(near, devices, 2))
        collected = pl.pallas_call(
            functools.partial(collect_kernel, rows_at, depth),
            out_shape=shape((len(even) * depth, parts, LANES), bf16),
            in_specs=[anywhere] * len(even),
            out_specs=vmem,
            scratch_shapes=[dma((len(even),))],
            compiler_params=some,
            name="collect_gains",
        )(*[arrived[x] for x in even])
        passed = [swap(collected, 1)]
    else:
        arrived = {
            0: lax.all_gather(sent[1], "bl", axis=0),
            1: lax.all_to_all(sent[0], "bl", split_axis=0, concat_axis=0, tiled=True),
        }
        order, late, passed = [0], [1], []

    gains, recip, slots, sums = pl.pallas_call(
        functools.partial(middle_kernel, capacity, near, stations, order),
        out_shape=(
            shape((parts, 2 * owned, channels), f32),
            shape((owned, LANES), f32),
            shape((devices, LANES), i32),
            shape((chunks, owned, parts, LANES), f32),
        ),
        in_specs=[smem] * 2 + [vmem] * (1 + len(order) + len(passed)),
        out_specs=(vmem,) * 4,
        scratch_shapes=[
            pltpu.VMEM((devices, gain_tiles * SUB, LANES), f32),
            pltpu.VMEM((2 * owned, LANES), f32),
            pltpu.VMEM((devices, LANES), f32),
            pltpu.VMEM((devices, LANES), f32),
            pltpu.VMEM((devices, LANES), i32),
            pltpu.SMEM((devices, LANES), i32),
            pltpu.VMEM((SUB, LANES), i32),
            pltpu.SMEM((SUB, LANES), i32),
            dma((2,)),
        ],
        compiler_params=some,
        name="gains_and_sums",
    )(turn, me, small, *[arrived[x] for x in order], *passed)
    return pl.pallas_call(
        functools.partial(finish_kernel, capacity, late),
        out_shape=shape((owned, parts, channels), bf16),
        in_specs=[smem] + [vmem] * (3 + len(late)),
        out_specs=hbm,
        scratch_shapes=[
            pltpu.VMEM((chunks, owned, parts, LANES), f32),
            pltpu.VMEM((chunks, owned, parts, LANES), f32),
            pltpu.VMEM((chunks, owned, parts, LANES), bf16),
            dma((chunks,)),
        ],
        compiler_params=some,
        name="sum_and_apply",
    )(slots, gains, recip, sums, *[arrived[x] for x in late])


def solution(mesh):
    placed = (
        P(("groups", "bl"), None, None),
        P(("groups", "bl"), None),
        P(("groups", "bl")),
        P("bl", None),
        P(("groups", "bl"), None, None),
        P("groups", None),
        P("groups"),
    )
    return jax.shard_map(
        on_device,
        mesh=mesh,
        in_specs=placed,
        out_specs=P(("groups", "bl"), None, None),
        check_vma=False,
    )
```

```python
import functools

import jax
import jax.numpy as jnp
from jax import lax
from jax.experimental import pallas as pl
from jax.experimental.pallas import tpu as pltpu
from jax.sharding import PartitionSpec as P

LANES = 128
SUB = 8
USED = 48
PARTS = 4
ALL_VMEM = 60 * 1024 * 1024
SOME_VMEM = 24 * 1024 * 1024


def round_up(value, unit):
    return -(-value // unit) * unit


def schedule(near):
    even, odd = list(range(near, 2 * near, 2)), list(range(near + 1, 2 * near, 2))
    close = list(range(near // 2, near)) + list(range(1, near // 2))
    cross, late = even[2:] + odd[1:-2], odd[-2:]
    order = [0] + even[:2] + close[:2]
    close = close[2:]
    while cross:
        order += cross[:1] + close[:1]
        cross, close = cross[1:], close[1:]
    return order + close + odd[:1], late


def with_gains(near):
    return list(range(near)) + list(range(near, 2 * near, 2))


def start_all(pairs, sems):
    moves = [pltpu.make_async_copy(src, dst, sems.at[i]) for i, (src, dst) in enumerate(pairs)]
    for move in moves:
        move.start()
    return moves


def pack_kernel(
    capacity,
    near,
    me_s,
    owner_hbm,
    owner_row_hbm,
    slot_row_hbm,
    vis_hbm,
    coarse_hbm,
    weights_hbm,
    offset_hbm,
    pairs_hbm,
    *rest,
):
    outs = rest[:-15]
    (
        weights_ref,
        offset_ref,
        pairs_ref,
        small_ref,
        owner_s,
        place_s,
        count_s,
        owner_ref,
        slot_ref,
        vis_ref,
        coarse_ref,
        turn_ref,
        meta_ref,
        block_ref,
        sems,
    ) = rest[-15:]
    rows = vis_ref.shape[0]
    chunks = vis_ref.shape[2] // LANES
    devices = block_ref.shape[0]
    terms, stations = coarse_ref.shape
    half = stations // 2
    depth = meta_ref.shape[0]
    gain_tiles = (depth - 1) // 2
    span = rows // PARTS
    moves = start_all(
        (
            (owner_hbm, owner_s),
            (coarse_hbm, coarse_ref),
            (owner_row_hbm, owner_ref),
            (slot_row_hbm, slot_ref),
            (weights_hbm, weights_ref),
            (offset_hbm, offset_ref),
            (pairs_hbm, pairs_ref),
        ),
        sems,
    )
    fetches = start_all(
        [
            (vis_hbm.at[pl.ds(i * span, span)], vis_ref.at[pl.ds(i * span, span)])
            for i in range(PARTS)
        ],
        sems.at[pl.ds(len(moves), PARTS)],
    )
    turn_ref[...] = jnp.zeros_like(turn_ref)
    for d in range(devices):
        count_s[d] = 0
    me = me_s[0]
    moves[0].wait()

    def rank(r, carry):
        x = owner_s[r] ^ me
        k = count_s[x]
        count_s[x] = k + 1
        place_s[r] = x * capacity + k
        return carry

    lax.fori_loop(0, rows, rank, 0, unroll=8)
    for move in moves[1:]:
        move.wait()

    turn_ref[0:terms, 0:half] = coarse_ref[:, 0:half]
    turn_ref[64 : 64 + terms, 0:half] = coarse_ref[:, half:stations]
    gains = turn_ref[...].T
    high = gains.astype(jnp.bfloat16)
    low = (gains - high.astype(jnp.float32)).astype(jnp.bfloat16)
    for i in range(gain_tiles):
        meta_ref[i] = high[i * SUB : (i + 1) * SUB, :]
        meta_ref[gain_tiles + i] = low[i * SUB : (i + 1) * SUB, :]
    sub = lax.broadcasted_iota(jnp.int32, (SUB, LANES), 0)
    codes = jnp.where(sub == 0, owner_ref[...], slot_ref[...])
    meta_ref[2 * gain_tiles] = codes.astype(jnp.float32).astype(jnp.bfloat16)
    steps = weights_ref.shape[0]
    small_ref[...] = jnp.zeros_like(small_ref)
    small_ref[0:steps, :] = weights_ref[...]
    for c in range(chunks):
        lanes = slice(c * LANES, (c + 1) * LANES)
        small_ref[steps : steps + 1, lanes] = offset_ref[c : c + 1, :].astype(jnp.float32)
    small_ref[4:6, 0 : pairs_ref.shape[1]] = pairs_ref[...].astype(jnp.float32)

    at = chunks * capacity
    if near > 1:
        pairs = [(meta_ref, outs[x].at[pl.ds(at, depth)]) for x in with_gains(near)]
    else:
        pairs = [(meta_ref, outs[1])]
    pairs += [(small_ref, outs[-1])]
    start = len(moves) + PARTS
    sends = start_all(pairs, sems.at[pl.ds(start, len(pairs))])
    start += len(pairs)

    def place(r, carry):
        p = place_s[r]
        for c in range(chunks):
            flat_ref[p * chunks + c] = vis_ref[r, :, c * LANES : (c + 1) * LANES]
        return carry

    flat_ref = block_ref.reshape(devices * at, SUB, LANES)
    for i in range(PARTS):
        fetches[i].wait()
        lax.fori_loop(i * span, (i + 1) * span, place, 0, unroll=8)
    if near > 1:
        pairs = [(block_ref.at[x], outs[x].at[pl.ds(0, at)]) for x in range(devices)]
    else:
        pairs = [(block_ref, outs[0])]
    sends += start_all(pairs, sems.at[pl.ds(start, len(pairs))])
    for send in sends:
        send.wait()


def ready_kernel(small_ref, own_ref, held_ref, own_out_ref, held_out_ref, high_ref, low_ref, pairs_ref, sems):
    moves = start_all([(own_ref, own_out_ref), (held_ref, held_out_ref)], sems)
    small = small_ref[...]
    channels = small.shape[1]
    pairs_ref[...] = small[:, 0:LANES].astype(jnp.int32)
    index = lax.broadcasted_iota(jnp.int32, (LANES, channels), 0)
    knot = ((index & 63) >> 3).astype(jnp.float32)
    basis = jnp.zeros((LANES, channels), jnp.float32)
    for step in range(3):
        basis = basis + jnp.where(knot == small[3:4, :] + float(step), small[step : step + 1, :], 0.0)
    high = basis.astype(jnp.bfloat16).astype(jnp.float32)
    low = basis - high
    part = index & 7
    for j in range(8):
        high_ref[j] = jnp.where(part == j, high, 0.0).astype(jnp.bfloat16)
        low_ref[j] = jnp.where(part == j, low, 0.0).astype(jnp.bfloat16)
    for move in moves:
        move.wait()


def collect_kernel(at, depth, *rest):
    blocks, (out_ref, sems) = rest[:-2], rest[-2:]
    moves = start_all(
        [
            (block.at[pl.ds(at, depth)], out_ref.at[pl.ds(i * depth, depth)])
            for i, block in enumerate(blocks)
        ],
        sems,
    )
    for move in moves:
        move.wait()


def list_rows(owner, slot, target, capacity):
    senders = owner.shape[0]
    mine = owner == target
    counted = mine.astype(jnp.float32)
    before = lax.broadcasted_iota(jnp.int32, (LANES, LANES), 0) < lax.broadcasted_iota(
        jnp.int32, (LANES, LANES), 1
    )
    rank = jnp.dot(
        counted.astype(jnp.bfloat16),
        before.astype(jnp.float32).astype(jnp.bfloat16),
        preferred_element_type=jnp.float32,
    )
    lane = lax.broadcasted_iota(jnp.int32, (senders, LANES), 1)
    count = jnp.sum(counted, axis=1, keepdims=True)
    listing = jnp.where(lane == capacity, count, 0.0)
    for k in range(capacity):
        here = jnp.logical_and(mine, rank == float(k))
        kth = jnp.sum(jnp.where(here, slot, 0.0), axis=1, keepdims=True)
        listing = jnp.where(lane == k, kth, listing)
    return listing.astype(jnp.int32), mine


def add_rows(acc_ref, slots_s, line, capacity, rows_ref):
    chunks = acc_ref.shape[0]

    def add(k, carry):
        b = slots_s[line, k]
        for c in range(chunks):
            acc_ref[c, b] += rows_ref[chunks * k + c].astype(jnp.float32)
        return carry

    lax.fori_loop(0, slots_s[line, capacity], add, 0)


def add_table(table_ref, x, block, at, depth):
    gain_tiles = (depth - 1) // 2
    for i in range(gain_tiles):
        table_ref[x, i * SUB : (i + 1) * SUB, :] = block[at + i].astype(jnp.float32) + block[
            at + gain_tiles + i
        ].astype(jnp.float32)
    return block[at + 2 * gain_tiles].astype(jnp.float32)


def count_rows(hits, mine, slot):
    which = lax.broadcasted_iota(jnp.int32, hits.shape, 0).astype(jnp.float32)
    slot = jnp.where(mine, slot, -1.0)
    for x in range(slot.shape[0]):
        hits = hits + (slot[x : x + 1, :] == which).astype(jnp.float32)
    return hits


def middle_kernel(capacity, near, stations, order, turn_s, me_s, pairs_s, high_ref, low_ref, *rest):
    arrived, passed = dict(zip(order, rest)), rest[len(order) : -11]
    gains_ref, recip_ref, slots_ref, sums_ref = rest[-11:-7]
    table_ref, pick_ref, owner_ref, slot_ref, slots_v, slots_s, sem = rest[-7:]
    devices = table_ref.shape[0]
    owned = recip_ref.shape[0]
    chunks = sums_ref.shape[0]
    half = stations // 2
    depth = 2 * (table_ref.shape[1] // SUB) + 1
    for x in range(devices):
        if near == 1:
            code = add_table(table_ref, x, arrived[0].at[x], 0, depth)
        elif x in with_gains(near):
            code = add_table(table_ref, x, arrived[x], chunks * capacity, depth)
        else:
            code = add_table(table_ref, x, passed[0], (x - near) // 2 * depth, depth)
        owner_ref[x : x + 1, :] = code[0:1, :]
        slot_ref[x : x + 1, :] = code[1:2, :]
    slot = slot_ref[...]
    listing, mine = list_rows(owner_ref[...], slot, me_s[0].astype(jnp.float32), capacity)
    slots_ref[...] = listing
    slots_v[...] = listing
    move = pltpu.make_async_copy(slots_v, slots_s, sem)
    move.start()
    hits = count_rows(jnp.zeros((owned, LANES), jnp.float32), mine, slot)
    tally = jnp.sum(hits, axis=1, keepdims=True)
    recip_ref[...] = jnp.broadcast_to(1.0 / jnp.maximum(tally, 1.0), recip_ref.shape)

    turn = turn_s[0]
    column = lax.broadcasted_iota(jnp.int32, (1, LANES), 1)
    used = (column & 63) < USED
    upper = column >> 6

    def pick(b, carry):
        for side in range(2):
            s = pairs_s[4 + side, b]
            d = s // stations
            within = s - d * stations
            second = jnp.where(within >= half, 1, 0)
            row = table_ref[d ^ turn, pl.ds(within - second * half, 1), :]
            keep = jnp.logical_and(used, upper == second)
            pick_ref[pl.ds(side * owned + b, 1), :] = jnp.where(keep, row, 0.0)
        return carry

    lax.fori_loop(0, owned, pick, 0, unroll=8)
    both = pick_ref[...]
    both_high = both.astype(jnp.bfloat16)
    both_low = (both - both_high.astype(jnp.float32)).astype(jnp.bfloat16)
    both_two = jnp.concatenate([both_high, both_low], axis=1)
    for j in range(8):
        high, low = high_ref[j], low_ref[j]
        fine = jnp.dot(
            both_two, jnp.concatenate([high, high], axis=0), preferred_element_type=jnp.float32
        ) + jnp.dot(both_high, low, preferred_element_type=jnp.float32)
        gains_ref[j] = fine.astype(jnp.bfloat16).astype(jnp.float32)

    sums_ref[...] = jnp.zeros_like(sums_ref)
    move.wait()
    if near > 1:
        for x in order:
            add_rows(sums_ref, slots_s, x, capacity, arrived[x])


def finish_kernel(capacity, late, slots_s, gains_ref, recip_ref, sums_ref, *rest):
    far = rest[: len(late)]
    out_hbm, acc_ref, res_ref, out_ref, sems = rest[len(late) :]
    owned, parts, channels = out_hbm.shape
    chunks = channels // LANES
    acc_ref[...] = sums_ref[...]
    if len(late) > 1:
        for x, rows_ref in zip(late, far):
            add_rows(acc_ref, slots_s, x, capacity, rows_ref)
    else:

        def from_device(d, carry):
            add_rows(acc_ref, slots_s, d, capacity, far[0].at[d])
            return carry

        lax.fori_loop(0, far[0].shape[0], from_device, 0)

    flat = acc_ref.reshape(chunks * owned * parts, LANES)
    done = res_ref.reshape(chunks * owned * parts, LANES)
    sends = []
    for c in range(chunks):
        cols = slice(c * LANES, (c + 1) * LANES)
        for b0 in range(0, owned, SUB):
            scale = recip_ref[b0 : b0 + SUB, :]
            row = (c * owned + b0) * parts
            vis = [flat[pl.ds(row + j, SUB, stride=parts), :] for j in range(parts)]
            lhs = [gains_ref[j, b0 : b0 + SUB, cols] for j in range(parts)]
            rhs = [gains_ref[j, owned + b0 : owned + b0 + SUB, cols] for j in range(parts)]
            mid_re, mid_im = [], []
            for row_a in range(2):
                for col_b in range(2):
                    re = im = 0.0
                    for inner in range(2):
                        lr, li = lhs[2 * row_a + inner], lhs[4 + 2 * row_a + inner]
                        vr, vi = vis[2 * inner + col_b], vis[4 + 2 * inner + col_b]
                        re = re + lr * vr - li * vi
                        im = im + lr * vi + li * vr
                    mid_re.append(re * scale)
                    mid_im.append(im * scale)
            for row_a in range(2):
                for col_b in range(2):
                    re = im = 0.0
                    for inner in range(2):
                        mr, mi = mid_re[2 * row_a + inner], mid_im[2 * row_a + inner]
                        rr, ri = rhs[2 * col_b + inner], rhs[4 + 2 * col_b + inner]
                        re = re + mr * rr + mi * ri
                        im = im + mi * rr - mr * ri
                    j = 2 * row_a + col_b
                    done[pl.ds(row + j, SUB, stride=parts), :] = re
                    done[pl.ds(row + 4 + j, SUB, stride=parts), :] = im
        out_ref[c] = res_ref[c].astype(out_ref.dtype)
        sends.append(
            pltpu.make_async_copy(
                out_ref.at[c], out_hbm.at[:, :, pl.ds(c * LANES, LANES)], sems.at[c]
            )
        )
        sends[-1].start()
    for send in sends:
        send.wait()


def on_device(
    visibilities,
    row_owner,
    row_slot,
    baseline_station_pairs,
    gains_coarse,
    band_weights,
    band_offset,
):
    devices = lax.axis_size("bl")
    rows, parts, channels = visibilities.shape
    capacity = 2 * rows // devices
    owned = baseline_station_pairs.shape[0]
    stations, _, knots = gains_coarse.shape
    chunks = channels // LANES
    gain_tiles = round_up(stations // 2, SUB) // SUB
    depth = 2 * gain_tiles + 1
    near = devices // 2 if devices <= 16 else 1
    halves = near > 1
    f32, bf16, i32 = jnp.float32, jnp.bfloat16, jnp.int32
    vmem = pl.BlockSpec(memory_space=pltpu.VMEM)
    smem = pl.BlockSpec(memory_space=pltpu.SMEM)
    hbm = pl.BlockSpec(memory_space=pltpu.HBM)
    anywhere = pl.BlockSpec(memory_space=pl.ANY)
    most = pltpu.CompilerParams(vmem_limit_bytes=ALL_VMEM)
    some = pltpu.CompilerParams(vmem_limit_bytes=SOME_VMEM)
    shape = jax.ShapeDtypeStruct
    dma = pltpu.SemaphoreType.DMA

    me = lax.axis_index("bl").astype(i32).reshape(1)
    turn = me if halves else jnp.zeros_like(me)
    owner = row_owner.reshape(rows)
    coarse = gains_coarse.transpose(2, 1, 0).reshape(knots * parts, stations)
    block = (chunks * capacity, parts, LANES)
    rows_at = chunks * capacity
    if halves:
        long = with_gains(near) + [near + 3]
        outs = [
            shape((rows_at + (depth if x in long else 0), parts, LANES), bf16)
            for x in range(devices)
        ]
    else:
        outs = [shape((devices,) + block, bf16), shape((depth, SUB, LANES), bf16)]
    outs += [shape((SUB, channels), f32)]
    pairs = baseline_station_pairs.T
    weights = band_weights.T
    offset = band_offset.reshape(chunks, LANES)
    sent = pl.pallas_call(
        functools.partial(pack_kernel, capacity, near),
        out_shape=outs,
        in_specs=[smem] + [hbm] * 8,
        out_specs=[hbm] * len(outs),
        scratch_shapes=[
            pltpu.VMEM(weights.shape, f32),
            pltpu.VMEM(offset.shape, i32),
            pltpu.VMEM(pairs.shape, i32),
            pltpu.VMEM((SUB, channels), f32),
            pltpu.SMEM((rows,), i32),
            pltpu.SMEM((rows,), i32),
            pltpu.SMEM((devices,), i32),
            pltpu.VMEM((1, rows), i32),
            pltpu.VMEM((1, rows), i32),
            pltpu.VMEM((rows, parts, channels), bf16),
            pltpu.VMEM((knots * parts, stations), f32),
            pltpu.VMEM((LANES, LANES), f32),
            pltpu.VMEM((depth, SUB, LANES), bf16),
            pltpu.VMEM((devices,) + block, bf16),
            dma((9 + PARTS + 2 * devices,)),
        ],
        compiler_params=most,
        name="pack_rows",
    )(
        turn,
        owner,
        row_owner.reshape(1, rows),
        row_slot.reshape(1, rows),
        visibilities,
        coarse,
        weights,
        offset,
        pairs,
    )


    def ready(own, held):
        return pl.pallas_call(
            ready_kernel,
            out_shape=[
                shape(own.shape, bf16),
                shape(held.shape, bf16),
                shape((parts, LANES, channels), bf16),
                shape((parts, LANES, channels), bf16),
                shape((SUB, LANES), i32),
            ],
            in_specs=[vmem, anywhere, anywhere],
            out_specs=[vmem] * 5,
            scratch_shapes=[dma((2,))],
            compiler_params=some,
            name="make_ready",
        )(sent[-1], own, held)

    def swap(array, x):
        return lax.ppermute(array, "bl", [(d, d ^ x) for d in range(devices)])

    if halves:
        held = near + 2
        own, through, high, low, ints = ready(sent[0], sent[held])
        arrived = {0: own, held: swap(through, held)}
        arrived.update({x: swap(sent[x], x) for x in range(1, devices) if x != held})
        order, late = schedule(near)
        even = list(range(near, devices, 2))
        collected = pl.pallas_call(
            functools.partial(collect_kernel, rows_at, depth),
            out_shape=shape((len(even) * depth, parts, LANES), bf16),
            in_specs=[anywhere] * len(even),
            out_specs=vmem,
            scratch_shapes=[dma((len(even),))],
            compiler_params=some,
            name="collect_gains",
        )(*[arrived[x] for x in even])
        passed = [swap(collected, 1)]
    else:
        arrived = {
            0: lax.all_gather(sent[1], "bl", axis=0),
            1: lax.all_to_all(sent[0], "bl", split_axis=0, concat_axis=0, tiled=True),
        }
        order, late, passed = [0], [1], []
        _, _, high, low, ints = ready(sent[1], sent[1])

    gains, recip, slots, sums = pl.pallas_call(
        functools.partial(middle_kernel, capacity, near, stations, order),
        out_shape=(
            shape((parts, 2 * owned, channels), f32),
            shape((owned, LANES), f32),
            shape((devices, LANES), i32),
            shape((chunks, owned, parts, LANES), f32),
        ),
        in_specs=[smem] * 3 + [vmem] * (2 + len(order) + len(passed)),
        out_specs=(vmem,) * 4,
        scratch_shapes=[
            pltpu.VMEM((devices, gain_tiles * SUB, LANES), f32),
            pltpu.VMEM((2 * owned, LANES), f32),
            pltpu.VMEM((devices, LANES), f32),
            pltpu.VMEM((devices, LANES), f32),
            pltpu.VMEM((devices, LANES), i32),
            pltpu.SMEM((devices, LANES), i32),
            dma,
        ],
        compiler_params=some,
        name="gains_and_sums",
    )(turn, me, ints, high, low, *[arrived[x] for x in order], *passed)
    return pl.pallas_call(
        functools.partial(finish_kernel, capacity, late),
        out_shape=shape((owned, parts, channels), bf16),
        in_specs=[smem] + [vmem] * (3 + len(late)),
        out_specs=hbm,
        scratch_shapes=[
            pltpu.VMEM((chunks, owned, parts, LANES), f32),
            pltpu.VMEM((chunks, owned, parts, LANES), f32),
            pltpu.VMEM((chunks, owned, parts, LANES), bf16),
            dma((chunks,)),
        ],
        compiler_params=some,
        name="sum_and_apply",
    )(slots, gains, recip, sums, *[arrived[x] for x in late])


def solution(mesh):
    placed = (
        P(("groups", "bl"), None, None),
        P(("groups", "bl"), None),
        P(("groups", "bl")),
        P("bl", None),
        P(("groups", "bl"), None, None),
        P("groups", None),
        P("groups"),
    )
    return jax.shard_map(
        on_device,
        mesh=mesh,
        in_specs=placed,
        out_specs=P(("groups", "bl"), None, None),
        check_vma=False,
    )
```

```python
import functools

import jax
import jax.numpy as jnp
from jax import lax
from jax.experimental import pallas as pl
from jax.experimental.pallas import tpu as pltpu
from jax.sharding import PartitionSpec as P

LANES = 128
SUB = 8
USED = 48
PARTS = 4
ALL_VMEM = 60 * 1024 * 1024
SOME_VMEM = 24 * 1024 * 1024


def round_up(value, unit):
    return -(-value // unit) * unit


def schedule(near):
    even, odd = list(range(near, 2 * near, 2)), list(range(near + 1, 2 * near, 2))
    close = list(range(near // 2, near)) + list(range(1, near // 2))
    cross, late = even[2:] + odd[1:-2], odd[-2:]
    order = [0] + even[:2] + close[:2]
    close = close[2:]
    while cross:
        order += cross[:1] + close[:1]
        cross, close = cross[1:], close[1:]
    return order + close + odd[:1], late


def with_gains(near):
    return list(range(near)) + list(range(near, 2 * near, 2))


def start_all(pairs, sems):
    moves = [pltpu.make_async_copy(src, dst, sems.at[i]) for i, (src, dst) in enumerate(pairs)]
    for move in moves:
        move.start()
    return moves


def pack_kernel(
    capacity,
    near,
    me_s,
    owner_row_hbm,
    slot_row_hbm,
    vis_hbm,
    coarse_hbm,
    weights_hbm,
    offset_hbm,
    pairs_hbm,
    *rest,
):
    outs = rest[:-14]
    (
        weights_ref,
        offset_ref,
        pairs_ref,
        small_ref,
        place_s,
        place_ref,
        owner_ref,
        slot_ref,
        vis_ref,
        coarse_ref,
        turn_ref,
        meta_ref,
        block_ref,
        sems,
    ) = rest[-14:]
    rows = vis_ref.shape[0]
    chunks = vis_ref.shape[2] // LANES
    devices = block_ref.shape[0]
    terms, stations = coarse_ref.shape
    half = stations // 2
    depth = meta_ref.shape[0]
    gain_tiles = (depth - 1) // 2
    span = rows // PARTS
    moves = start_all(
        (
            (owner_row_hbm, owner_ref),
            (coarse_hbm, coarse_ref),
            (slot_row_hbm, slot_ref),
            (weights_hbm, weights_ref),
            (offset_hbm, offset_ref),
            (pairs_hbm, pairs_ref),
        ),
        sems,
    )
    fetches = start_all(
        [
            (vis_hbm.at[pl.ds(i * span, span)], vis_ref.at[pl.ds(i * span, span)])
            for i in range(PARTS)
        ],
        sems.at[pl.ds(len(moves), PARTS)],
    )
    turn_ref[...] = jnp.zeros_like(turn_ref)
    moves[0].wait()

    owner = owner_ref[...]
    each = lax.broadcasted_iota(jnp.int32, (devices, rows), 0)
    member = owner == each
    rank = jnp.dot(
        member.astype(jnp.float32).astype(jnp.bfloat16),
        earlier(rows),
        preferred_element_type=jnp.float32,
    )
    base = ((each ^ me_s[0]) * capacity).astype(jnp.float32)
    place = jnp.sum(jnp.where(member, base + rank, 0.0), axis=0, keepdims=True)
    place_ref[...] = jnp.broadcast_to(place, place_ref.shape).astype(jnp.int32)
    placing = pltpu.make_async_copy(place_ref, place_s, sems.at[0])
    placing.start()
    for move in moves[1:]:
        move.wait()

    turn_ref[0:terms, 0:half] = coarse_ref[:, 0:half]
    turn_ref[64 : 64 + terms, 0:half] = coarse_ref[:, half:stations]
    gains = turn_ref[...].T
    high = gains.astype(jnp.bfloat16)
    low = (gains - high.astype(jnp.float32)).astype(jnp.bfloat16)
    for i in range(gain_tiles):
        meta_ref[i] = high[i * SUB : (i + 1) * SUB, :]
        meta_ref[gain_tiles + i] = low[i * SUB : (i + 1) * SUB, :]
    sub = lax.broadcasted_iota(jnp.int32, (SUB, LANES), 0)
    codes = jnp.where(sub == 0, owner, slot_ref[...])
    meta_ref[2 * gain_tiles] = codes.astype(jnp.float32).astype(jnp.bfloat16)
    steps = weights_ref.shape[0]
    small_ref[...] = jnp.zeros_like(small_ref)
    small_ref[0:steps, :] = weights_ref[...]
    for c in range(chunks):
        lanes = slice(c * LANES, (c + 1) * LANES)
        small_ref[steps : steps + 1, lanes] = offset_ref[c : c + 1, :].astype(jnp.float32)
    small_ref[4:6, 0 : pairs_ref.shape[1]] = pairs_ref[...].astype(jnp.float32)

    at = chunks * capacity
    if near > 1:
        pairs = [(meta_ref, outs[x].at[pl.ds(at, depth)]) for x in with_gains(near)]
    else:
        pairs = [(meta_ref, outs[1])]
    pairs += [(small_ref, outs[-1])]
    start = len(moves) + PARTS
    sends = start_all(pairs, sems.at[pl.ds(start, len(pairs))])
    start += len(pairs)

    def place(r, carry):
        p = place_s[0, r]
        for c in range(chunks):
            flat_ref[p * chunks + c] = vis_ref[r, :, c * LANES : (c + 1) * LANES]
        return carry

    flat_ref = block_ref.reshape(devices * at, SUB, LANES)
    placing.wait()
    for i in range(PARTS):
        fetches[i].wait()
        lax.fori_loop(i * span, (i + 1) * span, place, 0, unroll=8)
    if near > 1:
        pairs = [(block_ref.at[x], outs[x].at[pl.ds(0, at)]) for x in range(devices)]
    else:
        pairs = [(block_ref, outs[0])]
    sends += start_all(pairs, sems.at[pl.ds(start, len(pairs))])
    for send in sends:
        send.wait()


def ready_kernel(small_ref, own_ref, held_ref, own_out_ref, held_out_ref, high_ref, low_ref, pairs_ref, sems):
    moves = start_all([(own_ref, own_out_ref), (held_ref, held_out_ref)], sems)
    small = small_ref[...]
    channels = small.shape[1]
    pairs_ref[...] = small[:, 0:LANES].astype(jnp.int32)
    index = lax.broadcasted_iota(jnp.int32, (LANES, channels), 0)
    knot = ((index & 63) >> 3).astype(jnp.float32)
    basis = jnp.zeros((LANES, channels), jnp.float32)
    for step in range(3):
        basis = basis + jnp.where(knot == small[3:4, :] + float(step), small[step : step + 1, :], 0.0)
    high = basis.astype(jnp.bfloat16).astype(jnp.float32)
    low = basis - high
    part = index & 7
    for j in range(8):
        high_ref[j] = jnp.where(part == j, high, 0.0).astype(jnp.bfloat16)
        low_ref[j] = jnp.where(part == j, low, 0.0).astype(jnp.bfloat16)
    for move in moves:
        move.wait()


def collect_kernel(at, depth, *rest):
    blocks, (out_ref, sems) = rest[:-2], rest[-2:]
    moves = start_all(
        [
            (block.at[pl.ds(at, depth)], out_ref.at[pl.ds(i * depth, depth)])
            for i, block in enumerate(blocks)
        ],
        sems,
    )
    for move in moves:
        move.wait()


def earlier(width):
    first = lax.broadcasted_iota(jnp.int32, (width, width), 0)
    second = lax.broadcasted_iota(jnp.int32, (width, width), 1)
    return (first < second).astype(jnp.float32).astype(jnp.bfloat16)


def list_rows(owner, slot, target, capacity):
    senders = owner.shape[0]
    mine = owner == target
    counted = mine.astype(jnp.float32)
    rank = jnp.dot(
        counted.astype(jnp.bfloat16), earlier(LANES), preferred_element_type=jnp.float32
    )
    lane = lax.broadcasted_iota(jnp.int32, (senders, LANES), 1)
    count = jnp.sum(counted, axis=1, keepdims=True)
    listing = jnp.where(lane == capacity, count, 0.0)
    for k in range(capacity):
        here = jnp.logical_and(mine, rank == float(k))
        kth = jnp.sum(jnp.where(here, slot, 0.0), axis=1, keepdims=True)
        listing = jnp.where(lane == k, kth, listing)
    return listing.astype(jnp.int32), mine


def add_rows(acc_ref, slots_s, line, capacity, rows_ref):
    chunks = acc_ref.shape[0]

    def add(k, carry):
        b = slots_s[line, k]
        for c in range(chunks):
            acc_ref[c, b] += rows_ref[chunks * k + c].astype(jnp.float32)
        return carry

    lax.fori_loop(0, slots_s[line, capacity], add, 0)


def add_table(table_ref, x, block, at, depth):
    gain_tiles = (depth - 1) // 2
    for i in range(gain_tiles):
        table_ref[x, i * SUB : (i + 1) * SUB, :] = block[at + i].astype(jnp.float32) + block[
            at + gain_tiles + i
        ].astype(jnp.float32)
    return block[at + 2 * gain_tiles].astype(jnp.float32)


def count_rows(hits, mine, slot):
    which = lax.broadcasted_iota(jnp.int32, hits.shape, 0).astype(jnp.float32)
    slot = jnp.where(mine, slot, -1.0)
    for x in range(slot.shape[0]):
        hits = hits + (slot[x : x + 1, :] == which).astype(jnp.float32)
    return hits


def middle_kernel(capacity, near, stations, order, turn_s, me_s, pairs_s, high_ref, low_ref, *rest):
    arrived, passed = dict(zip(order, rest)), rest[len(order) : -11]
    gains_ref, recip_ref, slots_ref, sums_ref = rest[-11:-7]
    table_ref, pick_ref, owner_ref, slot_ref, slots_v, slots_s, sem = rest[-7:]
    devices = table_ref.shape[0]
    owned = recip_ref.shape[0]
    chunks = sums_ref.shape[0]
    half = stations // 2
    depth = 2 * (table_ref.shape[1] // SUB) + 1
    for x in range(devices):
        if near == 1:
            code = add_table(table_ref, x, arrived[0].at[x], 0, depth)
        elif x in with_gains(near):
            code = add_table(table_ref, x, arrived[x], chunks * capacity, depth)
        else:
            code = add_table(table_ref, x, passed[0], (x - near) // 2 * depth, depth)
        owner_ref[x : x + 1, :] = code[0:1, :]
        slot_ref[x : x + 1, :] = code[1:2, :]
    slot = slot_ref[...]
    listing, mine = list_rows(owner_ref[...], slot, me_s[0].astype(jnp.float32), capacity)
    slots_ref[...] = listing
    slots_v[...] = listing
    move = pltpu.make_async_copy(slots_v, slots_s, sem)
    move.start()
    hits = count_rows(jnp.zeros((owned, LANES), jnp.float32), mine, slot)
    tally = jnp.sum(hits, axis=1, keepdims=True)
    recip_ref[...] = jnp.broadcast_to(1.0 / jnp.maximum(tally, 1.0), recip_ref.shape)

    turn = turn_s[0]
    column = lax.broadcasted_iota(jnp.int32, (1, LANES), 1)
    used = (column & 63) < USED
    upper = column >> 6

    def pick(b, carry):
        for side in range(2):
            s = pairs_s[4 + side, b]
            d = s // stations
            within = s - d * stations
            second = jnp.where(within >= half, 1, 0)
            row = table_ref[d ^ turn, pl.ds(within - second * half, 1), :]
            keep = jnp.logical_and(used, upper == second)
            pick_ref[pl.ds(side * owned + b, 1), :] = jnp.where(keep, row, 0.0)
        return carry

    lax.fori_loop(0, owned, pick, 0, unroll=8)
    both = pick_ref[...]
    both_high = both.astype(jnp.bfloat16)
    both_low = (both - both_high.astype(jnp.float32)).astype(jnp.bfloat16)
    both_two = jnp.concatenate([both_high, both_low], axis=1)
    for j in range(8):
        high, low = high_ref[j], low_ref[j]
        fine = jnp.dot(
            both_two, jnp.concatenate([high, high], axis=0), preferred_element_type=jnp.float32
        ) + jnp.dot(both_high, low, preferred_element_type=jnp.float32)
        gains_ref[j] = fine.astype(jnp.bfloat16).astype(jnp.float32)

    sums_ref[...] = jnp.zeros_like(sums_ref)
    move.wait()
    if near > 1:
        for x in order:
            add_rows(sums_ref, slots_s, x, capacity, arrived[x])


def finish_kernel(capacity, late, slots_s, gains_ref, recip_ref, sums_ref, *rest):
    far = rest[: len(late)]
    out_hbm, acc_ref, res_ref, out_ref, sems = rest[len(late) :]
    owned, parts, channels = out_hbm.shape
    chunks = channels // LANES
    acc_ref[...] = sums_ref[...]
    if len(late) > 1:
        for x, rows_ref in zip(late, far):
            add_rows(acc_ref, slots_s, x, capacity, rows_ref)
    else:

        def from_device(d, carry):
            add_rows(acc_ref, slots_s, d, capacity, far[0].at[d])
            return carry

        lax.fori_loop(0, far[0].shape[0], from_device, 0)

    flat = acc_ref.reshape(chunks * owned * parts, LANES)
    done = res_ref.reshape(chunks * owned * parts, LANES)
    sends = []
    for c in range(chunks):
        cols = slice(c * LANES, (c + 1) * LANES)
        for b0 in range(0, owned, SUB):
            scale = recip_ref[b0 : b0 + SUB, :]
            row = (c * owned + b0) * parts
            vis = [flat[pl.ds(row + j, SUB, stride=parts), :] for j in range(parts)]
            lhs = [gains_ref[j, b0 : b0 + SUB, cols] for j in range(parts)]
            rhs = [gains_ref[j, owned + b0 : owned + b0 + SUB, cols] for j in range(parts)]
            mid_re, mid_im = [], []
            for row_a in range(2):
                for col_b in range(2):
                    re = im = 0.0
                    for inner in range(2):
                        lr, li = lhs[2 * row_a + inner], lhs[4 + 2 * row_a + inner]
                        vr, vi = vis[2 * inner + col_b], vis[4 + 2 * inner + col_b]
                        re = re + lr * vr - li * vi
                        im = im + lr * vi + li * vr
                    mid_re.append(re * scale)
                    mid_im.append(im * scale)
            for row_a in range(2):
                for col_b in range(2):
                    re = im = 0.0
                    for inner in range(2):
                        mr, mi = mid_re[2 * row_a + inner], mid_im[2 * row_a + inner]
                        rr, ri = rhs[2 * col_b + inner], rhs[4 + 2 * col_b + inner]
                        re = re + mr * rr + mi * ri
                        im = im + mi * rr - mr * ri
                    j = 2 * row_a + col_b
                    done[pl.ds(row + j, SUB, stride=parts), :] = re
                    done[pl.ds(row + 4 + j, SUB, stride=parts), :] = im
        out_ref[c] = res_ref[c].astype(out_ref.dtype)
        sends.append(
            pltpu.make_async_copy(
                out_ref.at[c], out_hbm.at[:, :, pl.ds(c * LANES, LANES)], sems.at[c]
            )
        )
        sends[-1].start()
    for send in sends:
        send.wait()


def on_device(
    visibilities,
    row_owner,
    row_slot,
    baseline_station_pairs,
    gains_coarse,
    band_weights,
    band_offset,
):
    devices = lax.axis_size("bl")
    rows, parts, channels = visibilities.shape
    capacity = 2 * rows // devices
    owned = baseline_station_pairs.shape[0]
    stations, _, knots = gains_coarse.shape
    chunks = channels // LANES
    gain_tiles = round_up(stations // 2, SUB) // SUB
    depth = 2 * gain_tiles + 1
    near = devices // 2 if devices <= 16 else 1
    halves = near > 1
    f32, bf16, i32 = jnp.float32, jnp.bfloat16, jnp.int32
    vmem = pl.BlockSpec(memory_space=pltpu.VMEM)
    smem = pl.BlockSpec(memory_space=pltpu.SMEM)
    hbm = pl.BlockSpec(memory_space=pltpu.HBM)
    anywhere = pl.BlockSpec(memory_space=pl.ANY)
    most = pltpu.CompilerParams(vmem_limit_bytes=ALL_VMEM)
    some = pltpu.CompilerParams(vmem_limit_bytes=SOME_VMEM)
    shape = jax.ShapeDtypeStruct
    dma = pltpu.SemaphoreType.DMA

    me = lax.axis_index("bl").astype(i32).reshape(1)
    turn = me if halves else jnp.zeros_like(me)
    coarse = gains_coarse.transpose(2, 1, 0).reshape(knots * parts, stations)
    block = (chunks * capacity, parts, LANES)
    rows_at = chunks * capacity
    if halves:
        long = with_gains(near)
        outs = [
            shape((rows_at + (depth if x in long else 0), parts, LANES), bf16)
            for x in range(devices)
        ]
    else:
        outs = [shape((devices,) + block, bf16), shape((depth, SUB, LANES), bf16)]
    outs += [shape((SUB, channels), f32)]
    pairs = baseline_station_pairs.T
    weights = band_weights.T
    offset = band_offset.reshape(chunks, LANES)
    sent = pl.pallas_call(
        functools.partial(pack_kernel, capacity, near),
        out_shape=outs,
        in_specs=[smem] + [hbm] * 7,
        out_specs=[hbm] * len(outs),
        scratch_shapes=[
            pltpu.VMEM(weights.shape, f32),
            pltpu.VMEM(offset.shape, i32),
            pltpu.VMEM(pairs.shape, i32),
            pltpu.VMEM((SUB, channels), f32),
            pltpu.SMEM((SUB, rows), i32),
            pltpu.VMEM((SUB, rows), i32),
            pltpu.VMEM((1, rows), i32),
            pltpu.VMEM((1, rows), i32),
            pltpu.VMEM((rows, parts, channels), bf16),
            pltpu.VMEM((knots * parts, stations), f32),
            pltpu.VMEM((LANES, LANES), f32),
            pltpu.VMEM((depth, SUB, LANES), bf16),
            pltpu.VMEM((devices,) + block, bf16),
            dma((9 + PARTS + 2 * devices,)),
        ],
        compiler_params=most,
        name="pack_rows",
    )(
        turn,
        row_owner.reshape(1, rows),
        row_slot.reshape(1, rows),
        visibilities,
        coarse,
        weights,
        offset,
        pairs,
    )


    def ready(own, held):
        return pl.pallas_call(
            ready_kernel,
            out_shape=[
                shape(own.shape, bf16),
                shape(held.shape, bf16),
                shape((parts, LANES, channels), bf16),
                shape((parts, LANES, channels), bf16),
                shape((SUB, LANES), i32),
            ],
            in_specs=[vmem, anywhere, anywhere],
            out_specs=[vmem] * 5,
            scratch_shapes=[dma((2,))],
            compiler_params=some,
            name="make_ready",
        )(sent[-1], own, held)

    def swap(array, x):
        return lax.ppermute(array, "bl", [(d, d ^ x) for d in range(devices)])

    if halves:
        held = near + 4
        own, through, high, low, ints = ready(sent[0], sent[held])
        arrived = {0: own, held: swap(through, held)}
        arrived.update({x: swap(sent[x], x) for x in range(1, devices) if x != held})
        order, late = schedule(near)
        even = list(range(near, devices, 2))
        collected = pl.pallas_call(
            functools.partial(collect_kernel, rows_at, depth),
            out_shape=shape((len(even) * depth, parts, LANES), bf16),
            in_specs=[anywhere] * len(even),
            out_specs=vmem,
            scratch_shapes=[dma((len(even),))],
            compiler_params=some,
            name="collect_gains",
        )(*[arrived[x] for x in even])
        passed = [swap(collected, 1)]
    else:
        arrived = {
            0: lax.all_gather(sent[1], "bl", axis=0),
            1: lax.all_to_all(sent[0], "bl", split_axis=0, concat_axis=0, tiled=True),
        }
        order, late, passed = [0], [1], []
        _, _, high, low, ints = ready(sent[1], sent[1])

    gains, recip, slots, sums = pl.pallas_call(
        functools.partial(middle_kernel, capacity, near, stations, order),
        out_shape=(
            shape((parts, 2 * owned, channels), f32),
            shape((owned, LANES), f32),
            shape((devices, LANES), i32),
            shape((chunks, owned, parts, LANES), f32),
        ),
        in_specs=[smem] * 3 + [vmem] * (2 + len(order) + len(passed)),
        out_specs=(vmem,) * 4,
        scratch_shapes=[
            pltpu.VMEM((devices, gain_tiles * SUB, LANES), f32),
            pltpu.VMEM((2 * owned, LANES), f32),
            pltpu.VMEM((devices, LANES), f32),
            pltpu.VMEM((devices, LANES), f32),
            pltpu.VMEM((devices, LANES), i32),
            pltpu.SMEM((devices, LANES), i32),
            dma,
        ],
        compiler_params=some,
        name="gains_and_sums",
    )(turn, me, ints, high, low, *[arrived[x] for x in order], *passed)
    return pl.pallas_call(
        functools.partial(finish_kernel, capacity, late),
        out_shape=shape((owned, parts, channels), bf16),
        in_specs=[smem] + [vmem] * (3 + len(late)),
        out_specs=hbm,
        scratch_shapes=[
            pltpu.VMEM((chunks, owned, parts, LANES), f32),
            pltpu.VMEM((chunks, owned, parts, LANES), f32),
            pltpu.VMEM((chunks, owned, parts, LANES), bf16),
            dma((chunks,)),
        ],
        compiler_params=some,
        name="sum_and_apply",
    )(slots, gains, recip, sums, *[arrived[x] for x in late])


def solution(mesh):
    placed = (
        P(("groups", "bl"), None, None),
        P(("groups", "bl"), None),
        P(("groups", "bl")),
        P("bl", None),
        P(("groups", "bl"), None, None),
        P("groups", None),
        P("groups"),
    )
    return jax.shard_map(
        on_device,
        mesh=mesh,
        in_specs=placed,
        out_specs=P(("groups", "bl"), None, None),
        check_vma=False,
    )
```

```python
import functools

import jax
import jax.numpy as jnp
from jax import lax
from jax.experimental import pallas as pl
from jax.experimental.pallas import tpu as pltpu
from jax.sharding import PartitionSpec as P

LANES = 128
SUB = 8
USED = 48
PARTS = 4
ALL_VMEM = 60 * 1024 * 1024
SOME_VMEM = 24 * 1024 * 1024


def round_up(value, unit):
    return -(-value // unit) * unit


def schedule(near):
    even, odd = list(range(near, 2 * near, 2)), list(range(near + 1, 2 * near, 2))
    close = list(range(near // 2, near)) + list(range(1, near // 2))
    cross, late = even[2:] + odd[1:-2], odd[-2:]
    order = [0] + even[:2] + close[:2]
    close = close[2:]
    while cross:
        order += cross[:1] + close[:1]
        cross, close = cross[1:], close[1:]
    return order + close + odd[:1], late


def with_gains(near):
    return list(range(near)) + list(range(near, 2 * near, 2))


def start_all(pairs, sems):
    moves = [pltpu.make_async_copy(src, dst, sems.at[i]) for i, (src, dst) in enumerate(pairs)]
    for move in moves:
        move.start()
    return moves


def pack_kernel(
    capacity,
    near,
    me_s,
    owner_hbm,
    owner_row_hbm,
    slot_row_hbm,
    vis_hbm,
    coarse_hbm,
    weights_hbm,
    offset_hbm,
    pairs_hbm,
    *rest,
):
    outs = rest[:-15]
    (
        weights_ref,
        offset_ref,
        pairs_ref,
        small_ref,
        owner_s,
        place_s,
        count_s,
        owner_ref,
        slot_ref,
        vis_ref,
        coarse_ref,
        turn_ref,
        meta_ref,
        block_ref,
        sems,
    ) = rest[-15:]
    rows = vis_ref.shape[0]
    chunks = vis_ref.shape[2] // LANES
    devices = block_ref.shape[0]
    terms, stations = coarse_ref.shape
    half = stations // 2
    depth = meta_ref.shape[0]
    gain_tiles = (depth - 1) // 2
    span = rows // PARTS
    moves = start_all(
        (
            (owner_hbm, owner_s),
            (coarse_hbm, coarse_ref),
            (owner_row_hbm, owner_ref),
            (slot_row_hbm, slot_ref),
            (weights_hbm, weights_ref),
            (offset_hbm, offset_ref),
            (pairs_hbm, pairs_ref),
        ),
        sems,
    )
    fetches = start_all(
        [
            (vis_hbm.at[pl.ds(i * span, span)], vis_ref.at[pl.ds(i * span, span)])
            for i in range(PARTS)
        ],
        sems.at[pl.ds(len(moves), PARTS)],
    )
    turn_ref[...] = jnp.zeros_like(turn_ref)
    for d in range(devices):
        count_s[d] = 0
    me = me_s[0]
    moves[0].wait()

    def rank(r, carry):
        x = owner_s[r] ^ me
        k = count_s[x]
        count_s[x] = k + 1
        place_s[r] = x * capacity + k
        return carry

    lax.fori_loop(0, rows, rank, 0, unroll=8)
    for move in moves[1:]:
        move.wait()

    turn_ref[0:terms, 0:half] = coarse_ref[:, 0:half]
    turn_ref[64 : 64 + terms, 0:half] = coarse_ref[:, half:stations]
    gains = turn_ref[...].T
    high = gains.astype(jnp.bfloat16)
    low = (gains - high.astype(jnp.float32)).astype(jnp.bfloat16)
    for i in range(gain_tiles):
        meta_ref[i] = high[i * SUB : (i + 1) * SUB, :]
        meta_ref[gain_tiles + i] = low[i * SUB : (i + 1) * SUB, :]
    sub = lax.broadcasted_iota(jnp.int32, (SUB, LANES), 0)
    codes = jnp.where(sub == 0, owner_ref[...], slot_ref[...])
    meta_ref[2 * gain_tiles] = codes.astype(jnp.float32).astype(jnp.bfloat16)
    steps = weights_ref.shape[0]
    small_ref[...] = jnp.zeros_like(small_ref)
    small_ref[0:steps, :] = weights_ref[...]
    for c in range(chunks):
        lanes = slice(c * LANES, (c + 1) * LANES)
        small_ref[steps : steps + 1, lanes] = offset_ref[c : c + 1, :].astype(jnp.float32)
    small_ref[4:6, 0 : pairs_ref.shape[1]] = pairs_ref[...].astype(jnp.float32)

    at = chunks * capacity
    if near > 1:
        pairs = [(meta_ref, outs[x].at[pl.ds(at, depth)]) for x in with_gains(near)]
    else:
        pairs = [(meta_ref, outs[1])]
    pairs += [(small_ref, outs[-1])]
    start = len(moves) + PARTS
    sends = start_all(pairs, sems.at[pl.ds(start, len(pairs))])
    start += len(pairs)

    def place(r, carry):
        p = place_s[r]
        for c in range(chunks):
            flat_ref[p * chunks + c] = vis_ref[r, :, c * LANES : (c + 1) * LANES]
        return carry

    flat_ref = block_ref.reshape(devices * at, SUB, LANES)
    for i in range(PARTS):
        fetches[i].wait()
        lax.fori_loop(i * span, (i + 1) * span, place, 0, unroll=8)
    if near > 1:
        pairs = [(block_ref.at[x], outs[x].at[pl.ds(0, at)]) for x in range(devices)]
    else:
        pairs = [(block_ref, outs[0])]
    sends += start_all(pairs, sems.at[pl.ds(start, len(pairs))])
    for send in sends:
        send.wait()


def ready_kernel(small_ref, own_ref, own_out_ref, high_ref, low_ref, pairs_ref, sem):
    move = pltpu.make_async_copy(own_ref, own_out_ref, sem)
    move.start()
    small = small_ref[...]
    channels = small.shape[1]
    pairs_ref[...] = small[:, 0:LANES].astype(jnp.int32)
    index = lax.broadcasted_iota(jnp.int32, (LANES, channels), 0)
    knot = ((index & 63) >> 3).astype(jnp.float32)
    basis = jnp.zeros((LANES, channels), jnp.float32)
    for step in range(3):
        basis = basis + jnp.where(knot == small[3:4, :] + float(step), small[step : step + 1, :], 0.0)
    high = basis.astype(jnp.bfloat16).astype(jnp.float32)
    low = basis - high
    part = index & 7
    for j in range(8):
        high_ref[j] = jnp.where(part == j, high, 0.0).astype(jnp.bfloat16)
        low_ref[j] = jnp.where(part == j, low, 0.0).astype(jnp.bfloat16)
    move.wait()


def collect_kernel(at, depth, *rest):
    blocks, (out_ref, sems) = rest[:-2], rest[-2:]
    moves = start_all(
        [
            (block.at[pl.ds(at, depth)], out_ref.at[pl.ds(i * depth, depth)])
            for i, block in enumerate(blocks)
        ],
        sems,
    )
    for move in moves:
        move.wait()


def list_rows(owner, slot, target, capacity, spare):
    senders = owner.shape[0]
    mine = owner == target
    counted = mine.astype(jnp.float32)
    before = lax.broadcasted_iota(jnp.int32, (LANES, LANES), 0) < lax.broadcasted_iota(
        jnp.int32, (LANES, LANES), 1
    )
    rank = jnp.dot(
        counted.astype(jnp.bfloat16),
        before.astype(jnp.float32).astype(jnp.bfloat16),
        preferred_element_type=jnp.float32,
    )
    lane = lax.broadcasted_iota(jnp.int32, (senders, LANES), 1)
    count = jnp.sum(counted, axis=1, keepdims=True)
    listing = jnp.where(lane == capacity, count, 0.0)
    for k in range(capacity):
        here = jnp.logical_and(mine, rank == float(k))
        kth = jnp.sum(jnp.where(here, slot, 0.0), axis=1, keepdims=True)
        kth = jnp.where(count > float(k), kth, float(spare))
        listing = jnp.where(lane == k, kth, listing)
    return listing.astype(jnp.int32), mine


def add_rows(acc_refs, slots_s, line, capacity, rows_ref):
    chunks, several = acc_refs[0].shape[0], len(acc_refs)

    def add(i, carry):
        for u, acc_ref in enumerate(acc_refs):
            k = several * i + u
            b = slots_s[line, k]
            for c in range(chunks):
                acc_ref[c, b] += rows_ref[chunks * k + c].astype(jnp.float32)
        return carry

    lax.fori_loop(0, (slots_s[line, capacity] + several - 1) // several, add, 0)


def add_table(table_ref, x, block, at, depth):
    gain_tiles = (depth - 1) // 2
    for i in range(gain_tiles):
        table_ref[x, i * SUB : (i + 1) * SUB, :] = block[at + i].astype(jnp.float32) + block[
            at + gain_tiles + i
        ].astype(jnp.float32)
    return block[at + 2 * gain_tiles].astype(jnp.float32)


def count_rows(hits, mine, slot):
    which = lax.broadcasted_iota(jnp.int32, hits.shape, 0).astype(jnp.float32)
    slot = jnp.where(mine, slot, -1.0)
    for x in range(slot.shape[0]):
        hits = hits + (slot[x : x + 1, :] == which).astype(jnp.float32)
    return hits


def middle_kernel(capacity, near, stations, order, turn_s, me_s, pairs_s, high_ref, low_ref, *rest):
    arrived, passed = dict(zip(order, rest)), rest[len(order) : -13]
    gains_ref, recip_ref, slots_ref, sums_ref = rest[-13:-9]
    table_ref, pick_ref, owner_ref, slot_ref, slots_v, slots_s, one_ref, two_ref, sem = rest[-9:]
    devices = table_ref.shape[0]
    owned = recip_ref.shape[0]
    chunks = sums_ref.shape[0]
    half = stations // 2
    depth = 2 * (table_ref.shape[1] // SUB) + 1
    for x in range(devices):
        if near == 1:
            code = add_table(table_ref, x, arrived[0].at[x], 0, depth)
        elif x in with_gains(near):
            code = add_table(table_ref, x, arrived[x], chunks * capacity, depth)
        else:
            code = add_table(table_ref, x, passed[0], (x - near) // 2 * depth, depth)
        owner_ref[x : x + 1, :] = code[0:1, :]
        slot_ref[x : x + 1, :] = code[1:2, :]
    slot = slot_ref[...]
    listing, mine = list_rows(
        owner_ref[...], slot, me_s[0].astype(jnp.float32), capacity, owned
    )
    slots_ref[...] = listing
    slots_v[...] = listing
    move = pltpu.make_async_copy(slots_v, slots_s, sem)
    move.start()
    hits = count_rows(jnp.zeros((owned, LANES), jnp.float32), mine, slot)
    tally = jnp.sum(hits, axis=1, keepdims=True)
    recip_ref[...] = jnp.broadcast_to(1.0 / jnp.maximum(tally, 1.0), recip_ref.shape)

    turn = turn_s[0]
    column = lax.broadcasted_iota(jnp.int32, (1, LANES), 1)
    used = (column & 63) < USED
    upper = column >> 6

    def pick(b, carry):
        for side in range(2):
            s = pairs_s[4 + side, b]
            d = s // stations
            within = s - d * stations
            second = jnp.where(within >= half, 1, 0)
            row = table_ref[d ^ turn, pl.ds(within - second * half, 1), :]
            keep = jnp.logical_and(used, upper == second)
            pick_ref[pl.ds(side * owned + b, 1), :] = jnp.where(keep, row, 0.0)
        return carry

    lax.fori_loop(0, owned, pick, 0, unroll=8)
    both = pick_ref[...]
    both_high = both.astype(jnp.bfloat16)
    both_low = (both - both_high.astype(jnp.float32)).astype(jnp.bfloat16)
    both_two = jnp.concatenate([both_high, both_low], axis=1)
    for j in range(8):
        high, low = high_ref[j], low_ref[j]
        fine = jnp.dot(
            both_two, jnp.concatenate([high, high], axis=0), preferred_element_type=jnp.float32
        ) + jnp.dot(both_high, low, preferred_element_type=jnp.float32)
        gains_ref[j] = fine.astype(jnp.bfloat16).astype(jnp.float32)

    one_ref[...] = jnp.zeros_like(one_ref)
    two_ref[...] = jnp.zeros_like(two_ref)
    move.wait()
    if near > 1:
        for x in order:
            add_rows((one_ref, two_ref), slots_s, x, capacity, arrived[x])
    sums_ref[...] = one_ref[:, 0:owned] + two_ref[:, 0:owned]


def finish_kernel(capacity, late, slots_s, gains_ref, recip_ref, sums_ref, *rest):
    far = rest[: len(late)]
    out_hbm, acc_ref, res_ref, out_ref, sems = rest[len(late) :]
    owned, parts, channels = out_hbm.shape
    chunks = channels // LANES
    acc_ref[...] = sums_ref[...]
    if len(late) > 1:
        for x, rows_ref in zip(late, far):
            add_rows((acc_ref,), slots_s, x, capacity, rows_ref)
    else:

        def from_device(d, carry):
            add_rows((acc_ref,), slots_s, d, capacity, far[0].at[d])
            return carry

        lax.fori_loop(0, far[0].shape[0], from_device, 0)

    flat = acc_ref.reshape(chunks * owned * parts, LANES)
    done = res_ref.reshape(chunks * owned * parts, LANES)
    sends = []
    for c in range(chunks):
        cols = slice(c * LANES, (c + 1) * LANES)
        for b0 in range(0, owned, SUB):
            scale = recip_ref[b0 : b0 + SUB, :]
            row = (c * owned + b0) * parts
            vis = [flat[pl.ds(row + j, SUB, stride=parts), :] for j in range(parts)]
            lhs = [gains_ref[j, b0 : b0 + SUB, cols] for j in range(parts)]
            rhs = [gains_ref[j, owned + b0 : owned + b0 + SUB, cols] for j in range(parts)]
            mid_re, mid_im = [], []
            for row_a in range(2):
                for col_b in range(2):
                    re = im = 0.0
                    for inner in range(2):
                        lr, li = lhs[2 * row_a + inner], lhs[4 + 2 * row_a + inner]
                        vr, vi = vis[2 * inner + col_b], vis[4 + 2 * inner + col_b]
                        re = re + lr * vr - li * vi
                        im = im + lr * vi + li * vr
                    mid_re.append(re * scale)
                    mid_im.append(im * scale)
            for row_a in range(2):
                for col_b in range(2):
                    re = im = 0.0
                    for inner in range(2):
                        mr, mi = mid_re[2 * row_a + inner], mid_im[2 * row_a + inner]
                        rr, ri = rhs[2 * col_b + inner], rhs[4 + 2 * col_b + inner]
                        re = re + mr * rr + mi * ri
                        im = im + mi * rr - mr * ri
                    j = 2 * row_a + col_b
                    done[pl.ds(row + j, SUB, stride=parts), :] = re
                    done[pl.ds(row + 4 + j, SUB, stride=parts), :] = im
        out_ref[c] = res_ref[c].astype(out_ref.dtype)
        sends.append(
            pltpu.make_async_copy(
                out_ref.at[c], out_hbm.at[:, :, pl.ds(c * LANES, LANES)], sems.at[c]
            )
        )
        sends[-1].start()
    for send in sends:
        send.wait()


def on_device(
    visibilities,
    row_owner,
    row_slot,
    baseline_station_pairs,
    gains_coarse,
    band_weights,
    band_offset,
):
    devices = lax.axis_size("bl")
    rows, parts, channels = visibilities.shape
    capacity = 2 * rows // devices
    owned = baseline_station_pairs.shape[0]
    stations, _, knots = gains_coarse.shape
    chunks = channels // LANES
    gain_tiles = round_up(stations // 2, SUB) // SUB
    depth = 2 * gain_tiles + 1
    near = devices // 2 if devices <= 16 else 1
    halves = near > 1
    f32, bf16, i32 = jnp.float32, jnp.bfloat16, jnp.int32
    vmem = pl.BlockSpec(memory_space=pltpu.VMEM)
    smem = pl.BlockSpec(memory_space=pltpu.SMEM)
    hbm = pl.BlockSpec(memory_space=pltpu.HBM)
    anywhere = pl.BlockSpec(memory_space=pl.ANY)
    most = pltpu.CompilerParams(vmem_limit_bytes=ALL_VMEM)
    some = pltpu.CompilerParams(vmem_limit_bytes=SOME_VMEM)
    shape = jax.ShapeDtypeStruct
    dma = pltpu.SemaphoreType.DMA

    me = lax.axis_index("bl").astype(i32).reshape(1)
    turn = me if halves else jnp.zeros_like(me)
    owner = row_owner.reshape(rows)
    coarse = gains_coarse.transpose(2, 1, 0).reshape(knots * parts, stations)
    block = (chunks * capacity, parts, LANES)
    rows_at = chunks * capacity
    if halves:
        long = with_gains(near) + [near + 3]
        outs = [
            shape((rows_at + (depth if x in long else 0), parts, LANES), bf16)
            for x in range(devices)
        ]
    else:
        outs = [shape((devices,) + block, bf16), shape((depth, SUB, LANES), bf16)]
    outs += [shape((SUB, channels), f32)]
    pairs = baseline_station_pairs.T
    weights = band_weights.T
    offset = band_offset.reshape(chunks, LANES)
    sent = pl.pallas_call(
        functools.partial(pack_kernel, capacity, near),
        out_shape=outs,
        in_specs=[smem] + [hbm] * 8,
        out_specs=[hbm] * len(outs),
        scratch_shapes=[
            pltpu.VMEM(weights.shape, f32),
            pltpu.VMEM(offset.shape, i32),
            pltpu.VMEM(pairs.shape, i32),
            pltpu.VMEM((SUB, channels), f32),
            pltpu.SMEM((rows,), i32),
            pltpu.SMEM((rows,), i32),
            pltpu.SMEM((devices,), i32),
            pltpu.VMEM((1, rows), i32),
            pltpu.VMEM((1, rows), i32),
            pltpu.VMEM((rows, parts, channels), bf16),
            pltpu.VMEM((knots * parts, stations), f32),
            pltpu.VMEM((LANES, LANES), f32),
            pltpu.VMEM((depth, SUB, LANES), bf16),
            pltpu.VMEM((devices,) + block, bf16),
            dma((9 + PARTS + 2 * devices,)),
        ],
        compiler_params=most,
        name="pack_rows",
    )(
        turn,
        owner,
        row_owner.reshape(1, rows),
        row_slot.reshape(1, rows),
        visibilities,
        coarse,
        weights,
        offset,
        pairs,
    )


    def ready(own):
        return pl.pallas_call(
            ready_kernel,
            out_shape=[
                shape(own.shape, bf16),
                shape((parts, LANES, channels), bf16),
                shape((parts, LANES, channels), bf16),
                shape((SUB, LANES), i32),
            ],
            in_specs=[vmem, anywhere],
            out_specs=[vmem] * 4,
            scratch_shapes=[dma],
            compiler_params=some,
            name="make_ready",
        )(sent[-1], own)

    def swap(array, x):
        return lax.ppermute(array, "bl", [(d, d ^ x) for d in range(devices)])

    if halves:
        own, high, low, ints = ready(sent[0])
        arrived = {x: swap(sent[x], x) if x else own for x in range(devices)}
        order, late = schedule(near)
        even = list(range(near, devices, 2))
        collected = pl.pallas_call(
            functools.partial(collect_kernel, rows_at, depth),
            out_shape=shape((len(even) * depth, parts, LANES), bf16),
            in_specs=[anywhere] * len(even),
            out_specs=vmem,
            scratch_shapes=[dma((len(even),))],
            compiler_params=some,
            name="collect_gains",
        )(*[arrived[x] for x in even])
        passed = [swap(collected, 1)]
    else:
        arrived = {
            0: lax.all_gather(sent[1], "bl", axis=0),
            1: lax.all_to_all(sent[0], "bl", split_axis=0, concat_axis=0, tiled=True),
        }
        order, late, passed = [0], [1], []
        _, high, low, ints = ready(sent[1])

    gains, recip, slots, sums = pl.pallas_call(
        functools.partial(middle_kernel, capacity, near, stations, order),
        out_shape=(
            shape((parts, 2 * owned, channels), f32),
            shape((owned, LANES), f32),
            shape((devices, LANES), i32),
            shape((chunks, owned, parts, LANES), f32),
        ),
        in_specs=[smem] * 3 + [vmem] * (2 + len(order) + len(passed)),
        out_specs=(vmem,) * 4,
        scratch_shapes=[
            pltpu.VMEM((devices, gain_tiles * SUB, LANES), f32),
            pltpu.VMEM((2 * owned, LANES), f32),
            pltpu.VMEM((devices, LANES), f32),
            pltpu.VMEM((devices, LANES), f32),
            pltpu.VMEM((devices, LANES), i32),
            pltpu.SMEM((devices, LANES), i32),
            pltpu.VMEM((chunks, owned + 1, parts, LANES), f32),
            pltpu.VMEM((chunks, owned + 1, parts, LANES), f32),
            dma,
        ],
        compiler_params=some,
        name="gains_and_sums",
    )(turn, me, ints, high, low, *[arrived[x] for x in order], *passed)
    return pl.pallas_call(
        functools.partial(finish_kernel, capacity, late),
        out_shape=shape((owned, parts, channels), bf16),
        in_specs=[smem] + [vmem] * (3 + len(late)),
        out_specs=hbm,
        scratch_shapes=[
            pltpu.VMEM((chunks, owned, parts, LANES), f32),
            pltpu.VMEM((chunks, owned, parts, LANES), f32),
            pltpu.VMEM((chunks, owned, parts, LANES), bf16),
            dma((chunks,)),
        ],
        compiler_params=some,
        name="sum_and_apply",
    )(slots, gains, recip, sums, *[arrived[x] for x in late])


def solution(mesh):
    placed = (
        P(("groups", "bl"), None, None),
        P(("groups", "bl"), None),
        P(("groups", "bl")),
        P("bl", None),
        P(("groups", "bl"), None, None),
        P("groups", None),
        P("groups"),
    )
    return jax.shard_map(
        on_device,
        mesh=mesh,
        in_specs=placed,
        out_specs=P(("groups", "bl"), None, None),
        check_vma=False,
    )
```

```python
import functools

import jax
import jax.numpy as jnp
from jax import lax
from jax.experimental import pallas as pl
from jax.experimental.pallas import tpu as pltpu
from jax.sharding import PartitionSpec as P

LANES = 128
SUB = 8
USED = 48
PARTS = 4
ALL_VMEM = 60 * 1024 * 1024
SOME_VMEM = 24 * 1024 * 1024


def round_up(value, unit):
    return -(-value // unit) * unit


def schedule(near):
    even, odd = list(range(near, 2 * near, 2)), list(range(near + 1, 2 * near, 2))
    close = list(range(near // 2, near)) + list(range(1, near // 2))
    cross, late = even[2:] + odd[1:-2], odd[-2:]
    order = [0] + even[:2] + close[:2]
    close = close[2:]
    while cross:
        order += cross[:1] + close[:1]
        cross, close = cross[1:], close[1:]
    return order + close + odd[:1], late


def with_gains(near):
    return list(range(near)) + list(range(near, 2 * near, 2))


def start_all(pairs, sems):
    moves = [pltpu.make_async_copy(src, dst, sems.at[i]) for i, (src, dst) in enumerate(pairs)]
    for move in moves:
        move.start()
    return moves


def pack_kernel(
    capacity,
    near,
    me_s,
    owner_hbm,
    owner_row_hbm,
    slot_row_hbm,
    vis_hbm,
    coarse_hbm,
    weights_hbm,
    offset_hbm,
    pairs_hbm,
    *rest,
):
    outs = rest[:-16]
    (
        weights_ref,
        offset_ref,
        pairs_ref,
        small_ref,
        parts_ref,
        owner_s,
        place_s,
        count_s,
        owner_ref,
        slot_ref,
        vis_ref,
        coarse_ref,
        turn_ref,
        meta_ref,
        block_ref,
        sems,
    ) = rest[-16:]
    rows = vis_ref.shape[0]
    chunks = vis_ref.shape[2] // LANES
    devices = block_ref.shape[0]
    terms, stations = coarse_ref.shape
    half = stations // 2
    depth = meta_ref.shape[0]
    gain_tiles = (depth - 1) // 2
    span = rows // PARTS
    moves = start_all(
        (
            (owner_hbm, owner_s),
            (coarse_hbm, coarse_ref),
            (owner_row_hbm, owner_ref),
            (slot_row_hbm, slot_ref),
            (weights_hbm, weights_ref),
            (offset_hbm, offset_ref),
            (pairs_hbm, pairs_ref),
        ),
        sems,
    )
    fetches = start_all(
        [
            (vis_hbm.at[pl.ds(i * span, span)], vis_ref.at[pl.ds(i * span, span)])
            for i in range(PARTS)
        ],
        sems.at[pl.ds(len(moves), PARTS)],
    )
    turn_ref[...] = jnp.zeros_like(turn_ref)
    for d in range(devices):
        count_s[d] = 0
    me = me_s[0]
    moves[0].wait()

    def rank(r, carry):
        x = owner_s[r] ^ me
        k = count_s[x]
        count_s[x] = k + 1
        place_s[r] = x * capacity + k
        return carry

    lax.fori_loop(0, rows, rank, 0, unroll=8)
    for move in moves[1:]:
        move.wait()

    turn_ref[0:terms, 0:half] = coarse_ref[:, 0:half]
    turn_ref[64 : 64 + terms, 0:half] = coarse_ref[:, half:stations]
    gains = turn_ref[...].T
    high = gains.astype(jnp.bfloat16)
    low = (gains - high.astype(jnp.float32)).astype(jnp.bfloat16)
    for i in range(gain_tiles):
        meta_ref[i] = high[i * SUB : (i + 1) * SUB, :]
        meta_ref[gain_tiles + i] = low[i * SUB : (i + 1) * SUB, :]
    sub = lax.broadcasted_iota(jnp.int32, (SUB, LANES), 0)
    codes = jnp.where(sub == 0, owner_ref[...], slot_ref[...])
    meta_ref[2 * gain_tiles] = codes.astype(jnp.float32).astype(jnp.bfloat16)
    steps = weights_ref.shape[0]
    small_ref[...] = jnp.zeros_like(small_ref)
    small_ref[0:steps, :] = weights_ref[...]
    for c in range(chunks):
        lanes = slice(c * LANES, (c + 1) * LANES)
        small_ref[steps : steps + 1, lanes] = offset_ref[c : c + 1, :].astype(jnp.float32)
    small_ref[4:6, 0 : pairs_ref.shape[1]] = pairs_ref[...].astype(jnp.float32)
    left = small_ref[...]
    for p in range(3):
        piece = left.astype(jnp.bfloat16)
        left = left - piece.astype(jnp.float32)
        for c in range(chunks):
            parts_ref[p * chunks + c] = piece[:, c * LANES : (c + 1) * LANES]

    at = chunks * capacity
    if near > 1:
        pairs = [(meta_ref, outs[x].at[pl.ds(at, depth)]) for x in with_gains(near)]
    else:
        pairs = [(meta_ref, outs[1])]
    at_small = at + depth if near > 1 else 0
    pairs += [(parts_ref, outs[0 if near > 1 else -1].at[pl.ds(at_small, 3 * chunks)])]
    start = len(moves) + PARTS
    sends = start_all(pairs, sems.at[pl.ds(start, len(pairs))])
    start += len(pairs)

    def place(r, carry):
        p = place_s[r]
        for c in range(chunks):
            flat_ref[p * chunks + c] = vis_ref[r, :, c * LANES : (c + 1) * LANES]
        return carry

    flat_ref = block_ref.reshape(devices * at, SUB, LANES)
    for i in range(PARTS):
        fetches[i].wait()
        lax.fori_loop(i * span, (i + 1) * span, place, 0, unroll=8)
    if near > 1:
        pairs = [(block_ref.at[x], outs[x].at[pl.ds(0, at)]) for x in range(devices)]
    else:
        pairs = [(block_ref, outs[0])]
    sends += start_all(pairs, sems.at[pl.ds(start, len(pairs))])
    for send in sends:
        send.wait()


def ready_kernel(
    at, chunks, owned, stations, trows, turn_s, own_ref, own_out_ref, choice_ref, basis_ref, sem
):
    move = pltpu.make_async_copy(own_ref, own_out_ref, sem)
    move.start()
    pieces = [
        jnp.concatenate(
            [own_ref[at + p * chunks + c].astype(jnp.float32) for c in range(chunks)], axis=1
        )
        for p in range(3)
    ]
    small = pieces[0] + pieces[1] + pieces[2]
    channels = small.shape[1]
    half = stations // 2

    station = small[4:6, 0:LANES]
    sender = jnp.floor((station + 0.5) * (1.0 / stations))
    within = station - sender * stations
    second = (within >= float(half)).astype(jnp.float32)
    line = (sender.astype(jnp.int32) ^ turn_s[0]).astype(jnp.float32) * trows + within - second * half
    diagonal = lax.broadcasted_iota(jnp.int32, (owned, LANES), 0) == lax.broadcasted_iota(
        jnp.int32, (owned, LANES), 1
    )

    def upright(row):
        return jnp.sum(jnp.where(diagonal, row, 0.0), axis=1, keepdims=True)

    lines = jnp.concatenate([upright(line[side : side + 1]) for side in range(2)], axis=0)
    seconds = jnp.concatenate([upright(second[side : side + 1]) for side in range(2)], axis=0)
    table = choice_ref.shape[1]
    same = lines == lax.broadcasted_iota(jnp.int32, (2 * owned, table), 1).astype(jnp.float32)
    for h in range(2):
        choice_ref[2 * owned * h : 2 * owned * (h + 1), :] = (
            jnp.where(jnp.logical_and(same, seconds == float(h)), 1.0, 0.0).astype(jnp.bfloat16)
        )

    index = lax.broadcasted_iota(jnp.int32, (64, channels), 0)
    knot = (index >> 3).astype(jnp.float32)
    basis = jnp.zeros((64, channels), jnp.float32)
    for step in range(3):
        basis = basis + jnp.where(knot == small[3:4, :] + float(step), small[step : step + 1, :], 0.0)
    high = basis.astype(jnp.bfloat16).astype(jnp.float32)
    component = index & 7
    for j in range(8):
        cols = slice(j * channels, (j + 1) * channels)
        main = jnp.where(component == j, high, 0.0).astype(jnp.bfloat16)
        rest = jnp.where(component == j, basis - high, 0.0).astype(jnp.bfloat16)
        basis_ref[0:64, cols] = main
        basis_ref[64:128, cols] = main
        basis_ref[128:192, cols] = rest
        basis_ref[192:256, cols] = jnp.zeros_like(rest)
    move.wait()


def collect_kernel(at, depth, *rest):
    blocks, (out_ref, sems) = rest[:-2], rest[-2:]
    moves = start_all(
        [
            (block.at[pl.ds(at, depth)], out_ref.at[pl.ds(i * depth, depth)])
            for i, block in enumerate(blocks)
        ],
        sems,
    )
    for move in moves:
        move.wait()


def list_rows(owner, slot, target, capacity, spare):
    senders = owner.shape[0]
    mine = owner == target
    counted = mine.astype(jnp.float32)
    before = lax.broadcasted_iota(jnp.int32, (LANES, LANES), 0) < lax.broadcasted_iota(
        jnp.int32, (LANES, LANES), 1
    )
    rank = jnp.dot(
        counted.astype(jnp.bfloat16),
        before.astype(jnp.float32).astype(jnp.bfloat16),
        preferred_element_type=jnp.float32,
    )
    lane = lax.broadcasted_iota(jnp.int32, (senders, LANES), 1)
    count = jnp.sum(counted, axis=1, keepdims=True)
    listing = jnp.where(lane == capacity, count, 0.0)
    for k in range(capacity):
        here = jnp.logical_and(mine, rank == float(k))
        kth = jnp.sum(jnp.where(here, slot, 0.0), axis=1, keepdims=True)
        kth = jnp.where(count > float(k), kth, float(spare))
        listing = jnp.where(lane == k, kth, listing)
    return listing.astype(jnp.int32), mine


def add_rows(acc_refs, slots_s, line, capacity, rows_ref):
    chunks, several = acc_refs[0].shape[0], len(acc_refs)

    def add(i, carry):
        for u, acc_ref in enumerate(acc_refs):
            k = several * i + u
            b = slots_s[line, k]
            for c in range(chunks):
                acc_ref[c, b] += rows_ref[chunks * k + c].astype(jnp.float32)
        return carry

    lax.fori_loop(0, (slots_s[line, capacity] + several - 1) // several, add, 0)


def add_table(table_ref, x, block, at, depth):
    gain_tiles = (depth - 1) // 2
    for i in range(gain_tiles):
        rows = slice((x * gain_tiles + i) * SUB, (x * gain_tiles + i + 1) * SUB)
        table_ref[rows, 0:LANES] = block[at + i].astype(jnp.float32)
        table_ref[rows, LANES : 2 * LANES] = block[at + gain_tiles + i].astype(jnp.float32)
    return block[at + 2 * gain_tiles].astype(jnp.float32)


def count_rows(hits, mine, slot):
    which = lax.broadcasted_iota(jnp.int32, hits.shape, 0).astype(jnp.float32)
    slot = jnp.where(mine, slot, -1.0)
    for x in range(slot.shape[0]):
        hits = hits + (slot[x : x + 1, :] == which).astype(jnp.float32)
    return hits


def middle_kernel(capacity, near, depth, order, me_s, choice_ref, basis_ref, *rest):
    arrived, passed = dict(zip(order, rest)), rest[len(order) : -12]
    gains_ref, recip_ref, slots_ref, sums_ref = rest[-12:-8]
    table_ref, owner_ref, slot_ref, slots_v, slots_s, one_ref, two_ref, sem = rest[-8:]
    devices = owner_ref.shape[0]
    owned = recip_ref.shape[0]
    chunks = sums_ref.shape[0]
    for x in range(devices):
        if near == 1:
            code = add_table(table_ref, x, arrived[0].at[x], 0, depth)
        elif x in with_gains(near):
            code = add_table(table_ref, x, arrived[x], chunks * capacity, depth)
        else:
            code = add_table(table_ref, x, passed[0], (x - near) // 2 * depth, depth)
        owner_ref[x : x + 1, :] = code[0:1, :]
        slot_ref[x : x + 1, :] = code[1:2, :]
    slot = slot_ref[...]
    listing, mine = list_rows(
        owner_ref[...], slot, me_s[0].astype(jnp.float32), capacity, owned
    )
    slots_ref[...] = listing
    slots_v[...] = listing
    move = pltpu.make_async_copy(slots_v, slots_s, sem)
    move.start()
    hits = count_rows(jnp.zeros((owned, LANES), jnp.float32), mine, slot)
    tally = jnp.sum(hits, axis=1, keepdims=True)
    recip_ref[...] = jnp.broadcast_to(1.0 / jnp.maximum(tally, 1.0), recip_ref.shape)

    picked = jnp.dot(
        choice_ref[...], table_ref[...].astype(jnp.bfloat16), preferred_element_type=jnp.float32
    )
    front, back = picked[0 : 2 * owned], picked[2 * owned : 4 * owned]
    lower = lax.broadcasted_iota(jnp.int32, (2 * owned, LANES), 1) < 64
    high = front[:, 0:LANES] + pltpu.roll(back[:, 0:LANES], 64, 1)
    low = pltpu.roll(front[:, LANES:], 64, 1) + back[:, LANES:]
    coarse = jnp.concatenate([jnp.where(lower, high, low), jnp.where(lower, high, 0.0)], axis=1)
    coarse = coarse.astype(jnp.bfloat16)
    width = 2 * LANES * chunks
    for n in range(0, basis_ref.shape[1], width):
        fine = jnp.dot(coarse, basis_ref[:, n : n + width], preferred_element_type=jnp.float32)
        gains_ref[:, n : n + width] = fine.astype(jnp.bfloat16).astype(jnp.float32)

    one_ref[...] = jnp.zeros_like(one_ref)
    two_ref[...] = jnp.zeros_like(two_ref)
    move.wait()
    if near > 1:
        for x in order:
            add_rows((one_ref, two_ref), slots_s, x, capacity, arrived[x])
    sums_ref[...] = one_ref[:, 0:owned] + two_ref[:, 0:owned]


def finish_kernel(capacity, late, slots_s, gains_ref, recip_ref, sums_ref, *rest):
    far = rest[: len(late)]
    out_hbm, acc_ref, res_ref, out_ref, sems = rest[len(late) :]
    owned, parts, channels = out_hbm.shape
    chunks = channels // LANES
    acc_ref[...] = sums_ref[...]
    if len(late) > 1:
        for x, rows_ref in zip(late, far):
            add_rows((acc_ref,), slots_s, x, capacity, rows_ref)
    else:

        def from_device(d, carry):
            add_rows((acc_ref,), slots_s, d, capacity, far[0].at[d])
            return carry

        lax.fori_loop(0, far[0].shape[0], from_device, 0)

    flat = acc_ref.reshape(chunks * owned * parts, LANES)
    done = res_ref.reshape(chunks * owned * parts, LANES)
    sends = []
    for c in range(chunks):
        for b0 in range(0, owned, SUB):
            scale = recip_ref[b0 : b0 + SUB, :]
            row = (c * owned + b0) * parts
            vis = [flat[pl.ds(row + j, SUB, stride=parts), :] for j in range(parts)]
            planes = [slice(j * channels + c * LANES, j * channels + (c + 1) * LANES) for j in range(parts)]
            lhs = [gains_ref[b0 : b0 + SUB, plane] for plane in planes]
            rhs = [gains_ref[owned + b0 : owned + b0 + SUB, plane] for plane in planes]
            mid_re, mid_im = [], []
            for row_a in range(2):
                for col_b in range(2):
                    re = im = 0.0
                    for inner in range(2):
                        lr, li = lhs[2 * row_a + inner], lhs[4 + 2 * row_a + inner]
                        vr, vi = vis[2 * inner + col_b], vis[4 + 2 * inner + col_b]
                        re = re + lr * vr - li * vi
                        im = im + lr * vi + li * vr
                    mid_re.append(re * scale)
                    mid_im.append(im * scale)
            for row_a in range(2):
                for col_b in range(2):
                    re = im = 0.0
                    for inner in range(2):
                        mr, mi = mid_re[2 * row_a + inner], mid_im[2 * row_a + inner]
                        rr, ri = rhs[2 * col_b + inner], rhs[4 + 2 * col_b + inner]
                        re = re + mr * rr + mi * ri
                        im = im + mi * rr - mr * ri
                    j = 2 * row_a + col_b
                    done[pl.ds(row + j, SUB, stride=parts), :] = re
                    done[pl.ds(row + 4 + j, SUB, stride=parts), :] = im
        out_ref[c] = res_ref[c].astype(out_ref.dtype)
        sends.append(
            pltpu.make_async_copy(
                out_ref.at[c], out_hbm.at[:, :, pl.ds(c * LANES, LANES)], sems.at[c]
            )
        )
        sends[-1].start()
    for send in sends:
        send.wait()


def on_device(
    visibilities,
    row_owner,
    row_slot,
    baseline_station_pairs,
    gains_coarse,
    band_weights,
    band_offset,
):
    devices = lax.axis_size("bl")
    rows, parts, channels = visibilities.shape
    capacity = 2 * rows // devices
    owned = baseline_station_pairs.shape[0]
    stations, _, knots = gains_coarse.shape
    chunks = channels // LANES
    gain_tiles = round_up(stations // 2, SUB) // SUB
    depth = 2 * gain_tiles + 1
    near = devices // 2 if devices <= 16 else 1
    halves = near > 1
    f32, bf16, i32 = jnp.float32, jnp.bfloat16, jnp.int32
    vmem = pl.BlockSpec(memory_space=pltpu.VMEM)
    smem = pl.BlockSpec(memory_space=pltpu.SMEM)
    hbm = pl.BlockSpec(memory_space=pltpu.HBM)
    anywhere = pl.BlockSpec(memory_space=pl.ANY)
    most = pltpu.CompilerParams(vmem_limit_bytes=ALL_VMEM)
    some = pltpu.CompilerParams(vmem_limit_bytes=SOME_VMEM)
    shape = jax.ShapeDtypeStruct
    dma = pltpu.SemaphoreType.DMA

    me = lax.axis_index("bl").astype(i32).reshape(1)
    turn = me if halves else jnp.zeros_like(me)
    owner = row_owner.reshape(rows)
    coarse = gains_coarse.transpose(2, 1, 0).reshape(knots * parts, stations)
    block = (chunks * capacity, parts, LANES)
    rows_at = chunks * capacity
    if halves:
        long = with_gains(near) + [near + 3]
        outs = [
            shape((rows_at + (depth if x in long else 0), parts, LANES), bf16)
            for x in range(devices)
        ]
        outs[0] = shape((rows_at + depth + 3 * chunks, parts, LANES), bf16)
    else:
        outs = [
            shape((devices,) + block, bf16),
            shape((depth, SUB, LANES), bf16),
            shape((3 * chunks, SUB, LANES), bf16),
        ]
    pairs = baseline_station_pairs.T
    weights = band_weights.T
    offset = band_offset.reshape(chunks, LANES)
    sent = pl.pallas_call(
        functools.partial(pack_kernel, capacity, near),
        out_shape=outs,
        in_specs=[smem] + [hbm] * 8,
        out_specs=[hbm] * len(outs),
        scratch_shapes=[
            pltpu.VMEM(weights.shape, f32),
            pltpu.VMEM(offset.shape, i32),
            pltpu.VMEM(pairs.shape, i32),
            pltpu.VMEM((SUB, channels), f32),
            pltpu.VMEM((3 * chunks, SUB, LANES), bf16),
            pltpu.SMEM((rows,), i32),
            pltpu.SMEM((rows,), i32),
            pltpu.SMEM((devices,), i32),
            pltpu.VMEM((1, rows), i32),
            pltpu.VMEM((1, rows), i32),
            pltpu.VMEM((rows, parts, channels), bf16),
            pltpu.VMEM((knots * parts, stations), f32),
            pltpu.VMEM((LANES, LANES), f32),
            pltpu.VMEM((depth, SUB, LANES), bf16),
            pltpu.VMEM((devices,) + block, bf16),
            dma((9 + PARTS + 2 * devices,)),
        ],
        compiler_params=most,
        name="pack_rows",
    )(
        turn,
        owner,
        row_owner.reshape(1, rows),
        row_slot.reshape(1, rows),
        visibilities,
        coarse,
        weights,
        offset,
        pairs,
    )


    trows = gain_tiles * SUB

    def ready(own, at):
        return pl.pallas_call(
            functools.partial(ready_kernel, at, chunks, owned, stations, trows),
            out_shape=[
                shape(own.shape, bf16),
                shape((4 * owned, devices * trows), bf16),
                shape((2 * LANES, parts * channels), bf16),
            ],
            in_specs=[smem, vmem],
            out_specs=[vmem] * 3,
            scratch_shapes=[dma],
            compiler_params=some,
            name="make_ready",
        )(turn, own)

    def swap(array, x):
        return lax.ppermute(array, "bl", [(d, d ^ x) for d in range(devices)])

    if halves:
        own, choice, basis = ready(sent[0], rows_at + depth)
        arrived = {x: swap(sent[x], x) if x else own for x in range(devices)}
        order, late = schedule(near)
        even = list(range(near, devices, 2))
        collected = pl.pallas_call(
            functools.partial(collect_kernel, rows_at, depth),
            out_shape=shape((len(even) * depth, parts, LANES), bf16),
            in_specs=[anywhere] * len(even),
            out_specs=vmem,
            scratch_shapes=[dma((len(even),))],
            compiler_params=some,
            name="collect_gains",
        )(*[arrived[x] for x in even])
        passed = [swap(collected, 1)]
    else:
        arrived = {
            0: lax.all_gather(sent[1], "bl", axis=0),
            1: lax.all_to_all(sent[0], "bl", split_axis=0, concat_axis=0, tiled=True),
        }
        order, late, passed = [0], [1], []
        _, choice, basis = ready(sent[2], 0)

    gains, recip, slots, sums = pl.pallas_call(
        functools.partial(middle_kernel, capacity, near, depth, order),
        out_shape=(
            shape((2 * owned, parts * channels), f32),
            shape((owned, LANES), f32),
            shape((devices, LANES), i32),
            shape((chunks, owned, parts, LANES), f32),
        ),
        in_specs=[smem] + [vmem] * (2 + len(order) + len(passed)),
        out_specs=(vmem,) * 4,
        scratch_shapes=[
            pltpu.VMEM((devices * trows, 2 * LANES), f32),
            pltpu.VMEM((devices, LANES), f32),
            pltpu.VMEM((devices, LANES), f32),
            pltpu.VMEM((devices, LANES), i32),
            pltpu.SMEM((devices, LANES), i32),
            pltpu.VMEM((chunks, owned + 1, parts, LANES), f32),
            pltpu.VMEM((chunks, owned + 1, parts, LANES), f32),
            dma,
        ],
        compiler_params=some,
        name="gains_and_sums",
    )(me, choice, basis, *[arrived[x] for x in order], *passed)
    return pl.pallas_call(
        functools.partial(finish_kernel, capacity, late),
        out_shape=shape((owned, parts, channels), bf16),
        in_specs=[smem] + [vmem] * (3 + len(late)),
        out_specs=hbm,
        scratch_shapes=[
            pltpu.VMEM((chunks, owned, parts, LANES), f32),
            pltpu.VMEM((chunks, owned, parts, LANES), f32),
            pltpu.VMEM((chunks, owned, parts, LANES), bf16),
            dma((chunks,)),
        ],
        compiler_params=some,
        name="sum_and_apply",
    )(slots, gains, recip, sums, *[arrived[x] for x in late])


def solution(mesh):
    placed = (
        P(("groups", "bl"), None, None),
        P(("groups", "bl"), None),
        P(("groups", "bl")),
        P("bl", None),
        P(("groups", "bl"), None, None),
        P("groups", None),
        P("groups"),
    )
    return jax.shard_map(
        on_device,
        mesh=mesh,
        in_specs=placed,
        out_specs=P(("groups", "bl"), None, None),
        check_vma=False,
    )
```

```python
import functools

import jax
import jax.numpy as jnp
from jax import lax
from jax.experimental import pallas as pl
from jax.experimental.pallas import tpu as pltpu
from jax.sharding import PartitionSpec as P

LANES = 128
SUB = 8
USED = 48
PARTS = 4
ALL_VMEM = 60 * 1024 * 1024
SOME_VMEM = 24 * 1024 * 1024


def round_up(value, unit):
    return -(-value // unit) * unit


def schedule(near):
    even, odd = list(range(near, 2 * near, 2)), list(range(near + 1, 2 * near, 2))
    close = list(range(near // 2, near)) + list(range(1, near // 2))
    order = [0] + even[:3] + close[:2] + even[3:] + close[2:4] + odd[1:-2] + close[4:] + odd[:1]
    return order, odd[-2:]


def with_gains(near):
    return list(range(near)) + list(range(near, 2 * near, 2))


def start_all(pairs, sems):
    moves = [pltpu.make_async_copy(src, dst, sems.at[i]) for i, (src, dst) in enumerate(pairs)]
    for move in moves:
        move.start()
    return moves


def pack_kernel(
    capacity,
    near,
    me_s,
    owner_hbm,
    owner_row_hbm,
    slot_row_hbm,
    vis_hbm,
    coarse_hbm,
    weights_hbm,
    offset_hbm,
    pairs_hbm,
    *rest,
):
    outs = rest[:-16]
    (
        weights_ref,
        offset_ref,
        pairs_ref,
        small_ref,
        parts_ref,
        owner_s,
        place_s,
        count_s,
        owner_ref,
        slot_ref,
        vis_ref,
        coarse_ref,
        turn_ref,
        meta_ref,
        block_ref,
        sems,
    ) = rest[-16:]
    rows = vis_ref.shape[0]
    chunks = vis_ref.shape[2] // LANES
    devices = block_ref.shape[0]
    terms, stations = coarse_ref.shape
    half = stations // 2
    depth = meta_ref.shape[0]
    gain_tiles = (depth - 1) // 2
    span = rows // PARTS
    moves = start_all(
        (
            (owner_hbm, owner_s),
            (coarse_hbm, coarse_ref),
            (owner_row_hbm, owner_ref),
            (slot_row_hbm, slot_ref),
            (weights_hbm, weights_ref),
            (offset_hbm, offset_ref),
            (pairs_hbm, pairs_ref),
        ),
        sems,
    )
    fetches = start_all(
        [
            (vis_hbm.at[pl.ds(i * span, span)], vis_ref.at[pl.ds(i * span, span)])
            for i in range(PARTS)
        ],
        sems.at[pl.ds(len(moves), PARTS)],
    )
    turn_ref[...] = jnp.zeros_like(turn_ref)
    for d in range(devices):
        count_s[d] = 0
    me = me_s[0]
    moves[0].wait()

    def rank(r, carry):
        x = owner_s[r] ^ me
        k = count_s[x]
        count_s[x] = k + 1
        place_s[r] = x * capacity + k
        return carry

    lax.fori_loop(0, rows, rank, 0, unroll=8)
    for move in moves[1:]:
        move.wait()

    turn_ref[0:terms, 0:half] = coarse_ref[:, 0:half]
    turn_ref[64 : 64 + terms, 0:half] = coarse_ref[:, half:stations]
    gains = turn_ref[...].T
    high = gains.astype(jnp.bfloat16)
    low = (gains - high.astype(jnp.float32)).astype(jnp.bfloat16)
    for i in range(gain_tiles):
        meta_ref[i] = high[i * SUB : (i + 1) * SUB, :]
        meta_ref[gain_tiles + i] = low[i * SUB : (i + 1) * SUB, :]
    sub = lax.broadcasted_iota(jnp.int32, (SUB, LANES), 0)
    codes = jnp.where(sub == 0, owner_ref[...], slot_ref[...])
    meta_ref[2 * gain_tiles] = codes.astype(jnp.float32).astype(jnp.bfloat16)
    steps = weights_ref.shape[0]
    small_ref[...] = jnp.zeros_like(small_ref)
    small_ref[0:steps, :] = weights_ref[...]
    for c in range(chunks):
        lanes = slice(c * LANES, (c + 1) * LANES)
        small_ref[steps : steps + 1, lanes] = offset_ref[c : c + 1, :].astype(jnp.float32)
    small_ref[4:6, 0 : pairs_ref.shape[1]] = pairs_ref[...].astype(jnp.float32)
    left = small_ref[...]
    for p in range(3):
        piece = left.astype(jnp.bfloat16)
        left = left - piece.astype(jnp.float32)
        for c in range(chunks):
            parts_ref[p * chunks + c] = piece[:, c * LANES : (c + 1) * LANES]

    at = chunks * capacity
    if near > 1:
        pairs = [(meta_ref, outs[x].at[pl.ds(at, depth)]) for x in with_gains(near)]
    else:
        pairs = [(meta_ref, outs[1])]
    at_small = at + depth if near > 1 else 0
    pairs += [(parts_ref, outs[0 if near > 1 else -1].at[pl.ds(at_small, 3 * chunks)])]
    start = len(moves) + PARTS
    sends = start_all(pairs, sems.at[pl.ds(start, len(pairs))])
    start += len(pairs)

    def place(r, carry):
        p = place_s[r]
        for c in range(chunks):
            flat_ref[p * chunks + c] = vis_ref[r, :, c * LANES : (c + 1) * LANES]
        return carry

    flat_ref = block_ref.reshape(devices * at, SUB, LANES)
    for i in range(PARTS):
        fetches[i].wait()
        lax.fori_loop(i * span, (i + 1) * span, place, 0, unroll=8)
    if near > 1:
        pairs = [(block_ref.at[x], outs[x].at[pl.ds(0, at)]) for x in range(devices)]
    else:
        pairs = [(block_ref, outs[0])]
    sends += start_all(pairs, sems.at[pl.ds(start, len(pairs))])
    for send in sends:
        send.wait()


def ready_kernel(
    at, chunks, owned, stations, trows, turn_s, own_ref, own_out_ref, choice_ref, basis_ref, sem
):
    move = pltpu.make_async_copy(own_ref, own_out_ref, sem)
    move.start()
    pieces = [
        jnp.concatenate(
            [own_ref[at + p * chunks + c].astype(jnp.float32) for c in range(chunks)], axis=1
        )
        for p in range(3)
    ]
    small = pieces[0] + pieces[1] + pieces[2]
    channels = small.shape[1]
    half = stations // 2

    station = small[4:6, 0:LANES]
    sender = jnp.floor((station + 0.5) * (1.0 / stations))
    within = station - sender * stations
    second = (within >= float(half)).astype(jnp.float32)
    line = (sender.astype(jnp.int32) ^ turn_s[0]).astype(jnp.float32) * trows + within - second * half
    diagonal = lax.broadcasted_iota(jnp.int32, (owned, LANES), 0) == lax.broadcasted_iota(
        jnp.int32, (owned, LANES), 1
    )

    def upright(row):
        return jnp.sum(jnp.where(diagonal, row, 0.0), axis=1, keepdims=True)

    lines = jnp.concatenate([upright(line[side : side + 1]) for side in range(2)], axis=0)
    seconds = jnp.concatenate([upright(second[side : side + 1]) for side in range(2)], axis=0)
    table = choice_ref.shape[1]
    same = lines == lax.broadcasted_iota(jnp.int32, (2 * owned, table), 1).astype(jnp.float32)
    for h in range(2):
        choice_ref[2 * owned * h : 2 * owned * (h + 1), :] = (
            jnp.where(jnp.logical_and(same, seconds == float(h)), 1.0, 0.0).astype(jnp.bfloat16)
        )

    index = lax.broadcasted_iota(jnp.int32, (64, channels), 0)
    knot = (index >> 3).astype(jnp.float32)
    basis = jnp.zeros((64, channels), jnp.float32)
    for step in range(3):
        basis = basis + jnp.where(knot == small[3:4, :] + float(step), small[step : step + 1, :], 0.0)
    high = basis.astype(jnp.bfloat16).astype(jnp.float32)
    component = index & 7
    for j in range(8):
        cols = slice(j * channels, (j + 1) * channels)
        main = jnp.where(component == j, high, 0.0).astype(jnp.bfloat16)
        rest = jnp.where(component == j, basis - high, 0.0).astype(jnp.bfloat16)
        basis_ref[0:64, cols] = main
        basis_ref[64:128, cols] = main
        basis_ref[128:192, cols] = rest
        basis_ref[192:256, cols] = jnp.zeros_like(rest)
    move.wait()


def collect_kernel(at, depth, *rest):
    blocks, (out_ref, sems) = rest[:-2], rest[-2:]
    moves = start_all(
        [
            (block.at[pl.ds(at, depth)], out_ref.at[pl.ds(i * depth, depth)])
            for i, block in enumerate(blocks)
        ],
        sems,
    )
    for move in moves:
        move.wait()


def list_rows(owner, slot, target, capacity, spare):
    senders = owner.shape[0]
    mine = owner == target
    counted = mine.astype(jnp.float32)
    before = lax.broadcasted_iota(jnp.int32, (LANES, LANES), 0) < lax.broadcasted_iota(
        jnp.int32, (LANES, LANES), 1
    )
    rank = jnp.dot(
        counted.astype(jnp.bfloat16),
        before.astype(jnp.float32).astype(jnp.bfloat16),
        preferred_element_type=jnp.float32,
    )
    lane = lax.broadcasted_iota(jnp.int32, (senders, LANES), 1)
    count = jnp.sum(counted, axis=1, keepdims=True)
    listing = jnp.where(lane == capacity, count, 0.0)
    for k in range(capacity):
        here = jnp.logical_and(mine, rank == float(k))
        kth = jnp.sum(jnp.where(here, slot, 0.0), axis=1, keepdims=True)
        kth = jnp.where(count > float(k), kth, float(spare))
        listing = jnp.where(lane == k, kth, listing)
    return listing.astype(jnp.int32), mine


def add_rows(acc_refs, slots_s, line, capacity, rows_ref):
    chunks, several = acc_refs[0].shape[0], len(acc_refs)

    def add(i, carry):
        for u, acc_ref in enumerate(acc_refs):
            k = several * i + u
            b = slots_s[line, k]
            for c in range(chunks):
                acc_ref[c, b] += rows_ref[chunks * k + c].astype(jnp.float32)
        return carry

    lax.fori_loop(0, (slots_s[line, capacity] + several - 1) // several, add, 0)


def add_table(table_ref, x, block, at, depth):
    gain_tiles = (depth - 1) // 2
    for i in range(gain_tiles):
        rows = slice((x * gain_tiles + i) * SUB, (x * gain_tiles + i + 1) * SUB)
        table_ref[rows, 0:LANES] = block[at + i].astype(jnp.float32)
        table_ref[rows, LANES : 2 * LANES] = block[at + gain_tiles + i].astype(jnp.float32)
    return block[at + 2 * gain_tiles].astype(jnp.float32)


def count_rows(hits, mine, slot):
    which = lax.broadcasted_iota(jnp.int32, hits.shape, 0).astype(jnp.float32)
    slot = jnp.where(mine, slot, -1.0)
    for x in range(slot.shape[0]):
        hits = hits + (slot[x : x + 1, :] == which).astype(jnp.float32)
    return hits


def middle_kernel(capacity, near, depth, order, me_s, choice_ref, basis_ref, *rest):
    arrived, passed = dict(zip(order, rest)), rest[len(order) : -12]
    gains_ref, recip_ref, slots_ref, sums_ref = rest[-12:-8]
    table_ref, owner_ref, slot_ref, slots_v, slots_s, one_ref, two_ref, sem = rest[-8:]
    devices = owner_ref.shape[0]
    owned = recip_ref.shape[0]
    chunks = sums_ref.shape[0]
    for x in range(devices):
        if near == 1:
            code = add_table(table_ref, x, arrived[0].at[x], 0, depth)
        elif x in with_gains(near):
            code = add_table(table_ref, x, arrived[x], chunks * capacity, depth)
        else:
            code = add_table(table_ref, x, passed[0], (x - near) // 2 * depth, depth)
        owner_ref[x : x + 1, :] = code[0:1, :]
        slot_ref[x : x + 1, :] = code[1:2, :]
    slot = slot_ref[...]
    listing, mine = list_rows(
        owner_ref[...], slot, me_s[0].astype(jnp.float32), capacity, owned
    )
    slots_ref[...] = listing
    slots_v[...] = listing
    move = pltpu.make_async_copy(slots_v, slots_s, sem)
    move.start()
    hits = count_rows(jnp.zeros((owned, LANES), jnp.float32), mine, slot)
    tally = jnp.sum(hits, axis=1, keepdims=True)
    recip_ref[...] = jnp.broadcast_to(1.0 / jnp.maximum(tally, 1.0), recip_ref.shape)

    picked = jnp.dot(
        choice_ref[...], table_ref[...].astype(jnp.bfloat16), preferred_element_type=jnp.float32
    )
    front, back = picked[0 : 2 * owned], picked[2 * owned : 4 * owned]
    lower = lax.broadcasted_iota(jnp.int32, (2 * owned, LANES), 1) < 64
    high = front[:, 0:LANES] + pltpu.roll(back[:, 0:LANES], 64, 1)
    low = pltpu.roll(front[:, LANES:], 64, 1) + back[:, LANES:]
    coarse = jnp.concatenate([jnp.where(lower, high, low), jnp.where(lower, high, 0.0)], axis=1)
    coarse = coarse.astype(jnp.bfloat16)
    width = 2 * LANES * chunks
    for n in range(0, basis_ref.shape[1], width):
        fine = jnp.dot(coarse, basis_ref[:, n : n + width], preferred_element_type=jnp.float32)
        gains_ref[:, n : n + width] = fine.astype(jnp.bfloat16).astype(jnp.float32)

    one_ref[...] = jnp.zeros_like(one_ref)
    two_ref[...] = jnp.zeros_like(two_ref)
    move.wait()
    if near > 1:
        for x in order:
            add_rows((one_ref, two_ref), slots_s, x, capacity, arrived[x])
    sums_ref[...] = one_ref[:, 0:owned] + two_ref[:, 0:owned]


def finish_kernel(capacity, late, slots_s, gains_ref, recip_ref, sums_ref, *rest):
    far = rest[: len(late)]
    out_hbm, acc_ref, res_ref, out_ref, sems = rest[len(late) :]
    owned, parts, channels = out_hbm.shape
    chunks = channels // LANES
    acc_ref[...] = sums_ref[...]
    if len(late) > 1:
        for x, rows_ref in zip(late, far):
            add_rows((acc_ref,), slots_s, x, capacity, rows_ref)
    else:

        def from_device(d, carry):
            add_rows((acc_ref,), slots_s, d, capacity, far[0].at[d])
            return carry

        lax.fori_loop(0, far[0].shape[0], from_device, 0)

    flat = acc_ref.reshape(chunks * owned * parts, LANES)
    done = res_ref.reshape(chunks * owned * parts, LANES)
    sends = []
    for c in range(chunks):
        for b0 in range(0, owned, SUB):
            scale = recip_ref[b0 : b0 + SUB, :]
            row = (c * owned + b0) * parts
            vis = [flat[pl.ds(row + j, SUB, stride=parts), :] for j in range(parts)]
            planes = [slice(j * channels + c * LANES, j * channels + (c + 1) * LANES) for j in range(parts)]
            lhs = [gains_ref[b0 : b0 + SUB, plane] for plane in planes]
            rhs = [gains_ref[owned + b0 : owned + b0 + SUB, plane] for plane in planes]
            mid_re, mid_im = [], []
            for row_a in range(2):
                for col_b in range(2):
                    re = im = 0.0
                    for inner in range(2):
                        lr, li = lhs[2 * row_a + inner], lhs[4 + 2 * row_a + inner]
                        vr, vi = vis[2 * inner + col_b], vis[4 + 2 * inner + col_b]
                        re = re + lr * vr - li * vi
                        im = im + lr * vi + li * vr
                    mid_re.append(re * scale)
                    mid_im.append(im * scale)
            for row_a in range(2):
                for col_b in range(2):
                    re = im = 0.0
                    for inner in range(2):
                        mr, mi = mid_re[2 * row_a + inner], mid_im[2 * row_a + inner]
                        rr, ri = rhs[2 * col_b + inner], rhs[4 + 2 * col_b + inner]
                        re = re + mr * rr + mi * ri
                        im = im + mi * rr - mr * ri
                    j = 2 * row_a + col_b
                    done[pl.ds(row + j, SUB, stride=parts), :] = re
                    done[pl.ds(row + 4 + j, SUB, stride=parts), :] = im
        out_ref[c] = res_ref[c].astype(out_ref.dtype)
        sends.append(
            pltpu.make_async_copy(
                out_ref.at[c], out_hbm.at[:, :, pl.ds(c * LANES, LANES)], sems.at[c]
            )
        )
        sends[-1].start()
    for send in sends:
        send.wait()


def on_device(
    visibilities,
    row_owner,
    row_slot,
    baseline_station_pairs,
    gains_coarse,
    band_weights,
    band_offset,
):
    devices = lax.axis_size("bl")
    rows, parts, channels = visibilities.shape
    capacity = 2 * rows // devices
    owned = baseline_station_pairs.shape[0]
    stations, _, knots = gains_coarse.shape
    chunks = channels // LANES
    gain_tiles = round_up(stations // 2, SUB) // SUB
    depth = 2 * gain_tiles + 1
    near = devices // 2 if devices <= 16 else 1
    halves = near > 1
    f32, bf16, i32 = jnp.float32, jnp.bfloat16, jnp.int32
    vmem = pl.BlockSpec(memory_space=pltpu.VMEM)
    smem = pl.BlockSpec(memory_space=pltpu.SMEM)
    hbm = pl.BlockSpec(memory_space=pltpu.HBM)
    anywhere = pl.BlockSpec(memory_space=pl.ANY)
    most = pltpu.CompilerParams(vmem_limit_bytes=ALL_VMEM)
    some = pltpu.CompilerParams(vmem_limit_bytes=SOME_VMEM)
    shape = jax.ShapeDtypeStruct
    dma = pltpu.SemaphoreType.DMA

    me = lax.axis_index("bl").astype(i32).reshape(1)
    turn = me if halves else jnp.zeros_like(me)
    owner = row_owner.reshape(rows)
    coarse = gains_coarse.transpose(2, 1, 0).reshape(knots * parts, stations)
    block = (chunks * capacity, parts, LANES)
    rows_at = chunks * capacity
    if halves:
        long = with_gains(near) + [near + 3]
        outs = [
            shape((rows_at + (depth if x in long else 0), parts, LANES), bf16)
            for x in range(devices)
        ]
        outs[0] = shape((rows_at + depth + 3 * chunks, parts, LANES), bf16)
    else:
        outs = [
            shape((devices,) + block, bf16),
            shape((depth, SUB, LANES), bf16),
            shape((3 * chunks, SUB, LANES), bf16),
        ]
    pairs = baseline_station_pairs.T
    weights = band_weights.T
    offset = band_offset.reshape(chunks, LANES)
    sent = pl.pallas_call(
        functools.partial(pack_kernel, capacity, near),
        out_shape=outs,
        in_specs=[smem] + [hbm] * 8,
        out_specs=[hbm] * len(outs),
        scratch_shapes=[
            pltpu.VMEM(weights.shape, f32),
            pltpu.VMEM(offset.shape, i32),
            pltpu.VMEM(pairs.shape, i32),
            pltpu.VMEM((SUB, channels), f32),
            pltpu.VMEM((3 * chunks, SUB, LANES), bf16),
            pltpu.SMEM((rows,), i32),
            pltpu.SMEM((rows,), i32),
            pltpu.SMEM((devices,), i32),
            pltpu.VMEM((1, rows), i32),
            pltpu.VMEM((1, rows), i32),
            pltpu.VMEM((rows, parts, channels), bf16),
            pltpu.VMEM((knots * parts, stations), f32),
            pltpu.VMEM((LANES, LANES), f32),
            pltpu.VMEM((depth, SUB, LANES), bf16),
            pltpu.VMEM((devices,) + block, bf16),
            dma((9 + PARTS + 2 * devices,)),
        ],
        compiler_params=most,
        name="pack_rows",
    )(
        turn,
        owner,
        row_owner.reshape(1, rows),
        row_slot.reshape(1, rows),
        visibilities,
        coarse,
        weights,
        offset,
        pairs,
    )


    trows = gain_tiles * SUB

    def ready(own, at):
        return pl.pallas_call(
            functools.partial(ready_kernel, at, chunks, owned, stations, trows),
            out_shape=[
                shape(own.shape, bf16),
                shape((4 * owned, devices * trows), bf16),
                shape((2 * LANES, parts * channels), bf16),
            ],
            in_specs=[smem, vmem],
            out_specs=[vmem] * 3,
            scratch_shapes=[dma],
            compiler_params=some,
            name="make_ready",
        )(turn, own)

    def swap(array, x):
        return lax.ppermute(array, "bl", [(d, d ^ x) for d in range(devices)])

    if halves:
        own, choice, basis = ready(sent[0], rows_at + depth)
        arrived = {x: swap(sent[x], x) if x else own for x in range(devices)}
        order, late = schedule(near)
        even = list(range(near, devices, 2))
        collected = pl.pallas_call(
            functools.partial(collect_kernel, rows_at, depth),
            out_shape=shape((len(even) * depth, parts, LANES), bf16),
            in_specs=[anywhere] * len(even),
            out_specs=vmem,
            scratch_shapes=[dma((len(even),))],
            compiler_params=some,
            name="collect_gains",
        )(*[arrived[x] for x in even])
        passed = [swap(collected, 1)]
    else:
        arrived = {
            0: lax.all_gather(sent[1], "bl", axis=0),
            1: lax.all_to_all(sent[0], "bl", split_axis=0, concat_axis=0, tiled=True),
        }
        order, late, passed = [0], [1], []
        _, choice, basis = ready(sent[2], 0)

    gains, recip, slots, sums = pl.pallas_call(
        functools.partial(middle_kernel, capacity, near, depth, order),
        out_shape=(
            shape((2 * owned, parts * channels), f32),
            shape((owned, LANES), f32),
            shape((devices, LANES), i32),
            shape((chunks, owned, parts, LANES), f32),
        ),
        in_specs=[smem] + [vmem] * (2 + len(order) + len(passed)),
        out_specs=(vmem,) * 4,
        scratch_shapes=[
            pltpu.VMEM((devices * trows, 2 * LANES), f32),
            pltpu.VMEM((devices, LANES), f32),
            pltpu.VMEM((devices, LANES), f32),
            pltpu.VMEM((devices, LANES), i32),
            pltpu.SMEM((devices, LANES), i32),
            pltpu.VMEM((chunks, owned + 1, parts, LANES), f32),
            pltpu.VMEM((chunks, owned + 1, parts, LANES), f32),
            dma,
        ],
        compiler_params=some,
        name="gains_and_sums",
    )(me, choice, basis, *[arrived[x] for x in order], *passed)
    return pl.pallas_call(
        functools.partial(finish_kernel, capacity, late),
        out_shape=shape((owned, parts, channels), bf16),
        in_specs=[smem] + [vmem] * (3 + len(late)),
        out_specs=hbm,
        scratch_shapes=[
            pltpu.VMEM((chunks, owned, parts, LANES), f32),
            pltpu.VMEM((chunks, owned, parts, LANES), f32),
            pltpu.VMEM((chunks, owned, parts, LANES), bf16),
            dma((chunks,)),
        ],
        compiler_params=some,
        name="sum_and_apply",
    )(slots, gains, recip, sums, *[arrived[x] for x in late])


def solution(mesh):
    placed = (
        P(("groups", "bl"), None, None),
        P(("groups", "bl"), None),
        P(("groups", "bl")),
        P("bl", None),
        P(("groups", "bl"), None, None),
        P("groups", None),
        P("groups"),
    )
    return jax.shard_map(
        on_device,
        mesh=mesh,
        in_specs=placed,
        out_specs=P(("groups", "bl"), None, None),
        check_vma=False,
    )
```

```python
import functools

import jax
import jax.numpy as jnp
from jax import lax
from jax.experimental import pallas as pl
from jax.experimental.pallas import tpu as pltpu
from jax.sharding import PartitionSpec as P

LANES = 128
SUB = 8
USED = 48
PARTS = 4
ALL_VMEM = 60 * 1024 * 1024
SOME_VMEM = 24 * 1024 * 1024


def round_up(value, unit):
    return -(-value // unit) * unit


def schedule(near):
    even, odd = list(range(near, 2 * near, 2)), list(range(near + 1, 2 * near, 2))
    close = list(range(near // 2, near)) + list(range(1, near // 2))
    order = [0] + even[:1] + close[:3] + even[1:3] + close[3:6] + even[3:] + odd[1:-2] + close[6:]
    return order + odd[:1], odd[-2:]


def with_gains(near):
    return list(range(near)) + list(range(near, 2 * near, 2))


def start_all(pairs, sems):
    moves = [pltpu.make_async_copy(src, dst, sems.at[i]) for i, (src, dst) in enumerate(pairs)]
    for move in moves:
        move.start()
    return moves


def pack_kernel(
    capacity,
    near,
    me_s,
    owner_hbm,
    owner_row_hbm,
    slot_row_hbm,
    vis_hbm,
    coarse_hbm,
    weights_hbm,
    offset_hbm,
    pairs_hbm,
    *rest,
):
    outs = rest[:-16]
    (
        weights_ref,
        offset_ref,
        pairs_ref,
        small_ref,
        parts_ref,
        owner_s,
        place_s,
        count_s,
        owner_ref,
        slot_ref,
        vis_ref,
        coarse_ref,
        turn_ref,
        meta_ref,
        block_ref,
        sems,
    ) = rest[-16:]
    rows = vis_ref.shape[0]
    chunks = vis_ref.shape[2] // LANES
    devices = block_ref.shape[0]
    terms, stations = coarse_ref.shape
    half = stations // 2
    depth = meta_ref.shape[0]
    gain_tiles = (depth - 1) // 2
    span = rows // PARTS
    moves = start_all(
        (
            (owner_hbm, owner_s),
            (coarse_hbm, coarse_ref),
            (owner_row_hbm, owner_ref),
            (slot_row_hbm, slot_ref),
            (weights_hbm, weights_ref),
            (offset_hbm, offset_ref),
            (pairs_hbm, pairs_ref),
        ),
        sems,
    )
    fetches = start_all(
        [
            (vis_hbm.at[pl.ds(i * span, span)], vis_ref.at[pl.ds(i * span, span)])
            for i in range(PARTS)
        ],
        sems.at[pl.ds(len(moves), PARTS)],
    )
    turn_ref[...] = jnp.zeros_like(turn_ref)
    for d in range(devices):
        count_s[d] = 0
    me = me_s[0]
    moves[0].wait()

    def rank(r, carry):
        x = owner_s[r] ^ me
        k = count_s[x]
        count_s[x] = k + 1
        place_s[r] = x * capacity + k
        return carry

    lax.fori_loop(0, rows, rank, 0, unroll=8)
    for move in moves[1:]:
        move.wait()

    turn_ref[0:terms, 0:half] = coarse_ref[:, 0:half]
    turn_ref[64 : 64 + terms, 0:half] = coarse_ref[:, half:stations]
    gains = turn_ref[...].T
    high = gains.astype(jnp.bfloat16)
    low = (gains - high.astype(jnp.float32)).astype(jnp.bfloat16)
    for i in range(gain_tiles):
        meta_ref[i] = high[i * SUB : (i + 1) * SUB, :]
        meta_ref[gain_tiles + i] = low[i * SUB : (i + 1) * SUB, :]
    sub = lax.broadcasted_iota(jnp.int32, (SUB, LANES), 0)
    codes = jnp.where(sub == 0, owner_ref[...], slot_ref[...])
    meta_ref[2 * gain_tiles] = codes.astype(jnp.float32).astype(jnp.bfloat16)
    steps = weights_ref.shape[0]
    small_ref[...] = jnp.zeros_like(small_ref)
    small_ref[0:steps, :] = weights_ref[...]
    for c in range(chunks):
        lanes = slice(c * LANES, (c + 1) * LANES)
        small_ref[steps : steps + 1, lanes] = offset_ref[c : c + 1, :].astype(jnp.float32)
    small_ref[4:6, 0 : pairs_ref.shape[1]] = pairs_ref[...].astype(jnp.float32)
    left = small_ref[...]
    for p in range(3):
        piece = left.astype(jnp.bfloat16)
        left = left - piece.astype(jnp.float32)
        for c in range(chunks):
            parts_ref[p * chunks + c] = piece[:, c * LANES : (c + 1) * LANES]

    at = chunks * capacity
    if near > 1:
        pairs = [(meta_ref, outs[x].at[pl.ds(at, depth)]) for x in with_gains(near)]
    else:
        pairs = [(meta_ref, outs[1])]
    at_small = at + depth if near > 1 else 0
    pairs += [(parts_ref, outs[0 if near > 1 else -1].at[pl.ds(at_small, 3 * chunks)])]
    start = len(moves) + PARTS
    sends = start_all(pairs, sems.at[pl.ds(start, len(pairs))])
    start += len(pairs)

    def place(r, carry):
        p = place_s[r]
        for c in range(chunks):
            flat_ref[p * chunks + c] = vis_ref[r, :, c * LANES : (c + 1) * LANES]
        return carry

    flat_ref = block_ref.reshape(devices * at, SUB, LANES)
    for i in range(PARTS):
        fetches[i].wait()
        lax.fori_loop(i * span, (i + 1) * span, place, 0, unroll=8)
    if near > 1:
        pairs = [(block_ref.at[x], outs[x].at[pl.ds(0, at)]) for x in range(devices)]
    else:
        pairs = [(block_ref, outs[0])]
    sends += start_all(pairs, sems.at[pl.ds(start, len(pairs))])
    for send in sends:
        send.wait()


def ready_kernel(
    at, chunks, owned, stations, trows, turn_s, own_ref, own_out_ref, choice_ref, basis_ref, sem
):
    move = pltpu.make_async_copy(own_ref, own_out_ref, sem)
    move.start()
    pieces = [
        jnp.concatenate(
            [own_ref[at + p * chunks + c].astype(jnp.float32) for c in range(chunks)], axis=1
        )
        for p in range(3)
    ]
    small = pieces[0] + pieces[1] + pieces[2]
    channels = small.shape[1]
    half = stations // 2

    station = small[4:6, 0:LANES]
    sender = jnp.floor((station + 0.5) * (1.0 / stations))
    within = station - sender * stations
    second = (within >= float(half)).astype(jnp.float32)
    line = (sender.astype(jnp.int32) ^ turn_s[0]).astype(jnp.float32) * trows + within - second * half
    diagonal = lax.broadcasted_iota(jnp.int32, (owned, LANES), 0) == lax.broadcasted_iota(
        jnp.int32, (owned, LANES), 1
    )

    def upright(row):
        return jnp.sum(jnp.where(diagonal, row, 0.0), axis=1, keepdims=True)

    lines = jnp.concatenate([upright(line[side : side + 1]) for side in range(2)], axis=0)
    seconds = jnp.concatenate([upright(second[side : side + 1]) for side in range(2)], axis=0)
    table = choice_ref.shape[1]
    same = lines == lax.broadcasted_iota(jnp.int32, (2 * owned, table), 1).astype(jnp.float32)
    for h in range(2):
        choice_ref[2 * owned * h : 2 * owned * (h + 1), :] = (
            jnp.where(jnp.logical_and(same, seconds == float(h)), 1.0, 0.0).astype(jnp.bfloat16)
        )

    index = lax.broadcasted_iota(jnp.int32, (64, channels), 0)
    knot = (index >> 3).astype(jnp.float32)
    basis = jnp.zeros((64, channels), jnp.float32)
    for step in range(3):
        basis = basis + jnp.where(knot == small[3:4, :] + float(step), small[step : step + 1, :], 0.0)
    high = basis.astype(jnp.bfloat16).astype(jnp.float32)
    component = index & 7
    for j in range(8):
        cols = slice(j * channels, (j + 1) * channels)
        main = jnp.where(component == j, high, 0.0).astype(jnp.bfloat16)
        rest = jnp.where(component == j, basis - high, 0.0).astype(jnp.bfloat16)
        basis_ref[0:64, cols] = main
        basis_ref[64:128, cols] = main
        basis_ref[128:192, cols] = rest
        basis_ref[192:256, cols] = jnp.zeros_like(rest)
    move.wait()


def collect_kernel(at, depth, *rest):
    blocks, (out_ref, sems) = rest[:-2], rest[-2:]
    moves = start_all(
        [
            (block.at[pl.ds(at, depth)], out_ref.at[pl.ds(i * depth, depth)])
            for i, block in enumerate(blocks)
        ],
        sems,
    )
    for move in moves:
        move.wait()


def list_rows(owner, slot, target, capacity, spare):
    senders = owner.shape[0]
    mine = owner == target
    counted = mine.astype(jnp.float32)
    before = lax.broadcasted_iota(jnp.int32, (LANES, LANES), 0) < lax.broadcasted_iota(
        jnp.int32, (LANES, LANES), 1
    )
    rank = jnp.dot(
        counted.astype(jnp.bfloat16),
        before.astype(jnp.float32).astype(jnp.bfloat16),
        preferred_element_type=jnp.float32,
    )
    lane = lax.broadcasted_iota(jnp.int32, (senders, LANES), 1)
    count = jnp.sum(counted, axis=1, keepdims=True)
    listing = jnp.where(lane == capacity, count, 0.0)
    for k in range(capacity):
        here = jnp.logical_and(mine, rank == float(k))
        kth = jnp.sum(jnp.where(here, slot, 0.0), axis=1, keepdims=True)
        kth = jnp.where(count > float(k), kth, float(spare))
        listing = jnp.where(lane == k, kth, listing)
    return listing.astype(jnp.int32), mine


def add_rows(acc_refs, slots_s, line, capacity, rows_ref):
    chunks, several = acc_refs[0].shape[0], len(acc_refs)

    def add(i, carry):
        for u, acc_ref in enumerate(acc_refs):
            k = several * i + u
            b = slots_s[line, k]
            for c in range(chunks):
                acc_ref[c, b] += rows_ref[chunks * k + c].astype(jnp.float32)
        return carry

    lax.fori_loop(0, (slots_s[line, capacity] + several - 1) // several, add, 0)


def add_table(table_ref, x, block, at, depth):
    gain_tiles = (depth - 1) // 2
    for i in range(gain_tiles):
        rows = slice((x * gain_tiles + i) * SUB, (x * gain_tiles + i + 1) * SUB)
        table_ref[rows, 0:LANES] = block[at + i].astype(jnp.float32)
        table_ref[rows, LANES : 2 * LANES] = block[at + gain_tiles + i].astype(jnp.float32)
    return block[at + 2 * gain_tiles].astype(jnp.float32)


def count_rows(hits, mine, slot):
    which = lax.broadcasted_iota(jnp.int32, hits.shape, 0).astype(jnp.float32)
    slot = jnp.where(mine, slot, -1.0)
    for x in range(slot.shape[0]):
        hits = hits + (slot[x : x + 1, :] == which).astype(jnp.float32)
    return hits


def middle_kernel(capacity, near, depth, order, me_s, choice_ref, basis_ref, *rest):
    arrived, passed = dict(zip(order, rest)), rest[len(order) : -12]
    gains_ref, recip_ref, slots_ref, sums_ref = rest[-12:-8]
    table_ref, owner_ref, slot_ref, slots_v, slots_s, one_ref, two_ref, sem = rest[-8:]
    devices = owner_ref.shape[0]
    owned = recip_ref.shape[0]
    chunks = sums_ref.shape[0]
    for x in range(devices):
        if near == 1:
            code = add_table(table_ref, x, arrived[0].at[x], 0, depth)
        elif x in with_gains(near):
            code = add_table(table_ref, x, arrived[x], chunks * capacity, depth)
        else:
            code = add_table(table_ref, x, passed[0], (x - near) // 2 * depth, depth)
        owner_ref[x : x + 1, :] = code[0:1, :]
        slot_ref[x : x + 1, :] = code[1:2, :]
    slot = slot_ref[...]
    listing, mine = list_rows(
        owner_ref[...], slot, me_s[0].astype(jnp.float32), capacity, owned
    )
    slots_ref[...] = listing
    slots_v[...] = listing
    move = pltpu.make_async_copy(slots_v, slots_s, sem)
    move.start()
    hits = count_rows(jnp.zeros((owned, LANES), jnp.float32), mine, slot)
    tally = jnp.sum(hits, axis=1, keepdims=True)
    recip_ref[...] = jnp.broadcast_to(1.0 / jnp.maximum(tally, 1.0), recip_ref.shape)

    picked = jnp.dot(
        choice_ref[...], table_ref[...].astype(jnp.bfloat16), preferred_element_type=jnp.float32
    )
    front, back = picked[0 : 2 * owned], picked[2 * owned : 4 * owned]
    lower = lax.broadcasted_iota(jnp.int32, (2 * owned, LANES), 1) < 64
    high = front[:, 0:LANES] + pltpu.roll(back[:, 0:LANES], 64, 1)
    low = pltpu.roll(front[:, LANES:], 64, 1) + back[:, LANES:]
    coarse = jnp.concatenate([jnp.where(lower, high, low), jnp.where(lower, high, 0.0)], axis=1)
    coarse = coarse.astype(jnp.bfloat16)
    width = 2 * LANES * chunks
    for n in range(0, basis_ref.shape[1], width):
        fine = jnp.dot(coarse, basis_ref[:, n : n + width], preferred_element_type=jnp.float32)
        gains_ref[:, n : n + width] = fine.astype(jnp.bfloat16).astype(jnp.float32)

    one_ref[...] = jnp.zeros_like(one_ref)
    two_ref[...] = jnp.zeros_like(two_ref)
    move.wait()
    if near > 1:
        for x in order:
            add_rows((one_ref, two_ref), slots_s, x, capacity, arrived[x])
    sums_ref[...] = one_ref[:, 0:owned] + two_ref[:, 0:owned]


def finish_kernel(capacity, late, slots_s, gains_ref, recip_ref, sums_ref, *rest):
    far = rest[: len(late)]
    out_hbm, acc_ref, res_ref, out_ref, sems = rest[len(late) :]
    owned, parts, channels = out_hbm.shape
    chunks = channels // LANES
    acc_ref[...] = sums_ref[...]
    if len(late) > 1:
        for x, rows_ref in zip(late, far):
            add_rows((acc_ref,), slots_s, x, capacity, rows_ref)
    else:

        def from_device(d, carry):
            add_rows((acc_ref,), slots_s, d, capacity, far[0].at[d])
            return carry

        lax.fori_loop(0, far[0].shape[0], from_device, 0)

    flat = acc_ref.reshape(chunks * owned * parts, LANES)
    done = res_ref.reshape(chunks * owned * parts, LANES)
    sends = []
    for c in range(chunks):
        for b0 in range(0, owned, SUB):
            scale = recip_ref[b0 : b0 + SUB, :]
            row = (c * owned + b0) * parts
            vis = [flat[pl.ds(row + j, SUB, stride=parts), :] for j in range(parts)]
            planes = [slice(j * channels + c * LANES, j * channels + (c + 1) * LANES) for j in range(parts)]
            lhs = [gains_ref[b0 : b0 + SUB, plane] for plane in planes]
            rhs = [gains_ref[owned + b0 : owned + b0 + SUB, plane] for plane in planes]
            mid_re, mid_im = [], []
            for row_a in range(2):
                for col_b in range(2):
                    re = im = 0.0
                    for inner in range(2):
                        lr, li = lhs[2 * row_a + inner], lhs[4 + 2 * row_a + inner]
                        vr, vi = vis[2 * inner + col_b], vis[4 + 2 * inner + col_b]
                        re = re + lr * vr - li * vi
                        im = im + lr * vi + li * vr
                    mid_re.append(re * scale)
                    mid_im.append(im * scale)
            for row_a in range(2):
                for col_b in range(2):
                    re = im = 0.0
                    for inner in range(2):
                        mr, mi = mid_re[2 * row_a + inner], mid_im[2 * row_a + inner]
                        rr, ri = rhs[2 * col_b + inner], rhs[4 + 2 * col_b + inner]
                        re = re + mr * rr + mi * ri
                        im = im + mi * rr - mr * ri
                    j = 2 * row_a + col_b
                    done[pl.ds(row + j, SUB, stride=parts), :] = re
                    done[pl.ds(row + 4 + j, SUB, stride=parts), :] = im
        out_ref[c] = res_ref[c].astype(out_ref.dtype)
        sends.append(
            pltpu.make_async_copy(
                out_ref.at[c], out_hbm.at[:, :, pl.ds(c * LANES, LANES)], sems.at[c]
            )
        )
        sends[-1].start()
    for send in sends:
        send.wait()


def on_device(
    visibilities,
    row_owner,
    row_slot,
    baseline_station_pairs,
    gains_coarse,
    band_weights,
    band_offset,
):
    devices = lax.axis_size("bl")
    rows, parts, channels = visibilities.shape
    capacity = 2 * rows // devices
    owned = baseline_station_pairs.shape[0]
    stations, _, knots = gains_coarse.shape
    chunks = channels // LANES
    gain_tiles = round_up(stations // 2, SUB) // SUB
    depth = 2 * gain_tiles + 1
    near = devices // 2 if devices <= 16 else 1
    halves = near > 1
    f32, bf16, i32 = jnp.float32, jnp.bfloat16, jnp.int32
    vmem = pl.BlockSpec(memory_space=pltpu.VMEM)
    smem = pl.BlockSpec(memory_space=pltpu.SMEM)
    hbm = pl.BlockSpec(memory_space=pltpu.HBM)
    anywhere = pl.BlockSpec(memory_space=pl.ANY)
    most = pltpu.CompilerParams(vmem_limit_bytes=ALL_VMEM)
    some = pltpu.CompilerParams(vmem_limit_bytes=SOME_VMEM)
    shape = jax.ShapeDtypeStruct
    dma = pltpu.SemaphoreType.DMA

    me = lax.axis_index("bl").astype(i32).reshape(1)
    turn = me if halves else jnp.zeros_like(me)
    owner = row_owner.reshape(rows)
    coarse = gains_coarse.transpose(2, 1, 0).reshape(knots * parts, stations)
    block = (chunks * capacity, parts, LANES)
    rows_at = chunks * capacity
    if halves:
        long = with_gains(near) + [near + 3]
        outs = [
            shape((rows_at + (depth if x in long else 0), parts, LANES), bf16)
            for x in range(devices)
        ]
        outs[0] = shape((rows_at + depth + 3 * chunks, parts, LANES), bf16)
    else:
        outs = [
            shape((devices,) + block, bf16),
            shape((depth, SUB, LANES), bf16),
            shape((3 * chunks, SUB, LANES), bf16),
        ]
    pairs = baseline_station_pairs.T
    weights = band_weights.T
    offset = band_offset.reshape(chunks, LANES)
    sent = pl.pallas_call(
        functools.partial(pack_kernel, capacity, near),
        out_shape=outs,
        in_specs=[smem] + [hbm] * 8,
        out_specs=[hbm] * len(outs),
        scratch_shapes=[
            pltpu.VMEM(weights.shape, f32),
            pltpu.VMEM(offset.shape, i32),
            pltpu.VMEM(pairs.shape, i32),
            pltpu.VMEM((SUB, channels), f32),
            pltpu.VMEM((3 * chunks, SUB, LANES), bf16),
            pltpu.SMEM((rows,), i32),
            pltpu.SMEM((rows,), i32),
            pltpu.SMEM((devices,), i32),
            pltpu.VMEM((1, rows), i32),
            pltpu.VMEM((1, rows), i32),
            pltpu.VMEM((rows, parts, channels), bf16),
            pltpu.VMEM((knots * parts, stations), f32),
            pltpu.VMEM((LANES, LANES), f32),
            pltpu.VMEM((depth, SUB, LANES), bf16),
            pltpu.VMEM((devices,) + block, bf16),
            dma((9 + PARTS + 2 * devices,)),
        ],
        compiler_params=most,
        name="pack_rows",
    )(
        turn,
        owner,
        row_owner.reshape(1, rows),
        row_slot.reshape(1, rows),
        visibilities,
        coarse,
        weights,
        offset,
        pairs,
    )


    trows = gain_tiles * SUB

    def ready(own, at):
        return pl.pallas_call(
            functools.partial(ready_kernel, at, chunks, owned, stations, trows),
            out_shape=[
                shape(own.shape, bf16),
                shape((4 * owned, devices * trows), bf16),
                shape((2 * LANES, parts * channels), bf16),
            ],
            in_specs=[smem, vmem],
            out_specs=[vmem] * 3,
            scratch_shapes=[dma],
            compiler_params=some,
            name="make_ready",
        )(turn, own)

    def swap(array, x):
        return lax.ppermute(array, "bl", [(d, d ^ x) for d in range(devices)])

    if halves:
        own, choice, basis = ready(sent[0], rows_at + depth)
        arrived = {x: swap(sent[x], x) if x else own for x in range(devices)}
        order, late = schedule(near)
        even = list(range(near, devices, 2))
        collected = pl.pallas_call(
            functools.partial(collect_kernel, rows_at, depth),
            out_shape=shape((len(even) * depth, parts, LANES), bf16),
            in_specs=[anywhere] * len(even),
            out_specs=vmem,
            scratch_shapes=[dma((len(even),))],
            compiler_params=some,
            name="collect_gains",
        )(*[arrived[x] for x in even])
        passed = [swap(collected, 1)]
    else:
        arrived = {
            0: lax.all_gather(sent[1], "bl", axis=0),
            1: lax.all_to_all(sent[0], "bl", split_axis=0, concat_axis=0, tiled=True),
        }
        order, late, passed = [0], [1], []
        _, choice, basis = ready(sent[2], 0)

    gains, recip, slots, sums = pl.pallas_call(
        functools.partial(middle_kernel, capacity, near, depth, order),
        out_shape=(
            shape((2 * owned, parts * channels), f32),
            shape((owned, LANES), f32),
            shape((devices, LANES), i32),
            shape((chunks, owned, parts, LANES), f32),
        ),
        in_specs=[smem] + [vmem] * (2 + len(order) + len(passed)),
        out_specs=(vmem,) * 4,
        scratch_shapes=[
            pltpu.VMEM((devices * trows, 2 * LANES), f32),
            pltpu.VMEM((devices, LANES), f32),
            pltpu.VMEM((devices, LANES), f32),
            pltpu.VMEM((devices, LANES), i32),
            pltpu.SMEM((devices, LANES), i32),
            pltpu.VMEM((chunks, owned + 1, parts, LANES), f32),
            pltpu.VMEM((chunks, owned + 1, parts, LANES), f32),
            dma,
        ],
        compiler_params=some,
        name="gains_and_sums",
    )(me, choice, basis, *[arrived[x] for x in order], *passed)
    return pl.pallas_call(
        functools.partial(finish_kernel, capacity, late),
        out_shape=shape((owned, parts, channels), bf16),
        in_specs=[smem] + [vmem] * (3 + len(late)),
        out_specs=hbm,
        scratch_shapes=[
            pltpu.VMEM((chunks, owned, parts, LANES), f32),
            pltpu.VMEM((chunks, owned, parts, LANES), f32),
            pltpu.VMEM((chunks, owned, parts, LANES), bf16),
            dma((chunks,)),
        ],
        compiler_params=some,
        name="sum_and_apply",
    )(slots, gains, recip, sums, *[arrived[x] for x in late])


def solution(mesh):
    placed = (
        P(("groups", "bl"), None, None),
        P(("groups", "bl"), None),
        P(("groups", "bl")),
        P("bl", None),
        P(("groups", "bl"), None, None),
        P("groups", None),
        P("groups"),
    )
    return jax.shard_map(
        on_device,
        mesh=mesh,
        in_specs=placed,
        out_specs=P(("groups", "bl"), None, None),
        check_vma=False,
    )
```

```python
import functools

import jax
import jax.numpy as jnp
from jax import lax
from jax.experimental import pallas as pl
from jax.experimental.pallas import tpu as pltpu
from jax.sharding import PartitionSpec as P

LANES = 128
SUB = 8
USED = 48
PARTS = 4
ALL_VMEM = 60 * 1024 * 1024
SOME_VMEM = 24 * 1024 * 1024


def round_up(value, unit):
    return -(-value // unit) * unit


def schedule(near):
    even, odd = list(range(near, 2 * near, 2)), list(range(near + 1, 2 * near, 2))
    close = list(range(near // 2, near)) + list(range(1, near // 2))
    cross, late = even[2:] + odd[1:-2], odd[-2:]
    order = [0] + even[:2] + close[:2]
    close = close[2:]
    while cross:
        order += cross[:1] + close[:1]
        cross, close = cross[1:], close[1:]
    return order + close + odd[:1], late


def with_gains(near):
    return list(range(near)) + list(range(near, 2 * near, 2))


def start_all(pairs, sems):
    moves = [pltpu.make_async_copy(src, dst, sems.at[i]) for i, (src, dst) in enumerate(pairs)]
    for move in moves:
        move.start()
    return moves


def pack_kernel(
    capacity,
    near,
    me_s,
    owner_hbm,
    owner_row_hbm,
    slot_row_hbm,
    vis_hbm,
    coarse_hbm,
    weights_hbm,
    offset_hbm,
    pairs_hbm,
    *rest,
):
    outs = rest[:-16]
    (
        weights_ref,
        offset_ref,
        pairs_ref,
        small_ref,
        parts_ref,
        owner_s,
        place_s,
        count_s,
        owner_ref,
        slot_ref,
        vis_ref,
        coarse_ref,
        turn_ref,
        meta_ref,
        block_ref,
        sems,
    ) = rest[-16:]
    rows = vis_ref.shape[0]
    chunks = vis_ref.shape[2] // LANES
    devices = block_ref.shape[0]
    terms, stations = coarse_ref.shape
    half = stations // 2
    depth = meta_ref.shape[0]
    gain_tiles = (depth - 1) // 2
    span = rows // PARTS
    moves = start_all(
        (
            (owner_hbm, owner_s),
            (coarse_hbm, coarse_ref),
            (owner_row_hbm, owner_ref),
            (slot_row_hbm, slot_ref),
            (weights_hbm, weights_ref),
            (offset_hbm, offset_ref),
            (pairs_hbm, pairs_ref),
        ),
        sems,
    )
    fetches = start_all(
        [
            (vis_hbm.at[pl.ds(i * span, span)], vis_ref.at[pl.ds(i * span, span)])
            for i in range(PARTS)
        ],
        sems.at[pl.ds(len(moves), PARTS)],
    )
    turn_ref[...] = jnp.zeros_like(turn_ref)
    for d in range(devices):
        count_s[d] = 0
    me = me_s[0]
    moves[0].wait()

    def rank(r, carry):
        x = owner_s[r] ^ me
        k = count_s[x]
        count_s[x] = k + 1
        place_s[r] = x * capacity + k
        return carry

    lax.fori_loop(0, rows, rank, 0, unroll=8)
    for move in moves[1:]:
        move.wait()

    turn_ref[0:terms, 0:half] = coarse_ref[:, 0:half]
    turn_ref[64 : 64 + terms, 0:half] = coarse_ref[:, half:stations]
    gains = turn_ref[...].T
    high = gains.astype(jnp.bfloat16)
    low = (gains - high.astype(jnp.float32)).astype(jnp.bfloat16)
    for i in range(gain_tiles):
        meta_ref[i] = high[i * SUB : (i + 1) * SUB, :]
        meta_ref[gain_tiles + i] = low[i * SUB : (i + 1) * SUB, :]
    sub = lax.broadcasted_iota(jnp.int32, (SUB, LANES), 0)
    codes = jnp.where(sub == 0, owner_ref[...], slot_ref[...])
    meta_ref[2 * gain_tiles] = codes.astype(jnp.float32).astype(jnp.bfloat16)
    steps = weights_ref.shape[0]
    small_ref[...] = jnp.zeros_like(small_ref)
    small_ref[0:steps, :] = weights_ref[...]
    for c in range(chunks):
        lanes = slice(c * LANES, (c + 1) * LANES)
        small_ref[steps : steps + 1, lanes] = offset_ref[c : c + 1, :].astype(jnp.float32)
    small_ref[4:6, 0 : pairs_ref.shape[1]] = pairs_ref[...].astype(jnp.float32)
    left = small_ref[...]
    for p in range(3):
        piece = left.astype(jnp.bfloat16)
        left = left - piece.astype(jnp.float32)
        for c in range(chunks):
            parts_ref[p * chunks + c] = piece[:, c * LANES : (c + 1) * LANES]

    at = chunks * capacity
    if near > 1:
        outs = list(outs[: near + 1]) + [None] + list(outs[near + 1 :])
        pairs = [(meta_ref, outs[x].at[pl.ds(at, depth)]) for x in with_gains(near)]
    else:
        pairs = [(meta_ref, outs[1])]
    at_small = at + depth if near > 1 else 0
    pairs += [(parts_ref, outs[0 if near > 1 else -1].at[pl.ds(at_small, 3 * chunks)])]
    start = len(moves) + PARTS
    sends = start_all(pairs, sems.at[pl.ds(start, len(pairs))])
    start += len(pairs)

    def place(r, carry):
        p = place_s[r]
        for c in range(chunks):
            flat_ref[p * chunks + c] = vis_ref[r, :, c * LANES : (c + 1) * LANES]
        return carry

    flat_ref = block_ref.reshape(devices * at, SUB, LANES)
    for i in range(PARTS):
        fetches[i].wait()
        lax.fori_loop(i * span, (i + 1) * span, place, 0, unroll=8)
    if near > 1:
        pairs = [
            (block_ref.at[x], outs[x].at[pl.ds(0, at)]) for x in range(devices) if x != near + 1
        ]
    else:
        pairs = [(block_ref, outs[0])]
    sends += start_all(pairs, sems.at[pl.ds(start, len(pairs))])
    for send in sends:
        send.wait()


def first_kernel(capacity, target, me_s, owner_hbm, vis_hbm, out_hbm, owner_s, list_s, vis_ref, block_ref, sems):
    rows = vis_ref.shape[0]
    chunks = vis_ref.shape[2] // LANES
    moves = start_all(((owner_hbm, owner_s), (vis_hbm, vis_ref)), sems)
    wanted = me_s[0] ^ target
    moves[0].wait()

    def note(r, k):
        list_s[k] = r
        return k + jnp.where(owner_s[r] == wanted, 1, 0)

    count = lax.fori_loop(0, rows, note, 0, unroll=8)
    moves[1].wait()

    def place(k, carry):
        r = list_s[k]
        for c in range(chunks):
            block_ref[chunks * k + c] = vis_ref[r, :, c * LANES : (c + 1) * LANES]
        return carry

    lax.fori_loop(0, count, place, 0)
    send = start_all([(block_ref, out_hbm)], sems)[0]
    send.wait()


def ready_kernel(
    at, chunks, owned, stations, trows, turn_s, own_ref, own_out_ref, choice_ref, basis_ref, sem
):
    move = pltpu.make_async_copy(own_ref, own_out_ref, sem)
    move.start()
    pieces = [
        jnp.concatenate(
            [own_ref[at + p * chunks + c].astype(jnp.float32) for c in range(chunks)], axis=1
        )
        for p in range(3)
    ]
    small = pieces[0] + pieces[1] + pieces[2]
    channels = small.shape[1]
    half = stations // 2

    station = small[4:6, 0:LANES]
    sender = jnp.floor((station + 0.5) * (1.0 / stations))
    within = station - sender * stations
    second = (within >= float(half)).astype(jnp.float32)
    line = (sender.astype(jnp.int32) ^ turn_s[0]).astype(jnp.float32) * trows + within - second * half
    diagonal = lax.broadcasted_iota(jnp.int32, (owned, LANES), 0) == lax.broadcasted_iota(
        jnp.int32, (owned, LANES), 1
    )

    def upright(row):
        return jnp.sum(jnp.where(diagonal, row, 0.0), axis=1, keepdims=True)

    lines = jnp.concatenate([upright(line[side : side + 1]) for side in range(2)], axis=0)
    seconds = jnp.concatenate([upright(second[side : side + 1]) for side in range(2)], axis=0)
    table = choice_ref.shape[1]
    same = lines == lax.broadcasted_iota(jnp.int32, (2 * owned, table), 1).astype(jnp.float32)
    for h in range(2):
        choice_ref[2 * owned * h : 2 * owned * (h + 1), :] = (
            jnp.where(jnp.logical_and(same, seconds == float(h)), 1.0, 0.0).astype(jnp.bfloat16)
        )

    index = lax.broadcasted_iota(jnp.int32, (64, channels), 0)
    knot = (index >> 3).astype(jnp.float32)
    basis = jnp.zeros((64, channels), jnp.float32)
    for step in range(3):
        basis = basis + jnp.where(knot == small[3:4, :] + float(step), small[step : step + 1, :], 0.0)
    high = basis.astype(jnp.bfloat16).astype(jnp.float32)
    component = index & 7
    for j in range(8):
        cols = slice(j * channels, (j + 1) * channels)
        main = jnp.where(component == j, high, 0.0).astype(jnp.bfloat16)
        rest = jnp.where(component == j, basis - high, 0.0).astype(jnp.bfloat16)
        basis_ref[0:64, cols] = main
        basis_ref[64:128, cols] = main
        basis_ref[128:192, cols] = rest
        basis_ref[192:256, cols] = jnp.zeros_like(rest)
    move.wait()


def collect_kernel(at, depth, *rest):
    blocks, (out_ref, sems) = rest[:-2], rest[-2:]
    moves = start_all(
        [
            (block.at[pl.ds(at, depth)], out_ref.at[pl.ds(i * depth, depth)])
            for i, block in enumerate(blocks)
        ],
        sems,
    )
    for move in moves:
        move.wait()


def list_rows(owner, slot, target, capacity, spare):
    senders = owner.shape[0]
    mine = owner == target
    counted = mine.astype(jnp.float32)
    before = lax.broadcasted_iota(jnp.int32, (LANES, LANES), 0) < lax.broadcasted_iota(
        jnp.int32, (LANES, LANES), 1
    )
    rank = jnp.dot(
        counted.astype(jnp.bfloat16),
        before.astype(jnp.float32).astype(jnp.bfloat16),
        preferred_element_type=jnp.float32,
    )
    lane = lax.broadcasted_iota(jnp.int32, (senders, LANES), 1)
    count = jnp.sum(counted, axis=1, keepdims=True)
    listing = jnp.where(lane == capacity, count, 0.0)
    for k in range(capacity):
        here = jnp.logical_and(mine, rank == float(k))
        kth = jnp.sum(jnp.where(here, slot, 0.0), axis=1, keepdims=True)
        kth = jnp.where(count > float(k), kth, float(spare))
        listing = jnp.where(lane == k, kth, listing)
    return listing.astype(jnp.int32), mine


def add_rows(acc_refs, slots_s, line, capacity, rows_ref):
    chunks, several = acc_refs[0].shape[0], len(acc_refs)

    def add(i, carry):
        for u, acc_ref in enumerate(acc_refs):
            k = several * i + u
            b = slots_s[line, k]
            for c in range(chunks):
                acc_ref[c, b] += rows_ref[chunks * k + c].astype(jnp.float32)
        return carry

    lax.fori_loop(0, (slots_s[line, capacity] + several - 1) // several, add, 0)


def add_table(table_ref, x, block, at, depth):
    gain_tiles = (depth - 1) // 2
    for i in range(gain_tiles):
        rows = slice((x * gain_tiles + i) * SUB, (x * gain_tiles + i + 1) * SUB)
        table_ref[rows, 0:LANES] = block[at + i].astype(jnp.float32)
        table_ref[rows, LANES : 2 * LANES] = block[at + gain_tiles + i].astype(jnp.float32)
    return block[at + 2 * gain_tiles].astype(jnp.float32)


def count_rows(hits, mine, slot):
    which = lax.broadcasted_iota(jnp.int32, hits.shape, 0).astype(jnp.float32)
    slot = jnp.where(mine, slot, -1.0)
    for x in range(slot.shape[0]):
        hits = hits + (slot[x : x + 1, :] == which).astype(jnp.float32)
    return hits


def middle_kernel(capacity, near, depth, order, me_s, choice_ref, basis_ref, *rest):
    arrived, passed = dict(zip(order, rest)), rest[len(order) : -12]
    gains_ref, recip_ref, slots_ref, sums_ref = rest[-12:-8]
    table_ref, owner_ref, slot_ref, slots_v, slots_s, one_ref, two_ref, sem = rest[-8:]
    devices = owner_ref.shape[0]
    owned = recip_ref.shape[0]
    chunks = sums_ref.shape[0]
    for x in range(devices):
        if near == 1:
            code = add_table(table_ref, x, arrived[0].at[x], 0, depth)
        elif x in with_gains(near):
            code = add_table(table_ref, x, arrived[x], chunks * capacity, depth)
        else:
            code = add_table(table_ref, x, passed[0], (x - near) // 2 * depth, depth)
        owner_ref[x : x + 1, :] = code[0:1, :]
        slot_ref[x : x + 1, :] = code[1:2, :]
    slot = slot_ref[...]
    listing, mine = list_rows(
        owner_ref[...], slot, me_s[0].astype(jnp.float32), capacity, owned
    )
    slots_ref[...] = listing
    slots_v[...] = listing
    move = pltpu.make_async_copy(slots_v, slots_s, sem)
    move.start()
    hits = count_rows(jnp.zeros((owned, LANES), jnp.float32), mine, slot)
    tally = jnp.sum(hits, axis=1, keepdims=True)
    recip_ref[...] = jnp.broadcast_to(1.0 / jnp.maximum(tally, 1.0), recip_ref.shape)

    picked = jnp.dot(
        choice_ref[...], table_ref[...].astype(jnp.bfloat16), preferred_element_type=jnp.float32
    )
    front, back = picked[0 : 2 * owned], picked[2 * owned : 4 * owned]
    lower = lax.broadcasted_iota(jnp.int32, (2 * owned, LANES), 1) < 64
    high = front[:, 0:LANES] + pltpu.roll(back[:, 0:LANES], 64, 1)
    low = pltpu.roll(front[:, LANES:], 64, 1) + back[:, LANES:]
    coarse = jnp.concatenate([jnp.where(lower, high, low), jnp.where(lower, high, 0.0)], axis=1)
    coarse = coarse.astype(jnp.bfloat16)
    width = 2 * LANES * chunks
    for n in range(0, basis_ref.shape[1], width):
        fine = jnp.dot(coarse, basis_ref[:, n : n + width], preferred_element_type=jnp.float32)
        gains_ref[:, n : n + width] = fine.astype(jnp.bfloat16).astype(jnp.float32)

    one_ref[...] = jnp.zeros_like(one_ref)
    two_ref[...] = jnp.zeros_like(two_ref)
    move.wait()
    if near > 1:
        for x in order:
            add_rows((one_ref, two_ref), slots_s, x, capacity, arrived[x])
    sums_ref[...] = one_ref[:, 0:owned] + two_ref[:, 0:owned]


def finish_kernel(capacity, late, slots_s, gains_ref, recip_ref, sums_ref, *rest):
    far = rest[: len(late)]
    out_hbm, acc_ref, res_ref, out_ref, sems = rest[len(late) :]
    owned, parts, channels = out_hbm.shape
    chunks = channels // LANES
    acc_ref[...] = sums_ref[...]
    if len(late) > 1:
        for x, rows_ref in zip(late, far):
            add_rows((acc_ref,), slots_s, x, capacity, rows_ref)
    else:

        def from_device(d, carry):
            add_rows((acc_ref,), slots_s, d, capacity, far[0].at[d])
            return carry

        lax.fori_loop(0, far[0].shape[0], from_device, 0)

    flat = acc_ref.reshape(chunks * owned * parts, LANES)
    done = res_ref.reshape(chunks * owned * parts, LANES)
    sends = []
    for c in range(chunks):
        for b0 in range(0, owned, SUB):
            scale = recip_ref[b0 : b0 + SUB, :]
            row = (c * owned + b0) * parts
            vis = [flat[pl.ds(row + j, SUB, stride=parts), :] for j in range(parts)]
            planes = [slice(j * channels + c * LANES, j * channels + (c + 1) * LANES) for j in range(parts)]
            lhs = [gains_ref[b0 : b0 + SUB, plane] for plane in planes]
            rhs = [gains_ref[owned + b0 : owned + b0 + SUB, plane] for plane in planes]
            mid_re, mid_im = [], []
            for row_a in range(2):
                for col_b in range(2):
                    re = im = 0.0
                    for inner in range(2):
                        lr, li = lhs[2 * row_a + inner], lhs[4 + 2 * row_a + inner]
                        vr, vi = vis[2 * inner + col_b], vis[4 + 2 * inner + col_b]
                        re = re + lr * vr - li * vi
                        im = im + lr * vi + li * vr
                    mid_re.append(re * scale)
                    mid_im.append(im * scale)
            for row_a in range(2):
                for col_b in range(2):
                    re = im = 0.0
                    for inner in range(2):
                        mr, mi = mid_re[2 * row_a + inner], mid_im[2 * row_a + inner]
                        rr, ri = rhs[2 * col_b + inner], rhs[4 + 2 * col_b + inner]
                        re = re + mr * rr + mi * ri
                        im = im + mi * rr - mr * ri
                    j = 2 * row_a + col_b
                    done[pl.ds(row + j, SUB, stride=parts), :] = re
                    done[pl.ds(row + 4 + j, SUB, stride=parts), :] = im
        out_ref[c] = res_ref[c].astype(out_ref.dtype)
        sends.append(
            pltpu.make_async_copy(
                out_ref.at[c], out_hbm.at[:, :, pl.ds(c * LANES, LANES)], sems.at[c]
            )
        )
        sends[-1].start()
    for send in sends:
        send.wait()


def on_device(
    visibilities,
    row_owner,
    row_slot,
    baseline_station_pairs,
    gains_coarse,
    band_weights,
    band_offset,
):
    devices = lax.axis_size("bl")
    rows, parts, channels = visibilities.shape
    capacity = 2 * rows // devices
    owned = baseline_station_pairs.shape[0]
    stations, _, knots = gains_coarse.shape
    chunks = channels // LANES
    gain_tiles = round_up(stations // 2, SUB) // SUB
    depth = 2 * gain_tiles + 1
    near = devices // 2 if devices <= 16 else 1
    halves = near > 1
    f32, bf16, i32 = jnp.float32, jnp.bfloat16, jnp.int32
    vmem = pl.BlockSpec(memory_space=pltpu.VMEM)
    smem = pl.BlockSpec(memory_space=pltpu.SMEM)
    hbm = pl.BlockSpec(memory_space=pltpu.HBM)
    anywhere = pl.BlockSpec(memory_space=pl.ANY)
    most = pltpu.CompilerParams(vmem_limit_bytes=ALL_VMEM)
    some = pltpu.CompilerParams(vmem_limit_bytes=SOME_VMEM)
    shape = jax.ShapeDtypeStruct
    dma = pltpu.SemaphoreType.DMA

    me = lax.axis_index("bl").astype(i32).reshape(1)
    turn = me if halves else jnp.zeros_like(me)
    owner = row_owner.reshape(rows)
    coarse = gains_coarse.transpose(2, 1, 0).reshape(knots * parts, stations)
    block = (chunks * capacity, parts, LANES)
    rows_at = chunks * capacity
    if halves:
        long = with_gains(near) + [near + 3]
        outs = [
            shape((rows_at + (depth if x in long else 0), parts, LANES), bf16)
            for x in range(devices)
        ]
        outs[0] = shape((rows_at + depth + 3 * chunks, parts, LANES), bf16)
    else:
        outs = [
            shape((devices,) + block, bf16),
            shape((depth, SUB, LANES), bf16),
            shape((3 * chunks, SUB, LANES), bf16),
        ]
    pairs = baseline_station_pairs.T
    weights = band_weights.T
    offset = band_offset.reshape(chunks, LANES)
    me_owner = row_owner.reshape(rows)
    if halves:
        first = outs.pop(near + 1)
        alone = pl.pallas_call(
            functools.partial(first_kernel, capacity, near + 1),
            out_shape=first,
            in_specs=[smem, hbm, hbm],
            out_specs=hbm,
            scratch_shapes=[
                pltpu.SMEM((rows,), i32),
                pltpu.SMEM((rows + 8,), i32),
                pltpu.VMEM((rows, parts, channels), bf16),
                pltpu.VMEM(first.shape, bf16),
                dma((2,)),
            ],
            compiler_params=most,
            name="pack_first",
        )(me, me_owner, visibilities)
    sent = pl.pallas_call(
        functools.partial(pack_kernel, capacity, near),
        out_shape=outs,
        in_specs=[smem] + [hbm] * 8,
        out_specs=[hbm] * len(outs),
        scratch_shapes=[
            pltpu.VMEM(weights.shape, f32),
            pltpu.VMEM(offset.shape, i32),
            pltpu.VMEM(pairs.shape, i32),
            pltpu.VMEM((SUB, channels), f32),
            pltpu.VMEM((3 * chunks, SUB, LANES), bf16),
            pltpu.SMEM((rows,), i32),
            pltpu.SMEM((rows,), i32),
            pltpu.SMEM((devices,), i32),
            pltpu.VMEM((1, rows), i32),
            pltpu.VMEM((1, rows), i32),
            pltpu.VMEM((rows, parts, channels), bf16),
            pltpu.VMEM((knots * parts, stations), f32),
            pltpu.VMEM((LANES, LANES), f32),
            pltpu.VMEM((depth, SUB, LANES), bf16),
            pltpu.VMEM((devices,) + block, bf16),
            dma((9 + PARTS + 2 * devices,)),
        ],
        compiler_params=most,
        name="pack_rows",
    )(
        turn,
        owner,
        row_owner.reshape(1, rows),
        row_slot.reshape(1, rows),
        visibilities,
        coarse,
        weights,
        offset,
        pairs,
    )


    trows = gain_tiles * SUB

    def ready(own, at):
        return pl.pallas_call(
            functools.partial(ready_kernel, at, chunks, owned, stations, trows),
            out_shape=[
                shape(own.shape, bf16),
                shape((4 * owned, devices * trows), bf16),
                shape((2 * LANES, parts * channels), bf16),
            ],
            in_specs=[smem, vmem],
            out_specs=[vmem] * 3,
            scratch_shapes=[dma],
            compiler_params=some,
            name="make_ready",
        )(turn, own)

    if halves:
        sent = list(sent)
        sent.insert(near + 1, alone)

    def swap(array, x):
        return lax.ppermute(array, "bl", [(d, d ^ x) for d in range(devices)])

    if halves:
        own, choice, basis = ready(sent[0], rows_at + depth)
        arrived = {x: swap(sent[x], x) if x else own for x in range(devices)}
        order, late = schedule(near)
        even = list(range(near, devices, 2))
        collected = pl.pallas_call(
            functools.partial(collect_kernel, rows_at, depth),
            out_shape=shape((len(even) * depth, parts, LANES), bf16),
            in_specs=[anywhere] * len(even),
            out_specs=vmem,
            scratch_shapes=[dma((len(even),))],
            compiler_params=some,
            name="collect_gains",
        )(*[arrived[x] for x in even])
        passed = [swap(collected, 1)]
    else:
        arrived = {
            0: lax.all_gather(sent[1], "bl", axis=0),
            1: lax.all_to_all(sent[0], "bl", split_axis=0, concat_axis=0, tiled=True),
        }
        order, late, passed = [0], [1], []
        _, choice, basis = ready(sent[2], 0)

    gains, recip, slots, sums = pl.pallas_call(
        functools.partial(middle_kernel, capacity, near, depth, order),
        out_shape=(
            shape((2 * owned, parts * channels), f32),
            shape((owned, LANES), f32),
            shape((devices, LANES), i32),
            shape((chunks, owned, parts, LANES), f32),
        ),
        in_specs=[smem] + [vmem] * (2 + len(order) + len(passed)),
        out_specs=(vmem,) * 4,
        scratch_shapes=[
            pltpu.VMEM((devices * trows, 2 * LANES), f32),
            pltpu.VMEM((devices, LANES), f32),
            pltpu.VMEM((devices, LANES), f32),
            pltpu.VMEM((devices, LANES), i32),
            pltpu.SMEM((devices, LANES), i32),
            pltpu.VMEM((chunks, owned + 1, parts, LANES), f32),
            pltpu.VMEM((chunks, owned + 1, parts, LANES), f32),
            dma,
        ],
        compiler_params=some,
        name="gains_and_sums",
    )(me, choice, basis, *[arrived[x] for x in order], *passed)
    return pl.pallas_call(
        functools.partial(finish_kernel, capacity, late),
        out_shape=shape((owned, parts, channels), bf16),
        in_specs=[smem] + [vmem] * (3 + len(late)),
        out_specs=hbm,
        scratch_shapes=[
            pltpu.VMEM((chunks, owned, parts, LANES), f32),
            pltpu.VMEM((chunks, owned, parts, LANES), f32),
            pltpu.VMEM((chunks, owned, parts, LANES), bf16),
            dma((chunks,)),
        ],
        compiler_params=some,
        name="sum_and_apply",
    )(slots, gains, recip, sums, *[arrived[x] for x in late])


def solution(mesh):
    placed = (
        P(("groups", "bl"), None, None),
        P(("groups", "bl"), None),
        P(("groups", "bl")),
        P("bl", None),
        P(("groups", "bl"), None, None),
        P("groups", None),
        P("groups"),
    )
    return jax.shard_map(
        on_device,
        mesh=mesh,
        in_specs=placed,
        out_specs=P(("groups", "bl"), None, None),
        check_vma=False,
    )
```

```python
import functools

import jax
import jax.numpy as jnp
from jax import lax
from jax.experimental import pallas as pl
from jax.experimental.pallas import tpu as pltpu
from jax.sharding import PartitionSpec as P

LANES = 128
SUB = 8
USED = 48
PARTS = 4
ALL_VMEM = 60 * 1024 * 1024
SOME_VMEM = 24 * 1024 * 1024


def round_up(value, unit):
    return -(-value // unit) * unit


def schedule(near):
    even, odd = far(near)
    close = list(range(near // 2, near)) + list(range(1, near // 2))
    order = [0] + even[:2] + close[:2]
    cross, close = even[2:] + odd[1:-2], close[2:]
    while cross:
        order += cross[:1] + close[:1]
        cross, close = cross[1:], close[1:]
    return order + close + odd[:1], odd[-2:]


def far(near):
    spans = list(range(near + near // 2, 2 * near)) + list(range(near, near + near // 2))
    return [x for x in spans if x % 2 == 0], [x for x in spans if x % 2]


def with_gains(near):
    return list(range(near)) + list(range(near, 2 * near, 2))


def start_all(pairs, sems):
    moves = [pltpu.make_async_copy(src, dst, sems.at[i]) for i, (src, dst) in enumerate(pairs)]
    for move in moves:
        move.start()
    return moves


def pack_kernel(
    capacity,
    near,
    me_s,
    owner_hbm,
    owner_row_hbm,
    slot_row_hbm,
    vis_hbm,
    coarse_hbm,
    weights_hbm,
    offset_hbm,
    pairs_hbm,
    *rest,
):
    outs = rest[:-16]
    (
        weights_ref,
        offset_ref,
        pairs_ref,
        small_ref,
        parts_ref,
        owner_s,
        place_s,
        count_s,
        owner_ref,
        slot_ref,
        vis_ref,
        coarse_ref,
        turn_ref,
        meta_ref,
        block_ref,
        sems,
    ) = rest[-16:]
    rows = vis_ref.shape[0]
    chunks = vis_ref.shape[2] // LANES
    devices = block_ref.shape[0]
    terms, stations = coarse_ref.shape
    half = stations // 2
    depth = meta_ref.shape[0]
    gain_tiles = (depth - 1) // 2
    span = rows // PARTS
    moves = start_all(
        (
            (owner_hbm, owner_s),
            (coarse_hbm, coarse_ref),
            (owner_row_hbm, owner_ref),
            (slot_row_hbm, slot_ref),
            (weights_hbm, weights_ref),
            (offset_hbm, offset_ref),
            (pairs_hbm, pairs_ref),
        ),
        sems,
    )
    fetches = start_all(
        [
            (vis_hbm.at[pl.ds(i * span, span)], vis_ref.at[pl.ds(i * span, span)])
            for i in range(PARTS)
        ],
        sems.at[pl.ds(len(moves), PARTS)],
    )
    turn_ref[...] = jnp.zeros_like(turn_ref)
    for d in range(devices):
        count_s[d] = 0
    me = me_s[0]
    moves[0].wait()

    def rank(r, carry):
        x = owner_s[r] ^ me
        k = count_s[x]
        count_s[x] = k + 1
        place_s[r] = x * capacity + k
        return carry

    lax.fori_loop(0, rows, rank, 0, unroll=8)
    for move in moves[1:]:
        move.wait()

    turn_ref[0:terms, 0:half] = coarse_ref[:, 0:half]
    turn_ref[64 : 64 + terms, 0:half] = coarse_ref[:, half:stations]
    gains = turn_ref[...].T
    high = gains.astype(jnp.bfloat16)
    low = (gains - high.astype(jnp.float32)).astype(jnp.bfloat16)
    for i in range(gain_tiles):
        meta_ref[i] = high[i * SUB : (i + 1) * SUB, :]
        meta_ref[gain_tiles + i] = low[i * SUB : (i + 1) * SUB, :]
    sub = lax.broadcasted_iota(jnp.int32, (SUB, LANES), 0)
    codes = jnp.where(sub == 0, owner_ref[...], slot_ref[...])
    meta_ref[2 * gain_tiles] = codes.astype(jnp.float32).astype(jnp.bfloat16)
    steps = weights_ref.shape[0]
    small_ref[...] = jnp.zeros_like(small_ref)
    small_ref[0:steps, :] = weights_ref[...]
    for c in range(chunks):
        lanes = slice(c * LANES, (c + 1) * LANES)
        small_ref[steps : steps + 1, lanes] = offset_ref[c : c + 1, :].astype(jnp.float32)
    small_ref[4:6, 0 : pairs_ref.shape[1]] = pairs_ref[...].astype(jnp.float32)
    left = small_ref[...]
    for p in range(3):
        piece = left.astype(jnp.bfloat16)
        left = left - piece.astype(jnp.float32)
        for c in range(chunks):
            parts_ref[p * chunks + c] = piece[:, c * LANES : (c + 1) * LANES]

    at = chunks * capacity
    if near > 1:
        target = far(near)[1][0]
        outs = list(outs[:target]) + [None] + list(outs[target:])
        pairs = [(meta_ref, outs[x].at[pl.ds(at, depth)]) for x in with_gains(near)]
    else:
        pairs = [(meta_ref, outs[1])]
    at_small = at + depth if near > 1 else 0
    pairs += [(parts_ref, outs[0 if near > 1 else -1].at[pl.ds(at_small, 3 * chunks)])]
    start = len(moves) + PARTS
    sends = start_all(pairs, sems.at[pl.ds(start, len(pairs))])
    start += len(pairs)

    def place(r, carry):
        p = place_s[r]
        for c in range(chunks):
            flat_ref[p * chunks + c] = vis_ref[r, :, c * LANES : (c + 1) * LANES]
        return carry

    flat_ref = block_ref.reshape(devices * at, SUB, LANES)
    for i in range(PARTS):
        fetches[i].wait()
        lax.fori_loop(i * span, (i + 1) * span, place, 0, unroll=8)
    if near > 1:
        pairs = [
            (block_ref.at[x], outs[x].at[pl.ds(0, at)]) for x in range(devices) if x != target
        ]
    else:
        pairs = [(block_ref, outs[0])]
    sends += start_all(pairs, sems.at[pl.ds(start, len(pairs))])
    for send in sends:
        send.wait()


def first_kernel(capacity, target, me_s, owner_hbm, vis_hbm, out_hbm, owner_s, list_s, vis_ref, block_ref, sems):
    rows = vis_ref.shape[0]
    chunks = vis_ref.shape[2] // LANES
    moves = start_all(((owner_hbm, owner_s), (vis_hbm, vis_ref)), sems)
    wanted = me_s[0] ^ target
    moves[0].wait()

    def note(r, k):
        list_s[k] = r
        return k + jnp.where(owner_s[r] == wanted, 1, 0)

    count = lax.fori_loop(0, rows, note, 0, unroll=8)
    moves[1].wait()

    def place(k, carry):
        r = list_s[k]
        for c in range(chunks):
            block_ref[chunks * k + c] = vis_ref[r, :, c * LANES : (c + 1) * LANES]
        return carry

    lax.fori_loop(0, count, place, 0)
    send = start_all([(block_ref, out_hbm)], sems)[0]
    send.wait()


def ready_kernel(
    at, chunks, owned, stations, trows, turn_s, own_ref, own_out_ref, choice_ref, basis_ref, sem
):
    move = pltpu.make_async_copy(own_ref, own_out_ref, sem)
    move.start()
    pieces = [
        jnp.concatenate(
            [own_ref[at + p * chunks + c].astype(jnp.float32) for c in range(chunks)], axis=1
        )
        for p in range(3)
    ]
    small = pieces[0] + pieces[1] + pieces[2]
    channels = small.shape[1]
    half = stations // 2

    station = small[4:6, 0:LANES]
    sender = jnp.floor((station + 0.5) * (1.0 / stations))
    within = station - sender * stations
    second = (within >= float(half)).astype(jnp.float32)
    line = (sender.astype(jnp.int32) ^ turn_s[0]).astype(jnp.float32) * trows + within - second * half
    diagonal = lax.broadcasted_iota(jnp.int32, (owned, LANES), 0) == lax.broadcasted_iota(
        jnp.int32, (owned, LANES), 1
    )

    def upright(row):
        return jnp.sum(jnp.where(diagonal, row, 0.0), axis=1, keepdims=True)

    lines = jnp.concatenate([upright(line[side : side + 1]) for side in range(2)], axis=0)
    seconds = jnp.concatenate([upright(second[side : side + 1]) for side in range(2)], axis=0)
    table = choice_ref.shape[1]
    same = lines == lax.broadcasted_iota(jnp.int32, (2 * owned, table), 1).astype(jnp.float32)
    for h in range(2):
        choice_ref[2 * owned * h : 2 * owned * (h + 1), :] = (
            jnp.where(jnp.logical_and(same, seconds == float(h)), 1.0, 0.0).astype(jnp.bfloat16)
        )

    index = lax.broadcasted_iota(jnp.int32, (64, channels), 0)
    knot = (index >> 3).astype(jnp.float32)
    basis = jnp.zeros((64, channels), jnp.float32)
    for step in range(3):
        basis = basis + jnp.where(knot == small[3:4, :] + float(step), small[step : step + 1, :], 0.0)
    high = basis.astype(jnp.bfloat16).astype(jnp.float32)
    component = index & 7
    for j in range(8):
        cols = slice(j * channels, (j + 1) * channels)
        main = jnp.where(component == j, high, 0.0).astype(jnp.bfloat16)
        rest = jnp.where(component == j, basis - high, 0.0).astype(jnp.bfloat16)
        basis_ref[0:64, cols] = main
        basis_ref[64:128, cols] = main
        basis_ref[128:192, cols] = rest
        basis_ref[192:256, cols] = jnp.zeros_like(rest)
    move.wait()


def collect_kernel(at, depth, *rest):
    blocks, (out_ref, sems) = rest[:-2], rest[-2:]
    moves = start_all(
        [
            (block.at[pl.ds(at, depth)], out_ref.at[pl.ds(i * depth, depth)])
            for i, block in enumerate(blocks)
        ],
        sems,
    )
    for move in moves:
        move.wait()


def list_rows(owner, slot, target, capacity, spare):
    senders = owner.shape[0]
    mine = owner == target
    counted = mine.astype(jnp.float32)
    before = lax.broadcasted_iota(jnp.int32, (LANES, LANES), 0) < lax.broadcasted_iota(
        jnp.int32, (LANES, LANES), 1
    )
    rank = jnp.dot(
        counted.astype(jnp.bfloat16),
        before.astype(jnp.float32).astype(jnp.bfloat16),
        preferred_element_type=jnp.float32,
    )
    lane = lax.broadcasted_iota(jnp.int32, (senders, LANES), 1)
    count = jnp.sum(counted, axis=1, keepdims=True)
    listing = jnp.where(lane == capacity, count, 0.0)
    for k in range(capacity):
        here = jnp.logical_and(mine, rank == float(k))
        kth = jnp.sum(jnp.where(here, slot, 0.0), axis=1, keepdims=True)
        kth = jnp.where(count > float(k), kth, float(spare))
        listing = jnp.where(lane == k, kth, listing)
    return listing.astype(jnp.int32), mine


def add_rows(acc_refs, slots_s, line, capacity, rows_ref):
    chunks, several = acc_refs[0].shape[0], len(acc_refs)

    def add(i, carry):
        for u, acc_ref in enumerate(acc_refs):
            k = several * i + u
            b = slots_s[line, k]
            for c in range(chunks):
                acc_ref[c, b] += rows_ref[chunks * k + c].astype(jnp.float32)
        return carry

    lax.fori_loop(0, (slots_s[line, capacity] + several - 1) // several, add, 0)


def add_table(table_ref, x, block, at, depth):
    gain_tiles = (depth - 1) // 2
    for i in range(gain_tiles):
        rows = slice((x * gain_tiles + i) * SUB, (x * gain_tiles + i + 1) * SUB)
        table_ref[rows, 0:LANES] = block[at + i].astype(jnp.float32)
        table_ref[rows, LANES : 2 * LANES] = block[at + gain_tiles + i].astype(jnp.float32)
    return block[at + 2 * gain_tiles].astype(jnp.float32)


def count_rows(hits, mine, slot):
    which = lax.broadcasted_iota(jnp.int32, hits.shape, 0).astype(jnp.float32)
    slot = jnp.where(mine, slot, -1.0)
    for x in range(slot.shape[0]):
        hits = hits + (slot[x : x + 1, :] == which).astype(jnp.float32)
    return hits


def middle_kernel(capacity, near, depth, order, me_s, choice_ref, basis_ref, *rest):
    arrived, passed = dict(zip(order, rest)), rest[len(order) : -12]
    gains_ref, recip_ref, slots_ref, sums_ref = rest[-12:-8]
    table_ref, owner_ref, slot_ref, slots_v, slots_s, one_ref, two_ref, sem = rest[-8:]
    devices = owner_ref.shape[0]
    owned = recip_ref.shape[0]
    chunks = sums_ref.shape[0]
    for x in range(devices):
        if near == 1:
            code = add_table(table_ref, x, arrived[0].at[x], 0, depth)
        elif x in with_gains(near):
            code = add_table(table_ref, x, arrived[x], chunks * capacity, depth)
        else:
            code = add_table(table_ref, x, passed[0], (x - near) // 2 * depth, depth)
        owner_ref[x : x + 1, :] = code[0:1, :]
        slot_ref[x : x + 1, :] = code[1:2, :]
    slot = slot_ref[...]
    listing, mine = list_rows(
        owner_ref[...], slot, me_s[0].astype(jnp.float32), capacity, owned
    )
    slots_ref[...] = listing
    slots_v[...] = listing
    move = pltpu.make_async_copy(slots_v, slots_s, sem)
    move.start()
    hits = count_rows(jnp.zeros((owned, LANES), jnp.float32), mine, slot)
    tally = jnp.sum(hits, axis=1, keepdims=True)
    recip_ref[...] = jnp.broadcast_to(1.0 / jnp.maximum(tally, 1.0), recip_ref.shape)

    picked = jnp.dot(
        choice_ref[...], table_ref[...].astype(jnp.bfloat16), preferred_element_type=jnp.float32
    )
    front, back = picked[0 : 2 * owned], picked[2 * owned : 4 * owned]
    lower = lax.broadcasted_iota(jnp.int32, (2 * owned, LANES), 1) < 64
    high = front[:, 0:LANES] + pltpu.roll(back[:, 0:LANES], 64, 1)
    low = pltpu.roll(front[:, LANES:], 64, 1) + back[:, LANES:]
    coarse = jnp.concatenate([jnp.where(lower, high, low), jnp.where(lower, high, 0.0)], axis=1)
    coarse = coarse.astype(jnp.bfloat16)
    width = 2 * LANES * chunks
    for n in range(0, basis_ref.shape[1], width):
        fine = jnp.dot(coarse, basis_ref[:, n : n + width], preferred_element_type=jnp.float32)
        gains_ref[:, n : n + width] = fine.astype(jnp.bfloat16).astype(jnp.float32)

    one_ref[...] = jnp.zeros_like(one_ref)
    two_ref[...] = jnp.zeros_like(two_ref)
    move.wait()
    if near > 1:
        for x in order:
            add_rows((one_ref, two_ref), slots_s, x, capacity, arrived[x])
    sums_ref[...] = one_ref[:, 0:owned] + two_ref[:, 0:owned]


def finish_kernel(capacity, late, slots_s, gains_ref, recip_ref, sums_ref, *rest):
    far = rest[: len(late)]
    out_hbm, acc_ref, res_ref, out_ref, sems = rest[len(late) :]
    owned, parts, channels = out_hbm.shape
    chunks = channels // LANES
    acc_ref[...] = sums_ref[...]
    if len(late) > 1:
        for x, rows_ref in zip(late, far):
            add_rows((acc_ref,), slots_s, x, capacity, rows_ref)
    else:

        def from_device(d, carry):
            add_rows((acc_ref,), slots_s, d, capacity, far[0].at[d])
            return carry

        lax.fori_loop(0, far[0].shape[0], from_device, 0)

    flat = acc_ref.reshape(chunks * owned * parts, LANES)
    done = res_ref.reshape(chunks * owned * parts, LANES)
    sends = []
    for c in range(chunks):
        for b0 in range(0, owned, SUB):
            scale = recip_ref[b0 : b0 + SUB, :]
            row = (c * owned + b0) * parts
            vis = [flat[pl.ds(row + j, SUB, stride=parts), :] for j in range(parts)]
            planes = [slice(j * channels + c * LANES, j * channels + (c + 1) * LANES) for j in range(parts)]
            lhs = [gains_ref[b0 : b0 + SUB, plane] for plane in planes]
            rhs = [gains_ref[owned + b0 : owned + b0 + SUB, plane] for plane in planes]
            mid_re, mid_im = [], []
            for row_a in range(2):
                for col_b in range(2):
                    re = im = 0.0
                    for inner in range(2):
                        lr, li = lhs[2 * row_a + inner], lhs[4 + 2 * row_a + inner]
                        vr, vi = vis[2 * inner + col_b], vis[4 + 2 * inner + col_b]
                        re = re + lr * vr - li * vi
                        im = im + lr * vi + li * vr
                    mid_re.append(re * scale)
                    mid_im.append(im * scale)
            for row_a in range(2):
                for col_b in range(2):
                    re = im = 0.0
                    for inner in range(2):
                        mr, mi = mid_re[2 * row_a + inner], mid_im[2 * row_a + inner]
                        rr, ri = rhs[2 * col_b + inner], rhs[4 + 2 * col_b + inner]
                        re = re + mr * rr + mi * ri
                        im = im + mi * rr - mr * ri
                    j = 2 * row_a + col_b
                    done[pl.ds(row + j, SUB, stride=parts), :] = re
                    done[pl.ds(row + 4 + j, SUB, stride=parts), :] = im
        out_ref[c] = res_ref[c].astype(out_ref.dtype)
        sends.append(
            pltpu.make_async_copy(
                out_ref.at[c], out_hbm.at[:, :, pl.ds(c * LANES, LANES)], sems.at[c]
            )
        )
        sends[-1].start()
    for send in sends:
        send.wait()


def on_device(
    visibilities,
    row_owner,
    row_slot,
    baseline_station_pairs,
    gains_coarse,
    band_weights,
    band_offset,
):
    devices = lax.axis_size("bl")
    rows, parts, channels = visibilities.shape
    capacity = 2 * rows // devices
    owned = baseline_station_pairs.shape[0]
    stations, _, knots = gains_coarse.shape
    chunks = channels // LANES
    gain_tiles = round_up(stations // 2, SUB) // SUB
    depth = 2 * gain_tiles + 1
    near = devices // 2 if devices <= 16 else 1
    halves = near > 1
    f32, bf16, i32 = jnp.float32, jnp.bfloat16, jnp.int32
    vmem = pl.BlockSpec(memory_space=pltpu.VMEM)
    smem = pl.BlockSpec(memory_space=pltpu.SMEM)
    hbm = pl.BlockSpec(memory_space=pltpu.HBM)
    anywhere = pl.BlockSpec(memory_space=pl.ANY)
    most = pltpu.CompilerParams(vmem_limit_bytes=ALL_VMEM)
    some = pltpu.CompilerParams(vmem_limit_bytes=SOME_VMEM)
    shape = jax.ShapeDtypeStruct
    dma = pltpu.SemaphoreType.DMA

    me = lax.axis_index("bl").astype(i32).reshape(1)
    turn = me if halves else jnp.zeros_like(me)
    owner = row_owner.reshape(rows)
    coarse = gains_coarse.transpose(2, 1, 0).reshape(knots * parts, stations)
    block = (chunks * capacity, parts, LANES)
    rows_at = chunks * capacity
    if halves:
        even, odd = far(near)
        long = with_gains(near) + odd[1:-2]
        outs = [
            shape((rows_at + (depth if x in long else 0), parts, LANES), bf16)
            for x in range(devices)
        ]
        outs[0] = shape((rows_at + depth + 3 * chunks, parts, LANES), bf16)
    else:
        outs = [
            shape((devices,) + block, bf16),
            shape((depth, SUB, LANES), bf16),
            shape((3 * chunks, SUB, LANES), bf16),
        ]
    pairs = baseline_station_pairs.T
    weights = band_weights.T
    offset = band_offset.reshape(chunks, LANES)
    me_owner = row_owner.reshape(rows)
    if halves:
        target = odd[0]
        first = outs.pop(target)
        alone = pl.pallas_call(
            functools.partial(first_kernel, capacity, target),
            out_shape=first,
            in_specs=[smem, hbm, hbm],
            out_specs=hbm,
            scratch_shapes=[
                pltpu.SMEM((rows,), i32),
                pltpu.SMEM((rows + 8,), i32),
                pltpu.VMEM((rows, parts, channels), bf16),
                pltpu.VMEM(first.shape, bf16),
                dma((2,)),
            ],
            compiler_params=most,
            name="pack_first",
        )(me, me_owner, visibilities)
    sent = pl.pallas_call(
        functools.partial(pack_kernel, capacity, near),
        out_shape=outs,
        in_specs=[smem] + [hbm] * 8,
        out_specs=[hbm] * len(outs),
        scratch_shapes=[
            pltpu.VMEM(weights.shape, f32),
            pltpu.VMEM(offset.shape, i32),
            pltpu.VMEM(pairs.shape, i32),
            pltpu.VMEM((SUB, channels), f32),
            pltpu.VMEM((3 * chunks, SUB, LANES), bf16),
            pltpu.SMEM((rows,), i32),
            pltpu.SMEM((rows,), i32),
            pltpu.SMEM((devices,), i32),
            pltpu.VMEM((1, rows), i32),
            pltpu.VMEM((1, rows), i32),
            pltpu.VMEM((rows, parts, channels), bf16),
            pltpu.VMEM((knots * parts, stations), f32),
            pltpu.VMEM((LANES, LANES), f32),
            pltpu.VMEM((depth, SUB, LANES), bf16),
            pltpu.VMEM((devices,) + block, bf16),
            dma((9 + PARTS + 2 * devices,)),
        ],
        compiler_params=most,
        name="pack_rows",
    )(
        turn,
        owner,
        row_owner.reshape(1, rows),
        row_slot.reshape(1, rows),
        visibilities,
        coarse,
        weights,
        offset,
        pairs,
    )


    trows = gain_tiles * SUB

    def ready(own, at):
        return pl.pallas_call(
            functools.partial(ready_kernel, at, chunks, owned, stations, trows),
            out_shape=[
                shape(own.shape, bf16),
                shape((4 * owned, devices * trows), bf16),
                shape((2 * LANES, parts * channels), bf16),
            ],
            in_specs=[smem, vmem],
            out_specs=[vmem] * 3,
            scratch_shapes=[dma],
            compiler_params=some,
            name="make_ready",
        )(turn, own)

    if halves:
        sent = list(sent)
        sent.insert(target, alone)

    def swap(array, x):
        return lax.ppermute(array, "bl", [(d, d ^ x) for d in range(devices)])

    if halves:
        own, choice, basis = ready(sent[0], rows_at + depth)
        arrived = {x: swap(sent[x], x) if x else own for x in range(devices)}
        order, late = schedule(near)
        even = list(range(near, devices, 2))
        collected = pl.pallas_call(
            functools.partial(collect_kernel, rows_at, depth),
            out_shape=shape((len(even) * depth, parts, LANES), bf16),
            in_specs=[anywhere] * len(even),
            out_specs=vmem,
            scratch_shapes=[dma((len(even),))],
            compiler_params=some,
            name="collect_gains",
        )(*[arrived[x] for x in even])
        passed = [swap(collected, 1)]
    else:
        arrived = {
            0: lax.all_gather(sent[1], "bl", axis=0),
            1: lax.all_to_all(sent[0], "bl", split_axis=0, concat_axis=0, tiled=True),
        }
        order, late, passed = [0], [1], []
        _, choice, basis = ready(sent[2], 0)

    gains, recip, slots, sums = pl.pallas_call(
        functools.partial(middle_kernel, capacity, near, depth, order),
        out_shape=(
            shape((2 * owned, parts * channels), f32),
            shape((owned, LANES), f32),
            shape((devices, LANES), i32),
            shape((chunks, owned, parts, LANES), f32),
        ),
        in_specs=[smem] + [vmem] * (2 + len(order) + len(passed)),
        out_specs=(vmem,) * 4,
        scratch_shapes=[
            pltpu.VMEM((devices * trows, 2 * LANES), f32),
            pltpu.VMEM((devices, LANES), f32),
            pltpu.VMEM((devices, LANES), f32),
            pltpu.VMEM((devices, LANES), i32),
            pltpu.SMEM((devices, LANES), i32),
            pltpu.VMEM((chunks, owned + 1, parts, LANES), f32),
            pltpu.VMEM((chunks, owned + 1, parts, LANES), f32),
            dma,
        ],
        compiler_params=some,
        name="gains_and_sums",
    )(me, choice, basis, *[arrived[x] for x in order], *passed)
    return pl.pallas_call(
        functools.partial(finish_kernel, capacity, late),
        out_shape=shape((owned, parts, channels), bf16),
        in_specs=[smem] + [vmem] * (3 + len(late)),
        out_specs=hbm,
        scratch_shapes=[
            pltpu.VMEM((chunks, owned, parts, LANES), f32),
            pltpu.VMEM((chunks, owned, parts, LANES), f32),
            pltpu.VMEM((chunks, owned, parts, LANES), bf16),
            dma((chunks,)),
        ],
        compiler_params=some,
        name="sum_and_apply",
    )(slots, gains, recip, sums, *[arrived[x] for x in late])


def solution(mesh):
    placed = (
        P(("groups", "bl"), None, None),
        P(("groups", "bl"), None),
        P(("groups", "bl")),
        P("bl", None),
        P(("groups", "bl"), None, None),
        P("groups", None),
        P("groups"),
    )
    return jax.shard_map(
        on_device,
        mesh=mesh,
        in_specs=placed,
        out_specs=P(("groups", "bl"), None, None),
        check_vma=False,
    )
```

```python
import functools

import jax
import jax.numpy as jnp
from jax import lax
from jax.experimental import pallas as pl
from jax.experimental.pallas import tpu as pltpu
from jax.sharding import PartitionSpec as P

LANES = 128
SUB = 8
USED = 48
PARTS = 4
ALL_VMEM = 60 * 1024 * 1024
SOME_VMEM = 24 * 1024 * 1024


def round_up(value, unit):
    return -(-value // unit) * unit


def schedule(near):
    even, odd = list(range(near, 2 * near, 2)), list(range(near + 1, 2 * near, 2))
    close = list(range(near // 2, near)) + list(range(1, near // 2))
    order = [0] + even[:1] + close[:2]
    cross, close = even[1:], close[2:]
    while cross:
        order += cross[:1] + close[:1]
        cross, close = cross[1:], close[1:]
    return order + close + odd[:-2], odd[-2:]


def with_gains(near):
    return list(range(near)) + list(range(near, 2 * near, 2))


def start_all(pairs, sems):
    moves = [pltpu.make_async_copy(src, dst, sems.at[i]) for i, (src, dst) in enumerate(pairs)]
    for move in moves:
        move.start()
    return moves


def pack_kernel(
    capacity,
    near,
    targets,
    me_s,
    owner_hbm,
    owner_row_hbm,
    slot_row_hbm,
    vis_hbm,
    coarse_hbm,
    weights_hbm,
    offset_hbm,
    pairs_hbm,
    *rest,
):
    outs = rest[:-16]
    (
        weights_ref,
        offset_ref,
        pairs_ref,
        small_ref,
        parts_ref,
        owner_s,
        place_s,
        count_s,
        owner_ref,
        slot_ref,
        vis_ref,
        coarse_ref,
        turn_ref,
        meta_ref,
        block_ref,
        sems,
    ) = rest[-16:]
    rows = vis_ref.shape[0]
    chunks = vis_ref.shape[2] // LANES
    devices = block_ref.shape[0]
    terms, stations = coarse_ref.shape
    half = stations // 2
    depth = meta_ref.shape[0]
    gain_tiles = (depth - 1) // 2
    span = rows // PARTS
    moves = start_all(
        (
            (owner_hbm, owner_s),
            (coarse_hbm, coarse_ref),
            (owner_row_hbm, owner_ref),
            (slot_row_hbm, slot_ref),
            (weights_hbm, weights_ref),
            (offset_hbm, offset_ref),
            (pairs_hbm, pairs_ref),
        ),
        sems,
    )
    fetches = start_all(
        [
            (vis_hbm.at[pl.ds(i * span, span)], vis_ref.at[pl.ds(i * span, span)])
            for i in range(PARTS)
        ],
        sems.at[pl.ds(len(moves), PARTS)],
    )
    turn_ref[...] = jnp.zeros_like(turn_ref)
    for d in range(devices):
        count_s[d] = 0
    me = me_s[0]
    moves[0].wait()

    def rank(r, carry):
        x = owner_s[r] ^ me
        k = count_s[x]
        count_s[x] = k + 1
        place_s[r] = x * capacity + k
        return carry

    lax.fori_loop(0, rows, rank, 0, unroll=8)
    for move in moves[1:]:
        move.wait()

    turn_ref[0:terms, 0:half] = coarse_ref[:, 0:half]
    turn_ref[64 : 64 + terms, 0:half] = coarse_ref[:, half:stations]
    gains = turn_ref[...].T
    high = gains.astype(jnp.bfloat16)
    low = (gains - high.astype(jnp.float32)).astype(jnp.bfloat16)
    for i in range(gain_tiles):
        meta_ref[i] = high[i * SUB : (i + 1) * SUB, :]
        meta_ref[gain_tiles + i] = low[i * SUB : (i + 1) * SUB, :]
    sub = lax.broadcasted_iota(jnp.int32, (SUB, LANES), 0)
    codes = jnp.where(sub == 0, owner_ref[...], slot_ref[...])
    meta_ref[2 * gain_tiles] = codes.astype(jnp.float32).astype(jnp.bfloat16)
    steps = weights_ref.shape[0]
    small_ref[...] = jnp.zeros_like(small_ref)
    small_ref[0:steps, :] = weights_ref[...]
    for c in range(chunks):
        lanes = slice(c * LANES, (c + 1) * LANES)
        small_ref[steps : steps + 1, lanes] = offset_ref[c : c + 1, :].astype(jnp.float32)
    small_ref[4:6, 0 : pairs_ref.shape[1]] = pairs_ref[...].astype(jnp.float32)
    left = small_ref[...]
    for p in range(3):
        piece = left.astype(jnp.bfloat16)
        left = left - piece.astype(jnp.float32)
        for c in range(chunks):
            parts_ref[p * chunks + c] = piece[:, c * LANES : (c + 1) * LANES]

    at = chunks * capacity
    if near > 1:
        outs = dict(zip(targets, outs))
        pairs = [(meta_ref, outs[x].at[pl.ds(at, depth)]) for x in targets if x in with_gains(near)]
    else:
        pairs = [(meta_ref, outs[1])]
    if near == 1:
        pairs += [(parts_ref, outs[2])]
    elif 0 in targets:
        pairs += [(parts_ref, outs[0].at[pl.ds(at + depth, 3 * chunks)])]
    start = len(moves) + PARTS
    sends = start_all(pairs, sems.at[pl.ds(start, len(pairs))])
    start += len(pairs)

    def place(r, carry):
        p = place_s[r]
        for c in range(chunks):
            flat_ref[p * chunks + c] = vis_ref[r, :, c * LANES : (c + 1) * LANES]
        return carry

    flat_ref = block_ref.reshape(devices * at, SUB, LANES)
    for i in range(PARTS):
        fetches[i].wait()
        lax.fori_loop(i * span, (i + 1) * span, place, 0, unroll=8)
    if near > 1:
        pairs = [(block_ref.at[x], outs[x].at[pl.ds(0, at)]) for x in targets]
    else:
        pairs = [(block_ref, outs[0])]
    sends += start_all(pairs, sems.at[pl.ds(start, len(pairs))])
    for send in sends:
        send.wait()


def first_kernel(capacity, target, me_s, owner_hbm, vis_hbm, out_hbm, owner_s, list_s, vis_ref, block_ref, sems):
    rows = vis_ref.shape[0]
    chunks = vis_ref.shape[2] // LANES
    moves = start_all(((owner_hbm, owner_s), (vis_hbm, vis_ref)), sems)
    wanted = me_s[0] ^ target
    moves[0].wait()

    def note(r, k):
        list_s[k] = r
        return k + jnp.where(owner_s[r] == wanted, 1, 0)

    count = lax.fori_loop(0, rows, note, 0, unroll=8)
    moves[1].wait()

    def place(k, carry):
        r = list_s[k]
        for c in range(chunks):
            block_ref[chunks * k + c] = vis_ref[r, :, c * LANES : (c + 1) * LANES]
        return carry

    lax.fori_loop(0, count, place, 0)
    send = start_all([(block_ref, out_hbm)], sems)[0]
    send.wait()


def ready_kernel(
    at, chunks, owned, stations, trows, turn_s, own_ref, own_out_ref, choice_ref, basis_ref, sem
):
    move = pltpu.make_async_copy(own_ref, own_out_ref, sem)
    move.start()
    pieces = [
        jnp.concatenate(
            [own_ref[at + p * chunks + c].astype(jnp.float32) for c in range(chunks)], axis=1
        )
        for p in range(3)
    ]
    small = pieces[0] + pieces[1] + pieces[2]
    channels = small.shape[1]
    half = stations // 2

    station = small[4:6, 0:LANES]
    sender = jnp.floor((station + 0.5) * (1.0 / stations))
    within = station - sender * stations
    second = (within >= float(half)).astype(jnp.float32)
    line = (sender.astype(jnp.int32) ^ turn_s[0]).astype(jnp.float32) * trows + within - second * half
    diagonal = lax.broadcasted_iota(jnp.int32, (owned, LANES), 0) == lax.broadcasted_iota(
        jnp.int32, (owned, LANES), 1
    )

    def upright(row):
        return jnp.sum(jnp.where(diagonal, row, 0.0), axis=1, keepdims=True)

    lines = jnp.concatenate([upright(line[side : side + 1]) for side in range(2)], axis=0)
    seconds = jnp.concatenate([upright(second[side : side + 1]) for side in range(2)], axis=0)
    table = choice_ref.shape[1]
    same = lines == lax.broadcasted_iota(jnp.int32, (2 * owned, table), 1).astype(jnp.float32)
    for h in range(2):
        choice_ref[2 * owned * h : 2 * owned * (h + 1), :] = (
            jnp.where(jnp.logical_and(same, seconds == float(h)), 1.0, 0.0).astype(jnp.bfloat16)
        )

    index = lax.broadcasted_iota(jnp.int32, (64, channels), 0)
    knot = (index >> 3).astype(jnp.float32)
    basis = jnp.zeros((64, channels), jnp.float32)
    for step in range(3):
        basis = basis + jnp.where(knot == small[3:4, :] + float(step), small[step : step + 1, :], 0.0)
    high = basis.astype(jnp.bfloat16).astype(jnp.float32)
    component = index & 7
    for j in range(8):
        cols = slice(j * channels, (j + 1) * channels)
        main = jnp.where(component == j, high, 0.0).astype(jnp.bfloat16)
        rest = jnp.where(component == j, basis - high, 0.0).astype(jnp.bfloat16)
        basis_ref[0:64, cols] = main
        basis_ref[64:128, cols] = main
        basis_ref[128:192, cols] = rest
        basis_ref[192:256, cols] = jnp.zeros_like(rest)
    move.wait()


def collect_kernel(at, depth, *rest):
    blocks, (out_ref, sems) = rest[:-2], rest[-2:]
    moves = start_all(
        [
            (block.at[pl.ds(at, depth)], out_ref.at[pl.ds(i * depth, depth)])
            for i, block in enumerate(blocks)
        ],
        sems,
    )
    for move in moves:
        move.wait()


def list_rows(owner, slot, target, capacity, spare):
    senders = owner.shape[0]
    mine = owner == target
    counted = mine.astype(jnp.float32)
    before = lax.broadcasted_iota(jnp.int32, (LANES, LANES), 0) < lax.broadcasted_iota(
        jnp.int32, (LANES, LANES), 1
    )
    rank = jnp.dot(
        counted.astype(jnp.bfloat16),
        before.astype(jnp.float32).astype(jnp.bfloat16),
        preferred_element_type=jnp.float32,
    )
    lane = lax.broadcasted_iota(jnp.int32, (senders, LANES), 1)
    count = jnp.sum(counted, axis=1, keepdims=True)
    listing = jnp.where(lane == capacity, count, 0.0)
    for k in range(capacity):
        here = jnp.logical_and(mine, rank == float(k))
        kth = jnp.sum(jnp.where(here, slot, 0.0), axis=1, keepdims=True)
        kth = jnp.where(count > float(k), kth, float(spare))
        listing = jnp.where(lane == k, kth, listing)
    return listing.astype(jnp.int32), mine


def add_rows(acc_refs, slots_s, line, capacity, rows_ref):
    chunks, several = acc_refs[0].shape[0], len(acc_refs)

    def add(i, carry):
        for u, acc_ref in enumerate(acc_refs):
            k = several * i + u
            b = slots_s[line, k]
            for c in range(chunks):
                acc_ref[c, b] += rows_ref[chunks * k + c].astype(jnp.float32)
        return carry

    lax.fori_loop(0, (slots_s[line, capacity] + several - 1) // several, add, 0)


def add_table(table_ref, x, block, at, depth):
    gain_tiles = (depth - 1) // 2
    for i in range(gain_tiles):
        rows = slice((x * gain_tiles + i) * SUB, (x * gain_tiles + i + 1) * SUB)
        table_ref[rows, 0:LANES] = block[at + i].astype(jnp.float32)
        table_ref[rows, LANES : 2 * LANES] = block[at + gain_tiles + i].astype(jnp.float32)
    return block[at + 2 * gain_tiles].astype(jnp.float32)


def count_rows(hits, mine, slot):
    which = lax.broadcasted_iota(jnp.int32, hits.shape, 0).astype(jnp.float32)
    slot = jnp.where(mine, slot, -1.0)
    for x in range(slot.shape[0]):
        hits = hits + (slot[x : x + 1, :] == which).astype(jnp.float32)
    return hits


def middle_kernel(capacity, near, depth, order, me_s, choice_ref, basis_ref, *rest):
    arrived, passed = dict(zip(order, rest)), rest[len(order) : -12]
    gains_ref, recip_ref, slots_ref, sums_ref = rest[-12:-8]
    table_ref, owner_ref, slot_ref, slots_v, slots_s, one_ref, two_ref, sem = rest[-8:]
    devices = owner_ref.shape[0]
    owned = recip_ref.shape[0]
    chunks = sums_ref.shape[0]
    for x in range(devices):
        if near == 1:
            code = add_table(table_ref, x, arrived[0].at[x], 0, depth)
        elif x in with_gains(near):
            code = add_table(table_ref, x, arrived[x], chunks * capacity, depth)
        else:
            code = add_table(table_ref, x, passed[0], (x - near) // 2 * depth, depth)
        owner_ref[x : x + 1, :] = code[0:1, :]
        slot_ref[x : x + 1, :] = code[1:2, :]
    slot = slot_ref[...]
    listing, mine = list_rows(
        owner_ref[...], slot, me_s[0].astype(jnp.float32), capacity, owned
    )
    slots_ref[...] = listing
    slots_v[...] = listing
    move = pltpu.make_async_copy(slots_v, slots_s, sem)
    move.start()
    hits = count_rows(jnp.zeros((owned, LANES), jnp.float32), mine, slot)
    tally = jnp.sum(hits, axis=1, keepdims=True)
    recip_ref[...] = jnp.broadcast_to(1.0 / jnp.maximum(tally, 1.0), recip_ref.shape)

    picked = jnp.dot(
        choice_ref[...], table_ref[...].astype(jnp.bfloat16), preferred_element_type=jnp.float32
    )
    front, back = picked[0 : 2 * owned], picked[2 * owned : 4 * owned]
    lower = lax.broadcasted_iota(jnp.int32, (2 * owned, LANES), 1) < 64
    high = front[:, 0:LANES] + pltpu.roll(back[:, 0:LANES], 64, 1)
    low = pltpu.roll(front[:, LANES:], 64, 1) + back[:, LANES:]
    coarse = jnp.concatenate([jnp.where(lower, high, low), jnp.where(lower, high, 0.0)], axis=1)
    coarse = coarse.astype(jnp.bfloat16)
    width = 2 * LANES * chunks
    for n in range(0, basis_ref.shape[1], width):
        fine = jnp.dot(coarse, basis_ref[:, n : n + width], preferred_element_type=jnp.float32)
        gains_ref[:, n : n + width] = fine.astype(jnp.bfloat16).astype(jnp.float32)

    one_ref[...] = jnp.zeros_like(one_ref)
    two_ref[...] = jnp.zeros_like(two_ref)
    move.wait()
    if near > 1:
        for x in order:
            add_rows((one_ref, two_ref), slots_s, x, capacity, arrived[x])
    sums_ref[...] = one_ref[:, 0:owned] + two_ref[:, 0:owned]


def finish_kernel(capacity, late, slots_s, gains_ref, recip_ref, sums_ref, *rest):
    far = rest[: len(late)]
    out_hbm, acc_ref, res_ref, out_ref, sems = rest[len(late) :]
    owned, parts, channels = out_hbm.shape
    chunks = channels // LANES
    acc_ref[...] = sums_ref[...]
    if len(late) > 1:
        for x, rows_ref in zip(late, far):
            add_rows((acc_ref,), slots_s, x, capacity, rows_ref)
    else:

        def from_device(d, carry):
            add_rows((acc_ref,), slots_s, d, capacity, far[0].at[d])
            return carry

        lax.fori_loop(0, far[0].shape[0], from_device, 0)

    flat = acc_ref.reshape(chunks * owned * parts, LANES)
    done = res_ref.reshape(chunks * owned * parts, LANES)
    sends = []
    for c in range(chunks):
        for b0 in range(0, owned, SUB):
            scale = recip_ref[b0 : b0 + SUB, :]
            row = (c * owned + b0) * parts
            vis = [flat[pl.ds(row + j, SUB, stride=parts), :] for j in range(parts)]
            planes = [slice(j * channels + c * LANES, j * channels + (c + 1) * LANES) for j in range(parts)]
            lhs = [gains_ref[b0 : b0 + SUB, plane] for plane in planes]
            rhs = [gains_ref[owned + b0 : owned + b0 + SUB, plane] for plane in planes]
            mid_re, mid_im = [], []
            for row_a in range(2):
                for col_b in range(2):
                    re = im = 0.0
                    for inner in range(2):
                        lr, li = lhs[2 * row_a + inner], lhs[4 + 2 * row_a + inner]
                        vr, vi = vis[2 * inner + col_b], vis[4 + 2 * inner + col_b]
                        re = re + lr * vr - li * vi
                        im = im + lr * vi + li * vr
                    mid_re.append(re * scale)
                    mid_im.append(im * scale)
            for row_a in range(2):
                for col_b in range(2):
                    re = im = 0.0
                    for inner in range(2):
                        mr, mi = mid_re[2 * row_a + inner], mid_im[2 * row_a + inner]
                        rr, ri = rhs[2 * col_b + inner], rhs[4 + 2 * col_b + inner]
                        re = re + mr * rr + mi * ri
                        im = im + mi * rr - mr * ri
                    j = 2 * row_a + col_b
                    done[pl.ds(row + j, SUB, stride=parts), :] = re
                    done[pl.ds(row + 4 + j, SUB, stride=parts), :] = im
        out_ref[c] = res_ref[c].astype(out_ref.dtype)
        sends.append(
            pltpu.make_async_copy(
                out_ref.at[c], out_hbm.at[:, :, pl.ds(c * LANES, LANES)], sems.at[c]
            )
        )
        sends[-1].start()
    for send in sends:
        send.wait()


def on_device(
    visibilities,
    row_owner,
    row_slot,
    baseline_station_pairs,
    gains_coarse,
    band_weights,
    band_offset,
):
    devices = lax.axis_size("bl")
    rows, parts, channels = visibilities.shape
    capacity = 2 * rows // devices
    owned = baseline_station_pairs.shape[0]
    stations, _, knots = gains_coarse.shape
    chunks = channels // LANES
    gain_tiles = round_up(stations // 2, SUB) // SUB
    depth = 2 * gain_tiles + 1
    near = devices // 2 if devices <= 16 else 1
    halves = near > 1
    f32, bf16, i32 = jnp.float32, jnp.bfloat16, jnp.int32
    vmem = pl.BlockSpec(memory_space=pltpu.VMEM)
    smem = pl.BlockSpec(memory_space=pltpu.SMEM)
    hbm = pl.BlockSpec(memory_space=pltpu.HBM)
    anywhere = pl.BlockSpec(memory_space=pl.ANY)
    most = pltpu.CompilerParams(vmem_limit_bytes=ALL_VMEM)
    some = pltpu.CompilerParams(vmem_limit_bytes=SOME_VMEM)
    shape = jax.ShapeDtypeStruct
    dma = pltpu.SemaphoreType.DMA

    me = lax.axis_index("bl").astype(i32).reshape(1)
    turn = me if halves else jnp.zeros_like(me)
    owner = row_owner.reshape(rows)
    coarse = gains_coarse.transpose(2, 1, 0).reshape(knots * parts, stations)
    block = (chunks * capacity, parts, LANES)
    rows_at = chunks * capacity
    if halves:
        long = with_gains(near)
        outs = [
            shape((rows_at + (depth if x in long else 0), parts, LANES), bf16)
            for x in range(devices)
        ]
        outs[0] = shape((rows_at + depth + 3 * chunks, parts, LANES), bf16)
    else:
        outs = [
            shape((devices,) + block, bf16),
            shape((depth, SUB, LANES), bf16),
            shape((3 * chunks, SUB, LANES), bf16),
        ]
    pairs = baseline_station_pairs.T
    weights = band_weights.T
    offset = band_offset.reshape(chunks, LANES)
    me_owner = row_owner.reshape(rows)
    if halves:
        target = near + 1
        alone = pl.pallas_call(
            functools.partial(first_kernel, capacity, target),
            out_shape=outs[target],
            in_specs=[smem, hbm, hbm],
            out_specs=hbm,
            scratch_shapes=[
                pltpu.SMEM((rows,), i32),
                pltpu.SMEM((rows + 8,), i32),
                pltpu.VMEM((rows, parts, channels), bf16),
                pltpu.VMEM(outs[target].shape, bf16),
                dma((2,)),
            ],
            compiler_params=most,
            name="pack_first",
        )(me, me_owner, visibilities)
    def pack(targets, outs):
        return pl.pallas_call(
            functools.partial(pack_kernel, capacity, near, targets),
            out_shape=outs,
            in_specs=[smem] + [hbm] * 8,
            out_specs=[hbm] * len(outs),
            scratch_shapes=[
                pltpu.VMEM(weights.shape, f32),
                pltpu.VMEM(offset.shape, i32),
                pltpu.VMEM(pairs.shape, i32),
                pltpu.VMEM((SUB, channels), f32),
                pltpu.VMEM((3 * chunks, SUB, LANES), bf16),
                pltpu.SMEM((rows,), i32),
                pltpu.SMEM((rows,), i32),
                pltpu.SMEM((devices,), i32),
                pltpu.VMEM((1, rows), i32),
                pltpu.VMEM((1, rows), i32),
                pltpu.VMEM((rows, parts, channels), bf16),
                pltpu.VMEM((knots * parts, stations), f32),
                pltpu.VMEM((LANES, LANES), f32),
                pltpu.VMEM((depth, SUB, LANES), bf16),
                pltpu.VMEM((devices,) + block, bf16),
                dma((9 + PARTS + 2 * devices,)),
            ],
            compiler_params=most,
            name="pack_rows",
        )(
            turn,
            owner,
            row_owner.reshape(1, rows),
            row_slot.reshape(1, rows),
            visibilities,
            coarse,
            weights,
            offset,
            pairs,
        )


    if halves:
        order, _ = schedule(near)
        soon = order[1:4] + [near + 3]
        later = [x for x in range(devices) if x not in soon + [target]]
        sent = {target: alone}
        for some_of in (soon, later):
            sent.update(zip(some_of, pack(some_of, [outs[x] for x in some_of])))
    else:
        sent = pack([0, 1, 2], outs)

    trows = gain_tiles * SUB

    def ready(own, at):
        return pl.pallas_call(
            functools.partial(ready_kernel, at, chunks, owned, stations, trows),
            out_shape=[
                shape(own.shape, bf16),
                shape((4 * owned, devices * trows), bf16),
                shape((2 * LANES, parts * channels), bf16),
            ],
            in_specs=[smem, vmem],
            out_specs=[vmem] * 3,
            scratch_shapes=[dma],
            compiler_params=some,
            name="make_ready",
        )(turn, own)

    def swap(array, x):
        return lax.ppermute(array, "bl", [(d, d ^ x) for d in range(devices)])

    if halves:
        own, choice, basis = ready(sent[0], rows_at + depth)
        arrived = {x: swap(sent[x], x) if x else own for x in range(devices)}
        order, late = schedule(near)
        even = list(range(near, devices, 2))
        collected = pl.pallas_call(
            functools.partial(collect_kernel, rows_at, depth),
            out_shape=shape((len(even) * depth, parts, LANES), bf16),
            in_specs=[anywhere] * len(even),
            out_specs=vmem,
            scratch_shapes=[dma((len(even),))],
            compiler_params=some,
            name="collect_gains",
        )(*[arrived[x] for x in even])
        passed = [swap(collected, 1)]
    else:
        arrived = {
            0: lax.all_gather(sent[1], "bl", axis=0),
            1: lax.all_to_all(sent[0], "bl", split_axis=0, concat_axis=0, tiled=True),
        }
        order, late, passed = [0], [1], []
        _, choice, basis = ready(sent[2], 0)

    gains, recip, slots, sums = pl.pallas_call(
        functools.partial(middle_kernel, capacity, near, depth, order),
        out_shape=(
            shape((2 * owned, parts * channels), f32),
            shape((owned, LANES), f32),
            shape((devices, LANES), i32),
            shape((chunks, owned, parts, LANES), f32),
        ),
        in_specs=[smem] + [vmem] * (2 + len(order) + len(passed)),
        out_specs=(vmem,) * 4,
        scratch_shapes=[
            pltpu.VMEM((devices * trows, 2 * LANES), f32),
            pltpu.VMEM((devices, LANES), f32),
            pltpu.VMEM((devices, LANES), f32),
            pltpu.VMEM((devices, LANES), i32),
            pltpu.SMEM((devices, LANES), i32),
            pltpu.VMEM((chunks, owned + 1, parts, LANES), f32),
            pltpu.VMEM((chunks, owned + 1, parts, LANES), f32),
            dma,
        ],
        compiler_params=some,
        name="gains_and_sums",
    )(me, choice, basis, *[arrived[x] for x in order], *passed)
    return pl.pallas_call(
        functools.partial(finish_kernel, capacity, late),
        out_shape=shape((owned, parts, channels), bf16),
        in_specs=[smem] + [vmem] * (3 + len(late)),
        out_specs=hbm,
        scratch_shapes=[
            pltpu.VMEM((chunks, owned, parts, LANES), f32),
            pltpu.VMEM((chunks, owned, parts, LANES), f32),
            pltpu.VMEM((chunks, owned, parts, LANES), bf16),
            dma((chunks,)),
        ],
        compiler_params=some,
        name="sum_and_apply",
    )(slots, gains, recip, sums, *[arrived[x] for x in late])


def solution(mesh):
    placed = (
        P(("groups", "bl"), None, None),
        P(("groups", "bl"), None),
        P(("groups", "bl")),
        P("bl", None),
        P(("groups", "bl"), None, None),
        P("groups", None),
        P("groups"),
    )
    return jax.shard_map(
        on_device,
        mesh=mesh,
        in_specs=placed,
        out_specs=P(("groups", "bl"), None, None),
        check_vma=False,
    )
```

```python
import functools

import jax
import jax.numpy as jnp
from jax import lax
from jax.experimental import pallas as pl
from jax.experimental.pallas import tpu as pltpu
from jax.sharding import PartitionSpec as P

LANES = 128
SUB = 8
USED = 48
PARTS = 4
ALL_VMEM = 60 * 1024 * 1024
SOME_VMEM = 24 * 1024 * 1024


def round_up(value, unit):
    return -(-value // unit) * unit


def schedule(near):
    even, odd = list(range(near, 2 * near, 2)), list(range(near + 1, 2 * near, 2))
    close = list(range(near // 2, near)) + list(range(1, near // 2))
    order = [0] + even[:2] + close[:2]
    cross, close = even[2:], close[2:]
    while cross:
        order += cross[:1] + close[:1]
        cross, close = cross[1:], close[1:]
    return order + close[:1] + odd[1:-2] + close[1:] + odd[:1], odd[-2:]


def with_gains(near):
    return list(range(near)) + list(range(near, 2 * near, 2))


def start_all(pairs, sems):
    moves = [pltpu.make_async_copy(src, dst, sems.at[i]) for i, (src, dst) in enumerate(pairs)]
    for move in moves:
        move.start()
    return moves


def pack_kernel(
    capacity,
    near,
    me_s,
    owner_hbm,
    owner_row_hbm,
    slot_row_hbm,
    vis_hbm,
    coarse_hbm,
    weights_hbm,
    offset_hbm,
    pairs_hbm,
    *rest,
):
    outs = rest[:-16]
    (
        weights_ref,
        offset_ref,
        pairs_ref,
        small_ref,
        parts_ref,
        owner_s,
        place_s,
        count_s,
        owner_ref,
        slot_ref,
        vis_ref,
        coarse_ref,
        turn_ref,
        meta_ref,
        block_ref,
        sems,
    ) = rest[-16:]
    rows = vis_ref.shape[0]
    chunks = vis_ref.shape[2] // LANES
    devices = block_ref.shape[0]
    terms, stations = coarse_ref.shape
    half = stations // 2
    depth = meta_ref.shape[0]
    gain_tiles = (depth - 1) // 2
    span = rows // PARTS
    moves = start_all(
        (
            (owner_hbm, owner_s),
            (coarse_hbm, coarse_ref),
            (owner_row_hbm, owner_ref),
            (slot_row_hbm, slot_ref),
            (weights_hbm, weights_ref),
            (offset_hbm, offset_ref),
            (pairs_hbm, pairs_ref),
        ),
        sems,
    )
    fetches = start_all(
        [
            (vis_hbm.at[pl.ds(i * span, span)], vis_ref.at[pl.ds(i * span, span)])
            for i in range(PARTS)
        ],
        sems.at[pl.ds(len(moves), PARTS)],
    )
    turn_ref[...] = jnp.zeros_like(turn_ref)
    for d in range(devices):
        count_s[d] = 0
    me = me_s[0]
    moves[0].wait()

    def rank(r, carry):
        x = owner_s[r] ^ me
        k = count_s[x]
        count_s[x] = k + 1
        place_s[r] = x * capacity + k
        return carry

    lax.fori_loop(0, rows, rank, 0, unroll=8)
    for move in moves[1:]:
        move.wait()

    turn_ref[0:terms, 0:half] = coarse_ref[:, 0:half]
    turn_ref[64 : 64 + terms, 0:half] = coarse_ref[:, half:stations]
    gains = turn_ref[...].T
    high = gains.astype(jnp.bfloat16)
    low = (gains - high.astype(jnp.float32)).astype(jnp.bfloat16)
    for i in range(gain_tiles):
        meta_ref[i] = high[i * SUB : (i + 1) * SUB, :]
        meta_ref[gain_tiles + i] = low[i * SUB : (i + 1) * SUB, :]
    sub = lax.broadcasted_iota(jnp.int32, (SUB, LANES), 0)
    codes = jnp.where(sub == 0, owner_ref[...], slot_ref[...])
    meta_ref[2 * gain_tiles] = codes.astype(jnp.float32).astype(jnp.bfloat16)
    steps = weights_ref.shape[0]
    small_ref[...] = jnp.zeros_like(small_ref)
    small_ref[0:steps, :] = weights_ref[...]
    for c in range(chunks):
        lanes = slice(c * LANES, (c + 1) * LANES)
        small_ref[steps : steps + 1, lanes] = offset_ref[c : c + 1, :].astype(jnp.float32)
    small_ref[4:6, 0 : pairs_ref.shape[1]] = pairs_ref[...].astype(jnp.float32)
    left = small_ref[...]
    for p in range(3):
        piece = left.astype(jnp.bfloat16)
        left = left - piece.astype(jnp.float32)
        for c in range(chunks):
            parts_ref[p * chunks + c] = piece[:, c * LANES : (c + 1) * LANES]

    at = chunks * capacity
    if near > 1:
        outs = list(outs[: near + 1]) + [None] + list(outs[near + 1 :])
        pairs = [(meta_ref, outs[x].at[pl.ds(at, depth)]) for x in with_gains(near)]
    else:
        pairs = [(meta_ref, outs[1])]
    at_small = at + depth if near > 1 else 0
    pairs += [(parts_ref, outs[0 if near > 1 else -1].at[pl.ds(at_small, 3 * chunks)])]
    start = len(moves) + PARTS
    sends = start_all(pairs, sems.at[pl.ds(start, len(pairs))])
    start += len(pairs)

    def place(r, carry):
        p = place_s[r]
        for c in range(chunks):
            flat_ref[p * chunks + c] = vis_ref[r, :, c * LANES : (c + 1) * LANES]
        return carry

    flat_ref = block_ref.reshape(devices * at, SUB, LANES)
    for i in range(PARTS):
        fetches[i].wait()
        lax.fori_loop(i * span, (i + 1) * span, place, 0, unroll=8)
    if near > 1:
        pairs = [
            (block_ref.at[x], outs[x].at[pl.ds(0, at)]) for x in range(devices) if x != near + 1
        ]
    else:
        pairs = [(block_ref, outs[0])]
    sends += start_all(pairs, sems.at[pl.ds(start, len(pairs))])
    for send in sends:
        send.wait()


def first_kernel(capacity, target, me_s, owner_hbm, vis_hbm, out_hbm, owner_s, list_s, vis_ref, block_ref, sems):
    rows = vis_ref.shape[0]
    chunks = vis_ref.shape[2] // LANES
    moves = start_all(((owner_hbm, owner_s), (vis_hbm, vis_ref)), sems)
    wanted = me_s[0] ^ target
    moves[0].wait()

    def note(r, k):
        list_s[k] = r
        return k + jnp.where(owner_s[r] == wanted, 1, 0)

    count = lax.fori_loop(0, rows, note, 0, unroll=8)
    moves[1].wait()

    def place(k, carry):
        r = list_s[k]
        for c in range(chunks):
            block_ref[chunks * k + c] = vis_ref[r, :, c * LANES : (c + 1) * LANES]
        return carry

    lax.fori_loop(0, count, place, 0)
    send = start_all([(block_ref, out_hbm)], sems)[0]
    send.wait()


def ready_kernel(
    at, chunks, owned, stations, trows, turn_s, own_ref, own_out_ref, choice_ref, basis_ref, sem
):
    move = pltpu.make_async_copy(own_ref, own_out_ref, sem)
    move.start()
    pieces = [
        jnp.concatenate(
            [own_ref[at + p * chunks + c].astype(jnp.float32) for c in range(chunks)], axis=1
        )
        for p in range(3)
    ]
    small = pieces[0] + pieces[1] + pieces[2]
    channels = small.shape[1]
    half = stations // 2

    station = small[4:6, 0:LANES]
    sender = jnp.floor((station + 0.5) * (1.0 / stations))
    within = station - sender * stations
    second = (within >= float(half)).astype(jnp.float32)
    line = (sender.astype(jnp.int32) ^ turn_s[0]).astype(jnp.float32) * trows + within - second * half
    diagonal = lax.broadcasted_iota(jnp.int32, (owned, LANES), 0) == lax.broadcasted_iota(
        jnp.int32, (owned, LANES), 1
    )

    def upright(row):
        return jnp.sum(jnp.where(diagonal, row, 0.0), axis=1, keepdims=True)

    lines = jnp.concatenate([upright(line[side : side + 1]) for side in range(2)], axis=0)
    seconds = jnp.concatenate([upright(second[side : side + 1]) for side in range(2)], axis=0)
    table = choice_ref.shape[1]
    same = lines == lax.broadcasted_iota(jnp.int32, (2 * owned, table), 1).astype(jnp.float32)
    for h in range(2):
        choice_ref[2 * owned * h : 2 * owned * (h + 1), :] = (
            jnp.where(jnp.logical_and(same, seconds == float(h)), 1.0, 0.0).astype(jnp.bfloat16)
        )

    index = lax.broadcasted_iota(jnp.int32, (64, channels), 0)
    knot = (index >> 3).astype(jnp.float32)
    basis = jnp.zeros((64, channels), jnp.float32)
    for step in range(3):
        basis = basis + jnp.where(knot == small[3:4, :] + float(step), small[step : step + 1, :], 0.0)
    high = basis.astype(jnp.bfloat16).astype(jnp.float32)
    component = index & 7
    for j in range(8):
        cols = slice(j * channels, (j + 1) * channels)
        main = jnp.where(component == j, high, 0.0).astype(jnp.bfloat16)
        rest = jnp.where(component == j, basis - high, 0.0).astype(jnp.bfloat16)
        basis_ref[0:64, cols] = main
        basis_ref[64:128, cols] = main
        basis_ref[128:192, cols] = rest
        basis_ref[192:256, cols] = jnp.zeros_like(rest)
    move.wait()


def collect_kernel(at, depth, *rest):
    blocks, (out_ref, sems) = rest[:-2], rest[-2:]
    moves = start_all(
        [
            (block.at[pl.ds(at, depth)], out_ref.at[pl.ds(i * depth, depth)])
            for i, block in enumerate(blocks)
        ],
        sems,
    )
    for move in moves:
        move.wait()


def list_rows(owner, slot, target, capacity, spare):
    senders = owner.shape[0]
    mine = owner == target
    counted = mine.astype(jnp.float32)
    before = lax.broadcasted_iota(jnp.int32, (LANES, LANES), 0) < lax.broadcasted_iota(
        jnp.int32, (LANES, LANES), 1
    )
    rank = jnp.dot(
        counted.astype(jnp.bfloat16),
        before.astype(jnp.float32).astype(jnp.bfloat16),
        preferred_element_type=jnp.float32,
    )
    lane = lax.broadcasted_iota(jnp.int32, (senders, LANES), 1)
    count = jnp.sum(counted, axis=1, keepdims=True)
    listing = jnp.where(lane == capacity, count, 0.0)
    for k in range(capacity):
        here = jnp.logical_and(mine, rank == float(k))
        kth = jnp.sum(jnp.where(here, slot, 0.0), axis=1, keepdims=True)
        kth = jnp.where(count > float(k), kth, float(spare))
        listing = jnp.where(lane == k, kth, listing)
    return listing.astype(jnp.int32), mine


def add_rows(acc_refs, slots_s, line, capacity, rows_ref):
    chunks, several = acc_refs[0].shape[0], len(acc_refs)

    def add(i, carry):
        for u, acc_ref in enumerate(acc_refs):
            k = several * i + u
            b = slots_s[line, k]
            for c in range(chunks):
                acc_ref[c, b] += rows_ref[chunks * k + c].astype(jnp.float32)
        return carry

    lax.fori_loop(0, (slots_s[line, capacity] + several - 1) // several, add, 0)


def add_table(table_ref, x, block, at, depth):
    gain_tiles = (depth - 1) // 2
    for i in range(gain_tiles):
        rows = slice((x * gain_tiles + i) * SUB, (x * gain_tiles + i + 1) * SUB)
        table_ref[rows, 0:LANES] = block[at + i].astype(jnp.float32)
        table_ref[rows, LANES : 2 * LANES] = block[at + gain_tiles + i].astype(jnp.float32)
    return block[at + 2 * gain_tiles].astype(jnp.float32)


def count_rows(hits, mine, slot):
    which = lax.broadcasted_iota(jnp.int32, hits.shape, 0).astype(jnp.float32)
    slot = jnp.where(mine, slot, -1.0)
    for x in range(slot.shape[0]):
        hits = hits + (slot[x : x + 1, :] == which).astype(jnp.float32)
    return hits


def middle_kernel(capacity, near, depth, order, me_s, choice_ref, basis_ref, *rest):
    arrived, passed = dict(zip(order, rest)), rest[len(order) : -12]
    gains_ref, recip_ref, slots_ref, sums_ref = rest[-12:-8]
    table_ref, owner_ref, slot_ref, slots_v, slots_s, one_ref, two_ref, sem = rest[-8:]
    devices = owner_ref.shape[0]
    owned = recip_ref.shape[0]
    chunks = sums_ref.shape[0]
    for x in range(devices):
        if near == 1:
            code = add_table(table_ref, x, arrived[0].at[x], 0, depth)
        elif x in with_gains(near):
            code = add_table(table_ref, x, arrived[x], chunks * capacity, depth)
        else:
            code = add_table(table_ref, x, passed[0], (x - near) // 2 * depth, depth)
        owner_ref[x : x + 1, :] = code[0:1, :]
        slot_ref[x : x + 1, :] = code[1:2, :]
    slot = slot_ref[...]
    listing, mine = list_rows(
        owner_ref[...], slot, me_s[0].astype(jnp.float32), capacity, owned
    )
    slots_ref[...] = listing
    slots_v[...] = listing
    move = pltpu.make_async_copy(slots_v, slots_s, sem)
    move.start()
    hits = count_rows(jnp.zeros((owned, LANES), jnp.float32), mine, slot)
    tally = jnp.sum(hits, axis=1, keepdims=True)
    recip_ref[...] = jnp.broadcast_to(1.0 / jnp.maximum(tally, 1.0), recip_ref.shape)

    picked = jnp.dot(
        choice_ref[...], table_ref[...].astype(jnp.bfloat16), preferred_element_type=jnp.float32
    )
    front, back = picked[0 : 2 * owned], picked[2 * owned : 4 * owned]
    lower = lax.broadcasted_iota(jnp.int32, (2 * owned, LANES), 1) < 64
    high = front[:, 0:LANES] + pltpu.roll(back[:, 0:LANES], 64, 1)
    low = pltpu.roll(front[:, LANES:], 64, 1) + back[:, LANES:]
    coarse = jnp.concatenate([jnp.where(lower, high, low), jnp.where(lower, high, 0.0)], axis=1)
    coarse = coarse.astype(jnp.bfloat16)
    width = 2 * LANES * chunks
    for n in range(0, basis_ref.shape[1], width):
        fine = jnp.dot(coarse, basis_ref[:, n : n + width], preferred_element_type=jnp.float32)
        gains_ref[:, n : n + width] = fine.astype(jnp.bfloat16).astype(jnp.float32)

    one_ref[...] = jnp.zeros_like(one_ref)
    two_ref[...] = jnp.zeros_like(two_ref)
    move.wait()
    if near > 1:
        for x in order:
            add_rows((one_ref, two_ref), slots_s, x, capacity, arrived[x])
    sums_ref[...] = one_ref[:, 0:owned] + two_ref[:, 0:owned]


def finish_kernel(capacity, late, slots_s, gains_ref, recip_ref, sums_ref, *rest):
    far = rest[: len(late)]
    out_hbm, acc_ref, res_ref, out_ref, sems = rest[len(late) :]
    owned, parts, channels = out_hbm.shape
    chunks = channels // LANES
    acc_ref[...] = sums_ref[...]
    if len(late) > 1:
        for x, rows_ref in zip(late, far):
            add_rows((acc_ref,), slots_s, x, capacity, rows_ref)
    else:

        def from_device(d, carry):
            add_rows((acc_ref,), slots_s, d, capacity, far[0].at[d])
            return carry

        lax.fori_loop(0, far[0].shape[0], from_device, 0)

    flat = acc_ref.reshape(chunks * owned * parts, LANES)
    done = res_ref.reshape(chunks * owned * parts, LANES)
    sends = []
    for c in range(chunks):
        for b0 in range(0, owned, SUB):
            scale = recip_ref[b0 : b0 + SUB, :]
            row = (c * owned + b0) * parts
            vis = [flat[pl.ds(row + j, SUB, stride=parts), :] for j in range(parts)]
            planes = [slice(j * channels + c * LANES, j * channels + (c + 1) * LANES) for j in range(parts)]
            lhs = [gains_ref[b0 : b0 + SUB, plane] for plane in planes]
            rhs = [gains_ref[owned + b0 : owned + b0 + SUB, plane] for plane in planes]
            mid_re, mid_im = [], []
            for row_a in range(2):
                for col_b in range(2):
                    re = im = 0.0
                    for inner in range(2):
                        lr, li = lhs[2 * row_a + inner], lhs[4 + 2 * row_a + inner]
                        vr, vi = vis[2 * inner + col_b], vis[4 + 2 * inner + col_b]
                        re = re + lr * vr - li * vi
                        im = im + lr * vi + li * vr
                    mid_re.append(re * scale)
                    mid_im.append(im * scale)
            for row_a in range(2):
                for col_b in range(2):
                    re = im = 0.0
                    for inner in range(2):
                        mr, mi = mid_re[2 * row_a + inner], mid_im[2 * row_a + inner]
                        rr, ri = rhs[2 * col_b + inner], rhs[4 + 2 * col_b + inner]
                        re = re + mr * rr + mi * ri
                        im = im + mi * rr - mr * ri
                    j = 2 * row_a + col_b
                    done[pl.ds(row + j, SUB, stride=parts), :] = re
                    done[pl.ds(row + 4 + j, SUB, stride=parts), :] = im
        out_ref[c] = res_ref[c].astype(out_ref.dtype)
        sends.append(
            pltpu.make_async_copy(
                out_ref.at[c], out_hbm.at[:, :, pl.ds(c * LANES, LANES)], sems.at[c]
            )
        )
        sends[-1].start()
    for send in sends:
        send.wait()


def on_device(
    visibilities,
    row_owner,
    row_slot,
    baseline_station_pairs,
    gains_coarse,
    band_weights,
    band_offset,
):
    devices = lax.axis_size("bl")
    rows, parts, channels = visibilities.shape
    capacity = 2 * rows // devices
    owned = baseline_station_pairs.shape[0]
    stations, _, knots = gains_coarse.shape
    chunks = channels // LANES
    gain_tiles = round_up(stations // 2, SUB) // SUB
    depth = 2 * gain_tiles + 1
    near = devices // 2 if devices <= 16 else 1
    halves = near > 1
    f32, bf16, i32 = jnp.float32, jnp.bfloat16, jnp.int32
    vmem = pl.BlockSpec(memory_space=pltpu.VMEM)
    smem = pl.BlockSpec(memory_space=pltpu.SMEM)
    hbm = pl.BlockSpec(memory_space=pltpu.HBM)
    anywhere = pl.BlockSpec(memory_space=pl.ANY)
    most = pltpu.CompilerParams(vmem_limit_bytes=ALL_VMEM)
    some = pltpu.CompilerParams(vmem_limit_bytes=SOME_VMEM)
    shape = jax.ShapeDtypeStruct
    dma = pltpu.SemaphoreType.DMA

    me = lax.axis_index("bl").astype(i32).reshape(1)
    turn = me if halves else jnp.zeros_like(me)
    owner = row_owner.reshape(rows)
    coarse = gains_coarse.transpose(2, 1, 0).reshape(knots * parts, stations)
    block = (chunks * capacity, parts, LANES)
    rows_at = chunks * capacity
    if halves:
        long = with_gains(near) + [near + 3]
        outs = [
            shape((rows_at + (depth if x in long else 0), parts, LANES), bf16)
            for x in range(devices)
        ]
        outs[0] = shape((rows_at + depth + 3 * chunks, parts, LANES), bf16)
    else:
        outs = [
            shape((devices,) + block, bf16),
            shape((depth, SUB, LANES), bf16),
            shape((3 * chunks, SUB, LANES), bf16),
        ]
    pairs = baseline_station_pairs.T
    weights = band_weights.T
    offset = band_offset.reshape(chunks, LANES)
    me_owner = row_owner.reshape(rows)
    if halves:
        first = outs.pop(near + 1)
        alone = pl.pallas_call(
            functools.partial(first_kernel, capacity, near + 1),
            out_shape=first,
            in_specs=[smem, hbm, hbm],
            out_specs=hbm,
            scratch_shapes=[
                pltpu.SMEM((rows,), i32),
                pltpu.SMEM((rows + 8,), i32),
                pltpu.VMEM((rows, parts, channels), bf16),
                pltpu.VMEM(first.shape, bf16),
                dma((2,)),
            ],
            compiler_params=most,
            name="pack_first",
        )(me, me_owner, visibilities)
    sent = pl.pallas_call(
        functools.partial(pack_kernel, capacity, near),
        out_shape=outs,
        in_specs=[smem] + [hbm] * 8,
        out_specs=[hbm] * len(outs),
        scratch_shapes=[
            pltpu.VMEM(weights.shape, f32),
            pltpu.VMEM(offset.shape, i32),
            pltpu.VMEM(pairs.shape, i32),
            pltpu.VMEM((SUB, channels), f32),
            pltpu.VMEM((3 * chunks, SUB, LANES), bf16),
            pltpu.SMEM((rows,), i32),
            pltpu.SMEM((rows,), i32),
            pltpu.SMEM((devices,), i32),
            pltpu.VMEM((1, rows), i32),
            pltpu.VMEM((1, rows), i32),
            pltpu.VMEM((rows, parts, channels), bf16),
            pltpu.VMEM((knots * parts, stations), f32),
            pltpu.VMEM((LANES, LANES), f32),
            pltpu.VMEM((depth, SUB, LANES), bf16),
            pltpu.VMEM((devices,) + block, bf16),
            dma((9 + PARTS + 2 * devices,)),
        ],
        compiler_params=most,
        name="pack_rows",
    )(
        turn,
        owner,
        row_owner.reshape(1, rows),
        row_slot.reshape(1, rows),
        visibilities,
        coarse,
        weights,
        offset,
        pairs,
    )


    trows = gain_tiles * SUB

    def ready(own, at):
        return pl.pallas_call(
            functools.partial(ready_kernel, at, chunks, owned, stations, trows),
            out_shape=[
                shape(own.shape, bf16),
                shape((4 * owned, devices * trows), bf16),
                shape((2 * LANES, parts * channels), bf16),
            ],
            in_specs=[smem, vmem],
            out_specs=[vmem] * 3,
            scratch_shapes=[dma],
            compiler_params=some,
            name="make_ready",
        )(turn, own)

    if halves:
        sent = list(sent)
        sent.insert(near + 1, alone)

    def swap(array, x):
        return lax.ppermute(array, "bl", [(d, d ^ x) for d in range(devices)])

    if halves:
        own, choice, basis = ready(sent[0], rows_at + depth)
        arrived = {x: swap(sent[x], x) if x else own for x in range(devices)}
        order, late = schedule(near)
        even = list(range(near, devices, 2))
        collected = pl.pallas_call(
            functools.partial(collect_kernel, rows_at, depth),
            out_shape=shape((len(even) * depth, parts, LANES), bf16),
            in_specs=[anywhere] * len(even),
            out_specs=vmem,
            scratch_shapes=[dma((len(even),))],
            compiler_params=some,
            name="collect_gains",
        )(*[arrived[x] for x in even])
        passed = [swap(collected, 1)]
    else:
        arrived = {
            0: lax.all_gather(sent[1], "bl", axis=0),
            1: lax.all_to_all(sent[0], "bl", split_axis=0, concat_axis=0, tiled=True),
        }
        order, late, passed = [0], [1], []
        _, choice, basis = ready(sent[2], 0)

    gains, recip, slots, sums = pl.pallas_call(
        functools.partial(middle_kernel, capacity, near, depth, order),
        out_shape=(
            shape((2 * owned, parts * channels), f32),
            shape((owned, LANES), f32),
            shape((devices, LANES), i32),
            shape((chunks, owned, parts, LANES), f32),
        ),
        in_specs=[smem] + [vmem] * (2 + len(order) + len(passed)),
        out_specs=(vmem,) * 4,
        scratch_shapes=[
            pltpu.VMEM((devices * trows, 2 * LANES), f32),
            pltpu.VMEM((devices, LANES), f32),
            pltpu.VMEM((devices, LANES), f32),
            pltpu.VMEM((devices, LANES), i32),
            pltpu.SMEM((devices, LANES), i32),
            pltpu.VMEM((chunks, owned + 1, parts, LANES), f32),
            pltpu.VMEM((chunks, owned + 1, parts, LANES), f32),
            dma,
        ],
        compiler_params=some,
        name="gains_and_sums",
    )(me, choice, basis, *[arrived[x] for x in order], *passed)
    return pl.pallas_call(
        functools.partial(finish_kernel, capacity, late),
        out_shape=shape((owned, parts, channels), bf16),
        in_specs=[smem] + [vmem] * (3 + len(late)),
        out_specs=hbm,
        scratch_shapes=[
            pltpu.VMEM((chunks, owned, parts, LANES), f32),
            pltpu.VMEM((chunks, owned, parts, LANES), f32),
            pltpu.VMEM((chunks, owned, parts, LANES), bf16),
            dma((chunks,)),
        ],
        compiler_params=some,
        name="sum_and_apply",
    )(slots, gains, recip, sums, *[arrived[x] for x in late])


def solution(mesh):
    placed = (
        P(("groups", "bl"), None, None),
        P(("groups", "bl"), None),
        P(("groups", "bl")),
        P("bl", None),
        P(("groups", "bl"), None, None),
        P("groups", None),
        P("groups"),
    )
    return jax.shard_map(
        on_device,
        mesh=mesh,
        in_specs=placed,
        out_specs=P(("groups", "bl"), None, None),
        check_vma=False,
    )
```

```python
import functools

import jax
import jax.numpy as jnp
from jax import lax
from jax.experimental import pallas as pl
from jax.experimental.pallas import tpu as pltpu
from jax.sharding import PartitionSpec as P

LANES = 128
SUB = 8
USED = 48
PARTS = 4
ALL_VMEM = 60 * 1024 * 1024
SOME_VMEM = 24 * 1024 * 1024


def round_up(value, unit):
    return -(-value // unit) * unit


def schedule(near):
    even, odd = list(range(near, 2 * near, 2)), list(range(near + 1, 2 * near, 2))
    close = list(range(near // 2, near)) + list(range(1, near // 2))
    cross, late = even[2:] + odd[1:-2], odd[-2:]
    order = [0] + even[:2] + close[:2]
    close = close[2:]
    while cross:
        order += cross[:1] + close[:1]
        cross, close = cross[1:], close[1:]
    return order + close + odd[:1], late


def with_gains(near):
    return list(range(near)) + list(range(near, 2 * near, 2))


def start_all(pairs, sems):
    moves = [pltpu.make_async_copy(src, dst, sems.at[i]) for i, (src, dst) in enumerate(pairs)]
    for move in moves:
        move.start()
    return moves


def pack_kernel(
    capacity,
    near,
    targets,
    me_s,
    owner_hbm,
    owner_row_hbm,
    slot_row_hbm,
    vis_hbm,
    coarse_hbm,
    weights_hbm,
    offset_hbm,
    pairs_hbm,
    *rest,
):
    outs = rest[:-16]
    (
        weights_ref,
        offset_ref,
        pairs_ref,
        small_ref,
        parts_ref,
        owner_s,
        place_s,
        count_s,
        owner_ref,
        slot_ref,
        vis_ref,
        coarse_ref,
        turn_ref,
        meta_ref,
        block_ref,
        sems,
    ) = rest[-16:]
    rows = vis_ref.shape[0]
    chunks = vis_ref.shape[2] // LANES
    devices = block_ref.shape[0]
    terms, stations = coarse_ref.shape
    half = stations // 2
    depth = meta_ref.shape[0]
    gain_tiles = (depth - 1) // 2
    span = rows // PARTS
    moves = start_all(
        (
            (owner_hbm, owner_s),
            (coarse_hbm, coarse_ref),
            (owner_row_hbm, owner_ref),
            (slot_row_hbm, slot_ref),
            (weights_hbm, weights_ref),
            (offset_hbm, offset_ref),
            (pairs_hbm, pairs_ref),
        ),
        sems,
    )
    fetches = start_all(
        [
            (vis_hbm.at[pl.ds(i * span, span)], vis_ref.at[pl.ds(i * span, span)])
            for i in range(PARTS)
        ],
        sems.at[pl.ds(len(moves), PARTS)],
    )
    turn_ref[...] = jnp.zeros_like(turn_ref)
    for d in range(devices):
        count_s[d] = 0
    me = me_s[0]
    moves[0].wait()

    def rank(r, carry):
        x = owner_s[r] ^ me
        k = count_s[x]
        count_s[x] = k + 1
        place_s[r] = x * capacity + k
        return carry

    lax.fori_loop(0, rows, rank, 0, unroll=8)
    for move in moves[1:]:
        move.wait()

    turn_ref[0:terms, 0:half] = coarse_ref[:, 0:half]
    turn_ref[64 : 64 + terms, 0:half] = coarse_ref[:, half:stations]
    gains = turn_ref[...].T
    high = gains.astype(jnp.bfloat16)
    low = (gains - high.astype(jnp.float32)).astype(jnp.bfloat16)
    for i in range(gain_tiles):
        meta_ref[i] = high[i * SUB : (i + 1) * SUB, :]
        meta_ref[gain_tiles + i] = low[i * SUB : (i + 1) * SUB, :]
    sub = lax.broadcasted_iota(jnp.int32, (SUB, LANES), 0)
    codes = jnp.where(sub == 0, owner_ref[...], slot_ref[...])
    meta_ref[2 * gain_tiles] = codes.astype(jnp.float32).astype(jnp.bfloat16)
    steps = weights_ref.shape[0]
    small_ref[...] = jnp.zeros_like(small_ref)
    small_ref[0:steps, :] = weights_ref[...]
    for c in range(chunks):
        lanes = slice(c * LANES, (c + 1) * LANES)
        small_ref[steps : steps + 1, lanes] = offset_ref[c : c + 1, :].astype(jnp.float32)
    small_ref[4:6, 0 : pairs_ref.shape[1]] = pairs_ref[...].astype(jnp.float32)
    left = small_ref[...]
    for p in range(3):
        piece = left.astype(jnp.bfloat16)
        left = left - piece.astype(jnp.float32)
        for c in range(chunks):
            parts_ref[p * chunks + c] = piece[:, c * LANES : (c + 1) * LANES]

    at = chunks * capacity
    if near > 1:
        outs = dict(zip(targets, outs))
        pairs = [(meta_ref, outs[x].at[pl.ds(at, depth)]) for x in targets if x in with_gains(near)]
    else:
        pairs = [(meta_ref, outs[1])]
    if near == 1:
        pairs += [(parts_ref, outs[2])]
    elif 0 in targets:
        pairs += [(parts_ref, outs[0].at[pl.ds(at + depth, 3 * chunks)])]
    start = len(moves) + PARTS
    sends = start_all(pairs, sems.at[pl.ds(start, len(pairs))])
    start += len(pairs)

    def place(r, carry):
        p = place_s[r]
        for c in range(chunks):
            flat_ref[p * chunks + c] = vis_ref[r, :, c * LANES : (c + 1) * LANES]
        return carry

    flat_ref = block_ref.reshape(devices * at, SUB, LANES)
    for i in range(PARTS):
        fetches[i].wait()
        lax.fori_loop(i * span, (i + 1) * span, place, 0, unroll=8)
    if near > 1:
        pairs = [(block_ref.at[x], outs[x].at[pl.ds(0, at)]) for x in targets]
    else:
        pairs = [(block_ref, outs[0])]
    sends += start_all(pairs, sems.at[pl.ds(start, len(pairs))])
    for send in sends:
        send.wait()


def first_kernel(capacity, target, me_s, owner_hbm, vis_hbm, out_hbm, owner_s, list_s, vis_ref, block_ref, sems):
    rows = vis_ref.shape[0]
    chunks = vis_ref.shape[2] // LANES
    moves = start_all(((owner_hbm, owner_s), (vis_hbm, vis_ref)), sems)
    wanted = me_s[0] ^ target
    moves[0].wait()

    def note(r, k):
        list_s[k] = r
        return k + jnp.where(owner_s[r] == wanted, 1, 0)

    count = lax.fori_loop(0, rows, note, 0, unroll=8)
    moves[1].wait()

    def place(k, carry):
        r = list_s[k]
        for c in range(chunks):
            block_ref[chunks * k + c] = vis_ref[r, :, c * LANES : (c + 1) * LANES]
        return carry

    lax.fori_loop(0, count, place, 0)
    send = start_all([(block_ref, out_hbm)], sems)[0]
    send.wait()


def ready_kernel(
    at, chunks, owned, stations, trows, turn_s, own_ref, own_out_ref, choice_ref, basis_ref, sem
):
    move = pltpu.make_async_copy(own_ref, own_out_ref, sem)
    move.start()
    pieces = [
        jnp.concatenate(
            [own_ref[at + p * chunks + c].astype(jnp.float32) for c in range(chunks)], axis=1
        )
        for p in range(3)
    ]
    small = pieces[0] + pieces[1] + pieces[2]
    channels = small.shape[1]
    half = stations // 2

    station = small[4:6, 0:LANES]
    sender = jnp.floor((station + 0.5) * (1.0 / stations))
    within = station - sender * stations
    second = (within >= float(half)).astype(jnp.float32)
    line = (sender.astype(jnp.int32) ^ turn_s[0]).astype(jnp.float32) * trows + within - second * half
    diagonal = lax.broadcasted_iota(jnp.int32, (owned, LANES), 0) == lax.broadcasted_iota(
        jnp.int32, (owned, LANES), 1
    )

    def upright(row):
        return jnp.sum(jnp.where(diagonal, row, 0.0), axis=1, keepdims=True)

    lines = jnp.concatenate([upright(line[side : side + 1]) for side in range(2)], axis=0)
    seconds = jnp.concatenate([upright(second[side : side + 1]) for side in range(2)], axis=0)
    table = choice_ref.shape[1]
    same = lines == lax.broadcasted_iota(jnp.int32, (2 * owned, table), 1).astype(jnp.float32)
    for h in range(2):
        choice_ref[2 * owned * h : 2 * owned * (h + 1), :] = (
            jnp.where(jnp.logical_and(same, seconds == float(h)), 1.0, 0.0).astype(jnp.bfloat16)
        )

    index = lax.broadcasted_iota(jnp.int32, (64, channels), 0)
    knot = (index >> 3).astype(jnp.float32)
    basis = jnp.zeros((64, channels), jnp.float32)
    for step in range(3):
        basis = basis + jnp.where(knot == small[3:4, :] + float(step), small[step : step + 1, :], 0.0)
    high = basis.astype(jnp.bfloat16).astype(jnp.float32)
    component = index & 7
    for j in range(8):
        cols = slice(j * channels, (j + 1) * channels)
        main = jnp.where(component == j, high, 0.0).astype(jnp.bfloat16)
        rest = jnp.where(component == j, basis - high, 0.0).astype(jnp.bfloat16)
        basis_ref[0:64, cols] = main
        basis_ref[64:128, cols] = main
        basis_ref[128:192, cols] = rest
        basis_ref[192:256, cols] = jnp.zeros_like(rest)
    move.wait()


def collect_kernel(at, depth, *rest):
    blocks, (out_ref, sems) = rest[:-2], rest[-2:]
    moves = start_all(
        [
            (block.at[pl.ds(at, depth)], out_ref.at[pl.ds(i * depth, depth)])
            for i, block in enumerate(blocks)
        ],
        sems,
    )
    for move in moves:
        move.wait()


def list_rows(owner, slot, target, capacity, spare):
    senders = owner.shape[0]
    mine = owner == target
    counted = mine.astype(jnp.float32)
    before = lax.broadcasted_iota(jnp.int32, (LANES, LANES), 0) < lax.broadcasted_iota(
        jnp.int32, (LANES, LANES), 1
    )
    rank = jnp.dot(
        counted.astype(jnp.bfloat16),
        before.astype(jnp.float32).astype(jnp.bfloat16),
        preferred_element_type=jnp.float32,
    )
    lane = lax.broadcasted_iota(jnp.int32, (senders, LANES), 1)
    count = jnp.sum(counted, axis=1, keepdims=True)
    listing = jnp.where(lane == capacity, count, 0.0)
    for k in range(capacity):
        here = jnp.logical_and(mine, rank == float(k))
        kth = jnp.sum(jnp.where(here, slot, 0.0), axis=1, keepdims=True)
        kth = jnp.where(count > float(k), kth, float(spare))
        listing = jnp.where(lane == k, kth, listing)
    return listing.astype(jnp.int32), mine


def add_rows(acc_refs, slots_s, line, capacity, rows_ref):
    chunks, several = acc_refs[0].shape[0], len(acc_refs)

    def add(i, carry):
        for u, acc_ref in enumerate(acc_refs):
            k = several * i + u
            b = slots_s[line, k]
            for c in range(chunks):
                acc_ref[c, b] += rows_ref[chunks * k + c].astype(jnp.float32)
        return carry

    lax.fori_loop(0, (slots_s[line, capacity] + several - 1) // several, add, 0)


def add_table(table_ref, x, block, at, depth):
    gain_tiles = (depth - 1) // 2
    for i in range(gain_tiles):
        rows = slice((x * gain_tiles + i) * SUB, (x * gain_tiles + i + 1) * SUB)
        table_ref[rows, 0:LANES] = block[at + i].astype(jnp.float32)
        table_ref[rows, LANES : 2 * LANES] = block[at + gain_tiles + i].astype(jnp.float32)
    return block[at + 2 * gain_tiles].astype(jnp.float32)


def count_rows(hits, mine, slot):
    which = lax.broadcasted_iota(jnp.int32, hits.shape, 0).astype(jnp.float32)
    slot = jnp.where(mine, slot, -1.0)
    for x in range(slot.shape[0]):
        hits = hits + (slot[x : x + 1, :] == which).astype(jnp.float32)
    return hits


def middle_kernel(capacity, near, depth, order, me_s, choice_ref, basis_ref, *rest):
    arrived, passed = dict(zip(order, rest)), rest[len(order) : -12]
    gains_ref, recip_ref, slots_ref, sums_ref = rest[-12:-8]
    table_ref, owner_ref, slot_ref, slots_v, slots_s, one_ref, two_ref, sem = rest[-8:]
    devices = owner_ref.shape[0]
    owned = recip_ref.shape[0]
    chunks = sums_ref.shape[0]
    for x in range(devices):
        if near == 1:
            code = add_table(table_ref, x, arrived[0].at[x], 0, depth)
        elif x in with_gains(near):
            code = add_table(table_ref, x, arrived[x], chunks * capacity, depth)
        else:
            code = add_table(table_ref, x, passed[0], (x - near) // 2 * depth, depth)
        owner_ref[x : x + 1, :] = code[0:1, :]
        slot_ref[x : x + 1, :] = code[1:2, :]
    slot = slot_ref[...]
    listing, mine = list_rows(
        owner_ref[...], slot, me_s[0].astype(jnp.float32), capacity, owned
    )
    slots_ref[...] = listing
    slots_v[...] = listing
    move = pltpu.make_async_copy(slots_v, slots_s, sem)
    move.start()
    hits = count_rows(jnp.zeros((owned, LANES), jnp.float32), mine, slot)
    tally = jnp.sum(hits, axis=1, keepdims=True)
    recip_ref[...] = jnp.broadcast_to(1.0 / jnp.maximum(tally, 1.0), recip_ref.shape)

    picked = jnp.dot(
        choice_ref[...], table_ref[...].astype(jnp.bfloat16), preferred_element_type=jnp.float32
    )
    front, back = picked[0 : 2 * owned], picked[2 * owned : 4 * owned]
    lower = lax.broadcasted_iota(jnp.int32, (2 * owned, LANES), 1) < 64
    high = front[:, 0:LANES] + pltpu.roll(back[:, 0:LANES], 64, 1)
    low = pltpu.roll(front[:, LANES:], 64, 1) + back[:, LANES:]
    coarse = jnp.concatenate([jnp.where(lower, high, low), jnp.where(lower, high, 0.0)], axis=1)
    coarse = coarse.astype(jnp.bfloat16)
    width = 2 * LANES * chunks
    for n in range(0, basis_ref.shape[1], width):
        fine = jnp.dot(coarse, basis_ref[:, n : n + width], preferred_element_type=jnp.float32)
        gains_ref[:, n : n + width] = fine.astype(jnp.bfloat16).astype(jnp.float32)

    one_ref[...] = jnp.zeros_like(one_ref)
    two_ref[...] = jnp.zeros_like(two_ref)
    move.wait()
    if near > 1:
        for x in order:
            add_rows((one_ref, two_ref), slots_s, x, capacity, arrived[x])
    sums_ref[...] = one_ref[:, 0:owned] + two_ref[:, 0:owned]


def finish_kernel(capacity, late, slots_s, gains_ref, recip_ref, sums_ref, *rest):
    far = rest[: len(late)]
    out_hbm, acc_ref, res_ref, out_ref, sems = rest[len(late) :]
    owned, parts, channels = out_hbm.shape
    chunks = channels // LANES
    acc_ref[...] = sums_ref[...]
    if len(late) > 1:
        for x, rows_ref in zip(late, far):
            add_rows((acc_ref,), slots_s, x, capacity, rows_ref)
    else:

        def from_device(d, carry):
            add_rows((acc_ref,), slots_s, d, capacity, far[0].at[d])
            return carry

        lax.fori_loop(0, far[0].shape[0], from_device, 0)

    flat = acc_ref.reshape(chunks * owned * parts, LANES)
    done = res_ref.reshape(chunks * owned * parts, LANES)
    sends = []
    for c in range(chunks):
        for b0 in range(0, owned, SUB):
            scale = recip_ref[b0 : b0 + SUB, :]
            row = (c * owned + b0) * parts
            vis = [flat[pl.ds(row + j, SUB, stride=parts), :] for j in range(parts)]
            planes = [slice(j * channels + c * LANES, j * channels + (c + 1) * LANES) for j in range(parts)]
            lhs = [gains_ref[b0 : b0 + SUB, plane] for plane in planes]
            rhs = [gains_ref[owned + b0 : owned + b0 + SUB, plane] for plane in planes]
            mid_re, mid_im = [], []
            for row_a in range(2):
                for col_b in range(2):
                    re = im = 0.0
                    for inner in range(2):
                        lr, li = lhs[2 * row_a + inner], lhs[4 + 2 * row_a + inner]
                        vr, vi = vis[2 * inner + col_b], vis[4 + 2 * inner + col_b]
                        re = re + lr * vr - li * vi
                        im = im + lr * vi + li * vr
                    mid_re.append(re * scale)
                    mid_im.append(im * scale)
            for row_a in range(2):
                for col_b in range(2):
                    re = im = 0.0
                    for inner in range(2):
                        mr, mi = mid_re[2 * row_a + inner], mid_im[2 * row_a + inner]
                        rr, ri = rhs[2 * col_b + inner], rhs[4 + 2 * col_b + inner]
                        re = re + mr * rr + mi * ri
                        im = im + mi * rr - mr * ri
                    j = 2 * row_a + col_b
                    done[pl.ds(row + j, SUB, stride=parts), :] = re
                    done[pl.ds(row + 4 + j, SUB, stride=parts), :] = im
        out_ref[c] = res_ref[c].astype(out_ref.dtype)
        sends.append(
            pltpu.make_async_copy(
                out_ref.at[c], out_hbm.at[:, :, pl.ds(c * LANES, LANES)], sems.at[c]
            )
        )
        sends[-1].start()
    for send in sends:
        send.wait()


def on_device(
    visibilities,
    row_owner,
    row_slot,
    baseline_station_pairs,
    gains_coarse,
    band_weights,
    band_offset,
):
    devices = lax.axis_size("bl")
    rows, parts, channels = visibilities.shape
    capacity = 2 * rows // devices
    owned = baseline_station_pairs.shape[0]
    stations, _, knots = gains_coarse.shape
    chunks = channels // LANES
    gain_tiles = round_up(stations // 2, SUB) // SUB
    depth = 2 * gain_tiles + 1
    near = devices // 2 if devices <= 16 else 1
    halves = near > 1
    f32, bf16, i32 = jnp.float32, jnp.bfloat16, jnp.int32
    vmem = pl.BlockSpec(memory_space=pltpu.VMEM)
    smem = pl.BlockSpec(memory_space=pltpu.SMEM)
    hbm = pl.BlockSpec(memory_space=pltpu.HBM)
    anywhere = pl.BlockSpec(memory_space=pl.ANY)
    most = pltpu.CompilerParams(vmem_limit_bytes=ALL_VMEM)
    some = pltpu.CompilerParams(vmem_limit_bytes=SOME_VMEM)
    shape = jax.ShapeDtypeStruct
    dma = pltpu.SemaphoreType.DMA

    me = lax.axis_index("bl").astype(i32).reshape(1)
    turn = me if halves else jnp.zeros_like(me)
    owner = row_owner.reshape(rows)
    coarse = gains_coarse.transpose(2, 1, 0).reshape(knots * parts, stations)
    block = (chunks * capacity, parts, LANES)
    rows_at = chunks * capacity
    if halves:
        long = with_gains(near) + [near + 3]
        outs = [
            shape((rows_at + (depth if x in long else 0), parts, LANES), bf16)
            for x in range(devices)
        ]
        outs[0] = shape((rows_at + depth + 3 * chunks, parts, LANES), bf16)
    else:
        outs = [
            shape((devices,) + block, bf16),
            shape((depth, SUB, LANES), bf16),
            shape((3 * chunks, SUB, LANES), bf16),
        ]
    pairs = baseline_station_pairs.T
    weights = band_weights.T
    offset = band_offset.reshape(chunks, LANES)
    me_owner = row_owner.reshape(rows)
    if halves:
        target = near + 1
        alone = pl.pallas_call(
            functools.partial(first_kernel, capacity, target),
            out_shape=outs[target],
            in_specs=[smem, hbm, hbm],
            out_specs=hbm,
            scratch_shapes=[
                pltpu.SMEM((rows,), i32),
                pltpu.SMEM((rows + 8,), i32),
                pltpu.VMEM((rows, parts, channels), bf16),
                pltpu.VMEM(outs[target].shape, bf16),
                dma((2,)),
            ],
            compiler_params=most,
            name="pack_first",
        )(me, me_owner, visibilities)
    def pack(targets, outs):
        return pl.pallas_call(
            functools.partial(pack_kernel, capacity, near, targets),
            out_shape=outs,
            in_specs=[smem] + [hbm] * 8,
            out_specs=[hbm] * len(outs),
            scratch_shapes=[
                pltpu.VMEM(weights.shape, f32),
                pltpu.VMEM(offset.shape, i32),
                pltpu.VMEM(pairs.shape, i32),
                pltpu.VMEM((SUB, channels), f32),
                pltpu.VMEM((3 * chunks, SUB, LANES), bf16),
                pltpu.SMEM((rows,), i32),
                pltpu.SMEM((rows,), i32),
                pltpu.SMEM((devices,), i32),
                pltpu.VMEM((1, rows), i32),
                pltpu.VMEM((1, rows), i32),
                pltpu.VMEM((rows, parts, channels), bf16),
                pltpu.VMEM((knots * parts, stations), f32),
                pltpu.VMEM((LANES, LANES), f32),
                pltpu.VMEM((depth, SUB, LANES), bf16),
                pltpu.VMEM((devices,) + block, bf16),
                dma((9 + PARTS + 2 * devices,)),
            ],
            compiler_params=most,
            name="pack_rows",
        )(
            turn,
            owner,
            row_owner.reshape(1, rows),
            row_slot.reshape(1, rows),
            visibilities,
            coarse,
            weights,
            offset,
            pairs,
        )


    if halves:
        order, _ = schedule(near)
        soon = order[1:5]
        later = [x for x in range(devices) if x not in soon + [target]]
        sent = {target: alone}
        for some_of in (soon, later):
            sent.update(zip(some_of, pack(some_of, [outs[x] for x in some_of])))
    else:
        sent = pack([0, 1, 2], outs)

    trows = gain_tiles * SUB

    def ready(own, at):
        return pl.pallas_call(
            functools.partial(ready_kernel, at, chunks, owned, stations, trows),
            out_shape=[
                shape(own.shape, bf16),
                shape((4 * owned, devices * trows), bf16),
                shape((2 * LANES, parts * channels), bf16),
            ],
            in_specs=[smem, vmem],
            out_specs=[vmem] * 3,
            scratch_shapes=[dma],
            compiler_params=some,
            name="make_ready",
        )(turn, own)

    def swap(array, x):
        return lax.ppermute(array, "bl", [(d, d ^ x) for d in range(devices)])

    if halves:
        own, choice, basis = ready(sent[0], rows_at + depth)
        arrived = {x: swap(sent[x], x) if x else own for x in range(devices)}
        order, late = schedule(near)
        even = list(range(near, devices, 2))
        collected = pl.pallas_call(
            functools.partial(collect_kernel, rows_at, depth),
            out_shape=shape((len(even) * depth, parts, LANES), bf16),
            in_specs=[anywhere] * len(even),
            out_specs=vmem,
            scratch_shapes=[dma((len(even),))],
            compiler_params=some,
            name="collect_gains",
        )(*[arrived[x] for x in even])
        passed = [swap(collected, 1)]
    else:
        arrived = {
            0: lax.all_gather(sent[1], "bl", axis=0),
            1: lax.all_to_all(sent[0], "bl", split_axis=0, concat_axis=0, tiled=True),
        }
        order, late, passed = [0], [1], []
        _, choice, basis = ready(sent[2], 0)

    gains, recip, slots, sums = pl.pallas_call(
        functools.partial(middle_kernel, capacity, near, depth, order),
        out_shape=(
            shape((2 * owned, parts * channels), f32),
            shape((owned, LANES), f32),
            shape((devices, LANES), i32),
            shape((chunks, owned, parts, LANES), f32),
        ),
        in_specs=[smem] + [vmem] * (2 + len(order) + len(passed)),
        out_specs=(vmem,) * 4,
        scratch_shapes=[
            pltpu.VMEM((devices * trows, 2 * LANES), f32),
            pltpu.VMEM((devices, LANES), f32),
            pltpu.VMEM((devices, LANES), f32),
            pltpu.VMEM((devices, LANES), i32),
            pltpu.SMEM((devices, LANES), i32),
            pltpu.VMEM((chunks, owned + 1, parts, LANES), f32),
            pltpu.VMEM((chunks, owned + 1, parts, LANES), f32),
            dma,
        ],
        compiler_params=some,
        name="gains_and_sums",
    )(me, choice, basis, *[arrived[x] for x in order], *passed)
    return pl.pallas_call(
        functools.partial(finish_kernel, capacity, late),
        out_shape=shape((owned, parts, channels), bf16),
        in_specs=[smem] + [vmem] * (3 + len(late)),
        out_specs=hbm,
        scratch_shapes=[
            pltpu.VMEM((chunks, owned, parts, LANES), f32),
            pltpu.VMEM((chunks, owned, parts, LANES), f32),
            pltpu.VMEM((chunks, owned, parts, LANES), bf16),
            dma((chunks,)),
        ],
        compiler_params=some,
        name="sum_and_apply",
    )(slots, gains, recip, sums, *[arrived[x] for x in late])


def solution(mesh):
    placed = (
        P(("groups", "bl"), None, None),
        P(("groups", "bl"), None),
        P(("groups", "bl")),
        P("bl", None),
        P(("groups", "bl"), None, None),
        P("groups", None),
        P("groups"),
    )
    return jax.shard_map(
        on_device,
        mesh=mesh,
        in_specs=placed,
        out_specs=P(("groups", "bl"), None, None),
        check_vma=False,
    )
```

```python
import functools

import jax
import jax.numpy as jnp
from jax import lax
from jax.experimental import pallas as pl
from jax.experimental.pallas import tpu as pltpu
from jax.sharding import PartitionSpec as P

LANES = 128
SUB = 8
USED = 48
PARTS = 4
ALL_VMEM = 60 * 1024 * 1024
SOME_VMEM = 24 * 1024 * 1024


def round_up(value, unit):
    return -(-value // unit) * unit


def schedule(near):
    even, odd = list(range(near, 2 * near, 2)), list(range(near + 1, 2 * near, 2))
    close = list(range(near // 2, near)) + list(range(1, near // 2))
    cross, late = even[2:] + odd[1:-2], odd[-2:]
    order = [0] + even[:2] + close[:2]
    close = close[2:]
    while cross:
        order += cross[:1] + close[:1]
        cross, close = cross[1:], close[1:]
    return order + close + odd[:1], late


def with_gains(near):
    return list(range(near)) + list(range(near, 2 * near, 2))


def start_all(pairs, sems):
    moves = [pltpu.make_async_copy(src, dst, sems.at[i]) for i, (src, dst) in enumerate(pairs)]
    for move in moves:
        move.start()
    return moves


def pack_kernel(
    capacity,
    near,
    me_s,
    owner_hbm,
    owner_row_hbm,
    slot_row_hbm,
    vis_hbm,
    coarse_hbm,
    weights_hbm,
    offset_hbm,
    pairs_hbm,
    *rest,
):
    outs = rest[:-16]
    (
        weights_ref,
        offset_ref,
        pairs_ref,
        small_ref,
        parts_ref,
        owner_s,
        place_s,
        count_s,
        owner_ref,
        slot_ref,
        vis_ref,
        coarse_ref,
        turn_ref,
        meta_ref,
        block_ref,
        sems,
    ) = rest[-16:]
    rows = vis_ref.shape[0]
    chunks = vis_ref.shape[2] // LANES
    devices = block_ref.shape[0]
    terms, stations = coarse_ref.shape
    half = stations // 2
    depth = meta_ref.shape[0]
    gain_tiles = (depth - 1) // 2
    span = rows // PARTS
    moves = start_all(
        (
            (owner_hbm, owner_s),
            (coarse_hbm, coarse_ref),
            (owner_row_hbm, owner_ref),
            (slot_row_hbm, slot_ref),
            (weights_hbm, weights_ref),
            (offset_hbm, offset_ref),
            (pairs_hbm, pairs_ref),
        ),
        sems,
    )
    fetches = start_all(
        [
            (vis_hbm.at[pl.ds(i * span, span)], vis_ref.at[pl.ds(i * span, span)])
            for i in range(PARTS)
        ],
        sems.at[pl.ds(len(moves), PARTS)],
    )
    turn_ref[...] = jnp.zeros_like(turn_ref)
    for d in range(devices):
        count_s[d] = 0
    me = me_s[0]
    moves[0].wait()

    def rank(r, carry):
        x = owner_s[r] ^ me
        k = count_s[x]
        count_s[x] = k + 1
        place_s[r] = x * capacity + k
        return carry

    lax.fori_loop(0, rows, rank, 0, unroll=8)
    for move in moves[1:]:
        move.wait()

    turn_ref[0:terms, 0:half] = coarse_ref[:, 0:half]
    turn_ref[64 : 64 + terms, 0:half] = coarse_ref[:, half:stations]
    gains = turn_ref[...].T
    high = gains.astype(jnp.bfloat16)
    low = (gains - high.astype(jnp.float32)).astype(jnp.bfloat16)
    for i in range(gain_tiles):
        meta_ref[i] = high[i * SUB : (i + 1) * SUB, :]
        meta_ref[gain_tiles + i] = low[i * SUB : (i + 1) * SUB, :]
    sub = lax.broadcasted_iota(jnp.int32, (SUB, LANES), 0)
    codes = jnp.where(sub == 0, owner_ref[...], slot_ref[...])
    meta_ref[2 * gain_tiles] = codes.astype(jnp.float32).astype(jnp.bfloat16)
    steps = weights_ref.shape[0]
    small_ref[...] = jnp.zeros_like(small_ref)
    small_ref[0:steps, :] = weights_ref[...]
    for c in range(chunks):
        lanes = slice(c * LANES, (c + 1) * LANES)
        small_ref[steps : steps + 1, lanes] = offset_ref[c : c + 1, :].astype(jnp.float32)
    small_ref[4:6, 0 : pairs_ref.shape[1]] = pairs_ref[...].astype(jnp.float32)
    left = small_ref[...]
    for p in range(3):
        piece = left.astype(jnp.bfloat16)
        left = left - piece.astype(jnp.float32)
        for c in range(chunks):
            parts_ref[p * chunks + c] = piece[:, c * LANES : (c + 1) * LANES]

    at = chunks * capacity
    if near > 1:
        outs = list(outs[: near + 1]) + [None] + list(outs[near + 1 :])
        pairs = [(meta_ref, outs[x].at[pl.ds(at, depth)]) for x in with_gains(near)]
    else:
        pairs = [(meta_ref, outs[1])]
    at_small = at + depth if near > 1 else 0
    pairs += [(parts_ref, outs[0 if near > 1 else -1].at[pl.ds(at_small, 3 * chunks)])]
    start = len(moves) + PARTS
    sends = start_all(pairs, sems.at[pl.ds(start, len(pairs))])
    start += len(pairs)

    def place(r, carry):
        p = place_s[r]
        for c in range(chunks):
            flat_ref[p * chunks + c] = vis_ref[r, :, c * LANES : (c + 1) * LANES]
        return carry

    flat_ref = block_ref.reshape(devices * at, SUB, LANES)
    for i in range(PARTS):
        fetches[i].wait()
        lax.fori_loop(i * span, (i + 1) * span, place, 0, unroll=8)
    if near > 1:
        pairs = [
            (block_ref.at[x], outs[x].at[pl.ds(0, at)]) for x in range(devices) if x != near + 1
        ]
    else:
        pairs = [(block_ref, outs[0])]
    sends += start_all(pairs, sems.at[pl.ds(start, len(pairs))])
    for send in sends:
        send.wait()


def first_kernel(capacity, target, me_s, owner_hbm, vis_hbm, out_hbm, owner_s, list_s, vis_ref, block_ref, sems):
    rows = vis_ref.shape[0]
    chunks = vis_ref.shape[2] // LANES
    moves = start_all(((owner_hbm, owner_s), (vis_hbm, vis_ref)), sems)
    wanted = me_s[0] ^ target
    moves[0].wait()

    def note(r, k):
        list_s[k] = r
        return k + jnp.where(owner_s[r] == wanted, 1, 0)

    count = lax.fori_loop(0, rows, note, 0, unroll=8)
    moves[1].wait()

    def place(k, carry):
        r = list_s[k]
        for c in range(chunks):
            block_ref[chunks * k + c] = vis_ref[r, :, c * LANES : (c + 1) * LANES]
        return carry

    lax.fori_loop(0, count, place, 0)
    send = start_all([(block_ref, out_hbm)], sems)[0]
    send.wait()


def ready_kernel(
    at, chunks, owned, stations, trows, turn_s, own_ref, own_out_ref, choice_ref, basis_ref, sem
):
    move = pltpu.make_async_copy(own_ref, own_out_ref, sem)
    move.start()
    pieces = [
        jnp.concatenate(
            [own_ref[at + p * chunks + c].astype(jnp.float32) for c in range(chunks)], axis=1
        )
        for p in range(3)
    ]
    small = pieces[0] + pieces[1] + pieces[2]
    channels = small.shape[1]
    half = stations // 2

    station = small[4:6, 0:LANES]
    sender = jnp.floor((station + 0.5) * (1.0 / stations))
    within = station - sender * stations
    second = (within >= float(half)).astype(jnp.float32)
    line = (sender.astype(jnp.int32) ^ turn_s[0]).astype(jnp.float32) * trows + within - second * half
    diagonal = lax.broadcasted_iota(jnp.int32, (owned, LANES), 0) == lax.broadcasted_iota(
        jnp.int32, (owned, LANES), 1
    )

    def upright(row):
        return jnp.sum(jnp.where(diagonal, row, 0.0), axis=1, keepdims=True)

    lines = jnp.concatenate([upright(line[side : side + 1]) for side in range(2)], axis=0)
    seconds = jnp.concatenate([upright(second[side : side + 1]) for side in range(2)], axis=0)
    table = choice_ref.shape[1]
    same = lines == lax.broadcasted_iota(jnp.int32, (2 * owned, table), 1).astype(jnp.float32)
    for h in range(2):
        choice_ref[2 * owned * h : 2 * owned * (h + 1), :] = (
            jnp.where(jnp.logical_and(same, seconds == float(h)), 1.0, 0.0).astype(jnp.bfloat16)
        )

    index = lax.broadcasted_iota(jnp.int32, (64, channels), 0)
    knot = (index >> 3).astype(jnp.float32)
    basis = jnp.zeros((64, channels), jnp.float32)
    for step in range(3):
        basis = basis + jnp.where(knot == small[3:4, :] + float(step), small[step : step + 1, :], 0.0)
    high = basis.astype(jnp.bfloat16).astype(jnp.float32)
    component = index & 7
    for j in range(8):
        cols = slice(j * channels, (j + 1) * channels)
        main = jnp.where(component == j, high, 0.0).astype(jnp.bfloat16)
        rest = jnp.where(component == j, basis - high, 0.0).astype(jnp.bfloat16)
        basis_ref[0:64, cols] = main
        basis_ref[64:128, cols] = main
        basis_ref[128:192, cols] = rest
        basis_ref[192:256, cols] = jnp.zeros_like(rest)
    move.wait()


def collect_kernel(at, depth, *rest):
    blocks, (out_ref, sems) = rest[:-2], rest[-2:]
    moves = start_all(
        [
            (block.at[pl.ds(at, depth)], out_ref.at[pl.ds(i * depth, depth)])
            for i, block in enumerate(blocks)
        ],
        sems,
    )
    for move in moves:
        move.wait()


def list_rows(owner, slot, target, capacity, spare):
    senders = owner.shape[0]
    mine = owner == target
    counted = mine.astype(jnp.float32)
    before = lax.broadcasted_iota(jnp.int32, (LANES, LANES), 0) < lax.broadcasted_iota(
        jnp.int32, (LANES, LANES), 1
    )
    rank = jnp.dot(
        counted.astype(jnp.bfloat16),
        before.astype(jnp.float32).astype(jnp.bfloat16),
        preferred_element_type=jnp.float32,
    )
    lane = lax.broadcasted_iota(jnp.int32, (senders, LANES), 1)
    count = jnp.sum(counted, axis=1, keepdims=True)
    listing = jnp.where(lane == capacity, count, 0.0)
    for k in range(capacity):
        here = jnp.logical_and(mine, rank == float(k))
        kth = jnp.sum(jnp.where(here, slot, 0.0), axis=1, keepdims=True)
        kth = jnp.where(count > float(k), kth, float(spare))
        listing = jnp.where(lane == k, kth, listing)
    return listing.astype(jnp.int32), mine


def add_rows(acc_refs, slots_s, line, capacity, rows_ref):
    chunks, several = acc_refs[0].shape[0], len(acc_refs)

    def add(i, carry):
        for u, acc_ref in enumerate(acc_refs):
            k = several * i + u
            b = slots_s[line, k]
            for c in range(chunks):
                acc_ref[c, b] += rows_ref[chunks * k + c].astype(jnp.float32)
        return carry

    lax.fori_loop(0, (slots_s[line, capacity] + several - 1) // several, add, 0)


def add_table(table_ref, x, block, at, depth):
    gain_tiles = (depth - 1) // 2
    for i in range(gain_tiles):
        rows = slice((x * gain_tiles + i) * SUB, (x * gain_tiles + i + 1) * SUB)
        table_ref[rows, 0:LANES] = block[at + i].astype(jnp.float32)
        table_ref[rows, LANES : 2 * LANES] = block[at + gain_tiles + i].astype(jnp.float32)
    return block[at + 2 * gain_tiles].astype(jnp.float32)


def count_rows(hits, mine, slot):
    which = lax.broadcasted_iota(jnp.int32, hits.shape, 0).astype(jnp.float32)
    slot = jnp.where(mine, slot, -1.0)
    for x in range(slot.shape[0]):
        hits = hits + (slot[x : x + 1, :] == which).astype(jnp.float32)
    return hits


def middle_kernel(capacity, near, depth, order, me_s, choice_ref, basis_ref, *rest):
    arrived, passed = dict(zip(order, rest)), rest[len(order) : -12]
    gains_ref, recip_ref, slots_ref, sums_ref = rest[-12:-8]
    table_ref, owner_ref, slot_ref, slots_v, slots_s, one_ref, two_ref, sem = rest[-8:]
    devices = owner_ref.shape[0]
    owned = recip_ref.shape[0]
    chunks = sums_ref.shape[0]
    for x in range(devices):
        if near == 1:
            code = add_table(table_ref, x, arrived[0].at[x], 0, depth)
        elif x in with_gains(near):
            code = add_table(table_ref, x, arrived[x], chunks * capacity, depth)
        else:
            code = add_table(table_ref, x, passed[0], (x - near) // 2 * depth, depth)
        owner_ref[x : x + 1, :] = code[0:1, :]
        slot_ref[x : x + 1, :] = code[1:2, :]
    slot = slot_ref[...]
    listing, mine = list_rows(
        owner_ref[...], slot, me_s[0].astype(jnp.float32), capacity, owned
    )
    slots_ref[...] = listing
    slots_v[...] = listing
    move = pltpu.make_async_copy(slots_v, slots_s, sem)
    move.start()
    hits = count_rows(jnp.zeros((owned, LANES), jnp.float32), mine, slot)
    tally = jnp.sum(hits, axis=1, keepdims=True)
    recip_ref[...] = jnp.broadcast_to(1.0 / jnp.maximum(tally, 1.0), recip_ref.shape)

    picked = jnp.dot(
        choice_ref[...], table_ref[...].astype(jnp.bfloat16), preferred_element_type=jnp.float32
    )
    front, back = picked[0 : 2 * owned], picked[2 * owned : 4 * owned]
    lower = lax.broadcasted_iota(jnp.int32, (2 * owned, LANES), 1) < 64
    high = front[:, 0:LANES] + pltpu.roll(back[:, 0:LANES], 64, 1)
    low = pltpu.roll(front[:, LANES:], 64, 1) + back[:, LANES:]
    coarse = jnp.concatenate([jnp.where(lower, high, low), jnp.where(lower, high, 0.0)], axis=1)
    coarse = coarse.astype(jnp.bfloat16)
    width = 2 * LANES * chunks
    for n in range(0, basis_ref.shape[1], width):
        fine = jnp.dot(coarse, basis_ref[:, n : n + width], preferred_element_type=jnp.float32)
        gains_ref[:, n : n + width] = fine.astype(jnp.bfloat16).astype(jnp.float32)

    one_ref[...] = jnp.zeros_like(one_ref)
    two_ref[...] = jnp.zeros_like(two_ref)
    move.wait()
    if near > 1:
        for x in order:
            add_rows((one_ref, two_ref), slots_s, x, capacity, arrived[x])
    sums_ref[...] = one_ref[:, 0:owned] + two_ref[:, 0:owned]


def next_kernel(capacity, x, slots_ref, sums_ref, rows_ref, out_ref, slots_s, sem):
    move = pltpu.make_async_copy(slots_ref, slots_s, sem)
    move.start()
    out_ref[...] = sums_ref[...]
    move.wait()
    add_rows((out_ref,), slots_s, x, capacity, rows_ref)


def finish_kernel(capacity, last, slots_ref, gains_ref, recip_ref, sums_ref, *rest):
    far, (out_hbm, slots_s, acc_ref, res_ref, out_ref, sems) = rest[:-6], rest[-6:]
    owned, parts, channels = out_hbm.shape
    chunks = channels // LANES
    move = pltpu.make_async_copy(slots_ref, slots_s, sems.at[chunks])
    move.start()
    acc_ref[...] = sums_ref[...]
    move.wait()
    if last is not None:
        add_rows((acc_ref,), slots_s, last, capacity, far[0])
    else:

        def from_device(d, carry):
            add_rows((acc_ref,), slots_s, d, capacity, far[0].at[d])
            return carry

        lax.fori_loop(0, far[0].shape[0], from_device, 0)

    flat = acc_ref.reshape(chunks * owned * parts, LANES)
    done = res_ref.reshape(chunks * owned * parts, LANES)
    sends = []
    for c in range(chunks):
        for b0 in range(0, owned, SUB):
            scale = recip_ref[b0 : b0 + SUB, :]
            row = (c * owned + b0) * parts
            vis = [flat[pl.ds(row + j, SUB, stride=parts), :] for j in range(parts)]
            planes = [slice(j * channels + c * LANES, j * channels + (c + 1) * LANES) for j in range(parts)]
            lhs = [gains_ref[b0 : b0 + SUB, plane] for plane in planes]
            rhs = [gains_ref[owned + b0 : owned + b0 + SUB, plane] for plane in planes]
            mid_re, mid_im = [], []
            for row_a in range(2):
                for col_b in range(2):
                    re = im = 0.0
                    for inner in range(2):
                        lr, li = lhs[2 * row_a + inner], lhs[4 + 2 * row_a + inner]
                        vr, vi = vis[2 * inner + col_b], vis[4 + 2 * inner + col_b]
                        re = re + lr * vr - li * vi
                        im = im + lr * vi + li * vr
                    mid_re.append(re * scale)
                    mid_im.append(im * scale)
            for row_a in range(2):
                for col_b in range(2):
                    re = im = 0.0
                    for inner in range(2):
                        mr, mi = mid_re[2 * row_a + inner], mid_im[2 * row_a + inner]
                        rr, ri = rhs[2 * col_b + inner], rhs[4 + 2 * col_b + inner]
                        re = re + mr * rr + mi * ri
                        im = im + mi * rr - mr * ri
                    j = 2 * row_a + col_b
                    done[pl.ds(row + j, SUB, stride=parts), :] = re
                    done[pl.ds(row + 4 + j, SUB, stride=parts), :] = im
        out_ref[c] = res_ref[c].astype(out_ref.dtype)
        sends.append(
            pltpu.make_async_copy(
                out_ref.at[c], out_hbm.at[:, :, pl.ds(c * LANES, LANES)], sems.at[c]
            )
        )
        sends[-1].start()
    for send in sends:
        send.wait()


def on_device(
    visibilities,
    row_owner,
    row_slot,
    baseline_station_pairs,
    gains_coarse,
    band_weights,
    band_offset,
):
    devices = lax.axis_size("bl")
    rows, parts, channels = visibilities.shape
    capacity = 2 * rows // devices
    owned = baseline_station_pairs.shape[0]
    stations, _, knots = gains_coarse.shape
    chunks = channels // LANES
    gain_tiles = round_up(stations // 2, SUB) // SUB
    depth = 2 * gain_tiles + 1
    near = devices // 2 if devices <= 16 else 1
    halves = near > 1
    f32, bf16, i32 = jnp.float32, jnp.bfloat16, jnp.int32
    vmem = pl.BlockSpec(memory_space=pltpu.VMEM)
    smem = pl.BlockSpec(memory_space=pltpu.SMEM)
    hbm = pl.BlockSpec(memory_space=pltpu.HBM)
    anywhere = pl.BlockSpec(memory_space=pl.ANY)
    most = pltpu.CompilerParams(vmem_limit_bytes=ALL_VMEM)
    some = pltpu.CompilerParams(vmem_limit_bytes=SOME_VMEM)
    shape = jax.ShapeDtypeStruct
    dma = pltpu.SemaphoreType.DMA

    me = lax.axis_index("bl").astype(i32).reshape(1)
    turn = me if halves else jnp.zeros_like(me)
    owner = row_owner.reshape(rows)
    coarse = gains_coarse.transpose(2, 1, 0).reshape(knots * parts, stations)
    block = (chunks * capacity, parts, LANES)
    rows_at = chunks * capacity
    if halves:
        long = with_gains(near) + [near + 3]
        outs = [
            shape((rows_at + (depth if x in long else 0), parts, LANES), bf16)
            for x in range(devices)
        ]
        outs[0] = shape((rows_at + depth + 3 * chunks, parts, LANES), bf16)
    else:
        outs = [
            shape((devices,) + block, bf16),
            shape((depth, SUB, LANES), bf16),
            shape((3 * chunks, SUB, LANES), bf16),
        ]
    pairs = baseline_station_pairs.T
    weights = band_weights.T
    offset = band_offset.reshape(chunks, LANES)
    me_owner = row_owner.reshape(rows)
    if halves:
        first = outs.pop(near + 1)
        alone = pl.pallas_call(
            functools.partial(first_kernel, capacity, near + 1),
            out_shape=first,
            in_specs=[smem, hbm, hbm],
            out_specs=hbm,
            scratch_shapes=[
                pltpu.SMEM((rows,), i32),
                pltpu.SMEM((rows + 8,), i32),
                pltpu.VMEM((rows, parts, channels), bf16),
                pltpu.VMEM(first.shape, bf16),
                dma((2,)),
            ],
            compiler_params=most,
            name="pack_first",
        )(me, me_owner, visibilities)
    sent = pl.pallas_call(
        functools.partial(pack_kernel, capacity, near),
        out_shape=outs,
        in_specs=[smem] + [hbm] * 8,
        out_specs=[hbm] * len(outs),
        scratch_shapes=[
            pltpu.VMEM(weights.shape, f32),
            pltpu.VMEM(offset.shape, i32),
            pltpu.VMEM(pairs.shape, i32),
            pltpu.VMEM((SUB, channels), f32),
            pltpu.VMEM((3 * chunks, SUB, LANES), bf16),
            pltpu.SMEM((rows,), i32),
            pltpu.SMEM((rows,), i32),
            pltpu.SMEM((devices,), i32),
            pltpu.VMEM((1, rows), i32),
            pltpu.VMEM((1, rows), i32),
            pltpu.VMEM((rows, parts, channels), bf16),
            pltpu.VMEM((knots * parts, stations), f32),
            pltpu.VMEM((LANES, LANES), f32),
            pltpu.VMEM((depth, SUB, LANES), bf16),
            pltpu.VMEM((devices,) + block, bf16),
            dma((9 + PARTS + 2 * devices,)),
        ],
        compiler_params=most,
        name="pack_rows",
    )(
        turn,
        owner,
        row_owner.reshape(1, rows),
        row_slot.reshape(1, rows),
        visibilities,
        coarse,
        weights,
        offset,
        pairs,
    )


    trows = gain_tiles * SUB

    def ready(own, at):
        return pl.pallas_call(
            functools.partial(ready_kernel, at, chunks, owned, stations, trows),
            out_shape=[
                shape(own.shape, bf16),
                shape((4 * owned, devices * trows), bf16),
                shape((2 * LANES, parts * channels), bf16),
            ],
            in_specs=[smem, vmem],
            out_specs=[vmem] * 3,
            scratch_shapes=[dma],
            compiler_params=some,
            name="make_ready",
        )(turn, own)

    if halves:
        sent = list(sent)
        sent.insert(near + 1, alone)

    def swap(array, x):
        return lax.ppermute(array, "bl", [(d, d ^ x) for d in range(devices)])

    if halves:
        own, choice, basis = ready(sent[0], rows_at + depth)
        arrived = {x: swap(sent[x], x) if x else own for x in range(devices)}
        order, late = schedule(near)
        even = list(range(near, devices, 2))
        collected = pl.pallas_call(
            functools.partial(collect_kernel, rows_at, depth),
            out_shape=shape((len(even) * depth, parts, LANES), bf16),
            in_specs=[anywhere] * len(even),
            out_specs=vmem,
            scratch_shapes=[dma((len(even),))],
            compiler_params=some,
            name="collect_gains",
        )(*[arrived[x] for x in even])
        passed = [swap(collected, 1)]
    else:
        arrived = {
            0: lax.all_gather(sent[1], "bl", axis=0),
            1: lax.all_to_all(sent[0], "bl", split_axis=0, concat_axis=0, tiled=True),
        }
        order, late, passed = [0], [1], []
        _, choice, basis = ready(sent[2], 0)

    gains, recip, slots, sums = pl.pallas_call(
        functools.partial(middle_kernel, capacity, near, depth, order),
        out_shape=(
            shape((2 * owned, parts * channels), f32),
            shape((owned, LANES), f32),
            shape((devices, LANES), i32),
            shape((chunks, owned, parts, LANES), f32),
        ),
        in_specs=[smem] + [vmem] * (2 + len(order) + len(passed)),
        out_specs=(vmem,) * 4,
        scratch_shapes=[
            pltpu.VMEM((devices * trows, 2 * LANES), f32),
            pltpu.VMEM((devices, LANES), f32),
            pltpu.VMEM((devices, LANES), f32),
            pltpu.VMEM((devices, LANES), i32),
            pltpu.SMEM((devices, LANES), i32),
            pltpu.VMEM((chunks, owned + 1, parts, LANES), f32),
            pltpu.VMEM((chunks, owned + 1, parts, LANES), f32),
            dma,
        ],
        compiler_params=some,
        name="gains_and_sums",
    )(me, choice, basis, *[arrived[x] for x in order], *passed)
    if halves:
        before, last = late
        sums = pl.pallas_call(
            functools.partial(next_kernel, capacity, before),
            out_shape=shape(sums.shape, f32),
            in_specs=[anywhere, vmem, vmem],
            out_specs=vmem,
            scratch_shapes=[pltpu.SMEM((devices, LANES), i32), dma],
            compiler_params=some,
            name="sum_next",
        )(slots, sums, arrived[before])
    else:
        last = None
    return pl.pallas_call(
        functools.partial(finish_kernel, capacity, last),
        out_shape=shape((owned, parts, channels), bf16),
        in_specs=[anywhere] + [vmem] * 4,
        out_specs=hbm,
        scratch_shapes=[
            pltpu.SMEM((devices, LANES), i32),
            pltpu.VMEM((chunks, owned, parts, LANES), f32),
            pltpu.VMEM((chunks, owned, parts, LANES), f32),
            pltpu.VMEM((chunks, owned, parts, LANES), bf16),
            dma((chunks + 1,)),
        ],
        compiler_params=some,
        name="sum_and_apply",
    )(slots, gains, recip, sums, arrived[late[-1]])


def solution(mesh):
    placed = (
        P(("groups", "bl"), None, None),
        P(("groups", "bl"), None),
        P(("groups", "bl")),
        P("bl", None),
        P(("groups", "bl"), None, None),
        P("groups", None),
        P("groups"),
    )
    return jax.shard_map(
        on_device,
        mesh=mesh,
        in_specs=placed,
        out_specs=P(("groups", "bl"), None, None),
        check_vma=False,
    )
```

```python
import functools

import jax
import jax.numpy as jnp
from jax import lax
from jax.experimental import pallas as pl
from jax.experimental.pallas import tpu as pltpu
from jax.sharding import PartitionSpec as P

LANES = 128
SUB = 8
USED = 48
PARTS = 4
ALL_VMEM = 60 * 1024 * 1024
SOME_VMEM = 24 * 1024 * 1024


def round_up(value, unit):
    return -(-value // unit) * unit


def schedule(near):
    even, odd = list(range(near, 2 * near, 2)), list(range(near + 1, 2 * near, 2))
    close = list(range(near // 2, near)) + list(range(1, near // 2))
    return [0] + even[:2] + close[:2] + even[2:] + close[2:] + odd[:1], odd[1:]


def with_gains(near):
    return list(range(near)) + list(range(near, 2 * near, 2))


def start_all(pairs, sems):
    moves = [pltpu.make_async_copy(src, dst, sems.at[i]) for i, (src, dst) in enumerate(pairs)]
    for move in moves:
        move.start()
    return moves


def pack_kernel(
    capacity,
    near,
    me_s,
    owner_hbm,
    owner_row_hbm,
    slot_row_hbm,
    vis_hbm,
    coarse_hbm,
    weights_hbm,
    offset_hbm,
    pairs_hbm,
    *rest,
):
    outs = rest[:-16]
    (
        weights_ref,
        offset_ref,
        pairs_ref,
        small_ref,
        parts_ref,
        owner_s,
        place_s,
        count_s,
        owner_ref,
        slot_ref,
        vis_ref,
        coarse_ref,
        turn_ref,
        meta_ref,
        block_ref,
        sems,
    ) = rest[-16:]
    rows = vis_ref.shape[0]
    chunks = vis_ref.shape[2] // LANES
    devices = block_ref.shape[0]
    terms, stations = coarse_ref.shape
    half = stations // 2
    depth = meta_ref.shape[0]
    gain_tiles = (depth - 1) // 2
    span = rows // PARTS
    moves = start_all(
        (
            (owner_hbm, owner_s),
            (coarse_hbm, coarse_ref),
            (owner_row_hbm, owner_ref),
            (slot_row_hbm, slot_ref),
            (weights_hbm, weights_ref),
            (offset_hbm, offset_ref),
            (pairs_hbm, pairs_ref),
        ),
        sems,
    )
    fetches = start_all(
        [
            (vis_hbm.at[pl.ds(i * span, span)], vis_ref.at[pl.ds(i * span, span)])
            for i in range(PARTS)
        ],
        sems.at[pl.ds(len(moves), PARTS)],
    )
    turn_ref[...] = jnp.zeros_like(turn_ref)
    for d in range(devices):
        count_s[d] = 0
    me = me_s[0]
    moves[0].wait()

    def rank(r, carry):
        x = owner_s[r] ^ me
        k = count_s[x]
        count_s[x] = k + 1
        place_s[r] = x * capacity + k
        return carry

    lax.fori_loop(0, rows, rank, 0, unroll=8)
    for move in moves[1:]:
        move.wait()

    turn_ref[0:terms, 0:half] = coarse_ref[:, 0:half]
    turn_ref[64 : 64 + terms, 0:half] = coarse_ref[:, half:stations]
    gains = turn_ref[...].T
    high = gains.astype(jnp.bfloat16)
    low = (gains - high.astype(jnp.float32)).astype(jnp.bfloat16)
    for i in range(gain_tiles):
        meta_ref[i] = high[i * SUB : (i + 1) * SUB, :]
        meta_ref[gain_tiles + i] = low[i * SUB : (i + 1) * SUB, :]
    sub = lax.broadcasted_iota(jnp.int32, (SUB, LANES), 0)
    codes = jnp.where(sub == 0, owner_ref[...], slot_ref[...])
    meta_ref[2 * gain_tiles] = codes.astype(jnp.float32).astype(jnp.bfloat16)
    steps = weights_ref.shape[0]
    small_ref[...] = jnp.zeros_like(small_ref)
    small_ref[0:steps, :] = weights_ref[...]
    for c in range(chunks):
        lanes = slice(c * LANES, (c + 1) * LANES)
        small_ref[steps : steps + 1, lanes] = offset_ref[c : c + 1, :].astype(jnp.float32)
    small_ref[4:6, 0 : pairs_ref.shape[1]] = pairs_ref[...].astype(jnp.float32)
    left = small_ref[...]
    for p in range(3):
        piece = left.astype(jnp.bfloat16)
        left = left - piece.astype(jnp.float32)
        for c in range(chunks):
            parts_ref[p * chunks + c] = piece[:, c * LANES : (c + 1) * LANES]

    at = chunks * capacity
    if near > 1:
        outs = list(outs[: near + 1]) + [None] + list(outs[near + 1 :])
        pairs = [(meta_ref, outs[x].at[pl.ds(at, depth)]) for x in with_gains(near)]
    else:
        pairs = [(meta_ref, outs[1])]
    at_small = at + depth if near > 1 else 0
    pairs += [(parts_ref, outs[0 if near > 1 else -1].at[pl.ds(at_small, 3 * chunks)])]
    start = len(moves) + PARTS
    sends = start_all(pairs, sems.at[pl.ds(start, len(pairs))])
    start += len(pairs)

    def place(r, carry):
        p = place_s[r]
        for c in range(chunks):
            flat_ref[p * chunks + c] = vis_ref[r, :, c * LANES : (c + 1) * LANES]
        return carry

    flat_ref = block_ref.reshape(devices * at, SUB, LANES)
    for i in range(PARTS):
        fetches[i].wait()
        lax.fori_loop(i * span, (i + 1) * span, place, 0, unroll=8)
    if near > 1:
        pairs = [
            (block_ref.at[x], outs[x].at[pl.ds(0, at)]) for x in range(devices) if x != near + 1
        ]
    else:
        pairs = [(block_ref, outs[0])]
    sends += start_all(pairs, sems.at[pl.ds(start, len(pairs))])
    for send in sends:
        send.wait()


def first_kernel(capacity, target, me_s, owner_hbm, vis_hbm, out_hbm, owner_s, list_s, vis_ref, block_ref, sems):
    rows = vis_ref.shape[0]
    chunks = vis_ref.shape[2] // LANES
    moves = start_all(((owner_hbm, owner_s), (vis_hbm, vis_ref)), sems)
    wanted = me_s[0] ^ target
    moves[0].wait()

    def note(r, k):
        list_s[k] = r
        return k + jnp.where(owner_s[r] == wanted, 1, 0)

    count = lax.fori_loop(0, rows, note, 0, unroll=8)
    moves[1].wait()

    def place(k, carry):
        r = list_s[k]
        for c in range(chunks):
            block_ref[chunks * k + c] = vis_ref[r, :, c * LANES : (c + 1) * LANES]
        return carry

    lax.fori_loop(0, count, place, 0)
    send = start_all([(block_ref, out_hbm)], sems)[0]
    send.wait()


def ready_kernel(
    at, chunks, owned, stations, trows, turn_s, own_ref, own_out_ref, choice_ref, basis_ref, sem
):
    move = pltpu.make_async_copy(own_ref, own_out_ref, sem)
    move.start()
    pieces = [
        jnp.concatenate(
            [own_ref[at + p * chunks + c].astype(jnp.float32) for c in range(chunks)], axis=1
        )
        for p in range(3)
    ]
    small = pieces[0] + pieces[1] + pieces[2]
    channels = small.shape[1]
    half = stations // 2

    station = small[4:6, 0:LANES]
    sender = jnp.floor((station + 0.5) * (1.0 / stations))
    within = station - sender * stations
    second = (within >= float(half)).astype(jnp.float32)
    line = (sender.astype(jnp.int32) ^ turn_s[0]).astype(jnp.float32) * trows + within - second * half
    diagonal = lax.broadcasted_iota(jnp.int32, (owned, LANES), 0) == lax.broadcasted_iota(
        jnp.int32, (owned, LANES), 1
    )

    def upright(row):
        return jnp.sum(jnp.where(diagonal, row, 0.0), axis=1, keepdims=True)

    lines = jnp.concatenate([upright(line[side : side + 1]) for side in range(2)], axis=0)
    seconds = jnp.concatenate([upright(second[side : side + 1]) for side in range(2)], axis=0)
    table = choice_ref.shape[1]
    same = lines == lax.broadcasted_iota(jnp.int32, (2 * owned, table), 1).astype(jnp.float32)
    for h in range(2):
        choice_ref[2 * owned * h : 2 * owned * (h + 1), :] = (
            jnp.where(jnp.logical_and(same, seconds == float(h)), 1.0, 0.0).astype(jnp.bfloat16)
        )

    index = lax.broadcasted_iota(jnp.int32, (64, channels), 0)
    knot = (index >> 3).astype(jnp.float32)
    basis = jnp.zeros((64, channels), jnp.float32)
    for step in range(3):
        basis = basis + jnp.where(knot == small[3:4, :] + float(step), small[step : step + 1, :], 0.0)
    high = basis.astype(jnp.bfloat16).astype(jnp.float32)
    component = index & 7
    for j in range(8):
        cols = slice(j * channels, (j + 1) * channels)
        main = jnp.where(component == j, high, 0.0).astype(jnp.bfloat16)
        rest = jnp.where(component == j, basis - high, 0.0).astype(jnp.bfloat16)
        basis_ref[0:64, cols] = main
        basis_ref[64:128, cols] = main
        basis_ref[128:192, cols] = rest
        basis_ref[192:256, cols] = jnp.zeros_like(rest)
    move.wait()


def collect_kernel(at, depth, *rest):
    blocks, (out_ref, sems) = rest[:-2], rest[-2:]
    moves = start_all(
        [
            (block.at[pl.ds(at, depth)], out_ref.at[pl.ds(i * depth, depth)])
            for i, block in enumerate(blocks)
        ],
        sems,
    )
    for move in moves:
        move.wait()


def list_rows(owner, slot, target, capacity, spare):
    senders = owner.shape[0]
    mine = owner == target
    counted = mine.astype(jnp.float32)
    before = lax.broadcasted_iota(jnp.int32, (LANES, LANES), 0) < lax.broadcasted_iota(
        jnp.int32, (LANES, LANES), 1
    )
    rank = jnp.dot(
        counted.astype(jnp.bfloat16),
        before.astype(jnp.float32).astype(jnp.bfloat16),
        preferred_element_type=jnp.float32,
    )
    lane = lax.broadcasted_iota(jnp.int32, (senders, LANES), 1)
    count = jnp.sum(counted, axis=1, keepdims=True)
    listing = jnp.where(lane == capacity, count, 0.0)
    for k in range(capacity):
        here = jnp.logical_and(mine, rank == float(k))
        kth = jnp.sum(jnp.where(here, slot, 0.0), axis=1, keepdims=True)
        kth = jnp.where(count > float(k), kth, float(spare))
        listing = jnp.where(lane == k, kth, listing)
    return listing.astype(jnp.int32), mine


def add_rows(acc_refs, slots_s, line, capacity, rows_ref):
    chunks, several = acc_refs[0].shape[0], len(acc_refs)

    def add(i, carry):
        for u, acc_ref in enumerate(acc_refs):
            k = several * i + u
            b = slots_s[line, k]
            for c in range(chunks):
                acc_ref[c, b] += rows_ref[chunks * k + c].astype(jnp.float32)
        return carry

    lax.fori_loop(0, (slots_s[line, capacity] + several - 1) // several, add, 0)


def add_table(table_ref, x, block, at, depth):
    gain_tiles = (depth - 1) // 2
    for i in range(gain_tiles):
        rows = slice((x * gain_tiles + i) * SUB, (x * gain_tiles + i + 1) * SUB)
        table_ref[rows, 0:LANES] = block[at + i].astype(jnp.float32)
        table_ref[rows, LANES : 2 * LANES] = block[at + gain_tiles + i].astype(jnp.float32)
    return block[at + 2 * gain_tiles].astype(jnp.float32)


def count_rows(hits, mine, slot):
    which = lax.broadcasted_iota(jnp.int32, hits.shape, 0).astype(jnp.float32)
    slot = jnp.where(mine, slot, -1.0)
    for x in range(slot.shape[0]):
        hits = hits + (slot[x : x + 1, :] == which).astype(jnp.float32)
    return hits


def middle_kernel(capacity, near, depth, order, me_s, choice_ref, basis_ref, *rest):
    arrived, passed = dict(zip(order, rest)), rest[len(order) : -12]
    gains_ref, recip_ref, slots_ref, sums_ref = rest[-12:-8]
    table_ref, owner_ref, slot_ref, slots_v, slots_s, one_ref, two_ref, sem = rest[-8:]
    devices = owner_ref.shape[0]
    owned = recip_ref.shape[0]
    chunks = sums_ref.shape[0]
    for x in range(devices):
        if near == 1:
            code = add_table(table_ref, x, arrived[0].at[x], 0, depth)
        elif x in with_gains(near):
            code = add_table(table_ref, x, arrived[x], chunks * capacity, depth)
        else:
            code = add_table(table_ref, x, passed[0], (x - near) // 2 * depth, depth)
        owner_ref[x : x + 1, :] = code[0:1, :]
        slot_ref[x : x + 1, :] = code[1:2, :]
    slot = slot_ref[...]
    listing, mine = list_rows(
        owner_ref[...], slot, me_s[0].astype(jnp.float32), capacity, owned
    )
    slots_ref[...] = listing
    slots_v[...] = listing
    move = pltpu.make_async_copy(slots_v, slots_s, sem)
    move.start()
    hits = count_rows(jnp.zeros((owned, LANES), jnp.float32), mine, slot)
    tally = jnp.sum(hits, axis=1, keepdims=True)
    recip_ref[...] = jnp.broadcast_to(1.0 / jnp.maximum(tally, 1.0), recip_ref.shape)

    picked = jnp.dot(
        choice_ref[...], table_ref[...].astype(jnp.bfloat16), preferred_element_type=jnp.float32
    )
    front, back = picked[0 : 2 * owned], picked[2 * owned : 4 * owned]
    lower = lax.broadcasted_iota(jnp.int32, (2 * owned, LANES), 1) < 64
    high = front[:, 0:LANES] + pltpu.roll(back[:, 0:LANES], 64, 1)
    low = pltpu.roll(front[:, LANES:], 64, 1) + back[:, LANES:]
    coarse = jnp.concatenate([jnp.where(lower, high, low), jnp.where(lower, high, 0.0)], axis=1)
    coarse = coarse.astype(jnp.bfloat16)
    width = 2 * LANES * chunks
    for n in range(0, basis_ref.shape[1], width):
        fine = jnp.dot(coarse, basis_ref[:, n : n + width], preferred_element_type=jnp.float32)
        gains_ref[:, n : n + width] = fine.astype(jnp.bfloat16).astype(jnp.float32)

    one_ref[...] = jnp.zeros_like(one_ref)
    two_ref[...] = jnp.zeros_like(two_ref)
    move.wait()
    if near > 1:
        for x in order:
            add_rows((one_ref, two_ref), slots_s, x, capacity, arrived[x])
    sums_ref[...] = one_ref[:, 0:owned] + two_ref[:, 0:owned]


def next_kernel(capacity, late, slots_ref, sums_ref, *rest):
    blocks, (out_ref, slots_s, sem) = rest[:-3], rest[-3:]
    move = pltpu.make_async_copy(slots_ref, slots_s, sem)
    move.start()
    out_ref[...] = sums_ref[...]
    move.wait()
    for x, rows_ref in zip(late, blocks):
        add_rows((out_ref,), slots_s, x, capacity, rows_ref)


def finish_kernel(capacity, last, slots_ref, gains_ref, recip_ref, sums_ref, *rest):
    far, (out_hbm, slots_s, acc_ref, res_ref, out_ref, sems) = rest[:-6], rest[-6:]
    owned, parts, channels = out_hbm.shape
    chunks = channels // LANES
    move = pltpu.make_async_copy(slots_ref, slots_s, sems.at[chunks])
    move.start()
    acc_ref[...] = sums_ref[...]
    move.wait()
    if last is not None:
        add_rows((acc_ref,), slots_s, last, capacity, far[0])
    else:

        def from_device(d, carry):
            add_rows((acc_ref,), slots_s, d, capacity, far[0].at[d])
            return carry

        lax.fori_loop(0, far[0].shape[0], from_device, 0)

    flat = acc_ref.reshape(chunks * owned * parts, LANES)
    done = res_ref.reshape(chunks * owned * parts, LANES)
    sends = []
    for c in range(chunks):
        for b0 in range(0, owned, SUB):
            scale = recip_ref[b0 : b0 + SUB, :]
            row = (c * owned + b0) * parts
            vis = [flat[pl.ds(row + j, SUB, stride=parts), :] for j in range(parts)]
            planes = [slice(j * channels + c * LANES, j * channels + (c + 1) * LANES) for j in range(parts)]
            lhs = [gains_ref[b0 : b0 + SUB, plane] for plane in planes]
            rhs = [gains_ref[owned + b0 : owned + b0 + SUB, plane] for plane in planes]
            mid_re, mid_im = [], []
            for row_a in range(2):
                for col_b in range(2):
                    re = im = 0.0
                    for inner in range(2):
                        lr, li = lhs[2 * row_a + inner], lhs[4 + 2 * row_a + inner]
                        vr, vi = vis[2 * inner + col_b], vis[4 + 2 * inner + col_b]
                        re = re + lr * vr - li * vi
                        im = im + lr * vi + li * vr
                    mid_re.append(re * scale)
                    mid_im.append(im * scale)
            for row_a in range(2):
                for col_b in range(2):
                    re = im = 0.0
                    for inner in range(2):
                        mr, mi = mid_re[2 * row_a + inner], mid_im[2 * row_a + inner]
                        rr, ri = rhs[2 * col_b + inner], rhs[4 + 2 * col_b + inner]
                        re = re + mr * rr + mi * ri
                        im = im + mi * rr - mr * ri
                    j = 2 * row_a + col_b
                    done[pl.ds(row + j, SUB, stride=parts), :] = re
                    done[pl.ds(row + 4 + j, SUB, stride=parts), :] = im
        out_ref[c] = res_ref[c].astype(out_ref.dtype)
        sends.append(
            pltpu.make_async_copy(
                out_ref.at[c], out_hbm.at[:, :, pl.ds(c * LANES, LANES)], sems.at[c]
            )
        )
        sends[-1].start()
    for send in sends:
        send.wait()


def on_device(
    visibilities,
    row_owner,
    row_slot,
    baseline_station_pairs,
    gains_coarse,
    band_weights,
    band_offset,
):
    devices = lax.axis_size("bl")
    rows, parts, channels = visibilities.shape
    capacity = 2 * rows // devices
    owned = baseline_station_pairs.shape[0]
    stations, _, knots = gains_coarse.shape
    chunks = channels // LANES
    gain_tiles = round_up(stations // 2, SUB) // SUB
    depth = 2 * gain_tiles + 1
    near = devices // 2 if devices <= 16 else 1
    halves = near > 1
    f32, bf16, i32 = jnp.float32, jnp.bfloat16, jnp.int32
    vmem = pl.BlockSpec(memory_space=pltpu.VMEM)
    smem = pl.BlockSpec(memory_space=pltpu.SMEM)
    hbm = pl.BlockSpec(memory_space=pltpu.HBM)
    anywhere = pl.BlockSpec(memory_space=pl.ANY)
    most = pltpu.CompilerParams(vmem_limit_bytes=ALL_VMEM)
    some = pltpu.CompilerParams(vmem_limit_bytes=SOME_VMEM)
    shape = jax.ShapeDtypeStruct
    dma = pltpu.SemaphoreType.DMA

    me = lax.axis_index("bl").astype(i32).reshape(1)
    turn = me if halves else jnp.zeros_like(me)
    owner = row_owner.reshape(rows)
    coarse = gains_coarse.transpose(2, 1, 0).reshape(knots * parts, stations)
    block = (chunks * capacity, parts, LANES)
    rows_at = chunks * capacity
    if halves:
        long = with_gains(near)
        outs = [
            shape((rows_at + (depth if x in long else 0), parts, LANES), bf16)
            for x in range(devices)
        ]
        outs[0] = shape((rows_at + depth + 3 * chunks, parts, LANES), bf16)
    else:
        outs = [
            shape((devices,) + block, bf16),
            shape((depth, SUB, LANES), bf16),
            shape((3 * chunks, SUB, LANES), bf16),
        ]
    pairs = baseline_station_pairs.T
    weights = band_weights.T
    offset = band_offset.reshape(chunks, LANES)
    me_owner = row_owner.reshape(rows)
    if halves:
        first = outs.pop(near + 1)
        alone = pl.pallas_call(
            functools.partial(first_kernel, capacity, near + 1),
            out_shape=first,
            in_specs=[smem, hbm, hbm],
            out_specs=hbm,
            scratch_shapes=[
                pltpu.SMEM((rows,), i32),
                pltpu.SMEM((rows + 8,), i32),
                pltpu.VMEM((rows, parts, channels), bf16),
                pltpu.VMEM(first.shape, bf16),
                dma((2,)),
            ],
            compiler_params=most,
            name="pack_first",
        )(me, me_owner, visibilities)
    sent = pl.pallas_call(
        functools.partial(pack_kernel, capacity, near),
        out_shape=outs,
        in_specs=[smem] + [hbm] * 8,
        out_specs=[hbm] * len(outs),
        scratch_shapes=[
            pltpu.VMEM(weights.shape, f32),
            pltpu.VMEM(offset.shape, i32),
            pltpu.VMEM(pairs.shape, i32),
            pltpu.VMEM((SUB, channels), f32),
            pltpu.VMEM((3 * chunks, SUB, LANES), bf16),
            pltpu.SMEM((rows,), i32),
            pltpu.SMEM((rows,), i32),
            pltpu.SMEM((devices,), i32),
            pltpu.VMEM((1, rows), i32),
            pltpu.VMEM((1, rows), i32),
            pltpu.VMEM((rows, parts, channels), bf16),
            pltpu.VMEM((knots * parts, stations), f32),
            pltpu.VMEM((LANES, LANES), f32),
            pltpu.VMEM((depth, SUB, LANES), bf16),
            pltpu.VMEM((devices,) + block, bf16),
            dma((9 + PARTS + 2 * devices,)),
        ],
        compiler_params=most,
        name="pack_rows",
    )(
        turn,
        owner,
        row_owner.reshape(1, rows),
        row_slot.reshape(1, rows),
        visibilities,
        coarse,
        weights,
        offset,
        pairs,
    )


    trows = gain_tiles * SUB

    def ready(own, at):
        return pl.pallas_call(
            functools.partial(ready_kernel, at, chunks, owned, stations, trows),
            out_shape=[
                shape(own.shape, bf16),
                shape((4 * owned, devices * trows), bf16),
                shape((2 * LANES, parts * channels), bf16),
            ],
            in_specs=[smem, vmem],
            out_specs=[vmem] * 3,
            scratch_shapes=[dma],
            compiler_params=some,
            name="make_ready",
        )(turn, own)

    if halves:
        sent = list(sent)
        sent.insert(near + 1, alone)

    def swap(array, x):
        return lax.ppermute(array, "bl", [(d, d ^ x) for d in range(devices)])

    if halves:
        own, choice, basis = ready(sent[0], rows_at + depth)
        arrived = {x: swap(sent[x], x) if x else own for x in range(devices)}
        order, late = schedule(near)
        even = list(range(near, devices, 2))
        collected = pl.pallas_call(
            functools.partial(collect_kernel, rows_at, depth),
            out_shape=shape((len(even) * depth, parts, LANES), bf16),
            in_specs=[anywhere] * len(even),
            out_specs=vmem,
            scratch_shapes=[dma((len(even),))],
            compiler_params=some,
            name="collect_gains",
        )(*[arrived[x] for x in even])
        passed = [swap(collected, 1)]
    else:
        arrived = {
            0: lax.all_gather(sent[1], "bl", axis=0),
            1: lax.all_to_all(sent[0], "bl", split_axis=0, concat_axis=0, tiled=True),
        }
        order, late, passed = [0], [1], []
        _, choice, basis = ready(sent[2], 0)

    gains, recip, slots, sums = pl.pallas_call(
        functools.partial(middle_kernel, capacity, near, depth, order),
        out_shape=(
            shape((2 * owned, parts * channels), f32),
            shape((owned, LANES), f32),
            shape((devices, LANES), i32),
            shape((chunks, owned, parts, LANES), f32),
        ),
        in_specs=[smem] + [vmem] * (2 + len(order) + len(passed)),
        out_specs=(vmem,) * 4,
        scratch_shapes=[
            pltpu.VMEM((devices * trows, 2 * LANES), f32),
            pltpu.VMEM((devices, LANES), f32),
            pltpu.VMEM((devices, LANES), f32),
            pltpu.VMEM((devices, LANES), i32),
            pltpu.SMEM((devices, LANES), i32),
            pltpu.VMEM((chunks, owned + 1, parts, LANES), f32),
            pltpu.VMEM((chunks, owned + 1, parts, LANES), f32),
            dma,
        ],
        compiler_params=some,
        name="gains_and_sums",
    )(me, choice, basis, *[arrived[x] for x in order], *passed)
    if halves:
        *before, last = late
        sums = pl.pallas_call(
            functools.partial(next_kernel, capacity, before),
            out_shape=shape(sums.shape, f32),
            in_specs=[anywhere, vmem] + [vmem] * len(before),
            out_specs=vmem,
            scratch_shapes=[pltpu.SMEM((devices, LANES), i32), dma],
            compiler_params=some,
            name="sum_next",
        )(slots, sums, *[arrived[x] for x in before])
    else:
        last = None
    return pl.pallas_call(
        functools.partial(finish_kernel, capacity, last),
        out_shape=shape((owned, parts, channels), bf16),
        in_specs=[anywhere] + [vmem] * 4,
        out_specs=hbm,
        scratch_shapes=[
            pltpu.SMEM((devices, LANES), i32),
            pltpu.VMEM((chunks, owned, parts, LANES), f32),
            pltpu.VMEM((chunks, owned, parts, LANES), f32),
            pltpu.VMEM((chunks, owned, parts, LANES), bf16),
            dma((chunks + 1,)),
        ],
        compiler_params=some,
        name="sum_and_apply",
    )(slots, gains, recip, sums, arrived[late[-1]])


def solution(mesh):
    placed = (
        P(("groups", "bl"), None, None),
        P(("groups", "bl"), None),
        P(("groups", "bl")),
        P("bl", None),
        P(("groups", "bl"), None, None),
        P("groups", None),
        P("groups"),
    )
    return jax.shard_map(
        on_device,
        mesh=mesh,
        in_specs=placed,
        out_specs=P(("groups", "bl"), None, None),
        check_vma=False,
    )
```

```python
import functools

import jax
import jax.numpy as jnp
from jax import lax
from jax.experimental import pallas as pl
from jax.experimental.pallas import tpu as pltpu
from jax.sharding import PartitionSpec as P

LANES = 128
SUB = 8
USED = 48
PARTS = 4
ALL_VMEM = 60 * 1024 * 1024
SOME_VMEM = 24 * 1024 * 1024


def round_up(value, unit):
    return -(-value // unit) * unit


def schedule(near):
    even, odd = list(range(near, 2 * near, 2)), list(range(near + 1, 2 * near, 2))
    close = list(range(near // 2, near)) + list(range(1, near // 2))
    order = [0] + even[:2] + close[:2]
    cross, close = even[2:], close[2:]
    while cross:
        order += cross[:1] + close[:1]
        cross, close = cross[1:], close[1:]
    return order + close[:1] + odd[1:-2] + close[1:] + odd[:1], odd[-2:]


def with_gains(near):
    return list(range(near)) + list(range(near, 2 * near, 2))


def start_all(pairs, sems):
    moves = [pltpu.make_async_copy(src, dst, sems.at[i]) for i, (src, dst) in enumerate(pairs)]
    for move in moves:
        move.start()
    return moves


def pack_kernel(
    capacity,
    near,
    me_s,
    owner_hbm,
    owner_row_hbm,
    slot_row_hbm,
    vis_hbm,
    coarse_hbm,
    weights_hbm,
    offset_hbm,
    pairs_hbm,
    *rest,
):
    outs = rest[:-16]
    (
        weights_ref,
        offset_ref,
        pairs_ref,
        small_ref,
        parts_ref,
        owner_s,
        place_s,
        count_s,
        owner_ref,
        slot_ref,
        vis_ref,
        coarse_ref,
        turn_ref,
        meta_ref,
        block_ref,
        sems,
    ) = rest[-16:]
    rows = vis_ref.shape[0]
    chunks = vis_ref.shape[2] // LANES
    devices = block_ref.shape[0]
    terms, stations = coarse_ref.shape
    half = stations // 2
    depth = meta_ref.shape[0]
    gain_tiles = (depth - 1) // 2
    span = rows // PARTS
    moves = start_all(
        (
            (owner_hbm, owner_s),
            (coarse_hbm, coarse_ref),
            (owner_row_hbm, owner_ref),
            (slot_row_hbm, slot_ref),
            (weights_hbm, weights_ref),
            (offset_hbm, offset_ref),
            (pairs_hbm, pairs_ref),
        ),
        sems,
    )
    fetches = start_all(
        [
            (vis_hbm.at[pl.ds(i * span, span)], vis_ref.at[pl.ds(i * span, span)])
            for i in range(PARTS)
        ],
        sems.at[pl.ds(len(moves), PARTS)],
    )
    turn_ref[...] = jnp.zeros_like(turn_ref)
    for d in range(devices):
        count_s[d] = 0
    me = me_s[0]
    moves[0].wait()

    def rank(r, carry):
        x = owner_s[r] ^ me
        k = count_s[x]
        count_s[x] = k + 1
        place_s[r] = x * capacity + k
        return carry

    lax.fori_loop(0, rows, rank, 0, unroll=8)
    for move in moves[1:]:
        move.wait()

    turn_ref[0:terms, 0:half] = coarse_ref[:, 0:half]
    turn_ref[64 : 64 + terms, 0:half] = coarse_ref[:, half:stations]
    gains = turn_ref[...].T
    high = gains.astype(jnp.bfloat16)
    low = (gains - high.astype(jnp.float32)).astype(jnp.bfloat16)
    for i in range(gain_tiles):
        meta_ref[i] = high[i * SUB : (i + 1) * SUB, :]
        meta_ref[gain_tiles + i] = low[i * SUB : (i + 1) * SUB, :]
    sub = lax.broadcasted_iota(jnp.int32, (SUB, LANES), 0)
    codes = jnp.where(sub == 0, owner_ref[...], slot_ref[...])
    meta_ref[2 * gain_tiles] = codes.astype(jnp.float32).astype(jnp.bfloat16)
    steps = weights_ref.shape[0]
    small_ref[...] = jnp.zeros_like(small_ref)
    small_ref[0:steps, :] = weights_ref[...]
    for c in range(chunks):
        lanes = slice(c * LANES, (c + 1) * LANES)
        small_ref[steps : steps + 1, lanes] = offset_ref[c : c + 1, :].astype(jnp.float32)
    small_ref[4:6, 0 : pairs_ref.shape[1]] = pairs_ref[...].astype(jnp.float32)
    left = small_ref[...]
    for p in range(3):
        piece = left.astype(jnp.bfloat16)
        left = left - piece.astype(jnp.float32)
        for c in range(chunks):
            parts_ref[p * chunks + c] = piece[:, c * LANES : (c + 1) * LANES]

    at = chunks * capacity
    if near > 1:
        outs = list(outs[: near + 1]) + [None] + list(outs[near + 1 :])
        pairs = [(meta_ref, outs[x].at[pl.ds(at, depth)]) for x in with_gains(near)]
    else:
        pairs = [(meta_ref, outs[1])]
    at_small = at + depth if near > 1 else 0
    pairs += [(parts_ref, outs[0 if near > 1 else -1].at[pl.ds(at_small, 3 * chunks)])]
    start = len(moves) + PARTS
    sends = start_all(pairs, sems.at[pl.ds(start, len(pairs))])
    start += len(pairs)

    def place(r, carry):
        p = place_s[r]
        for c in range(chunks):
            flat_ref[p * chunks + c] = vis_ref[r, :, c * LANES : (c + 1) * LANES]
        return carry

    flat_ref = block_ref.reshape(devices * at, SUB, LANES)
    for i in range(PARTS):
        fetches[i].wait()
        lax.fori_loop(i * span, (i + 1) * span, place, 0, unroll=8)
    if near > 1:
        pairs = [
            (block_ref.at[x], outs[x].at[pl.ds(0, at)]) for x in range(devices) if x != near + 1
        ]
    else:
        pairs = [(block_ref, outs[0])]
    sends += start_all(pairs, sems.at[pl.ds(start, len(pairs))])
    for send in sends:
        send.wait()


def first_kernel(capacity, target, me_s, owner_hbm, vis_hbm, out_hbm, owner_s, list_s, vis_ref, block_ref, sems):
    rows = vis_ref.shape[0]
    chunks = vis_ref.shape[2] // LANES
    moves = start_all(((owner_hbm, owner_s), (vis_hbm, vis_ref)), sems)
    wanted = me_s[0] ^ target
    moves[0].wait()

    def note(r, k):
        list_s[k] = r
        return k + jnp.where(owner_s[r] == wanted, 1, 0)

    count = lax.fori_loop(0, rows, note, 0, unroll=8)
    moves[1].wait()

    def place(k, carry):
        r = list_s[k]
        for c in range(chunks):
            block_ref[chunks * k + c] = vis_ref[r, :, c * LANES : (c + 1) * LANES]
        return carry

    lax.fori_loop(0, count, place, 0)
    send = start_all([(block_ref, out_hbm)], sems)[0]
    send.wait()


def ready_kernel(
    at, chunks, owned, stations, trows, turn_s, own_ref, own_out_ref, choice_ref, basis_ref, sem
):
    move = pltpu.make_async_copy(own_ref, own_out_ref, sem)
    move.start()
    pieces = [
        jnp.concatenate(
            [own_ref[at + p * chunks + c].astype(jnp.float32) for c in range(chunks)], axis=1
        )
        for p in range(3)
    ]
    small = pieces[0] + pieces[1] + pieces[2]
    channels = small.shape[1]
    half = stations // 2

    station = small[4:6, 0:LANES]
    sender = jnp.floor((station + 0.5) * (1.0 / stations))
    within = station - sender * stations
    second = (within >= float(half)).astype(jnp.float32)
    line = (sender.astype(jnp.int32) ^ turn_s[0]).astype(jnp.float32) * trows + within - second * half
    diagonal = lax.broadcasted_iota(jnp.int32, (owned, LANES), 0) == lax.broadcasted_iota(
        jnp.int32, (owned, LANES), 1
    )

    def upright(row):
        return jnp.sum(jnp.where(diagonal, row, 0.0), axis=1, keepdims=True)

    lines = jnp.concatenate([upright(line[side : side + 1]) for side in range(2)], axis=0)
    seconds = jnp.concatenate([upright(second[side : side + 1]) for side in range(2)], axis=0)
    table = choice_ref.shape[1]
    same = lines == lax.broadcasted_iota(jnp.int32, (2 * owned, table), 1).astype(jnp.float32)
    for h in range(2):
        choice_ref[2 * owned * h : 2 * owned * (h + 1), :] = (
            jnp.where(jnp.logical_and(same, seconds == float(h)), 1.0, 0.0).astype(jnp.bfloat16)
        )

    index = lax.broadcasted_iota(jnp.int32, (64, channels), 0)
    knot = (index >> 3).astype(jnp.float32)
    basis = jnp.zeros((64, channels), jnp.float32)
    for step in range(3):
        basis = basis + jnp.where(knot == small[3:4, :] + float(step), small[step : step + 1, :], 0.0)
    high = basis.astype(jnp.bfloat16).astype(jnp.float32)
    component = index & 7
    for j in range(8):
        cols = slice(j * channels, (j + 1) * channels)
        main = jnp.where(component == j, high, 0.0).astype(jnp.bfloat16)
        rest = jnp.where(component == j, basis - high, 0.0).astype(jnp.bfloat16)
        basis_ref[0:64, cols] = main
        basis_ref[64:128, cols] = main
        basis_ref[128:192, cols] = rest
        basis_ref[192:256, cols] = jnp.zeros_like(rest)
    move.wait()


def collect_kernel(at, depth, *rest):
    blocks, (out_ref, sems) = rest[:-2], rest[-2:]
    moves = start_all(
        [
            (block.at[pl.ds(at, depth)], out_ref.at[pl.ds(i * depth, depth)])
            for i, block in enumerate(blocks)
        ],
        sems,
    )
    for move in moves:
        move.wait()


def list_rows(owner, slot, target, capacity, spare):
    senders = owner.shape[0]
    mine = owner == target
    counted = mine.astype(jnp.float32)
    before = lax.broadcasted_iota(jnp.int32, (LANES, LANES), 0) < lax.broadcasted_iota(
        jnp.int32, (LANES, LANES), 1
    )
    rank = jnp.dot(
        counted.astype(jnp.bfloat16),
        before.astype(jnp.float32).astype(jnp.bfloat16),
        preferred_element_type=jnp.float32,
    )
    lane = lax.broadcasted_iota(jnp.int32, (senders, LANES), 1)
    count = jnp.sum(counted, axis=1, keepdims=True)
    listing = jnp.where(lane == capacity, count, 0.0)
    for k in range(capacity):
        here = jnp.logical_and(mine, rank == float(k))
        kth = jnp.sum(jnp.where(here, slot, 0.0), axis=1, keepdims=True)
        kth = jnp.where(count > float(k), kth, float(spare))
        listing = jnp.where(lane == k, kth, listing)
    return listing.astype(jnp.int32), mine


def add_rows(acc_refs, slots_s, line, capacity, rows_ref):
    chunks, several = acc_refs[0].shape[0], len(acc_refs)

    def add(i, carry):
        for u, acc_ref in enumerate(acc_refs):
            k = several * i + u
            b = slots_s[line, k]
            for c in range(chunks):
                acc_ref[c, b] += rows_ref[chunks * k + c].astype(jnp.float32)
        return carry

    lax.fori_loop(0, (slots_s[line, capacity] + several - 1) // several, add, 0)


def add_table(table_ref, x, block, at, depth):
    gain_tiles = (depth - 1) // 2
    for i in range(gain_tiles):
        rows = slice((x * gain_tiles + i) * SUB, (x * gain_tiles + i + 1) * SUB)
        table_ref[rows, 0:LANES] = block[at + i].astype(jnp.float32)
        table_ref[rows, LANES : 2 * LANES] = block[at + gain_tiles + i].astype(jnp.float32)
    return block[at + 2 * gain_tiles].astype(jnp.float32)


def count_rows(hits, mine, slot):
    which = lax.broadcasted_iota(jnp.int32, hits.shape, 0).astype(jnp.float32)
    slot = jnp.where(mine, slot, -1.0)
    for x in range(slot.shape[0]):
        hits = hits + (slot[x : x + 1, :] == which).astype(jnp.float32)
    return hits


def middle_kernel(capacity, near, depth, order, me_s, choice_ref, basis_ref, *rest):
    arrived, passed = dict(zip(order, rest)), rest[len(order) : -12]
    gains_ref, recip_ref, slots_ref, sums_ref = rest[-12:-8]
    table_ref, owner_ref, slot_ref, slots_v, slots_s, one_ref, two_ref, sem = rest[-8:]
    devices = owner_ref.shape[0]
    owned = recip_ref.shape[0]
    chunks = sums_ref.shape[0]
    for x in range(devices):
        if near == 1:
            code = add_table(table_ref, x, arrived[0].at[x], 0, depth)
        elif x in with_gains(near):
            code = add_table(table_ref, x, arrived[x], chunks * capacity, depth)
        else:
            code = add_table(table_ref, x, passed[0], (x - near) // 2 * depth, depth)
        owner_ref[x : x + 1, :] = code[0:1, :]
        slot_ref[x : x + 1, :] = code[1:2, :]
    slot = slot_ref[...]
    listing, mine = list_rows(
        owner_ref[...], slot, me_s[0].astype(jnp.float32), capacity, owned
    )
    slots_ref[...] = listing
    slots_v[...] = listing
    move = pltpu.make_async_copy(slots_v, slots_s, sem)
    move.start()
    hits = count_rows(jnp.zeros((owned, LANES), jnp.float32), mine, slot)
    tally = jnp.sum(hits, axis=1, keepdims=True)
    recip_ref[...] = jnp.broadcast_to(1.0 / jnp.maximum(tally, 1.0), recip_ref.shape)

    picked = jnp.dot(
        choice_ref[...], table_ref[...].astype(jnp.bfloat16), preferred_element_type=jnp.float32
    )
    front, back = picked[0 : 2 * owned], picked[2 * owned : 4 * owned]
    lower = lax.broadcasted_iota(jnp.int32, (2 * owned, LANES), 1) < 64
    high = front[:, 0:LANES] + pltpu.roll(back[:, 0:LANES], 64, 1)
    low = pltpu.roll(front[:, LANES:], 64, 1) + back[:, LANES:]
    coarse = jnp.concatenate([jnp.where(lower, high, low), jnp.where(lower, high, 0.0)], axis=1)
    coarse = coarse.astype(jnp.bfloat16)
    width = 2 * LANES * chunks
    for n in range(0, basis_ref.shape[1], width):
        fine = jnp.dot(coarse, basis_ref[:, n : n + width], preferred_element_type=jnp.float32)
        gains_ref[:, n : n + width] = fine.astype(jnp.bfloat16).astype(jnp.float32)

    one_ref[...] = jnp.zeros_like(one_ref)
    two_ref[...] = jnp.zeros_like(two_ref)
    move.wait()
    if near > 1:
        for x in order:
            add_rows((one_ref, two_ref), slots_s, x, capacity, arrived[x])
    sums_ref[...] = one_ref[:, 0:owned] + two_ref[:, 0:owned]


def next_kernel(capacity, x, slots_ref, sums_ref, rows_ref, out_ref, slots_s, sem):
    move = pltpu.make_async_copy(slots_ref, slots_s, sem)
    move.start()
    out_ref[...] = sums_ref[...]
    move.wait()
    add_rows((out_ref,), slots_s, x, capacity, rows_ref)


def finish_kernel(capacity, last, slots_ref, gains_ref, recip_ref, sums_ref, *rest):
    far, (out_hbm, slots_s, acc_ref, res_ref, out_ref, sems) = rest[:-6], rest[-6:]
    owned, parts, channels = out_hbm.shape
    chunks = channels // LANES
    move = pltpu.make_async_copy(slots_ref, slots_s, sems.at[chunks])
    move.start()
    acc_ref[...] = sums_ref[...]
    move.wait()
    if last is not None:
        add_rows((acc_ref,), slots_s, last, capacity, far[0])
    else:

        def from_device(d, carry):
            add_rows((acc_ref,), slots_s, d, capacity, far[0].at[d])
            return carry

        lax.fori_loop(0, far[0].shape[0], from_device, 0)

    flat = acc_ref.reshape(chunks * owned * parts, LANES)
    done = res_ref.reshape(chunks * owned * parts, LANES)
    sends = []
    for c in range(chunks):
        for b0 in range(0, owned, SUB):
            scale = recip_ref[b0 : b0 + SUB, :]
            row = (c * owned + b0) * parts
            vis = [flat[pl.ds(row + j, SUB, stride=parts), :] for j in range(parts)]
            planes = [slice(j * channels + c * LANES, j * channels + (c + 1) * LANES) for j in range(parts)]
            lhs = [gains_ref[b0 : b0 + SUB, plane] for plane in planes]
            rhs = [gains_ref[owned + b0 : owned + b0 + SUB, plane] for plane in planes]
            mid_re, mid_im = [], []
            for row_a in range(2):
                for col_b in range(2):
                    re = im = 0.0
                    for inner in range(2):
                        lr, li = lhs[2 * row_a + inner], lhs[4 + 2 * row_a + inner]
                        vr, vi = vis[2 * inner + col_b], vis[4 + 2 * inner + col_b]
                        re = re + lr * vr - li * vi
                        im = im + lr * vi + li * vr
                    mid_re.append(re * scale)
                    mid_im.append(im * scale)
            for row_a in range(2):
                for col_b in range(2):
                    re = im = 0.0
                    for inner in range(2):
                        mr, mi = mid_re[2 * row_a + inner], mid_im[2 * row_a + inner]
                        rr, ri = rhs[2 * col_b + inner], rhs[4 + 2 * col_b + inner]
                        re = re + mr * rr + mi * ri
                        im = im + mi * rr - mr * ri
                    j = 2 * row_a + col_b
                    done[pl.ds(row + j, SUB, stride=parts), :] = re
                    done[pl.ds(row + 4 + j, SUB, stride=parts), :] = im
        out_ref[c] = res_ref[c].astype(out_ref.dtype)
        sends.append(
            pltpu.make_async_copy(
                out_ref.at[c], out_hbm.at[:, :, pl.ds(c * LANES, LANES)], sems.at[c]
            )
        )
        sends[-1].start()
    for send in sends:
        send.wait()


def on_device(
    visibilities,
    row_owner,
    row_slot,
    baseline_station_pairs,
    gains_coarse,
    band_weights,
    band_offset,
):
    devices = lax.axis_size("bl")
    rows, parts, channels = visibilities.shape
    capacity = 2 * rows // devices
    owned = baseline_station_pairs.shape[0]
    stations, _, knots = gains_coarse.shape
    chunks = channels // LANES
    gain_tiles = round_up(stations // 2, SUB) // SUB
    depth = 2 * gain_tiles + 1
    near = devices // 2 if devices <= 16 else 1
    halves = near > 1
    f32, bf16, i32 = jnp.float32, jnp.bfloat16, jnp.int32
    vmem = pl.BlockSpec(memory_space=pltpu.VMEM)
    smem = pl.BlockSpec(memory_space=pltpu.SMEM)
    hbm = pl.BlockSpec(memory_space=pltpu.HBM)
    anywhere = pl.BlockSpec(memory_space=pl.ANY)
    most = pltpu.CompilerParams(vmem_limit_bytes=ALL_VMEM)
    some = pltpu.CompilerParams(vmem_limit_bytes=SOME_VMEM)
    shape = jax.ShapeDtypeStruct
    dma = pltpu.SemaphoreType.DMA

    me = lax.axis_index("bl").astype(i32).reshape(1)
    turn = me if halves else jnp.zeros_like(me)
    owner = row_owner.reshape(rows)
    coarse = gains_coarse.transpose(2, 1, 0).reshape(knots * parts, stations)
    block = (chunks * capacity, parts, LANES)
    rows_at = chunks * capacity
    if halves:
        long = with_gains(near) + [near + 3]
        outs = [
            shape((rows_at + (depth if x in long else 0), parts, LANES), bf16)
            for x in range(devices)
        ]
        outs[0] = shape((rows_at + depth + 3 * chunks, parts, LANES), bf16)
    else:
        outs = [
            shape((devices,) + block, bf16),
            shape((depth, SUB, LANES), bf16),
            shape((3 * chunks, SUB, LANES), bf16),
        ]
    pairs = baseline_station_pairs.T
    weights = band_weights.T
    offset = band_offset.reshape(chunks, LANES)
    me_owner = row_owner.reshape(rows)
    if halves:
        first = outs.pop(near + 1)
        alone = pl.pallas_call(
            functools.partial(first_kernel, capacity, near + 1),
            out_shape=first,
            in_specs=[smem, hbm, hbm],
            out_specs=hbm,
            scratch_shapes=[
                pltpu.SMEM((rows,), i32),
                pltpu.SMEM((rows + 8,), i32),
                pltpu.VMEM((rows, parts, channels), bf16),
                pltpu.VMEM(first.shape, bf16),
                dma((2,)),
            ],
            compiler_params=most,
            name="pack_first",
        )(me, me_owner, visibilities)
    sent = pl.pallas_call(
        functools.partial(pack_kernel, capacity, near),
        out_shape=outs,
        in_specs=[smem] + [hbm] * 8,
        out_specs=[hbm] * len(outs),
        scratch_shapes=[
            pltpu.VMEM(weights.shape, f32),
            pltpu.VMEM(offset.shape, i32),
            pltpu.VMEM(pairs.shape, i32),
            pltpu.VMEM((SUB, channels), f32),
            pltpu.VMEM((3 * chunks, SUB, LANES), bf16),
            pltpu.SMEM((rows,), i32),
            pltpu.SMEM((rows,), i32),
            pltpu.SMEM((devices,), i32),
            pltpu.VMEM((1, rows), i32),
            pltpu.VMEM((1, rows), i32),
            pltpu.VMEM((rows, parts, channels), bf16),
            pltpu.VMEM((knots * parts, stations), f32),
            pltpu.VMEM((LANES, LANES), f32),
            pltpu.VMEM((depth, SUB, LANES), bf16),
            pltpu.VMEM((devices,) + block, bf16),
            dma((9 + PARTS + 2 * devices,)),
        ],
        compiler_params=most,
        name="pack_rows",
    )(
        turn,
        owner,
        row_owner.reshape(1, rows),
        row_slot.reshape(1, rows),
        visibilities,
        coarse,
        weights,
        offset,
        pairs,
    )


    trows = gain_tiles * SUB

    def ready(own, at):
        return pl.pallas_call(
            functools.partial(ready_kernel, at, chunks, owned, stations, trows),
            out_shape=[
                shape(own.shape, bf16),
                shape((4 * owned, devices * trows), bf16),
                shape((2 * LANES, parts * channels), bf16),
            ],
            in_specs=[smem, vmem],
            out_specs=[vmem] * 3,
            scratch_shapes=[dma],
            compiler_params=some,
            name="make_ready",
        )(turn, own)

    if halves:
        sent = list(sent)
        sent.insert(near + 1, alone)

    def swap(array, x):
        return lax.ppermute(array, "bl", [(d, d ^ x) for d in range(devices)])

    if halves:
        own, choice, basis = ready(sent[0], rows_at + depth)
        arrived = {x: swap(sent[x], x) if x else own for x in range(devices)}
        order, late = schedule(near)
        even = list(range(near, devices, 2))
        collected = pl.pallas_call(
            functools.partial(collect_kernel, rows_at, depth),
            out_shape=shape((len(even) * depth, parts, LANES), bf16),
            in_specs=[anywhere] * len(even),
            out_specs=vmem,
            scratch_shapes=[dma((len(even),))],
            compiler_params=some,
            name="collect_gains",
        )(*[arrived[x] for x in even])
        passed = [swap(collected, 1)]
    else:
        arrived = {
            0: lax.all_gather(sent[1], "bl", axis=0),
            1: lax.all_to_all(sent[0], "bl", split_axis=0, concat_axis=0, tiled=True),
        }
        order, late, passed = [0], [1], []
        _, choice, basis = ready(sent[2], 0)

    gains, recip, slots, sums = pl.pallas_call(
        functools.partial(middle_kernel, capacity, near, depth, order),
        out_shape=(
            shape((2 * owned, parts * channels), f32),
            shape((owned, LANES), f32),
            shape((devices, LANES), i32),
            shape((chunks, owned, parts, LANES), f32),
        ),
        in_specs=[smem] + [vmem] * (2 + len(order) + len(passed)),
        out_specs=(vmem,) * 4,
        scratch_shapes=[
            pltpu.VMEM((devices * trows, 2 * LANES), f32),
            pltpu.VMEM((devices, LANES), f32),
            pltpu.VMEM((devices, LANES), f32),
            pltpu.VMEM((devices, LANES), i32),
            pltpu.SMEM((devices, LANES), i32),
            pltpu.VMEM((chunks, owned + 1, parts, LANES), f32),
            pltpu.VMEM((chunks, owned + 1, parts, LANES), f32),
            dma,
        ],
        compiler_params=some,
        name="gains_and_sums",
    )(me, choice, basis, *[arrived[x] for x in order], *passed)
    if halves:
        before, last = late
        sums = pl.pallas_call(
            functools.partial(next_kernel, capacity, before),
            out_shape=shape(sums.shape, f32),
            in_specs=[anywhere, vmem, vmem],
            out_specs=vmem,
            scratch_shapes=[pltpu.SMEM((devices, LANES), i32), dma],
            compiler_params=some,
            name="sum_next",
        )(slots, sums, arrived[before])
    else:
        last = None
    return pl.pallas_call(
        functools.partial(finish_kernel, capacity, last),
        out_shape=shape((owned, parts, channels), bf16),
        in_specs=[anywhere] + [vmem] * 4,
        out_specs=hbm,
        scratch_shapes=[
            pltpu.SMEM((devices, LANES), i32),
            pltpu.VMEM((chunks, owned, parts, LANES), f32),
            pltpu.VMEM((chunks, owned, parts, LANES), f32),
            pltpu.VMEM((chunks, owned, parts, LANES), bf16),
            dma((chunks + 1,)),
        ],
        compiler_params=some,
        name="sum_and_apply",
    )(slots, gains, recip, sums, arrived[late[-1]])


def solution(mesh):
    placed = (
        P(("groups", "bl"), None, None),
        P(("groups", "bl"), None),
        P(("groups", "bl")),
        P("bl", None),
        P(("groups", "bl"), None, None),
        P("groups", None),
        P("groups"),
    )
    return jax.shard_map(
        on_device,
        mesh=mesh,
        in_specs=placed,
        out_specs=P(("groups", "bl"), None, None),
        check_vma=False,
    )
```

```python
import functools

import jax
import jax.numpy as jnp
from jax import lax
from jax.experimental import pallas as pl
from jax.experimental.pallas import tpu as pltpu
from jax.sharding import PartitionSpec as P

LANES = 128
SUB = 8
USED = 48
PARTS = 4
ALL_VMEM = 60 * 1024 * 1024
SOME_VMEM = 24 * 1024 * 1024


def round_up(value, unit):
    return -(-value // unit) * unit


def schedule(near):
    even, odd = list(range(near, 2 * near, 2)), list(range(near + 1, 2 * near, 2))
    close = list(range(near // 2, near)) + list(range(1, near // 2))
    order = [0] + even[:2] + close[:2]
    cross, close = even[2:], close[2:]
    while cross:
        order += cross[:1] + close[:1]
        cross, close = cross[1:], close[1:]
    return order + close[:1] + odd[1:-2] + close[1:] + odd[:1], odd[-2:]


def with_gains(near):
    return list(range(near)) + list(range(near, 2 * near, 2))


def start_all(pairs, sems):
    moves = [pltpu.make_async_copy(src, dst, sems.at[i]) for i, (src, dst) in enumerate(pairs)]
    for move in moves:
        move.start()
    return moves


def pack_kernel(
    capacity,
    near,
    me_s,
    owner_hbm,
    owner_row_hbm,
    slot_row_hbm,
    vis_hbm,
    coarse_hbm,
    weights_hbm,
    offset_hbm,
    pairs_hbm,
    *rest,
):
    outs = rest[:-16]
    (
        weights_ref,
        offset_ref,
        pairs_ref,
        small_ref,
        parts_ref,
        owner_s,
        place_s,
        count_s,
        owner_ref,
        slot_ref,
        vis_ref,
        coarse_ref,
        turn_ref,
        meta_ref,
        block_ref,
        sems,
    ) = rest[-16:]
    rows = vis_ref.shape[0]
    chunks = vis_ref.shape[2] // LANES
    devices = block_ref.shape[0]
    terms, stations = coarse_ref.shape
    half = stations // 2
    depth = meta_ref.shape[0]
    gain_tiles = (depth - 1) // 2
    span = rows // PARTS
    moves = start_all(
        (
            (owner_hbm, owner_s),
            (coarse_hbm, coarse_ref),
            (owner_row_hbm, owner_ref),
            (slot_row_hbm, slot_ref),
            (weights_hbm, weights_ref),
            (offset_hbm, offset_ref),
            (pairs_hbm, pairs_ref),
        ),
        sems,
    )
    fetches = start_all(
        [
            (vis_hbm.at[pl.ds(i * span, span)], vis_ref.at[pl.ds(i * span, span)])
            for i in range(PARTS)
        ],
        sems.at[pl.ds(len(moves), PARTS)],
    )
    turn_ref[...] = jnp.zeros_like(turn_ref)
    for d in range(devices):
        count_s[d] = 0
    me = me_s[0]
    moves[0].wait()

    def rank(r, carry):
        x = owner_s[r] ^ me
        k = count_s[x]
        count_s[x] = k + 1
        place_s[r] = x * capacity + k
        return carry

    lax.fori_loop(0, rows, rank, 0, unroll=32)
    for move in moves[1:]:
        move.wait()

    turn_ref[0:terms, 0:half] = coarse_ref[:, 0:half]
    turn_ref[64 : 64 + terms, 0:half] = coarse_ref[:, half:stations]
    gains = turn_ref[...].T
    high = gains.astype(jnp.bfloat16)
    low = (gains - high.astype(jnp.float32)).astype(jnp.bfloat16)
    for i in range(gain_tiles):
        meta_ref[i] = high[i * SUB : (i + 1) * SUB, :]
        meta_ref[gain_tiles + i] = low[i * SUB : (i + 1) * SUB, :]
    sub = lax.broadcasted_iota(jnp.int32, (SUB, LANES), 0)
    codes = jnp.where(sub == 0, owner_ref[...], slot_ref[...])
    meta_ref[2 * gain_tiles] = codes.astype(jnp.float32).astype(jnp.bfloat16)
    steps = weights_ref.shape[0]
    small_ref[...] = jnp.zeros_like(small_ref)
    small_ref[0:steps, :] = weights_ref[...]
    for c in range(chunks):
        lanes = slice(c * LANES, (c + 1) * LANES)
        small_ref[steps : steps + 1, lanes] = offset_ref[c : c + 1, :].astype(jnp.float32)
    small_ref[4:6, 0 : pairs_ref.shape[1]] = pairs_ref[...].astype(jnp.float32)
    left = small_ref[...]
    for p in range(3):
        piece = left.astype(jnp.bfloat16)
        left = left - piece.astype(jnp.float32)
        for c in range(chunks):
            parts_ref[p * chunks + c] = piece[:, c * LANES : (c + 1) * LANES]

    at = chunks * capacity
    if near > 1:
        outs = list(outs[: near + 1]) + [None] + list(outs[near + 1 :])
        pairs = [(meta_ref, outs[x].at[pl.ds(at, depth)]) for x in with_gains(near)]
    else:
        pairs = [(meta_ref, outs[1])]
    at_small = at + depth if near > 1 else 0
    pairs += [(parts_ref, outs[0 if near > 1 else -1].at[pl.ds(at_small, 3 * chunks)])]
    start = len(moves) + PARTS
    sends = start_all(pairs, sems.at[pl.ds(start, len(pairs))])
    start += len(pairs)

    def place(r, carry):
        p = place_s[r]
        for c in range(chunks):
            flat_ref[p * chunks + c] = vis_ref[r, :, c * LANES : (c + 1) * LANES]
        return carry

    flat_ref = block_ref.reshape(devices * at, SUB, LANES)
    for i in range(PARTS):
        fetches[i].wait()
        lax.fori_loop(i * span, (i + 1) * span, place, 0, unroll=32)
    if near > 1:
        pairs = [
            (block_ref.at[x], outs[x].at[pl.ds(0, at)]) for x in range(devices) if x != near + 1
        ]
    else:
        pairs = [(block_ref, outs[0])]
    sends += start_all(pairs, sems.at[pl.ds(start, len(pairs))])
    for send in sends:
        send.wait()


def first_kernel(capacity, target, me_s, owner_hbm, vis_hbm, out_hbm, owner_s, list_s, vis_ref, block_ref, sems):
    rows = vis_ref.shape[0]
    chunks = vis_ref.shape[2] // LANES
    moves = start_all(((owner_hbm, owner_s), (vis_hbm, vis_ref)), sems)
    wanted = me_s[0] ^ target
    moves[0].wait()

    def note(r, k):
        list_s[k] = r
        return k + jnp.where(owner_s[r] == wanted, 1, 0)

    count = lax.fori_loop(0, rows, note, 0, unroll=32)
    moves[1].wait()

    def place(k, carry):
        r = list_s[k]
        for c in range(chunks):
            block_ref[chunks * k + c] = vis_ref[r, :, c * LANES : (c + 1) * LANES]
        return carry

    lax.fori_loop(0, count, place, 0)
    send = start_all([(block_ref, out_hbm)], sems)[0]
    send.wait()


def ready_kernel(
    at, chunks, owned, stations, trows, turn_s, own_ref, own_out_ref, choice_ref, basis_ref, sem
):
    move = pltpu.make_async_copy(own_ref, own_out_ref, sem)
    move.start()
    pieces = [
        jnp.concatenate(
            [own_ref[at + p * chunks + c].astype(jnp.float32) for c in range(chunks)], axis=1
        )
        for p in range(3)
    ]
    small = pieces[0] + pieces[1] + pieces[2]
    channels = small.shape[1]
    half = stations // 2

    station = small[4:6, 0:LANES]
    sender = jnp.floor((station + 0.5) * (1.0 / stations))
    within = station - sender * stations
    second = (within >= float(half)).astype(jnp.float32)
    line = (sender.astype(jnp.int32) ^ turn_s[0]).astype(jnp.float32) * trows + within - second * half
    diagonal = lax.broadcasted_iota(jnp.int32, (owned, LANES), 0) == lax.broadcasted_iota(
        jnp.int32, (owned, LANES), 1
    )

    def upright(row):
        return jnp.sum(jnp.where(diagonal, row, 0.0), axis=1, keepdims=True)

    lines = jnp.concatenate([upright(line[side : side + 1]) for side in range(2)], axis=0)
    seconds = jnp.concatenate([upright(second[side : side + 1]) for side in range(2)], axis=0)
    table = choice_ref.shape[1]
    same = lines == lax.broadcasted_iota(jnp.int32, (2 * owned, table), 1).astype(jnp.float32)
    for h in range(2):
        choice_ref[2 * owned * h : 2 * owned * (h + 1), :] = (
            jnp.where(jnp.logical_and(same, seconds == float(h)), 1.0, 0.0).astype(jnp.bfloat16)
        )

    index = lax.broadcasted_iota(jnp.int32, (64, channels), 0)
    knot = (index >> 3).astype(jnp.float32)
    basis = jnp.zeros((64, channels), jnp.float32)
    for step in range(3):
        basis = basis + jnp.where(knot == small[3:4, :] + float(step), small[step : step + 1, :], 0.0)
    high = basis.astype(jnp.bfloat16).astype(jnp.float32)
    component = index & 7
    for j in range(8):
        cols = slice(j * channels, (j + 1) * channels)
        main = jnp.where(component == j, high, 0.0).astype(jnp.bfloat16)
        rest = jnp.where(component == j, basis - high, 0.0).astype(jnp.bfloat16)
        basis_ref[0:64, cols] = main
        basis_ref[64:128, cols] = main
        basis_ref[128:192, cols] = rest
        basis_ref[192:256, cols] = jnp.zeros_like(rest)
    move.wait()


def collect_kernel(at, depth, *rest):
    blocks, (out_ref, sems) = rest[:-2], rest[-2:]
    moves = start_all(
        [
            (block.at[pl.ds(at, depth)], out_ref.at[pl.ds(i * depth, depth)])
            for i, block in enumerate(blocks)
        ],
        sems,
    )
    for move in moves:
        move.wait()


def list_rows(owner, slot, target, capacity, spare):
    senders = owner.shape[0]
    mine = owner == target
    counted = mine.astype(jnp.float32)
    before = lax.broadcasted_iota(jnp.int32, (LANES, LANES), 0) < lax.broadcasted_iota(
        jnp.int32, (LANES, LANES), 1
    )
    rank = jnp.dot(
        counted.astype(jnp.bfloat16),
        before.astype(jnp.float32).astype(jnp.bfloat16),
        preferred_element_type=jnp.float32,
    )
    lane = lax.broadcasted_iota(jnp.int32, (senders, LANES), 1)
    count = jnp.sum(counted, axis=1, keepdims=True)
    listing = jnp.where(lane == capacity, count, 0.0)
    for k in range(capacity):
        here = jnp.logical_and(mine, rank == float(k))
        kth = jnp.sum(jnp.where(here, slot, 0.0), axis=1, keepdims=True)
        kth = jnp.where(count > float(k), kth, float(spare))
        listing = jnp.where(lane == k, kth, listing)
    return listing.astype(jnp.int32), mine


def add_rows(acc_refs, slots_s, line, capacity, rows_ref):
    chunks, several = acc_refs[0].shape[0], len(acc_refs)

    def add(i, carry):
        for u, acc_ref in enumerate(acc_refs):
            k = several * i + u
            b = slots_s[line, k]
            for c in range(chunks):
                acc_ref[c, b] += rows_ref[chunks * k + c].astype(jnp.float32)
        return carry

    lax.fori_loop(0, (slots_s[line, capacity] + several - 1) // several, add, 0)


def add_table(table_ref, x, block, at, depth):
    gain_tiles = (depth - 1) // 2
    for i in range(gain_tiles):
        rows = slice((x * gain_tiles + i) * SUB, (x * gain_tiles + i + 1) * SUB)
        table_ref[rows, 0:LANES] = block[at + i].astype(jnp.float32)
        table_ref[rows, LANES : 2 * LANES] = block[at + gain_tiles + i].astype(jnp.float32)
    return block[at + 2 * gain_tiles].astype(jnp.float32)


def count_rows(hits, mine, slot):
    which = lax.broadcasted_iota(jnp.int32, hits.shape, 0).astype(jnp.float32)
    slot = jnp.where(mine, slot, -1.0)
    for x in range(slot.shape[0]):
        hits = hits + (slot[x : x + 1, :] == which).astype(jnp.float32)
    return hits


def middle_kernel(capacity, near, depth, order, me_s, choice_ref, basis_ref, *rest):
    arrived, passed = dict(zip(order, rest)), rest[len(order) : -12]
    gains_ref, recip_ref, slots_ref, sums_ref = rest[-12:-8]
    table_ref, owner_ref, slot_ref, slots_v, slots_s, one_ref, two_ref, sem = rest[-8:]
    devices = owner_ref.shape[0]
    owned = recip_ref.shape[0]
    chunks = sums_ref.shape[0]
    for x in range(devices):
        if near == 1:
            code = add_table(table_ref, x, arrived[0].at[x], 0, depth)
        elif x in with_gains(near):
            code = add_table(table_ref, x, arrived[x], chunks * capacity, depth)
        else:
            code = add_table(table_ref, x, passed[0], (x - near) // 2 * depth, depth)
        owner_ref[x : x + 1, :] = code[0:1, :]
        slot_ref[x : x + 1, :] = code[1:2, :]
    slot = slot_ref[...]
    listing, mine = list_rows(
        owner_ref[...], slot, me_s[0].astype(jnp.float32), capacity, owned
    )
    slots_ref[...] = listing
    slots_v[...] = listing
    move = pltpu.make_async_copy(slots_v, slots_s, sem)
    move.start()
    hits = count_rows(jnp.zeros((owned, LANES), jnp.float32), mine, slot)
    tally = jnp.sum(hits, axis=1, keepdims=True)
    recip_ref[...] = jnp.broadcast_to(1.0 / jnp.maximum(tally, 1.0), recip_ref.shape)

    picked = jnp.dot(
        choice_ref[...], table_ref[...].astype(jnp.bfloat16), preferred_element_type=jnp.float32
    )
    front, back = picked[0 : 2 * owned], picked[2 * owned : 4 * owned]
    lower = lax.broadcasted_iota(jnp.int32, (2 * owned, LANES), 1) < 64
    high = front[:, 0:LANES] + pltpu.roll(back[:, 0:LANES], 64, 1)
    low = pltpu.roll(front[:, LANES:], 64, 1) + back[:, LANES:]
    coarse = jnp.concatenate([jnp.where(lower, high, low), jnp.where(lower, high, 0.0)], axis=1)
    coarse = coarse.astype(jnp.bfloat16)
    width = 2 * LANES * chunks
    for n in range(0, basis_ref.shape[1], width):
        fine = jnp.dot(coarse, basis_ref[:, n : n + width], preferred_element_type=jnp.float32)
        gains_ref[:, n : n + width] = fine.astype(jnp.bfloat16).astype(jnp.float32)

    one_ref[...] = jnp.zeros_like(one_ref)
    two_ref[...] = jnp.zeros_like(two_ref)
    move.wait()
    if near > 1:
        for x in order:
            add_rows((one_ref, two_ref), slots_s, x, capacity, arrived[x])
    sums_ref[...] = one_ref[:, 0:owned] + two_ref[:, 0:owned]


def next_kernel(capacity, x, slots_ref, sums_ref, rows_ref, out_ref, slots_s, sem):
    move = pltpu.make_async_copy(slots_ref, slots_s, sem)
    move.start()
    out_ref[...] = sums_ref[...]
    move.wait()
    add_rows((out_ref,), slots_s, x, capacity, rows_ref)


def finish_kernel(capacity, last, slots_ref, gains_ref, recip_ref, sums_ref, *rest):
    far, (out_hbm, slots_s, acc_ref, res_ref, out_ref, sems) = rest[:-6], rest[-6:]
    owned, parts, channels = out_hbm.shape
    chunks = channels // LANES
    move = pltpu.make_async_copy(slots_ref, slots_s, sems.at[chunks])
    move.start()
    acc_ref[...] = sums_ref[...]
    move.wait()
    if last is not None:
        add_rows((acc_ref,), slots_s, last, capacity, far[0])
    else:

        def from_device(d, carry):
            add_rows((acc_ref,), slots_s, d, capacity, far[0].at[d])
            return carry

        lax.fori_loop(0, far[0].shape[0], from_device, 0)

    flat = acc_ref.reshape(chunks * owned * parts, LANES)
    done = res_ref.reshape(chunks * owned * parts, LANES)
    sends = []
    for c in range(chunks):
        for b0 in range(0, owned, SUB):
            scale = recip_ref[b0 : b0 + SUB, :]
            row = (c * owned + b0) * parts
            vis = [flat[pl.ds(row + j, SUB, stride=parts), :] for j in range(parts)]
            planes = [slice(j * channels + c * LANES, j * channels + (c + 1) * LANES) for j in range(parts)]
            lhs = [gains_ref[b0 : b0 + SUB, plane] for plane in planes]
            rhs = [gains_ref[owned + b0 : owned + b0 + SUB, plane] for plane in planes]
            mid_re, mid_im = [], []
            for row_a in range(2):
                for col_b in range(2):
                    re = im = 0.0
                    for inner in range(2):
                        lr, li = lhs[2 * row_a + inner], lhs[4 + 2 * row_a + inner]
                        vr, vi = vis[2 * inner + col_b], vis[4 + 2 * inner + col_b]
                        re = re + lr * vr - li * vi
                        im = im + lr * vi + li * vr
                    mid_re.append(re * scale)
                    mid_im.append(im * scale)
            for row_a in range(2):
                for col_b in range(2):
                    re = im = 0.0
                    for inner in range(2):
                        mr, mi = mid_re[2 * row_a + inner], mid_im[2 * row_a + inner]
                        rr, ri = rhs[2 * col_b + inner], rhs[4 + 2 * col_b + inner]
                        re = re + mr * rr + mi * ri
                        im = im + mi * rr - mr * ri
                    j = 2 * row_a + col_b
                    done[pl.ds(row + j, SUB, stride=parts), :] = re
                    done[pl.ds(row + 4 + j, SUB, stride=parts), :] = im
        out_ref[c] = res_ref[c].astype(out_ref.dtype)
        sends.append(
            pltpu.make_async_copy(
                out_ref.at[c], out_hbm.at[:, :, pl.ds(c * LANES, LANES)], sems.at[c]
            )
        )
        sends[-1].start()
    for send in sends:
        send.wait()


def on_device(
    visibilities,
    row_owner,
    row_slot,
    baseline_station_pairs,
    gains_coarse,
    band_weights,
    band_offset,
):
    devices = lax.axis_size("bl")
    rows, parts, channels = visibilities.shape
    capacity = 2 * rows // devices
    owned = baseline_station_pairs.shape[0]
    stations, _, knots = gains_coarse.shape
    chunks = channels // LANES
    gain_tiles = round_up(stations // 2, SUB) // SUB
    depth = 2 * gain_tiles + 1
    near = devices // 2 if devices <= 16 else 1
    halves = near > 1
    f32, bf16, i32 = jnp.float32, jnp.bfloat16, jnp.int32
    vmem = pl.BlockSpec(memory_space=pltpu.VMEM)
    smem = pl.BlockSpec(memory_space=pltpu.SMEM)
    hbm = pl.BlockSpec(memory_space=pltpu.HBM)
    anywhere = pl.BlockSpec(memory_space=pl.ANY)
    most = pltpu.CompilerParams(vmem_limit_bytes=ALL_VMEM)
    some = pltpu.CompilerParams(vmem_limit_bytes=SOME_VMEM)
    shape = jax.ShapeDtypeStruct
    dma = pltpu.SemaphoreType.DMA

    me = lax.axis_index("bl").astype(i32).reshape(1)
    turn = me if halves else jnp.zeros_like(me)
    owner = row_owner.reshape(rows)
    coarse = gains_coarse.transpose(2, 1, 0).reshape(knots * parts, stations)
    block = (chunks * capacity, parts, LANES)
    rows_at = chunks * capacity
    if halves:
        long = with_gains(near) + [near + 3]
        outs = [
            shape((rows_at + (depth if x in long else 0), parts, LANES), bf16)
            for x in range(devices)
        ]
        outs[0] = shape((rows_at + depth + 3 * chunks, parts, LANES), bf16)
    else:
        outs = [
            shape((devices,) + block, bf16),
            shape((depth, SUB, LANES), bf16),
            shape((3 * chunks, SUB, LANES), bf16),
        ]
    pairs = baseline_station_pairs.T
    weights = band_weights.T
    offset = band_offset.reshape(chunks, LANES)
    me_owner = row_owner.reshape(rows)
    if halves:
        first = outs.pop(near + 1)
        alone = pl.pallas_call(
            functools.partial(first_kernel, capacity, near + 1),
            out_shape=first,
            in_specs=[smem, hbm, hbm],
            out_specs=hbm,
            scratch_shapes=[
                pltpu.SMEM((rows,), i32),
                pltpu.SMEM((rows + 8,), i32),
                pltpu.VMEM((rows, parts, channels), bf16),
                pltpu.VMEM(first.shape, bf16),
                dma((2,)),
            ],
            compiler_params=most,
            name="pack_first",
        )(me, me_owner, visibilities)
    sent = pl.pallas_call(
        functools.partial(pack_kernel, capacity, near),
        out_shape=outs,
        in_specs=[smem] + [hbm] * 8,
        out_specs=[hbm] * len(outs),
        scratch_shapes=[
            pltpu.VMEM(weights.shape, f32),
            pltpu.VMEM(offset.shape, i32),
            pltpu.VMEM(pairs.shape, i32),
            pltpu.VMEM((SUB, channels), f32),
            pltpu.VMEM((3 * chunks, SUB, LANES), bf16),
            pltpu.SMEM((rows,), i32),
            pltpu.SMEM((rows,), i32),
            pltpu.SMEM((devices,), i32),
            pltpu.VMEM((1, rows), i32),
            pltpu.VMEM((1, rows), i32),
            pltpu.VMEM((rows, parts, channels), bf16),
            pltpu.VMEM((knots * parts, stations), f32),
            pltpu.VMEM((LANES, LANES), f32),
            pltpu.VMEM((depth, SUB, LANES), bf16),
            pltpu.VMEM((devices,) + block, bf16),
            dma((9 + PARTS + 2 * devices,)),
        ],
        compiler_params=most,
        name="pack_rows",
    )(
        turn,
        owner,
        row_owner.reshape(1, rows),
        row_slot.reshape(1, rows),
        visibilities,
        coarse,
        weights,
        offset,
        pairs,
    )


    trows = gain_tiles * SUB

    def ready(own, at):
        return pl.pallas_call(
            functools.partial(ready_kernel, at, chunks, owned, stations, trows),
            out_shape=[
                shape(own.shape, bf16),
                shape((4 * owned, devices * trows), bf16),
                shape((2 * LANES, parts * channels), bf16),
            ],
            in_specs=[smem, vmem],
            out_specs=[vmem] * 3,
            scratch_shapes=[dma],
            compiler_params=some,
            name="make_ready",
        )(turn, own)

    if halves:
        sent = list(sent)
        sent.insert(near + 1, alone)

    def swap(array, x):
        return lax.ppermute(array, "bl", [(d, d ^ x) for d in range(devices)])

    if halves:
        own, choice, basis = ready(sent[0], rows_at + depth)
        arrived = {x: swap(sent[x], x) if x else own for x in range(devices)}
        order, late = schedule(near)
        even = list(range(near, devices, 2))
        collected = pl.pallas_call(
            functools.partial(collect_kernel, rows_at, depth),
            out_shape=shape((len(even) * depth, parts, LANES), bf16),
            in_specs=[anywhere] * len(even),
            out_specs=vmem,
            scratch_shapes=[dma((len(even),))],
            compiler_params=some,
            name="collect_gains",
        )(*[arrived[x] for x in even])
        passed = [swap(collected, 1)]
    else:
        arrived = {
            0: lax.all_gather(sent[1], "bl", axis=0),
            1: lax.all_to_all(sent[0], "bl", split_axis=0, concat_axis=0, tiled=True),
        }
        order, late, passed = [0], [1], []
        _, choice, basis = ready(sent[2], 0)

    gains, recip, slots, sums = pl.pallas_call(
        functools.partial(middle_kernel, capacity, near, depth, order),
        out_shape=(
            shape((2 * owned, parts * channels), f32),
            shape((owned, LANES), f32),
            shape((devices, LANES), i32),
            shape((chunks, owned, parts, LANES), f32),
        ),
        in_specs=[smem] + [vmem] * (2 + len(order) + len(passed)),
        out_specs=(vmem,) * 4,
        scratch_shapes=[
            pltpu.VMEM((devices * trows, 2 * LANES), f32),
            pltpu.VMEM((devices, LANES), f32),
            pltpu.VMEM((devices, LANES), f32),
            pltpu.VMEM((devices, LANES), i32),
            pltpu.SMEM((devices, LANES), i32),
            pltpu.VMEM((chunks, owned + 1, parts, LANES), f32),
            pltpu.VMEM((chunks, owned + 1, parts, LANES), f32),
            dma,
        ],
        compiler_params=some,
        name="gains_and_sums",
    )(me, choice, basis, *[arrived[x] for x in order], *passed)
    if halves:
        before, last = late
        sums = pl.pallas_call(
            functools.partial(next_kernel, capacity, before),
            out_shape=shape(sums.shape, f32),
            in_specs=[anywhere, vmem, vmem],
            out_specs=vmem,
            scratch_shapes=[pltpu.SMEM((devices, LANES), i32), dma],
            compiler_params=some,
            name="sum_next",
        )(slots, sums, arrived[before])
    else:
        last = None
    return pl.pallas_call(
        functools.partial(finish_kernel, capacity, last),
        out_shape=shape((owned, parts, channels), bf16),
        in_specs=[anywhere] + [vmem] * 4,
        out_specs=hbm,
        scratch_shapes=[
            pltpu.SMEM((devices, LANES), i32),
            pltpu.VMEM((chunks, owned, parts, LANES), f32),
            pltpu.VMEM((chunks, owned, parts, LANES), f32),
            pltpu.VMEM((chunks, owned, parts, LANES), bf16),
            dma((chunks + 1,)),
        ],
        compiler_params=some,
        name="sum_and_apply",
    )(slots, gains, recip, sums, arrived[late[-1]])


def solution(mesh):
    placed = (
        P(("groups", "bl"), None, None),
        P(("groups", "bl"), None),
        P(("groups", "bl")),
        P("bl", None),
        P(("groups", "bl"), None, None),
        P("groups", None),
        P("groups"),
    )
    return jax.shard_map(
        on_device,
        mesh=mesh,
        in_specs=placed,
        out_specs=P(("groups", "bl"), None, None),
        check_vma=False,
    )
```
